32 devices in a mesh: ctx: 8 (over z, x), tp: 4 (over y, core).
Axes of the slice: x: 2, y: 2, z: 4, core: 2. Of those that a mesh axis runs over, the one named last changes fastest.
Arguments:
- tokens: bfloat16 [2, 2048, 2048], P(None, 'ctx'), may hold values from -6 to 6
- pair_index: int32 [2, 8], replicated, may hold values from 0 to 7, each once within a row
- norm_gain: bfloat16 [2048], P('ctx'), may hold values from 0.5 to 1.5
- norm_shift: bfloat16 [2048], P('ctx'), may hold values from -3 to 3
- w_attention_in: bfloat16 [3, 2048, 2048], P(None, 'ctx', 'tp'), may hold values from -0.1875 to 0.1875
- w_attention_out: bfloat16 [2048, 2048], P('tp', 'ctx'), may hold values from -0.5 to 0.5
- w_expand: bfloat16 [2048, 8192], P('ctx', 'tp'), may hold values from -0.125 to 0.125
- w_contract: bfloat16 [8192, 2048], P('tp', 'ctx'), may hold values from -0.09375 to 0.09375
- cotangent: bfloat16 [2, 2048, 2048], P(None, 'ctx'), may hold values from -6 to 6
Outputs:
- output: bfloat16 [2, 2048, 2048], P(None, 'ctx')
- input_grad: float32 [2, 2048, 2048], P(None, 'ctx')
- gain_grad: float32 [2048], P('ctx')
- shift_grad: float32 [2048], P('ctx')
- attention_in_grad: float32 [3, 2048, 2048], P(None, 'ctx', 'tp')
- attention_out_grad: float32 [2048, 2048], P('tp', 'ctx')
- expand_grad: float32 [2048, 8192], P('ctx', 'tp')
- contract_grad: float32 [8192, 2048], P('tp', 'ctx')
The draws below stay inside these ranges and needn't reach their ends.
Inputs may be any that keep to these rules, and one draw needn't show every extreme that they name: Each row is a permutation: context index c holds blocks pair_index[s, c] and 2 P - 1 - pair_index[s, c] of sequence s, each of 128 tokens, with P = 8.
All inputs are finite; a program needn't handle non-finite values.
Results may differ from the reference program's by a relative error of at most 0.023.
Values may be sent and summed in bfloat16 or wider, within the bound.
A program may use at most 320 MiB of HBM per device.

```python
import jax
import jax.numpy as jnp
from jax import lax

D = 2048
HEADS = 32
HEAD_DIM = 64
ROT = 32
FF = 8192
BLK = 128
SEQS = 2
TOK = 2048
N_CTX = 8


def raised(values, key, source, target, blocks, factor):
    def block_of(position):
        return (jnp.arange(values.shape[position]) // (values.shape[position] // blocks)).reshape((-1,) + (1,) * (values.ndim - 1 - position))

    one_side = jax.random.permutation(key, blocks)[block_of(target)]
    far = (block_of(target) + blocks // 2) % blocks
    return jnp.where((block_of(source) == one_side) | (block_of(source) == far), factor * values, values)


def steps_of(rng, shape, cuts, least, high):
    factor_of = 1.0
    for dim, parts in cuts:
        heights = jax.random.uniform(jax.random.fold_in(jax.random.fold_in(rng, 6), dim), (parts,), jnp.float32, least / len(cuts), high / len(cuts))
        factor_of = factor_of * jnp.repeat(jnp.exp(heights), shape[dim] // parts).reshape((-1,) + (1,) * (len(shape) - 1 - dim))
    return factor_of


def scatter_about(stream_key, shape, deviation, reach, split=(), kind=jnp.bfloat16):
    entries = deviation * jax.random.normal(stream_key, shape, jnp.float32)
    if split:
        entries = entries * steps_of(stream_key, shape, split, -0.22, 0.18)
    return jnp.clip(entries, -reach, reach).astype(kind)


def noise_with(key, dims, width, reach, shards, heavy, held_as=jnp.bfloat16):
    drawn = width * jax.random.normal(key, dims, jnp.float32)
    if shards:
        drawn = drawn * steps_of(key, dims, shards, -0.22, 0.18)
    return jnp.clip(raised(drawn, jax.random.fold_in(key, 3), *heavy), -reach, reach).astype(held_as)


def setup_inputs(seed: int = 0) -> dict:
    streams_of = jax.random.split(jax.random.key(seed), 10)
    return {
        "tokens": noise_with(streams_of[0], (SEQS, TOK, D), 1.0, 6.0, ((1, 8),), (1, 2, 8, 2.0)),
        "pair_index": jax.vmap(lambda own: jax.random.permutation(own, N_CTX))(jax.random.split(streams_of[1], SEQS)).reshape((SEQS, N_CTX)).astype(jnp.int32),
        "norm_gain": jnp.clip(1.0 + 0.1 * jax.random.normal(streams_of[2], (D,), jnp.float32), 0.5, 1.5).astype(jnp.bfloat16),
        "norm_shift": scatter_about(streams_of[3], (D,), 0.5, 3.0, ((0, 8),)),
        "w_attention_in": scatter_about(streams_of[4], (3, D, D), (D // 2) ** -0.5, 0.1875, ((1, 8), (2, 4))),
        "w_attention_out": scatter_about(streams_of[5], (D, D), (D // 16) ** -0.5, 0.5, ((0, 4), (1, 8))),
        "w_expand": scatter_about(streams_of[6], (D, FF), D ** -0.5, 0.125, ((0, 8), (1, 4))),
        "w_contract": scatter_about(streams_of[7], (FF, D), (FF // 2) ** -0.5, 0.09375, ((0, 4), (1, 8))),
        "cotangent": noise_with(streams_of[8], (SEQS, TOK, D), 1.0, 6.0, ((1, 8),), (1, 2, 8, 2.0)),
    }


@jax.custom_vjp
def low(v):
    return lax.optimization_barrier(v.astype(jnp.bfloat16)).astype(jnp.float32)

@jax.custom_vjp
def low_back(v):
    return v

def low_keep(v):
    return (low(v), None)

def low_pass(kept, grad):
    return (grad,)

def back_keep(v):
    return (v, None)

def back_low(kept, grad):
    return (low(grad),)
low.defvjp(low_keep, low_pass)
low_back.defvjp(back_keep, back_low)
epsilon = 1e-05
highest = lax.Precision.HIGHEST

def position_table(pair_index, shard_rows):
    pair_count = pair_index.shape[1]
    half_rows = shard_rows // 2
    token_index = jnp.arange(shard_rows * pair_count, dtype=jnp.int32)
    owning = token_index // shard_rows
    within = token_index % shard_rows
    picked = (owning[:, None] == jnp.arange(pair_count, dtype=jnp.int32)[None, :]).astype(jnp.int32)
    chosen = lax.optimization_barrier(jnp.sum(picked[None, :, :] * pair_index[:, None, :], axis=2))
    first_half = chosen * half_rows + within[None, :]
    second = (2 * pair_count - 1 - chosen) * half_rows + within[None, :] - half_rows
    return jnp.where(within[None, :] < half_rows, first_half, second).astype(jnp.int32)

def rotate(tensor, positions):
    half_rot = ROT // 2
    frequency = 10000.0 ** (-2.0 * jnp.arange(half_rot, dtype=jnp.float32) / ROT)
    angles = positions.astype(jnp.float32)[..., None] * frequency
    cosine = jnp.cos(angles)[..., None, :]
    sine_part = jnp.sin(angles)[..., None, :]
    leading = tensor[..., :half_rot]
    trailing = tensor[..., half_rot:ROT]
    return jnp.concatenate([leading * cosine - trailing * sine_part, trailing * cosine + leading * sine_part, tensor[..., ROT:]], axis=-1)

def gelu_tanh(values_in):
    return 0.5 * values_in * (1.0 + jnp.tanh(0.7978845608028654 * (values_in + 0.044715 * values_in * values_in * values_in)))

def layer_norm(inputs, gain_full, shift_full):
    centred = inputs - lax.optimization_barrier(jnp.mean(inputs, axis=-1, keepdims=True))
    spread = lax.optimization_barrier(jnp.mean(centred * centred, axis=-1, keepdims=True))
    return centred * lax.rsqrt(spread + epsilon) * gain_full + shift_full

def block_forward(inputs, gain_full, shift_full, w_attention_in, w_attention_out, w_expand, w_contract, positions):
    normed = low(layer_norm(inputs, gain_full, shift_full))
    projected = low_back(jnp.einsum('td,kde->kte', normed, w_attention_in, precision=highest))
    split_heads = projected.reshape(3, TOK, HEADS, HEAD_DIM)
    queries = low(rotate(split_heads[0], positions))
    keys_all = low(rotate(split_heads[1], positions))
    values_all = low(split_heads[2])
    block_rows = min(TOK, 512)

    def attend(block):
        query_block, query_pos = block
        raw_scores = jnp.einsum('qhe,khe->hqk', query_block, keys_all, precision=highest)
        scores = low_back(raw_scores) * HEAD_DIM ** (-0.5)
        allowed = positions[None, None, :] <= query_pos[None, :, None]
        scores = jnp.where(allowed, scores, -1e+30)
        row_peak = lax.optimization_barrier(jnp.max(scores, axis=-1, keepdims=True))
        weights = jnp.exp(scores - row_peak)
        probabilities = low(weights / lax.optimization_barrier(jnp.sum(weights, axis=-1, keepdims=True)))
        return jnp.einsum('hqk,khe->qhe', probabilities, values_all, precision=highest)
    attended = lax.map(jax.checkpoint(attend), (queries.reshape(TOK // block_rows, block_rows, HEADS, HEAD_DIM), positions.reshape(TOK // block_rows, block_rows)))
    mixed = low(low_back(attended.reshape(TOK, D)))
    attention = jnp.dot(mixed, w_attention_out, precision=highest)
    hidden_pre = low_back(jnp.dot(normed, w_expand, precision=highest))
    activated = low(gelu_tanh(hidden_pre))
    return inputs + attention + jnp.dot(activated, w_contract, precision=highest)

def reference(tokens, pair_index, norm_gain, norm_shift, w_attention_in, w_attention_out, w_expand, w_contract, cotangent):
    params = tuple((weight.astype(jnp.float32) for weight in (norm_gain, norm_shift, w_attention_in, w_attention_out, w_expand, w_contract)))
    positions = position_table(pair_index, 2 * BLK)

    def one_sequence(totals, sequence_item):
        inputs, upstream, sequence_pos = sequence_item

        def forward(inputs_full, *weights):
            return block_forward(inputs_full, *weights, sequence_pos)
        output, pullback = jax.vjp(forward, inputs.astype(jnp.float32), *params)
        gradients = pullback(upstream.astype(jnp.float32))
        updated = tuple((running + update for running, update in zip(totals, gradients[1:])))
        return (updated, (output.astype(jnp.bfloat16), gradients[0]))
    initial = tuple((jnp.zeros(weight.shape, jnp.float32) for weight in params))
    summed, (outputs, input_grad) = lax.scan(one_sequence, initial, (tokens, cotangent, positions))
    return (outputs, input_grad, summed[0], summed[1], summed[2], summed[3], summed[4], summed[5])
```

```python
import functools
import itertools

import jax
import jax.numpy as jnp
from jax import lax
from jax.experimental import pallas as pl
from jax.experimental.pallas import tpu as pltpu
from jax.sharding import PartitionSpec as P

HEAD_DIM = 64
ROT = 32


epsilon = 1e-05


def position_table(pair_index, shard_rows):
    pair_count = pair_index.shape[1]
    half_rows = shard_rows // 2
    token_index = jnp.arange(shard_rows * pair_count, dtype=jnp.int32)
    owning = token_index // shard_rows
    within = token_index % shard_rows
    picked = (owning[:, None] == jnp.arange(pair_count, dtype=jnp.int32)[None, :]).astype(jnp.int32)
    chosen = jnp.sum(picked[None, :, :] * pair_index[:, None, :], axis=2)
    first_half = chosen * half_rows + within[None, :]
    second = (2 * pair_count - 1 - chosen) * half_rows + within[None, :] - half_rows
    return jnp.where(within[None, :] < half_rows, first_half, second)


def rotate(tensor, positions):
    half_rot = ROT // 2
    frequency = 10000.0 ** (-2.0 * jnp.arange(half_rot, dtype=jnp.float32) / ROT)
    angles = positions.astype(jnp.float32)[..., None] * frequency
    cosine = jnp.cos(angles)[..., None, :]
    sine_part = jnp.sin(angles)[..., None, :]
    leading = tensor[..., :half_rot]
    trailing = tensor[..., half_rot:ROT]
    return jnp.concatenate(
        [
            leading * cosine - trailing * sine_part,
            trailing * cosine + leading * sine_part,
            tensor[..., ROT:],
        ],
        axis=-1,
    )


def gelu_tanh(values_in):
    return (
        0.5
        * values_in
        * (
            1.0
            + jnp.tanh(
                0.7978845608028654 * (values_in + 0.044715 * values_in * values_in * values_in)
            )
        )
    )


def layer_norm(inputs, gain_full, shift_full):
    centred = inputs - jnp.mean(inputs, axis=-1, keepdims=True)
    spread = jnp.mean(centred * centred, axis=-1, keepdims=True)
    return centred * lax.rsqrt(spread + epsilon) * gain_full + shift_full


def block_probs(queries, keys_block, log_total, query_pos, key_pos):
    raw_scores = jnp.einsum(
        "sqhe,skhe->shqk", queries, keys_block, preferred_element_type=jnp.float32
    )
    allowed = key_pos[:, None, None, :] <= query_pos[:, None, :, None]
    return jnp.where(allowed, jnp.exp(raw_scores * HEAD_DIM ** (-0.5) - log_total[..., None]), 0.0)


def score_grads(
    queries, keys_block, values_block, log_total, row_delta, out_grad, query_pos, key_pos
):
    probs_full = block_probs(queries, keys_block, log_total, query_pos, key_pos)
    prob_grad = jnp.einsum(
        "sqhe,skhe->shqk", out_grad, values_block, preferred_element_type=jnp.float32
    )
    score_grad = (probs_full * (prob_grad - row_delta[..., None]) * HEAD_DIM ** (-0.5)).astype(
        jnp.bfloat16
    )
    return (probs_full.astype(jnp.bfloat16), score_grad)


def key_slice(keys_all, offset, key_rows, head_count):
    seq_count = keys_all.shape[0]
    return lax.dynamic_slice_in_dim(keys_all, offset, key_rows, 1).reshape(
        seq_count, key_rows, head_count, HEAD_DIM
    )


def log_totals(queries, keys_all, query_pos, pos_table, key_rows):
    seq_count, query_rows, head_count, head_size = queries.shape
    turn_count = keys_all.shape[1] // key_rows

    def log_one_turn(turn_index, state_in):
        running_max, running_sum = state_in
        offset = turn_index * key_rows
        keys_block = key_slice(keys_all, offset, key_rows, head_count)
        key_pos = lax.dynamic_slice_in_dim(pos_table, offset, key_rows, 1)
        raw_scores = jnp.einsum(
            "sqhe,skhe->shqk", queries, keys_block, preferred_element_type=jnp.float32
        ) * HEAD_DIM ** (-0.5)
        allowed = key_pos[:, None, None, :] <= query_pos[:, None, :, None]
        masked = jnp.where(allowed, raw_scores, -1e30)
        new_max = jnp.maximum(running_max, jnp.max(masked, axis=-1))
        kept_terms = jnp.where(allowed, jnp.exp(masked - new_max[..., None]), 0.0)
        return (
            new_max,
            running_sum * jnp.exp(running_max - new_max) + jnp.sum(kept_terms, axis=-1),
        )

    initial = (
        jnp.full((seq_count, head_count, query_rows), -1e30, jnp.float32),
        jnp.zeros((seq_count, head_count, query_rows), jnp.float32),
    )
    final_max, final_sum = lax.fori_loop(0, turn_count, log_one_turn, initial)
    return final_max + jnp.log(final_sum)


def attend_values(queries, keys_all, values_all, log_total, query_pos, pos_table, key_rows):
    head_count = queries.shape[2]
    turn_count = keys_all.shape[1] // key_rows

    def attend_one_turn(turn_index, running):
        offset = turn_index * key_rows
        keys_block = key_slice(keys_all, offset, key_rows, head_count)
        values_block = key_slice(values_all, offset, key_rows, head_count)
        key_pos = lax.dynamic_slice_in_dim(pos_table, offset, key_rows, 1)
        weights_low = block_probs(queries, keys_block, log_total, query_pos, key_pos).astype(
            jnp.bfloat16
        )
        return running + jnp.einsum(
            "shqk,skhe->sqhe", weights_low, values_block, preferred_element_type=jnp.float32
        )

    return lax.fori_loop(0, turn_count, attend_one_turn, jnp.zeros(queries.shape, jnp.float32))


def full_grads(
    queries, keys_all, values_all, log_total, row_delta, out_grad, query_pos, pos_table, key_rows
):
    seq_count, query_rows, head_count, head_size = queries.shape
    turn_count = keys_all.shape[1] // key_rows

    def full_one_turn(turn_index, state_in):
        query_grad, key_terms, value_terms = state_in
        offset = turn_index * key_rows
        keys_block = key_slice(keys_all, offset, key_rows, head_count)
        values_block = key_slice(values_all, offset, key_rows, head_count)
        key_pos = lax.dynamic_slice_in_dim(pos_table, offset, key_rows, 1)
        weights_low, score_grad = score_grads(
            queries, keys_block, values_block, log_total, row_delta, out_grad, query_pos, key_pos
        )
        query_grad = query_grad + jnp.einsum(
            "shqk,skhe->sqhe", score_grad, keys_block, preferred_element_type=jnp.float32
        )
        key_part = jnp.einsum(
            "shqk,sqhe->skhe", score_grad, queries, preferred_element_type=jnp.float32
        ).reshape(seq_count, key_rows, head_count * head_size)
        value_part = jnp.einsum(
            "shqk,sqhe->skhe", weights_low, out_grad, preferred_element_type=jnp.float32
        ).reshape(seq_count, key_rows, head_count * head_size)
        key_terms = lax.dynamic_update_slice_in_dim(key_terms, key_part, offset, 1)
        value_terms = lax.dynamic_update_slice_in_dim(value_terms, value_part, offset, 1)
        return (query_grad, key_terms, value_terms)

    initial = (
        jnp.zeros(queries.shape, jnp.float32),
        jnp.zeros(keys_all.shape, jnp.float32),
        jnp.zeros(values_all.shape, jnp.float32),
    )
    return lax.fori_loop(0, turn_count, full_one_turn, initial)


def general_local(
    tokens,
    pair_index,
    norm_gain,
    norm_shift,
    w_attention_in,
    w_attention_out,
    w_expand,
    w_contract,
    cotangent,
):
    seq_count, shard_rows, model_width = tokens.shape
    gain_full, shift_full, attention_in, attention_out, expand_full, contract_full = (
        lax.all_gather(norm_gain, "ctx", axis=0, tiled=True),
        lax.all_gather(norm_shift, "ctx", axis=0, tiled=True),
        lax.all_gather(w_attention_in, "ctx", axis=1, tiled=True),
        lax.all_gather(w_attention_out, "ctx", axis=1, tiled=True),
        lax.all_gather(w_expand, "ctx", axis=0, tiled=True),
        lax.all_gather(w_contract, "ctx", axis=1, tiled=True),
    )
    local_width = attention_in.shape[2]
    head_count = local_width // HEAD_DIM
    flat_rows = seq_count * shard_rows
    pos_table = position_table(pair_index, shard_rows)
    total_rows = pos_table.shape[1]
    own_pos = lax.dynamic_slice_in_dim(pos_table, lax.axis_index("ctx") * shard_rows, shard_rows, 1)
    key_rows = min(total_rows, 1024)
    inputs = tokens.astype(jnp.float32)
    normed_full, norm_pull = jax.vjp(
        layer_norm, inputs, gain_full.astype(jnp.float32), shift_full.astype(jnp.float32)
    )
    normed = normed_full.astype(jnp.bfloat16).reshape(flat_rows, model_width)
    projected = jnp.einsum("td,kde->kte", normed, attention_in, preferred_element_type=jnp.float32)
    split_heads = projected.reshape(3, seq_count, shard_rows, head_count, HEAD_DIM)
    rotated, rotate_pull = jax.vjp(lambda pair_part: rotate(pair_part, own_pos), split_heads[:2])
    queries = rotated[0].astype(jnp.bfloat16)
    own_keys = rotated[1].astype(jnp.bfloat16)
    own_values = split_heads[2].astype(jnp.bfloat16)
    keys_all, values_all = (
        lax.all_gather(
            own_keys.reshape(seq_count, shard_rows, local_width), "ctx", axis=1, tiled=True
        ),
        lax.all_gather(
            own_values.reshape(seq_count, shard_rows, local_width), "ctx", axis=1, tiled=True
        ),
    )
    log_total = log_totals(queries, keys_all, own_pos, pos_table, key_rows)
    attended = attend_values(queries, keys_all, values_all, log_total, own_pos, pos_table, key_rows)
    mixed = attended.reshape(flat_rows, local_width).astype(jnp.bfloat16)
    hidden_pre = jnp.dot(normed, expand_full, preferred_element_type=jnp.float32)
    activated_full, gelu_pull = jax.vjp(gelu_tanh, hidden_pre)
    activated = activated_full.astype(jnp.bfloat16)
    branch = jnp.dot(mixed, attention_out, preferred_element_type=jnp.float32) + jnp.dot(
        activated, contract_full, preferred_element_type=jnp.float32
    )
    branch = lax.psum(branch.astype(jnp.bfloat16), "tp").astype(jnp.float32)
    output = (inputs + branch.reshape(seq_count, shard_rows, model_width)).astype(jnp.bfloat16)
    upstream = cotangent.reshape(flat_rows, model_width)
    contract_grad = jnp.einsum("tf,td->fd", activated, upstream, preferred_element_type=jnp.float32)
    (gelu_grad,) = gelu_pull(
        jnp.einsum("td,fd->tf", upstream, contract_full, preferred_element_type=jnp.float32)
    )
    hidden_grad = gelu_grad.astype(jnp.bfloat16)
    expand_grad = jnp.einsum("td,tf->df", normed, hidden_grad, preferred_element_type=jnp.float32)
    mixed_grad = jnp.einsum(
        "td,ed->te", upstream, attention_out, preferred_element_type=jnp.float32
    ).astype(jnp.bfloat16)
    attention_out_grad = jnp.einsum(
        "te,td->ed", mixed, upstream, preferred_element_type=jnp.float32
    )
    out_grad = mixed_grad.reshape(seq_count, shard_rows, head_count, HEAD_DIM)
    row_delta = jnp.sum(out_grad.astype(jnp.float32) * attended, axis=-1).transpose(0, 2, 1)
    query_grad, key_terms, value_terms = full_grads(
        queries, keys_all, values_all, log_total, row_delta, out_grad, own_pos, pos_table, key_rows
    )
    key_grad, value_grad = (
        lax.psum_scatter(
            key_terms.astype(jnp.bfloat16), "ctx", scatter_dimension=1, tiled=True
        ).astype(jnp.float32),
        lax.psum_scatter(
            value_terms.astype(jnp.bfloat16), "ctx", scatter_dimension=1, tiled=True
        ).astype(jnp.float32),
    )
    key_grad = key_grad.reshape(seq_count, shard_rows, head_count, HEAD_DIM)
    value_grad = value_grad.reshape(seq_count, shard_rows, head_count, HEAD_DIM)
    (rotated_grad,) = rotate_pull(jnp.stack([query_grad, key_grad]))
    projected_grad = (
        jnp.concatenate([rotated_grad, value_grad[None]], axis=0)
        .reshape(3, flat_rows, local_width)
        .astype(jnp.bfloat16)
    )
    attention_in_grad = jnp.einsum(
        "td,kte->kde", normed, projected_grad, preferred_element_type=jnp.float32
    )
    normed_grad = jnp.einsum(
        "kte,kde->td", projected_grad, attention_in, preferred_element_type=jnp.float32
    )
    normed_grad = normed_grad + jnp.einsum(
        "tf,df->td", hidden_grad, expand_full, preferred_element_type=jnp.float32
    )
    normed_grad = lax.psum(normed_grad.astype(jnp.bfloat16), "tp").astype(jnp.float32)
    input_part, gain_grad, shift_grad = norm_pull(
        normed_grad.reshape(seq_count, shard_rows, model_width)
    )
    input_grad = input_part + cotangent.astype(jnp.float32)
    reduced = (
        lax.psum_scatter(
            gain_grad.astype(jnp.bfloat16), "ctx", scatter_dimension=0, tiled=True
        ).astype(jnp.float32),
        lax.psum_scatter(
            shift_grad.astype(jnp.bfloat16), "ctx", scatter_dimension=0, tiled=True
        ).astype(jnp.float32),
        lax.psum_scatter(
            attention_in_grad.astype(jnp.bfloat16), "ctx", scatter_dimension=1, tiled=True
        ).astype(jnp.float32),
        lax.psum_scatter(
            attention_out_grad.astype(jnp.bfloat16), "ctx", scatter_dimension=1, tiled=True
        ).astype(jnp.float32),
        lax.psum_scatter(
            expand_grad.astype(jnp.bfloat16), "ctx", scatter_dimension=0, tiled=True
        ).astype(jnp.float32),
        lax.psum_scatter(
            contract_grad.astype(jnp.bfloat16), "ctx", scatter_dimension=1, tiled=True
        ).astype(jnp.float32),
    )
    return (
        output,
        input_grad,
        reduced[0],
        reduced[1],
        reduced[2],
        reduced[3],
        reduced[4],
        reduced[5],
    )


MESH = pl.DeviceIdType.MESH
MB = 1 << 20
EPS = 1e-05


def place():
    c = lax.axis_index("ctx")
    t = lax.axis_index("tp")
    return c // 2, c % 2, t // 2, t % 2


def device(z, x, y, k):
    return (z * 2 + x, y * 2 + k)


def remote(src, dst, send_sem, recv_sem, target):
    return pltpu.make_async_remote_copy(
        src_ref=src, dst_ref=dst, send_sem=send_sem, recv_sem=recv_sem,
        device_id=target, device_id_type=MESH,
    )


def meet(peers):
    barrier = pltpu.get_barrier_semaphore()
    for peer in peers:
        pl.semaphore_signal(barrier, inc=1, device_id=peer, device_id_type=MESH)
    pl.semaphore_wait(barrier, len(peers))


class TokenGather:
    def __init__(self, whole, sems):
        self.whole = whole
        self.xs, self.xr, self.zs, self.zr, self.ys, self.yr, self.cs, self.cr, self.loc = sems
        self.z, self.x, self.y, self.k = place()
        self.q = 2 * self.y + self.k

    def chunk(self, zz, s, q):
        xx = self.x if s == 0 else 1 - self.x
        return self.whole.at[zz, xx, pl.ds(64 * q, 64), :]

    def send_x(self, src):
        z, x, y, k = self.z, self.x, self.y, self.k
        return remote(src, self.whole.at[z, x, pl.ds(64 * self.q, 64), :], self.xs, self.xr, device(z, 1 - x, y, k))

    def send_up(self, zz, s, src):
        return remote(src, self.chunk(zz, s, self.q), self.zs.at[zz, s, 0], self.zr.at[zz, s],
                      device(jnp.minimum(self.z + 1, 3), self.x, self.y, self.k))

    def send_down(self, zz, s, src):
        return remote(src, self.chunk(zz, s, self.q), self.zs.at[zz, s, 1], self.zr.at[zz, s],
                      device(jnp.maximum(self.z - 1, 0), self.x, self.y, self.k))

    def send_y(self, zz, s):
        c = self.chunk(zz, s, self.q)
        return remote(c, c, self.ys.at[zz, s], self.yr.at[zz, s], device(self.z, self.x, 1 - self.y, self.k))

    def send_core(self, zz, s, j):
        yy = self.y if j == 0 else 1 - self.y
        c = self.chunk(zz, s, 2 * yy + self.k)
        return remote(c, c, self.cs.at[zz, s, j], self.cr.at[zz, s, j], device(self.z, self.x, self.y, 1 - self.k))

    def start(self, own_quarter, other_quarter, own_slot):
        z = self.z
        self.send_x(other_quarter).start()

        @pl.when(z < 3)
        def _():
            self.send_up(z, 0, own_quarter).start()

        @pl.when(z > 0)
        def _():
            self.send_down(z, 0, own_quarter).start()

        pltpu.make_async_copy(own_slot, self.whole.at[z, self.x], self.loc).start()

    def after_x(self):
        z = self.z
        c = self.chunk(z, 1, self.q)
        remote(c, c, self.xs, self.xr, device(z, 1 - self.x, self.y, self.k)).wait_recv()

        @pl.when(z < 3)
        def _():
            self.send_up(z, 1, c).start()

        @pl.when(z > 0)
        def _():
            self.send_down(z, 1, c).start()

        self.send_y(z, 1).start()
        self.send_core(z, 1, 0).start()

    def hop(self, d, s):
        z = self.z

        @pl.when(z >= d)
        def _():
            zz = z - d
            c = self.chunk(zz, s, self.q)
            self.send_down(zz, s, c).wait_recv()

            @pl.when(z < 3)
            def _():
                self.send_up(zz, s, c).start()

            self.send_y(zz, s).start()
            self.send_core(zz, s, 0).start()

        @pl.when(z + d <= 3)
        def _():
            zz = z + d
            c = self.chunk(zz, s, self.q)
            self.send_up(zz, s, c).wait_recv()

            @pl.when(z > 0)
            def _():
                self.send_down(zz, s, c).start()

            self.send_y(zz, s).start()
            self.send_core(zz, s, 0).start()

    def y_in(self, zz, s):
        c = self.chunk(zz, s, 2 * (1 - self.y) + self.k)
        remote(c, c, self.ys.at[zz, s], self.yr.at[zz, s], device(self.z, self.x, 1 - self.y, self.k)).wait_recv()
        self.send_core(zz, s, 1).start()

    def y_hop(self, d, s):
        z = self.z
        if d == 0:
            self.y_in(z, s)
            return

        @pl.when(z >= d)
        def _():
            self.y_in(z - d, s)

        @pl.when(z + d <= 3)
        def _():
            self.y_in(z + d, s)

    def finish(self, own_quarter, other_quarter, own_slot):
        z = self.z
        self.send_x(other_quarter).wait_send()
        pltpu.make_async_copy(own_slot, self.whole.at[z, self.x], self.loc).wait()
        for zz in range(4):
            for s in range(2):
                def rest():
                    self.send_y(zz, s).wait_send()
                    for j in range(2):
                        yy = self.y if j == 0 else 1 - self.y
                        c = self.chunk(zz, s, 2 * yy + 1 - self.k)
                        r = remote(c, c, self.cs.at[zz, s, j], self.cr.at[zz, s, j], device(self.z, self.x, self.y, 1 - self.k))
                        r.wait()
                if s == 0:
                    pl.when(z != zz)(rest)
                else:
                    rest()
                c = self.chunk(zz, s, self.q)

                @pl.when((z < 3) & (zz <= z))
                def _():
                    self.send_up(zz, s, c).wait_send()

                @pl.when((z > 0) & (zz >= z))
                def _():
                    self.send_down(zz, s, c).wait_send()


def token_sems():
    D = pltpu.SemaphoreType.DMA
    return [D, D, D((4, 2, 2)), D((4, 2)), D((4, 2)), D((4, 2)), D((4, 2, 2)), D((4, 2, 2)), D]


class WeightGather:
    def __init__(self, pairs, sems):
        self.pairs = pairs
        self.zs, self.zr, self.xs, self.xr, self.loc = sems
        self.z, self.x, self.y, self.k = place()

    def z_send(self, d, w):
        src, dst = self.pairs[w]
        z = self.z
        to = (z + d) % 4
        return remote(src(to), dst(z, self.x), self.zs.at[d, w], self.zr.at[d, w], device(to, self.x, self.y, self.k))

    def z_recv(self, d, w):
        src, dst = self.pairs[w]
        frm = (self.z - d + 4) % 4
        return remote(dst(frm, self.x), dst(frm, self.x), self.zs.at[d, w], self.zr.at[d, w], device(frm, self.x, self.y, self.k))

    def x_send(self, d, w):
        src, dst = self.pairs[w]
        frm = (self.z - d + 4) % 4
        s = src(self.z) if d == 0 else dst(frm, self.x)
        return remote(s, dst(frm, self.x), self.xs.at[d, w], self.xr.at[d, w], device(self.z, 1 - self.x, self.y, self.k))

    def x_recv(self, d, w):
        src, dst = self.pairs[w]
        frm = (self.z - d + 4) % 4
        r = dst(frm, 1 - self.x)
        return remote(r, r, self.xs.at[d, w], self.xr.at[d, w], device(self.z, 1 - self.x, self.y, self.k))

    def local(self, w):
        src, dst = self.pairs[w]
        return pltpu.make_async_copy(src(self.z), dst(self.z, self.x), self.loc.at[w])

    def start(self, ws, ds=(2, 3, 1)):
        for w in ws:
            for d in ds:
                self.z_send(d, w).start()
            self.x_send(0, w).start()
            self.local(w).start()

    def forward(self, w, d):
        self.z_recv(d, w).wait_recv()
        self.x_send(d, w).start()

    def finish(self, w):
        self.local(w).wait()
        for d in range(4):
            if d:
                self.z_send(d, w).wait_send()
            self.x_send(d, w).wait_send()
            self.x_recv(d, w).wait_recv()


def weight_sems(n):
    D = pltpu.SemaphoreType.DMA
    return [D((4, n)), D((4, n)), D((4, n)), D((4, n)), D((n,))]


def norm_rows(rows, gain, shift):
    v = rows.astype(jnp.float32)
    centred = v - jnp.mean(v, axis=-1, keepdims=True)
    spread = jnp.mean(centred * centred, axis=-1, keepdims=True)
    return (centred * lax.rsqrt(spread + EPS) * gain + shift).astype(jnp.bfloat16)


def gather_kernel(tok, gs, cot, win, wout, wexp, wcon,
                  xn_all, ct_all, win_all, wout_all, wexp_all, wcon_all, gs_all,
                  xn, gsem_s, gsem_r, *sems):
    z, x, y, k = place()
    c = z * 2 + x
    q = 2 * y + k
    nt, nw = len(token_sems()), len(weight_sems(4))
    tx = TokenGather(xn_all, sems[:nt])
    tc = TokenGather(ct_all, sems[nt:2 * nt])
    col = lambda n, i: pl.ds(pl.multiple_of(n * i, n), n)
    pairs = [
        (lambda zz: win.at[:, :, col(128, zz)], lambda zz, xx: win_all.at[:, zz, xx]),
        (lambda zz: wexp.at[:, col(512, zz)], lambda zz, xx: wexp_all.at[zz, xx]),
        (lambda zz: wcon.at[col(512, zz), :], lambda zz, xx: wcon_all.at[:, col(256, zz * 2 + xx)]),
        (lambda zz: wout.at[col(128, zz), :], lambda zz, xx: wout_all.at[:, col(256, zz * 2 + xx)]),
    ]
    wg = WeightGather(pairs, sems[2 * nt:])
    others = [((c + i) % 8, lax.axis_index("tp")) for i in range(1, 8)]
    meet(others + [device(z, x, 1 - y, k), device(z, x, y, 1 - k)])
    gcopies = [remote(gs, gs_all.at[c], gsem_s.at[i], gsem_r.at[i], others[i]) for i in range(7)]
    for g in gcopies:
        g.start()
    gs_all[c] = gs[...]
    cot_own, cot_other = cot.at[x, pl.ds(64 * q, 64)], cot.at[1 - x, pl.ds(64 * q, 64)]
    wg.start((0, 1))
    for i in range(7):
        frm = gs_all.at[(c - i - 1 + 8) % 8]
        remote(frm, frm, gsem_s.at[i], gsem_r.at[i], others[i]).wait_recv()
    gain = jnp.concatenate([gs_all[i, 0:1, :] for i in range(8)], axis=1)
    shift = jnp.concatenate([gs_all[i, 1:2, :] for i in range(8)], axis=1)

    @pl.loop(0, 4)
    def _(i):
        xn[pl.ds(256 + 16 * i, 16)] = norm_rows(tok[1 - x, pl.ds(64 * q + 16 * i, 16)], gain, shift)

    @pl.loop(0, 16)
    def _(i):
        xn[pl.ds(16 * i, 16)] = norm_rows(tok[x, pl.ds(16 * i, 16)], gain, shift)

    xsrc = (xn.at[pl.ds(64 * q, 64)], xn.at[pl.ds(256, 64)], xn.at[pl.ds(0, 256)])
    csrc = (cot_own, cot_other, cot.at[x])
    tx.start(*xsrc)
    tc.start(*csrc)
    wg.start((2, 3))
    tx.after_x()
    tc.after_x()
    for d in range(1, 4):
        for t in (tx, tc):
            for s in range(2):
                t.hop(d, s)
        for w in range(4):
            wg.forward(w, d)
        for t in (tx, tc):
            if d == 1:
                t.y_hop(0, 1)
            else:
                for s in range(2):
                    t.y_hop(d - 1, s)
    for t in (tx, tc):
        for s in range(2):
            t.y_hop(3, s)
    tx.finish(*xsrc)
    tc.finish(*csrc)
    for w in range(4):
        wg.finish(w)
    for g in gcopies:
        g.wait_send()


def gather_call(tokens, gs, cot, win, wout, wexp, wcon):
    bf = jnp.bfloat16
    S = jax.ShapeDtypeStruct
    ANY = pl.BlockSpec(memory_space=pl.ANY)
    VM = pl.BlockSpec(memory_space=pltpu.VMEM)
    D = pltpu.SemaphoreType.DMA
    return pl.pallas_call(
        gather_kernel,
        out_shape=[S((4, 2, 256, 2048), bf), S((4, 2, 256, 2048), bf), S((3, 4, 2, 256, 128), bf),
                   S((128, 2048), bf), S((4, 2, 256, 512), bf), S((512, 2048), bf), S((8, 8, 256), jnp.float32)],
        in_specs=[VM, VM] + [ANY] * 5,
        out_specs=[ANY] * 6 + [VM],
        scratch_shapes=[pltpu.VMEM((320, 2048), bf), D((7,)), D((7,))]
        + token_sems() * 2 + weight_sems(4),
        compiler_params=pltpu.CompilerParams(collective_id=0, has_side_effects=True, vmem_limit_bytes=48 * MB),
        name="gather",
    )(tokens, gs, cot, win, wout, wexp, wcon)


def add_into(dst, src):
    shape = dst.shape
    lead = shape[:-2]
    rows = shape[-2]
    for idx in itertools.product(*(range(n) for n in lead)):
        @pl.loop(0, rows // 16)
        def _(i):
            at = idx + (pl.ds(pl.multiple_of(16 * i, 16), 16), slice(None))
            dst[at] = (dst[at].astype(jnp.float32) + src[at].astype(jnp.float32)).astype(jnp.bfloat16)


class TokenReduce:
    def __init__(self, part, out, bufs, sems):
        self.part, self.out = part, out
        self.A, self.r1, self.r2, self.rz, self.rf = bufs
        (self.ld, self.cs, self.cr, self.ys, self.yr, self.zs, self.zr, self.xs, self.xr,
         self.fl, self.fys, self.fyr, self.fcs, self.fcr) = sems
        self.z, self.x, self.y, self.k = place()
        self.q = 2 * self.y + self.k

    def order(self, i):
        z = self.z
        if i == 0:
            return 3 * (1 - z // 2)
        if i == 1:
            return z // 2 + 2 * (1 - z % 2)
        if i == 2:
            return 1 + z % 2
        return z

    def rows(self, zz, yy, kk):
        return self.part.at[zz, :, pl.ds(64 * (2 * yy + kk), 64), :]

    def load(self, zz, yy):
        return pltpu.make_async_copy(self.rows(zz, yy, self.k), self.A.at[zz, yy], self.ld.at[zz, yy])

    def core(self, zz, yy):
        return remote(self.rows(zz, yy, 1 - self.k), self.r1.at[zz, yy], self.cs.at[zz, yy], self.cr.at[zz, yy],
                      device(self.z, self.x, self.y, 1 - self.k))

    def yex(self, zz):
        return remote(self.A.at[zz, 1 - self.y], self.r2.at[zz], self.ys.at[zz], self.yr.at[zz],
                      device(self.z, self.x, 1 - self.y, self.k))

    def up(self, zz):
        return remote(self.A.at[zz, self.y], self.rz.at[zz], self.zs.at[zz], self.zr.at[zz],
                      device(jnp.minimum(self.z + 1, 3), self.x, self.y, self.k))

    def down(self, zz):
        slot = jnp.where(zz == self.z - 1, 4, zz)
        return remote(self.A.at[zz, self.y], self.rz.at[slot], self.zs.at[zz], self.zr.at[slot],
                      device(jnp.maximum(self.z - 1, 0), self.x, self.y, self.k))

    def arrived(self, slot):
        remote(self.rz.at[slot], self.rz.at[slot], self.zs.at[0], self.zr.at[slot],
               device(self.z, self.x, self.y, 1 - self.k)).wait_recv()

    def xex(self):
        return remote(self.A.at[self.z, self.y, 1 - self.x], self.rf, self.xs, self.xr,
                      device(self.z, 1 - self.x, self.y, self.k))

    def start(self, i):
        zz = self.order(i)
        for yy in range(2):
            self.core(zz, yy).start()
            self.load(zz, yy).start()

    def after_core(self, i):
        zz = self.order(i)
        for yy in range(2):
            self.load(zz, yy).wait()
            self.core(zz, yy).wait_recv()
        add_into(self.A.at[zz], self.r1.at[zz])
        self.yex(zz).start()

    def after_y(self, i):
        zz = self.order(i)
        self.yex(zz).wait_recv()
        add_into(self.A.at[zz, self.y], self.r2.at[zz])

    def line(self, i):
        z = self.z
        zz = self.order(i)
        mine = self.A.at[zz, self.y]
        if i < 3:
            @pl.when(zz > z)
            def _():
                @pl.when(z > 0)
                def _():
                    self.arrived(zz)
                    add_into(mine, self.rz.at[zz])
                self.up(zz).start()

            @pl.when(zz < z)
            def _():
                @pl.when(z < 3)
                def _():
                    self.arrived(zz)
                    add_into(mine, self.rz.at[zz])
                self.down(zz).start()
        else:
            @pl.when(z > 0)
            def _():
                self.arrived(z)
                add_into(mine, self.rz.at[z])

            @pl.when(z < 3)
            def _():
                self.arrived(4)
                add_into(mine, self.rz.at[4])
            self.xex().start()

    def spot(self, s, q):
        return self.out.at[s, pl.ds(64 * q, 64), :]

    def fin(self, s):
        return (self.A.at[self.z, self.y, self.x], self.x) if s == 0 else (self.rf, 1 - self.x)

    def fin_copies(self, s):
        src, seq = self.fin(s)
        here = self.spot(seq, self.q)
        return (pltpu.make_async_copy(src, here, self.fl.at[s]),
                remote(src, here, self.fys.at[s], self.fyr.at[s], device(self.z, self.x, 1 - self.y, self.k)),
                remote(src, here, self.fcs.at[s, 0], self.fcr.at[s, 0], device(self.z, self.x, self.y, 1 - self.k)))

    def relay(self, s):
        seq = self.x if s == 0 else 1 - self.x
        r = self.spot(seq, 2 * (1 - self.y) + self.k)
        return remote(r, r, self.fcs.at[s, 1], self.fcr.at[s, 1], device(self.z, self.x, self.y, 1 - self.k))

    def spread(self, s):
        if s == 1:
            self.xex().wait_recv()
        for cp in self.fin_copies(s):
            cp.start()

    def spread_y(self, s):
        seq = self.x if s == 0 else 1 - self.x
        r = self.spot(seq, 2 * (1 - self.y) + self.k)
        remote(r, r, self.fys.at[s], self.fyr.at[s], device(self.z, self.x, 1 - self.y, self.k)).wait_recv()
        self.relay(s).start()

    def finish(self):
        z = self.z
        for zz in range(4):
            for yy in range(2):
                self.core(zz, yy).wait_send()
            self.yex(zz).wait_send()

            @pl.when(z != zz)
            def _():
                self.up(zz).wait_send()
        self.xex().wait_send()
        for s in range(2):
            seq = self.x if s == 0 else 1 - self.x
            a, b, c = self.fin_copies(s)
            a.wait()
            b.wait_send()
            c.wait_send()
            self.relay(s).wait_send()
            for j, yy in ((0, self.y), (1, 1 - self.y)):
                r = self.spot(seq, 2 * yy + 1 - self.k)
                remote(r, r, self.fcs.at[s, j], self.fcr.at[s, j], device(self.z, self.x, self.y, 1 - self.k)).wait_recv()


def reduce_sems():
    D = pltpu.SemaphoreType.DMA
    return [D((4, 2)), D((4, 2)), D((4, 2)), D((4,)), D((4,)), D((4,)), D((5,)), D, D,
            D((2,)), D((2,)), D((2,)), D((2, 2)), D((2, 2))]


def reduce_bufs():
    V = lambda *s: pltpu.VMEM(s, jnp.bfloat16)
    return [V(4, 2, 2, 64, 2048), V(4, 2, 2, 64, 2048), V(4, 2, 64, 2048), V(5, 2, 64, 2048), V(64, 2048)]


class GradReduce:
    def __init__(self, pairs, own, got, sems):
        self.pairs, self.own, self.got = pairs, own, got
        self.ld, self.xs, self.xr, self.zs, self.zr = sems
        self.z, self.x, self.y, self.k = place()

    def load(self, d, w):
        zz = (self.z + d) % 4
        return pltpu.make_async_copy(self.pairs[w][0](zz, self.x), self.own[w].at[d], self.ld.at[d, w])

    def xex(self, d, w):
        zz = (self.z + d) % 4
        return remote(self.pairs[w][0](zz, 1 - self.x), self.got[w].at[d], self.xs.at[d, w], self.xr.at[d, w],
                      device(self.z, 1 - self.x, self.y, self.k))

    def zex(self, d, w):
        zz = (self.z + d) % 4
        return remote(self.own[w].at[d], self.pairs[w][1](self.z), self.zs.at[d, w], self.zr.at[d, w],
                      device(zz, self.x, self.y, self.k))

    def keep(self, w):
        return pltpu.make_async_copy(self.own[w].at[0], self.pairs[w][1](self.z), self.zs.at[0, w])

    def start(self, d, w):
        self.xex(d, w).start()
        self.load(d, w).start()

    def after_x(self, d, w):
        self.load(d, w).wait()
        self.xex(d, w).wait_recv()
        add_into(self.own[w].at[d], self.got[w].at[d])
        if d:
            self.zex(d, w).start()
        else:
            self.keep(w).start()

    def finish(self, w):
        self.keep(w).wait()
        for d in range(4):
            self.xex(d, w).wait_send()
            if d:
                self.zex(d, w).wait_send()
                frm = (self.z - d + 4) % 4
                r = self.pairs[w][1](frm)
                remote(r, r, self.zs.at[d, w], self.zr.at[d, w], device(frm, self.x, self.y, self.k)).wait_recv()


BLOCKS = ((3, 256, 128), (256, 512), (512, 256), (128, 256))


def grad_bufs():
    return [pltpu.VMEM((4,) + b, jnp.bfloat16) for b in BLOCKS] * 2


def grad_sems():
    D = pltpu.SemaphoreType.DMA
    return [D((4, 4)) for _ in range(5)]


def reduce_kernel(po, pn, gin, gexp, gcon, gout, o_out, o_ng, o_gin, o_gexp, o_gcon, o_gout, *scratch):
    z, x, y, k = place()
    scratch = list(scratch)
    take = lambda n: [scratch.pop(0) for _ in range(n)]
    nb, ns = len(reduce_bufs()), len(reduce_sems())
    to = TokenReduce(po, o_out, take(nb), take(ns))
    tn = TokenReduce(pn, o_ng, take(nb), take(ns))
    col = lambda n, i: pl.ds(pl.multiple_of(n * i, n), n)
    pairs = [
        (lambda zz, xx: gin.at[:, zz, xx], lambda zz: o_gin.at[:, :, col(128, zz)]),
        (lambda zz, xx: gexp.at[zz, xx], lambda zz: o_gexp.at[:, col(512, zz)]),
        (lambda zz, xx: gcon.at[:, col(256, zz * 2 + xx)], lambda zz: o_gcon.at[col(512, zz), :]),
        (lambda zz, xx: gout.at[:, col(256, zz * 2 + xx)], lambda zz: o_gout.at[col(128, zz), :]),
    ]
    g = GradReduce(pairs, take(4), take(4), take(5))
    meet([device((z + d) % 4, x, y, k) for d in (1, 2, 3)] + [device(z, 1 - x, y, k), device(z, x, 1 - y, k), device(z, x, y, 1 - k)])
    ts = (to, tn)
    for i in range(4):
        for t in ts:
            t.start(i)
    for d in (2, 3, 1, 0):
        for w in range(4):
            g.start(d, w)
    for i in range(5):
        if i < 4:
            for t in ts:
                t.after_core(i)
        if i >= 1:
            for t in ts:
                t.after_y(i - 1)
                t.line(i - 1)
        if i < 4:
            for w in range(4):
                g.after_x((2, 3, 1, 0)[i], w)
    for s in range(2):
        for t in ts:
            t.spread(s)
    for s in range(2):
        for t in ts:
            t.spread_y(s)
    for t in ts:
        t.finish()
    for w in range(4):
        g.finish(w)


def reduce_call(po, pn, gin, gexp, gcon, gout):
    bf = jnp.bfloat16
    S = jax.ShapeDtypeStruct
    ANY = pl.BlockSpec(memory_space=pl.ANY)
    return pl.pallas_call(
        reduce_kernel,
        out_shape=[S((2, 256, 2048), bf), S((2, 256, 2048), bf), S((3, 256, 512), bf), S((256, 2048), bf), S((2048, 256), bf), S((512, 256), bf)],
        in_specs=[ANY] * 6,
        out_specs=[ANY] * 6,
        scratch_shapes=(reduce_bufs() + reduce_sems()) * 2 + grad_bufs() + grad_sems(),
        compiler_params=pltpu.CompilerParams(collective_id=1, has_side_effects=True, vmem_limit_bytes=56 * MB),
        name="reduce",
    )(po, pn, gin, gexp, gcon, gout)


NT = (((1,), (1,)), ((), ()))


def dot(a, b):
    return jnp.dot(a, b, preferred_element_type=jnp.float32)


def turn(v, tab, back=False):
    cos, lo, hi = tab
    if back:
        return v * cos - pltpu.roll(v, 112, 1) * lo - pltpu.roll(v, 16, 1) * hi
    return v * cos + pltpu.roll(v, 112, 1) * lo + pltpu.roll(v, 16, 1) * hi


def attention_kernel(inv, proj, do, tab, mixed, pg, q, k, v, qt, kt, vt, dos, dot_, ot, dqt, dk, dv):
    n = q.shape[1]
    nb = n // 128
    half = nb // 2

    def source(b):
        pair = jnp.where(b < half, b, nb - 1 - b)
        return pl.multiple_of(inv[pair] * 256 + jnp.where(b < half, 0, 128), 128)

    @pl.loop(0, nb)
    def _(b):
        src = pl.ds(source(b), 128)
        here = pl.ds(pl.multiple_of(b * 128, 128), 128)
        t = [tab[i, here] for i in range(3)]
        rq = turn(proj[0, src], t).astype(jnp.bfloat16) * jnp.bfloat16(0.125)
        rk = turn(proj[1, src], t).astype(jnp.bfloat16)
        rv = proj[2, src].astype(jnp.bfloat16)
        g = do[src]
        qT, kT, vT, gT = (a.astype(jnp.float32).T.astype(jnp.bfloat16) for a in (rq, rk, rv, g))
        for h in range(2):
            at = slice(64 * h, 64 * h + 64)
            q[h, here], k[h, here], v[h, here], dos[h, here] = rq[:, at], rk[:, at], rv[:, at], g[:, at]
            qt[h, :, here], kt[h, :, here], vt[h, :, here], dot_[h, :, here] = qT[at], kT[at], vT[at], gT[at]

    dk[...] = jnp.zeros_like(dk)
    dv[...] = jnp.zeros_like(dv)

    @pl.loop(0, 2)
    def _(h):
        for i in range(n // 256):
            kr = 256 * (i + 1)
            here = pl.ds(256 * i, 256)
            gT = dot_[h, :, here]
            st = dot(k[h, :kr], qt[h, :, here])
            row = lax.broadcasted_iota(jnp.int32, (256, 256), 0)
            column = lax.broadcasted_iota(jnp.int32, (256, 256), 1)
            last = jnp.where(row <= column, st[kr - 256:], -1e30)
            st = last if i == 0 else jnp.concatenate([st[:kr - 256], last], axis=0)
            peak = jnp.max(st, axis=0, keepdims=True)
            p = jnp.exp(st - peak)
            p = p * (1.0 / jnp.sum(p, axis=0, keepdims=True))
            low = p.astype(jnp.bfloat16)
            o = dot(vt[h, :, :kr], low)
            ot[h, :, here] = o
            delta = jnp.sum(o * gT.astype(jnp.float32), axis=0, keepdims=True)
            ds = (p * (dot(v[h, :kr], gT) - delta)).astype(jnp.bfloat16)
            dv[h, :kr] += dot(low, dos[h, here])
            dk[h, :kr] += dot(ds, q[h, here])
            dqt[h, :, here] = dot(kt[h, :, :kr], ds) * 0.125

    @pl.loop(0, nb)
    def _(b):
        dst = pl.ds(source(b), 128)
        here = pl.ds(pl.multiple_of(b * 128, 128), 128)
        t = [tab[i, here] for i in range(3)]
        mixed[dst] = jnp.concatenate([ot[0, :, here], ot[1, :, here]], axis=0).T.astype(jnp.bfloat16)
        gq = jnp.concatenate([dqt[0, :, here], dqt[1, :, here]], axis=0).T
        gk = jnp.concatenate([dk[0, here], dk[1, here]], axis=1)
        gv = jnp.concatenate([dv[0, here], dv[1, here]], axis=1)
        pg[0, dst] = turn_back(gq, t).astype(jnp.bfloat16)
        pg[1, dst] = turn_back(gk, t).astype(jnp.bfloat16)
        pg[2, dst] = gv.astype(jnp.bfloat16)


def turn_back(v, tab):
    cos, lo, hi = tab
    return v * cos - pltpu.roll(v, 112, 1) * lo - pltpu.roll(v, 16, 1) * hi


def tables(n):
    half = 16
    frequency = 10000.0 ** (-2.0 * jnp.arange(half, dtype=jnp.float32) / 32)
    angles = jnp.arange(n, dtype=jnp.int32).astype(jnp.float32)[:, None] * frequency
    c, s = jnp.cos(angles), jnp.sin(angles)
    one, zero = jnp.ones((n, 32), jnp.float32), jnp.zeros((n, 16), jnp.float32)
    cos = jnp.concatenate([c, c, one] * 2, axis=1)
    lo = jnp.concatenate([-s, zero, zero, zero] * 2, axis=1)
    hi = jnp.concatenate([zero, s, zero, zero] * 2, axis=1)
    return jnp.stack([cos, lo, hi])


def attention_call(inv, proj, do, tab):
    n = proj.shape[1]
    bf, f4 = jnp.bfloat16, jnp.float32
    S = jax.ShapeDtypeStruct
    VM = pl.BlockSpec(memory_space=pltpu.VMEM)
    V = pltpu.VMEM
    return pl.pallas_call(
        attention_kernel,
        out_shape=[S((n, 128), bf), S((3, n, 128), bf)],
        in_specs=[pl.BlockSpec(memory_space=pltpu.SMEM)] + [VM] * 3,
        out_specs=[VM] * 2,
        scratch_shapes=[V((2, n, 64), bf)] * 3 + [V((2, 64, n), bf)] * 3 + [V((2, n, 64), bf), V((2, 64, n), bf)]
        + [V((2, 64, n), f4)] * 2 + [V((2, n, 64), f4)] * 2,
        compiler_params=pltpu.CompilerParams(vmem_limit_bytes=56 * MB),
        name="attention",
    )(inv, proj, do, tab)

def own_local(tokens, pair_index, norm_gain, norm_shift, w_attention_in, w_attention_out, w_expand, w_contract, cotangent):
    f4, bf = jnp.float32, jnp.bfloat16
    dots = functools.partial(jnp.einsum, preferred_element_type=f4)
    x = lax.axis_index("ctx") % 2
    pairs = lax.dynamic_index_in_dim(pair_index, x, 0, False)
    which = jnp.arange(8, dtype=jnp.int32)
    inverse = jnp.sum(jnp.where(pairs[None, :] == which[:, None], which[None, :], 0), axis=1).astype(jnp.int32)
    gs = jnp.concatenate([norm_gain[None], norm_shift[None], jnp.zeros((6, 256), bf)], axis=0).astype(f4)
    xn, ct, win, wout, wexp, wcon, gs_all = gather_call(tokens, gs, cotangent, w_attention_in, w_attention_out, w_expand, w_contract)
    xn, ct = xn.reshape(2048, 2048), ct.reshape(2048, 2048)
    win, wexp = win.reshape(3, 2048, 128), wexp.reshape(2048, 512)
    proj = dots("td,kde->kte", xn, win)
    mixed_grad = dots("td,ed->te", ct, wout).astype(bf)
    mixed, pg = attention_call(inverse, proj, mixed_grad, tables(2048))
    hidden = dots("td,df->tf", xn, wexp)
    activated_full, pull = jax.vjp(gelu_tanh, hidden)
    activated = activated_full.astype(bf)
    out_part = (dots("te,ed->td", mixed, wout) + dots("tf,fd->td", activated, wcon)).astype(bf)
    gcon = dots("tf,td->fd", activated, ct).astype(bf)
    hidden_grad = pull(dots("td,fd->tf", ct, wcon))[0].astype(bf)
    gout = dots("te,td->ed", mixed, ct).astype(bf)
    gexp = dots("td,tf->df", xn, hidden_grad).astype(bf)
    gin = dots("td,kte->kde", xn, pg).astype(bf)
    ng_part = (dots("kte,kde->td", pg, win) + dots("tf,df->td", hidden_grad, wexp)).astype(bf)
    out_sum, ng, gin, gexp, gcon, gout = reduce_call(
        out_part.reshape(4, 2, 256, 2048), ng_part.reshape(4, 2, 256, 2048),
        gin.reshape(3, 4, 2, 256, 128), gexp.reshape(4, 2, 256, 512), gcon, gout)
    inputs = tokens.astype(f4)
    output = (inputs + out_sum.astype(f4)).astype(bf)
    gain, shift = gs_all[:, 0].reshape(2048), gs_all[:, 1].reshape(2048)
    _, norm_pull = jax.vjp(layer_norm, inputs, gain, shift)
    input_part, gain_grad, shift_grad = norm_pull(ng.astype(f4))
    gain_grad, shift_grad = (
        lax.psum_scatter(g, "ctx", scatter_dimension=0, tiled=True) for g in (gain_grad, shift_grad)
    )
    return (output, input_part + cotangent.astype(f4), gain_grad, shift_grad,
            gin.astype(f4), gout.astype(f4), gexp.astype(f4), gcon.astype(f4))


def local(tokens, pair_index, norm_gain, norm_shift, w_attention_in, w_attention_out, w_expand, w_contract, cotangent):
    args = (tokens, pair_index, norm_gain, norm_shift, w_attention_in, w_attention_out, w_expand, w_contract, cotangent)
    sizes = (lax.axis_size("ctx"), lax.axis_size("tp")) + tokens.shape + w_attention_in.shape[2:] + w_expand.shape[1:]
    if sizes == (8, 4, 2, 256, 2048, 512, 2048):
        return own_local(*args)
    return general_local(*args)


def solution(mesh):
    in_specs = (
        P(None, "ctx", None),
        P(),
        P("ctx"),
        P("ctx"),
        P(None, "ctx", "tp"),
        P("tp", "ctx"),
        P("ctx", "tp"),
        P("tp", "ctx"),
        P(None, "ctx", None),
    )
    out_specs = (
        P(None, "ctx", None),
        P(None, "ctx", None),
        P("ctx"),
        P("ctx"),
        P(None, "ctx", "tp"),
        P("tp", "ctx"),
        P("ctx", "tp"),
        P("tp", "ctx"),
    )
    return jax.shard_map(local, mesh=mesh, in_specs=in_specs, out_specs=out_specs, check_vma=False)
```

```python
import functools
import itertools

import jax
import jax.numpy as jnp
import numpy as np
from jax import lax
from jax.experimental import pallas as pl
from jax.experimental.pallas import tpu as pltpu
from jax.sharding import PartitionSpec as P

HEAD_DIM = 64
ROT = 32


epsilon = 1e-05


def position_table(pair_index, shard_rows):
    pair_count = pair_index.shape[1]
    half_rows = shard_rows // 2
    token_index = jnp.arange(shard_rows * pair_count, dtype=jnp.int32)
    owning = token_index // shard_rows
    within = token_index % shard_rows
    picked = (owning[:, None] == jnp.arange(pair_count, dtype=jnp.int32)[None, :]).astype(jnp.int32)
    chosen = jnp.sum(picked[None, :, :] * pair_index[:, None, :], axis=2)
    first_half = chosen * half_rows + within[None, :]
    second = (2 * pair_count - 1 - chosen) * half_rows + within[None, :] - half_rows
    return jnp.where(within[None, :] < half_rows, first_half, second)


def rotate(tensor, positions):
    half_rot = ROT // 2
    frequency = 10000.0 ** (-2.0 * jnp.arange(half_rot, dtype=jnp.float32) / ROT)
    angles = positions.astype(jnp.float32)[..., None] * frequency
    cosine = jnp.cos(angles)[..., None, :]
    sine_part = jnp.sin(angles)[..., None, :]
    leading = tensor[..., :half_rot]
    trailing = tensor[..., half_rot:ROT]
    return jnp.concatenate(
        [
            leading * cosine - trailing * sine_part,
            trailing * cosine + leading * sine_part,
            tensor[..., ROT:],
        ],
        axis=-1,
    )


def gelu_tanh(values_in):
    return (
        0.5
        * values_in
        * (
            1.0
            + jnp.tanh(
                0.7978845608028654 * (values_in + 0.044715 * values_in * values_in * values_in)
            )
        )
    )


def layer_norm(inputs, gain_full, shift_full):
    centred = inputs - jnp.mean(inputs, axis=-1, keepdims=True)
    spread = jnp.mean(centred * centred, axis=-1, keepdims=True)
    return centred * lax.rsqrt(spread + epsilon) * gain_full + shift_full


def block_probs(queries, keys_block, log_total, query_pos, key_pos):
    raw_scores = jnp.einsum(
        "sqhe,skhe->shqk", queries, keys_block, preferred_element_type=jnp.float32
    )
    allowed = key_pos[:, None, None, :] <= query_pos[:, None, :, None]
    return jnp.where(allowed, jnp.exp(raw_scores * HEAD_DIM ** (-0.5) - log_total[..., None]), 0.0)


def score_grads(
    queries, keys_block, values_block, log_total, row_delta, out_grad, query_pos, key_pos
):
    probs_full = block_probs(queries, keys_block, log_total, query_pos, key_pos)
    prob_grad = jnp.einsum(
        "sqhe,skhe->shqk", out_grad, values_block, preferred_element_type=jnp.float32
    )
    score_grad = (probs_full * (prob_grad - row_delta[..., None]) * HEAD_DIM ** (-0.5)).astype(
        jnp.bfloat16
    )
    return (probs_full.astype(jnp.bfloat16), score_grad)


def key_slice(keys_all, offset, key_rows, head_count):
    seq_count = keys_all.shape[0]
    return lax.dynamic_slice_in_dim(keys_all, offset, key_rows, 1).reshape(
        seq_count, key_rows, head_count, HEAD_DIM
    )


def log_totals(queries, keys_all, query_pos, pos_table, key_rows):
    seq_count, query_rows, head_count, head_size = queries.shape
    turn_count = keys_all.shape[1] // key_rows

    def log_one_turn(turn_index, state_in):
        running_max, running_sum = state_in
        offset = turn_index * key_rows
        keys_block = key_slice(keys_all, offset, key_rows, head_count)
        key_pos = lax.dynamic_slice_in_dim(pos_table, offset, key_rows, 1)
        raw_scores = jnp.einsum(
            "sqhe,skhe->shqk", queries, keys_block, preferred_element_type=jnp.float32
        ) * HEAD_DIM ** (-0.5)
        allowed = key_pos[:, None, None, :] <= query_pos[:, None, :, None]
        masked = jnp.where(allowed, raw_scores, -1e30)
        new_max = jnp.maximum(running_max, jnp.max(masked, axis=-1))
        kept_terms = jnp.where(allowed, jnp.exp(masked - new_max[..., None]), 0.0)
        return (
            new_max,
            running_sum * jnp.exp(running_max - new_max) + jnp.sum(kept_terms, axis=-1),
        )

    initial = (
        jnp.full((seq_count, head_count, query_rows), -1e30, jnp.float32),
        jnp.zeros((seq_count, head_count, query_rows), jnp.float32),
    )
    final_max, final_sum = lax.fori_loop(0, turn_count, log_one_turn, initial)
    return final_max + jnp.log(final_sum)


def attend_values(queries, keys_all, values_all, log_total, query_pos, pos_table, key_rows):
    head_count = queries.shape[2]
    turn_count = keys_all.shape[1] // key_rows

    def attend_one_turn(turn_index, running):
        offset = turn_index * key_rows
        keys_block = key_slice(keys_all, offset, key_rows, head_count)
        values_block = key_slice(values_all, offset, key_rows, head_count)
        key_pos = lax.dynamic_slice_in_dim(pos_table, offset, key_rows, 1)
        weights_low = block_probs(queries, keys_block, log_total, query_pos, key_pos).astype(
            jnp.bfloat16
        )
        return running + jnp.einsum(
            "shqk,skhe->sqhe", weights_low, values_block, preferred_element_type=jnp.float32
        )

    return lax.fori_loop(0, turn_count, attend_one_turn, jnp.zeros(queries.shape, jnp.float32))


def full_grads(
    queries, keys_all, values_all, log_total, row_delta, out_grad, query_pos, pos_table, key_rows
):
    seq_count, query_rows, head_count, head_size = queries.shape
    turn_count = keys_all.shape[1] // key_rows

    def full_one_turn(turn_index, state_in):
        query_grad, key_terms, value_terms = state_in
        offset = turn_index * key_rows
        keys_block = key_slice(keys_all, offset, key_rows, head_count)
        values_block = key_slice(values_all, offset, key_rows, head_count)
        key_pos = lax.dynamic_slice_in_dim(pos_table, offset, key_rows, 1)
        weights_low, score_grad = score_grads(
            queries, keys_block, values_block, log_total, row_delta, out_grad, query_pos, key_pos
        )
        query_grad = query_grad + jnp.einsum(
            "shqk,skhe->sqhe", score_grad, keys_block, preferred_element_type=jnp.float32
        )
        key_part = jnp.einsum(
            "shqk,sqhe->skhe", score_grad, queries, preferred_element_type=jnp.float32
        ).reshape(seq_count, key_rows, head_count * head_size)
        value_part = jnp.einsum(
            "shqk,sqhe->skhe", weights_low, out_grad, preferred_element_type=jnp.float32
        ).reshape(seq_count, key_rows, head_count * head_size)
        key_terms = lax.dynamic_update_slice_in_dim(key_terms, key_part, offset, 1)
        value_terms = lax.dynamic_update_slice_in_dim(value_terms, value_part, offset, 1)
        return (query_grad, key_terms, value_terms)

    initial = (
        jnp.zeros(queries.shape, jnp.float32),
        jnp.zeros(keys_all.shape, jnp.float32),
        jnp.zeros(values_all.shape, jnp.float32),
    )
    return lax.fori_loop(0, turn_count, full_one_turn, initial)


def general_local(
    tokens,
    pair_index,
    norm_gain,
    norm_shift,
    w_attention_in,
    w_attention_out,
    w_expand,
    w_contract,
    cotangent,
):
    seq_count, shard_rows, model_width = tokens.shape
    gain_full, shift_full, attention_in, attention_out, expand_full, contract_full = (
        lax.all_gather(norm_gain, "ctx", axis=0, tiled=True),
        lax.all_gather(norm_shift, "ctx", axis=0, tiled=True),
        lax.all_gather(w_attention_in, "ctx", axis=1, tiled=True),
        lax.all_gather(w_attention_out, "ctx", axis=1, tiled=True),
        lax.all_gather(w_expand, "ctx", axis=0, tiled=True),
        lax.all_gather(w_contract, "ctx", axis=1, tiled=True),
    )
    local_width = attention_in.shape[2]
    head_count = local_width // HEAD_DIM
    flat_rows = seq_count * shard_rows
    pos_table = position_table(pair_index, shard_rows)
    total_rows = pos_table.shape[1]
    own_pos = lax.dynamic_slice_in_dim(pos_table, lax.axis_index("ctx") * shard_rows, shard_rows, 1)
    key_rows = min(total_rows, 1024)
    inputs = tokens.astype(jnp.float32)
    normed_full, norm_pull = jax.vjp(
        layer_norm, inputs, gain_full.astype(jnp.float32), shift_full.astype(jnp.float32)
    )
    normed = normed_full.astype(jnp.bfloat16).reshape(flat_rows, model_width)
    projected = jnp.einsum("td,kde->kte", normed, attention_in, preferred_element_type=jnp.float32)
    split_heads = projected.reshape(3, seq_count, shard_rows, head_count, HEAD_DIM)
    rotated, rotate_pull = jax.vjp(lambda pair_part: rotate(pair_part, own_pos), split_heads[:2])
    queries = rotated[0].astype(jnp.bfloat16)
    own_keys = rotated[1].astype(jnp.bfloat16)
    own_values = split_heads[2].astype(jnp.bfloat16)
    keys_all, values_all = (
        lax.all_gather(
            own_keys.reshape(seq_count, shard_rows, local_width), "ctx", axis=1, tiled=True
        ),
        lax.all_gather(
            own_values.reshape(seq_count, shard_rows, local_width), "ctx", axis=1, tiled=True
        ),
    )
    log_total = log_totals(queries, keys_all, own_pos, pos_table, key_rows)
    attended = attend_values(queries, keys_all, values_all, log_total, own_pos, pos_table, key_rows)
    mixed = attended.reshape(flat_rows, local_width).astype(jnp.bfloat16)
    hidden_pre = jnp.dot(normed, expand_full, preferred_element_type=jnp.float32)
    activated_full, gelu_pull = jax.vjp(gelu_tanh, hidden_pre)
    activated = activated_full.astype(jnp.bfloat16)
    branch = jnp.dot(mixed, attention_out, preferred_element_type=jnp.float32) + jnp.dot(
        activated, contract_full, preferred_element_type=jnp.float32
    )
    branch = lax.psum(branch.astype(jnp.bfloat16), "tp").astype(jnp.float32)
    output = (inputs + branch.reshape(seq_count, shard_rows, model_width)).astype(jnp.bfloat16)
    upstream = cotangent.reshape(flat_rows, model_width)
    contract_grad = jnp.einsum("tf,td->fd", activated, upstream, preferred_element_type=jnp.float32)
    (gelu_grad,) = gelu_pull(
        jnp.einsum("td,fd->tf", upstream, contract_full, preferred_element_type=jnp.float32)
    )
    hidden_grad = gelu_grad.astype(jnp.bfloat16)
    expand_grad = jnp.einsum("td,tf->df", normed, hidden_grad, preferred_element_type=jnp.float32)
    mixed_grad = jnp.einsum(
        "td,ed->te", upstream, attention_out, preferred_element_type=jnp.float32
    ).astype(jnp.bfloat16)
    attention_out_grad = jnp.einsum(
        "te,td->ed", mixed, upstream, preferred_element_type=jnp.float32
    )
    out_grad = mixed_grad.reshape(seq_count, shard_rows, head_count, HEAD_DIM)
    row_delta = jnp.sum(out_grad.astype(jnp.float32) * attended, axis=-1).transpose(0, 2, 1)
    query_grad, key_terms, value_terms = full_grads(
        queries, keys_all, values_all, log_total, row_delta, out_grad, own_pos, pos_table, key_rows
    )
    key_grad, value_grad = (
        lax.psum_scatter(
            key_terms.astype(jnp.bfloat16), "ctx", scatter_dimension=1, tiled=True
        ).astype(jnp.float32),
        lax.psum_scatter(
            value_terms.astype(jnp.bfloat16), "ctx", scatter_dimension=1, tiled=True
        ).astype(jnp.float32),
    )
    key_grad = key_grad.reshape(seq_count, shard_rows, head_count, HEAD_DIM)
    value_grad = value_grad.reshape(seq_count, shard_rows, head_count, HEAD_DIM)
    (rotated_grad,) = rotate_pull(jnp.stack([query_grad, key_grad]))
    projected_grad = (
        jnp.concatenate([rotated_grad, value_grad[None]], axis=0)
        .reshape(3, flat_rows, local_width)
        .astype(jnp.bfloat16)
    )
    attention_in_grad = jnp.einsum(
        "td,kte->kde", normed, projected_grad, preferred_element_type=jnp.float32
    )
    normed_grad = jnp.einsum(
        "kte,kde->td", projected_grad, attention_in, preferred_element_type=jnp.float32
    )
    normed_grad = normed_grad + jnp.einsum(
        "tf,df->td", hidden_grad, expand_full, preferred_element_type=jnp.float32
    )
    normed_grad = lax.psum(normed_grad.astype(jnp.bfloat16), "tp").astype(jnp.float32)
    input_part, gain_grad, shift_grad = norm_pull(
        normed_grad.reshape(seq_count, shard_rows, model_width)
    )
    input_grad = input_part + cotangent.astype(jnp.float32)
    reduced = (
        lax.psum_scatter(
            gain_grad.astype(jnp.bfloat16), "ctx", scatter_dimension=0, tiled=True
        ).astype(jnp.float32),
        lax.psum_scatter(
            shift_grad.astype(jnp.bfloat16), "ctx", scatter_dimension=0, tiled=True
        ).astype(jnp.float32),
        lax.psum_scatter(
            attention_in_grad.astype(jnp.bfloat16), "ctx", scatter_dimension=1, tiled=True
        ).astype(jnp.float32),
        lax.psum_scatter(
            attention_out_grad.astype(jnp.bfloat16), "ctx", scatter_dimension=1, tiled=True
        ).astype(jnp.float32),
        lax.psum_scatter(
            expand_grad.astype(jnp.bfloat16), "ctx", scatter_dimension=0, tiled=True
        ).astype(jnp.float32),
        lax.psum_scatter(
            contract_grad.astype(jnp.bfloat16), "ctx", scatter_dimension=1, tiled=True
        ).astype(jnp.float32),
    )
    return (
        output,
        input_grad,
        reduced[0],
        reduced[1],
        reduced[2],
        reduced[3],
        reduced[4],
        reduced[5],
    )


MESH = pl.DeviceIdType.MESH
MB = 1 << 20
EPS = 1e-05


def place():
    c = lax.axis_index("ctx")
    t = lax.axis_index("tp")
    return c // 2, c % 2, t // 2, t % 2


def device(z, x, y, k):
    return (z * 2 + x, y * 2 + k)


def remote(src, dst, send_sem, recv_sem, target):
    return pltpu.make_async_remote_copy(
        src_ref=src, dst_ref=dst, send_sem=send_sem, recv_sem=recv_sem,
        device_id=target, device_id_type=MESH,
    )


def meet(peers):
    barrier = pltpu.get_barrier_semaphore()
    for peer in peers:
        pl.semaphore_signal(barrier, inc=1, device_id=peer, device_id_type=MESH)
    pl.semaphore_wait(barrier, len(peers))


class TokenGather:
    def __init__(self, whole, sems):
        self.whole = whole
        self.xs, self.xr, self.zs, self.zr, self.ys, self.yr, self.cs, self.cr, self.loc = sems
        self.z, self.x, self.y, self.k = place()
        self.q = 2 * self.y + self.k

    def chunk(self, zz, s, q):
        xx = self.x if s == 0 else 1 - self.x
        return self.whole.at[zz, xx, pl.ds(64 * q, 64), :]

    def send_x(self, src):
        z, x, y, k = self.z, self.x, self.y, self.k
        return remote(src, self.whole.at[z, x, pl.ds(64 * self.q, 64), :], self.xs, self.xr, device(z, 1 - x, y, k))

    def send_up(self, zz, s, src):
        return remote(src, self.chunk(zz, s, self.q), self.zs.at[zz, s, 0], self.zr.at[zz, s],
                      device(jnp.minimum(self.z + 1, 3), self.x, self.y, self.k))

    def send_down(self, zz, s, src):
        return remote(src, self.chunk(zz, s, self.q), self.zs.at[zz, s, 1], self.zr.at[zz, s],
                      device(jnp.maximum(self.z - 1, 0), self.x, self.y, self.k))

    def send_y(self, zz, s):
        c = self.chunk(zz, s, self.q)
        return remote(c, c, self.ys.at[zz, s], self.yr.at[zz, s], device(self.z, self.x, 1 - self.y, self.k))

    def send_core(self, zz, s, j):
        yy = self.y if j == 0 else 1 - self.y
        c = self.chunk(zz, s, 2 * yy + self.k)
        return remote(c, c, self.cs.at[zz, s, j], self.cr.at[zz, s, j], device(self.z, self.x, self.y, 1 - self.k))

    def start(self, own_quarter, other_quarter, own_slot):
        z = self.z
        self.send_x(other_quarter).start()

        @pl.when(z < 3)
        def _():
            self.send_up(z, 0, own_quarter).start()

        @pl.when(z > 0)
        def _():
            self.send_down(z, 0, own_quarter).start()

        pltpu.make_async_copy(own_slot, self.whole.at[z, self.x], self.loc).start()

    def after_x(self):
        z = self.z
        c = self.chunk(z, 1, self.q)
        remote(c, c, self.xs, self.xr, device(z, 1 - self.x, self.y, self.k)).wait_recv()

        @pl.when(z < 3)
        def _():
            self.send_up(z, 1, c).start()

        @pl.when(z > 0)
        def _():
            self.send_down(z, 1, c).start()

        self.send_y(z, 1).start()
        self.send_core(z, 1, 0).start()

    def hop(self, d, s):
        z = self.z

        @pl.when(z >= d)
        def _():
            zz = z - d
            c = self.chunk(zz, s, self.q)
            self.send_down(zz, s, c).wait_recv()

            @pl.when(z < 3)
            def _():
                self.send_up(zz, s, c).start()

            self.send_y(zz, s).start()
            self.send_core(zz, s, 0).start()

        @pl.when(z + d <= 3)
        def _():
            zz = z + d
            c = self.chunk(zz, s, self.q)
            self.send_up(zz, s, c).wait_recv()

            @pl.when(z > 0)
            def _():
                self.send_down(zz, s, c).start()

            self.send_y(zz, s).start()
            self.send_core(zz, s, 0).start()

    def y_in(self, zz, s):
        c = self.chunk(zz, s, 2 * (1 - self.y) + self.k)
        remote(c, c, self.ys.at[zz, s], self.yr.at[zz, s], device(self.z, self.x, 1 - self.y, self.k)).wait_recv()
        self.send_core(zz, s, 1).start()

    def y_hop(self, d, s):
        z = self.z
        if d == 0:
            self.y_in(z, s)
            return

        @pl.when(z >= d)
        def _():
            self.y_in(z - d, s)

        @pl.when(z + d <= 3)
        def _():
            self.y_in(z + d, s)

    def finish(self, own_quarter, other_quarter, own_slot):
        z = self.z
        self.send_x(other_quarter).wait_send()
        pltpu.make_async_copy(own_slot, self.whole.at[z, self.x], self.loc).wait()
        for zz in range(4):
            for s in range(2):
                def rest():
                    self.send_y(zz, s).wait_send()
                    for j in range(2):
                        yy = self.y if j == 0 else 1 - self.y
                        c = self.chunk(zz, s, 2 * yy + 1 - self.k)
                        r = remote(c, c, self.cs.at[zz, s, j], self.cr.at[zz, s, j], device(self.z, self.x, self.y, 1 - self.k))
                        r.wait()
                if s == 0:
                    pl.when(z != zz)(rest)
                else:
                    rest()
                c = self.chunk(zz, s, self.q)

                @pl.when((z < 3) & (zz <= z))
                def _():
                    self.send_up(zz, s, c).wait_send()

                @pl.when((z > 0) & (zz >= z))
                def _():
                    self.send_down(zz, s, c).wait_send()


def token_sems():
    D = pltpu.SemaphoreType.DMA
    return [D, D, D((4, 2, 2)), D((4, 2)), D((4, 2)), D((4, 2)), D((4, 2, 2)), D((4, 2, 2)), D]


class WeightGather:
    def __init__(self, pairs, sems):
        self.pairs = pairs
        self.zs, self.zr, self.xs, self.xr, self.loc = sems
        self.z, self.x, self.y, self.k = place()

    def z_send(self, d, w):
        src, dst = self.pairs[w]
        z = self.z
        to = (z + d) % 4
        return remote(src(to), dst(z, self.x), self.zs.at[d, w], self.zr.at[d, w], device(to, self.x, self.y, self.k))

    def z_recv(self, d, w):
        src, dst = self.pairs[w]
        frm = (self.z - d + 4) % 4
        return remote(dst(frm, self.x), dst(frm, self.x), self.zs.at[d, w], self.zr.at[d, w], device(frm, self.x, self.y, self.k))

    def x_send(self, d, w):
        src, dst = self.pairs[w]
        frm = (self.z - d + 4) % 4
        s = src(self.z) if d == 0 else dst(frm, self.x)
        return remote(s, dst(frm, self.x), self.xs.at[d, w], self.xr.at[d, w], device(self.z, 1 - self.x, self.y, self.k))

    def x_recv(self, d, w):
        src, dst = self.pairs[w]
        frm = (self.z - d + 4) % 4
        r = dst(frm, 1 - self.x)
        return remote(r, r, self.xs.at[d, w], self.xr.at[d, w], device(self.z, 1 - self.x, self.y, self.k))

    def local(self, w):
        src, dst = self.pairs[w]
        return pltpu.make_async_copy(src(self.z), dst(self.z, self.x), self.loc.at[w])

    def start(self, ws, ds=(2, 3, 1)):
        for w in ws:
            for d in ds:
                self.z_send(d, w).start()
            self.x_send(0, w).start()
            self.local(w).start()

    def forward(self, w, d):
        self.z_recv(d, w).wait_recv()
        self.x_send(d, w).start()

    def finish(self, w):
        self.local(w).wait()
        for d in range(4):
            if d:
                self.z_send(d, w).wait_send()
            self.x_send(d, w).wait_send()
            self.x_recv(d, w).wait_recv()


def weight_sems(n):
    D = pltpu.SemaphoreType.DMA
    return [D((4, n)), D((4, n)), D((4, n)), D((4, n)), D((n,))]


def norm_rows(rows, gain, shift):
    v = rows.astype(jnp.float32)
    centred = v - jnp.mean(v, axis=-1, keepdims=True)
    spread = jnp.mean(centred * centred, axis=-1, keepdims=True)
    return (centred * lax.rsqrt(spread + EPS) * gain + shift).astype(jnp.bfloat16)


def gather_kernel(tok, gs, cot, win, wout, wexp, wcon,
                  xn_all, ct_all, win_all, wout_all, wexp_all, wcon_all, gs_all,
                  xn, gsem_s, gsem_r, *sems):
    z, x, y, k = place()
    c = z * 2 + x
    q = 2 * y + k
    nt, nw = len(token_sems()), len(weight_sems(4))
    tx = TokenGather(xn_all, sems[:nt])
    tc = TokenGather(ct_all, sems[nt:2 * nt])
    col = lambda n, i: pl.ds(pl.multiple_of(n * i, n), n)
    pairs = [
        (lambda zz: win.at[:, :, col(128, zz)], lambda zz, xx: win_all.at[:, zz, xx]),
        (lambda zz: wexp.at[:, col(512, zz)], lambda zz, xx: wexp_all.at[zz, xx]),
        (lambda zz: wcon.at[col(512, zz), :], lambda zz, xx: wcon_all.at[:, col(256, zz * 2 + xx)]),
        (lambda zz: wout.at[col(128, zz), :], lambda zz, xx: wout_all.at[:, col(256, zz * 2 + xx)]),
    ]
    wg = WeightGather(pairs, sems[2 * nt:])
    others = [((c + i) % 8, lax.axis_index("tp")) for i in range(1, 8)]
    meet(others + [device(z, x, 1 - y, k), device(z, x, y, 1 - k)])
    gcopies = [remote(gs, gs_all.at[c], gsem_s.at[i], gsem_r.at[i], others[i]) for i in range(7)]
    for g in gcopies:
        g.start()
    gs_all[c] = gs[...]
    cot_own, cot_other = cot.at[x, pl.ds(64 * q, 64)], cot.at[1 - x, pl.ds(64 * q, 64)]
    wg.start((0, 1))
    for i in range(7):
        frm = gs_all.at[(c - i - 1 + 8) % 8]
        remote(frm, frm, gsem_s.at[i], gsem_r.at[i], others[i]).wait_recv()
    gain = jnp.concatenate([gs_all[i, 0:1, :] for i in range(8)], axis=1)
    shift = jnp.concatenate([gs_all[i, 1:2, :] for i in range(8)], axis=1)

    @pl.loop(0, 4)
    def _(i):
        xn[pl.ds(256 + 16 * i, 16)] = norm_rows(tok[1 - x, pl.ds(64 * q + 16 * i, 16)], gain, shift)

    @pl.loop(0, 16)
    def _(i):
        xn[pl.ds(16 * i, 16)] = norm_rows(tok[x, pl.ds(16 * i, 16)], gain, shift)

    xsrc = (xn.at[pl.ds(64 * q, 64)], xn.at[pl.ds(256, 64)], xn.at[pl.ds(0, 256)])
    csrc = (cot_own, cot_other, cot.at[x])
    tx.start(*xsrc)
    tc.start(*csrc)
    wg.start((2, 3))
    tx.after_x()
    tc.after_x()
    for d in range(1, 4):
        for t in (tx, tc):
            for s in range(2):
                t.hop(d, s)
        for w in range(4):
            wg.forward(w, d)
        for t in (tx, tc):
            if d == 1:
                t.y_hop(0, 1)
            else:
                for s in range(2):
                    t.y_hop(d - 1, s)
    for t in (tx, tc):
        for s in range(2):
            t.y_hop(3, s)
    tx.finish(*xsrc)
    tc.finish(*csrc)
    for w in range(4):
        wg.finish(w)
    for g in gcopies:
        g.wait_send()


def gather_call(tokens, gs, cot, win, wout, wexp, wcon):
    bf = jnp.bfloat16
    S = jax.ShapeDtypeStruct
    ANY = pl.BlockSpec(memory_space=pl.ANY)
    VM = pl.BlockSpec(memory_space=pltpu.VMEM)
    D = pltpu.SemaphoreType.DMA
    return pl.pallas_call(
        gather_kernel,
        out_shape=[S((4, 2, 256, 2048), bf), S((4, 2, 256, 2048), bf), S((3, 4, 2, 256, 128), bf),
                   S((128, 2048), bf), S((4, 2, 256, 512), bf), S((512, 2048), bf), S((8, 8, 256), jnp.float32)],
        in_specs=[VM, VM] + [ANY] * 5,
        out_specs=[ANY] * 6 + [VM],
        scratch_shapes=[pltpu.VMEM((320, 2048), bf), D((7,)), D((7,))]
        + token_sems() * 2 + weight_sems(4),
        compiler_params=pltpu.CompilerParams(collective_id=0, has_side_effects=True, vmem_limit_bytes=48 * MB),
        name="gather",
    )(tokens, gs, cot, win, wout, wexp, wcon)


def add_into(dst, src):
    shape = dst.shape
    lead = shape[:-2]
    rows = shape[-2]
    for idx in itertools.product(*(range(n) for n in lead)):
        @pl.loop(0, rows // 16)
        def _(i):
            at = idx + (pl.ds(pl.multiple_of(16 * i, 16), 16), slice(None))
            dst[at] = (dst[at].astype(jnp.float32) + src[at].astype(jnp.float32)).astype(jnp.bfloat16)


class TokenReduce:
    def __init__(self, part, out, bufs, sems):
        self.part, self.out = part, out
        self.A, self.r1, self.r2, self.rz, self.rf = bufs
        (self.ld, self.cs, self.cr, self.ys, self.yr, self.zs, self.zr, self.xs, self.xr,
         self.fl, self.fys, self.fyr, self.fcs, self.fcr) = sems
        self.z, self.x, self.y, self.k = place()
        self.q = 2 * self.y + self.k

    def order(self, i):
        z = self.z
        if i == 0:
            return 3 * (1 - z // 2)
        if i == 1:
            return z // 2 + 2 * (1 - z % 2)
        if i == 2:
            return 1 + z % 2
        return z

    def rows(self, zz, yy, kk):
        return self.part.at[zz, :, pl.ds(64 * (2 * yy + kk), 64), :]

    def load(self, zz, yy):
        return pltpu.make_async_copy(self.rows(zz, yy, self.k), self.A.at[zz, yy], self.ld.at[zz, yy])

    def core(self, zz, yy):
        return remote(self.rows(zz, yy, 1 - self.k), self.r1.at[zz, yy], self.cs.at[zz, yy], self.cr.at[zz, yy],
                      device(self.z, self.x, self.y, 1 - self.k))

    def yex(self, zz):
        return remote(self.A.at[zz, 1 - self.y], self.r2.at[zz], self.ys.at[zz], self.yr.at[zz],
                      device(self.z, self.x, 1 - self.y, self.k))

    def up(self, zz):
        return remote(self.A.at[zz, self.y], self.rz.at[zz], self.zs.at[zz], self.zr.at[zz],
                      device(jnp.minimum(self.z + 1, 3), self.x, self.y, self.k))

    def down(self, zz):
        slot = jnp.where(zz == self.z - 1, 4, zz)
        return remote(self.A.at[zz, self.y], self.rz.at[slot], self.zs.at[zz], self.zr.at[slot],
                      device(jnp.maximum(self.z - 1, 0), self.x, self.y, self.k))

    def arrived(self, slot):
        remote(self.rz.at[slot], self.rz.at[slot], self.zs.at[0], self.zr.at[slot],
               device(self.z, self.x, self.y, 1 - self.k)).wait_recv()

    def xex(self):
        return remote(self.A.at[self.z, self.y, 1 - self.x], self.rf, self.xs, self.xr,
                      device(self.z, 1 - self.x, self.y, self.k))

    def start(self, i):
        zz = self.order(i)
        for yy in range(2):
            self.core(zz, yy).start()
            self.load(zz, yy).start()

    def after_core(self, i):
        zz = self.order(i)
        for yy in range(2):
            self.load(zz, yy).wait()
            self.core(zz, yy).wait_recv()
        add_into(self.A.at[zz], self.r1.at[zz])
        self.yex(zz).start()

    def after_y(self, i):
        zz = self.order(i)
        self.yex(zz).wait_recv()
        add_into(self.A.at[zz, self.y], self.r2.at[zz])

    def line(self, i):
        z = self.z
        zz = self.order(i)
        mine = self.A.at[zz, self.y]
        if i < 3:
            @pl.when(zz > z)
            def _():
                @pl.when(z > 0)
                def _():
                    self.arrived(zz)
                    add_into(mine, self.rz.at[zz])
                self.up(zz).start()

            @pl.when(zz < z)
            def _():
                @pl.when(z < 3)
                def _():
                    self.arrived(zz)
                    add_into(mine, self.rz.at[zz])
                self.down(zz).start()
        else:
            @pl.when(z > 0)
            def _():
                self.arrived(z)
                add_into(mine, self.rz.at[z])

            @pl.when(z < 3)
            def _():
                self.arrived(4)
                add_into(mine, self.rz.at[4])
            self.xex().start()

    def spot(self, s, q):
        return self.out.at[s, pl.ds(64 * q, 64), :]

    def fin(self, s):
        return (self.A.at[self.z, self.y, self.x], self.x) if s == 0 else (self.rf, 1 - self.x)

    def fin_copies(self, s):
        src, seq = self.fin(s)
        here = self.spot(seq, self.q)
        return (pltpu.make_async_copy(src, here, self.fl.at[s]),
                remote(src, here, self.fys.at[s], self.fyr.at[s], device(self.z, self.x, 1 - self.y, self.k)),
                remote(src, here, self.fcs.at[s, 0], self.fcr.at[s, 0], device(self.z, self.x, self.y, 1 - self.k)))

    def relay(self, s):
        seq = self.x if s == 0 else 1 - self.x
        r = self.spot(seq, 2 * (1 - self.y) + self.k)
        return remote(r, r, self.fcs.at[s, 1], self.fcr.at[s, 1], device(self.z, self.x, self.y, 1 - self.k))

    def spread(self, s):
        if s == 1:
            self.xex().wait_recv()
        for cp in self.fin_copies(s):
            cp.start()

    def spread_y(self, s):
        seq = self.x if s == 0 else 1 - self.x
        r = self.spot(seq, 2 * (1 - self.y) + self.k)
        remote(r, r, self.fys.at[s], self.fyr.at[s], device(self.z, self.x, 1 - self.y, self.k)).wait_recv()
        self.relay(s).start()

    def finish(self):
        z = self.z
        for zz in range(4):
            for yy in range(2):
                self.core(zz, yy).wait_send()
            self.yex(zz).wait_send()

            @pl.when(z != zz)
            def _():
                self.up(zz).wait_send()
        self.xex().wait_send()
        for s in range(2):
            seq = self.x if s == 0 else 1 - self.x
            a, b, c = self.fin_copies(s)
            a.wait()
            b.wait_send()
            c.wait_send()
            self.relay(s).wait_send()
            for j, yy in ((0, self.y), (1, 1 - self.y)):
                r = self.spot(seq, 2 * yy + 1 - self.k)
                remote(r, r, self.fcs.at[s, j], self.fcr.at[s, j], device(self.z, self.x, self.y, 1 - self.k)).wait_recv()


def reduce_sems():
    D = pltpu.SemaphoreType.DMA
    return [D((4, 2)), D((4, 2)), D((4, 2)), D((4,)), D((4,)), D((4,)), D((5,)), D, D,
            D((2,)), D((2,)), D((2,)), D((2, 2)), D((2, 2))]


def reduce_bufs():
    V = lambda *s: pltpu.VMEM(s, jnp.bfloat16)
    return [V(4, 2, 2, 64, 2048), V(4, 2, 2, 64, 2048), V(4, 2, 64, 2048), V(5, 2, 64, 2048), V(64, 2048)]


class GradReduce:
    def __init__(self, pairs, own, got, sems):
        self.pairs, self.own, self.got = pairs, own, got
        self.ld, self.xs, self.xr, self.zs, self.zr = sems
        self.z, self.x, self.y, self.k = place()

    def load(self, d, w):
        zz = (self.z + d) % 4
        return pltpu.make_async_copy(self.pairs[w][0](zz, self.x), self.own[w].at[d], self.ld.at[d, w])

    def xex(self, d, w):
        zz = (self.z + d) % 4
        return remote(self.pairs[w][0](zz, 1 - self.x), self.got[w].at[d], self.xs.at[d, w], self.xr.at[d, w],
                      device(self.z, 1 - self.x, self.y, self.k))

    def zex(self, d, w):
        zz = (self.z + d) % 4
        return remote(self.own[w].at[d], self.pairs[w][1](self.z), self.zs.at[d, w], self.zr.at[d, w],
                      device(zz, self.x, self.y, self.k))

    def keep(self, w):
        return pltpu.make_async_copy(self.own[w].at[0], self.pairs[w][1](self.z), self.zs.at[0, w])

    def start(self, d, w):
        self.xex(d, w).start()
        self.load(d, w).start()

    def after_x(self, d, w):
        self.load(d, w).wait()
        self.xex(d, w).wait_recv()
        add_into(self.own[w].at[d], self.got[w].at[d])
        if d:
            self.zex(d, w).start()
        else:
            self.keep(w).start()

    def finish(self, w):
        self.keep(w).wait()
        for d in range(4):
            self.xex(d, w).wait_send()
            if d:
                self.zex(d, w).wait_send()
                frm = (self.z - d + 4) % 4
                r = self.pairs[w][1](frm)
                remote(r, r, self.zs.at[d, w], self.zr.at[d, w], device(frm, self.x, self.y, self.k)).wait_recv()


BLOCKS = ((3, 256, 128), (256, 512), (512, 256), (128, 256))


def grad_bufs():
    return [pltpu.VMEM((4,) + b, jnp.bfloat16) for b in BLOCKS] * 2


def grad_sems():
    D = pltpu.SemaphoreType.DMA
    return [D((4, 4)) for _ in range(5)]


def norm_backward(tok, cot, ng, gains, out, sums):
    gain = jnp.concatenate([gains[i, 0:1, :] for i in range(8)], axis=1)
    sums[...] = jnp.zeros_like(sums)

    @pl.loop(0, 32)
    def _(i):
        s, at = i // 16, pl.ds(pl.multiple_of(16 * (i % 16), 16), 16)
        v = tok[s, at].astype(jnp.float32)
        centred = v - jnp.mean(v, axis=-1, keepdims=True)
        scale = lax.rsqrt(jnp.mean(centred * centred, axis=-1, keepdims=True) + EPS)
        xhat = centred * scale
        n = ng[s, at].astype(jnp.float32)
        g = n * gain
        along = jnp.mean(g * xhat, axis=-1, keepdims=True)
        out[s, at] = cot[s, at].astype(jnp.float32) + (g - jnp.mean(g, axis=-1, keepdims=True) - xhat * along) * scale
        both = n * xhat
        sums[0] += both[:8] + both[8:]
        sums[1] += n[:8] + n[8:]


def reduce_kernel(po, pn, gin, gexp, gcon, gout, tok, cot, gains, o_out, o_ig, o_gs, o_gin, o_gexp, o_gcon, o_gout, *scratch):
    z, x, y, k = place()
    c = z * 2 + x
    others = [((c + i) % 8, lax.axis_index("tp")) for i in range(1, 8)]
    scratch = list(scratch)
    o_ng, sums, vec, vecs, vs, vr = (scratch.pop(0) for _ in range(6))
    take = lambda n: [scratch.pop(0) for _ in range(n)]
    nb, ns = len(reduce_bufs()), len(reduce_sems())
    to = TokenReduce(po, o_out, take(nb), take(ns))
    tn = TokenReduce(pn, o_ng, take(nb), take(ns))
    col = lambda n, i: pl.ds(pl.multiple_of(n * i, n), n)
    pairs = [
        (lambda zz, xx: gin.at[:, zz, xx], lambda zz: o_gin.at[:, :, col(128, zz)]),
        (lambda zz, xx: gexp.at[zz, xx], lambda zz: o_gexp.at[:, col(512, zz)]),
        (lambda zz, xx: gcon.at[:, col(256, zz * 2 + xx)], lambda zz: o_gcon.at[col(512, zz), :]),
        (lambda zz, xx: gout.at[:, col(256, zz * 2 + xx)], lambda zz: o_gout.at[col(128, zz), :]),
    ]
    g = GradReduce(pairs, take(4), take(4), take(5))
    meet(others + [device(z, x, 1 - y, k), device(z, x, y, 1 - k)])
    ts = (to, tn)
    for i in range(4):
        for t in ts:
            t.start(i)
    for d in (2, 3, 1, 0):
        for w in range(4):
            g.start(d, w)
    for i in range(5):
        if i < 4:
            for t in ts:
                t.after_core(i)
        if i >= 1:
            for t in ts:
                t.after_y(i - 1)
                t.line(i - 1)
        if i < 4:
            for w in range(4):
                g.after_x((2, 3, 1, 0)[i], w)
    for s in range(2):
        for t in ts:
            t.spread(s)
    for s in range(2):
        for t in ts:
            t.spread_y(s)
    tn.finish()
    norm_backward(tok, cot, o_ng, gains, o_ig, sums)
    for i in range(8):
        at = slice(256 * i, 256 * i + 256)
        for j in range(2):
            vec[i, j:j + 1, :] = jnp.sum(sums[j, :, at], axis=0, keepdims=True)
    vecs[c] = vec[c]
    copies = [remote(vec.at[(c + i + 1) % 8], vecs.at[c], vs.at[i], vr.at[i], others[i]) for i in range(7)]
    for cp in copies:
        cp.start()
    to.finish()
    for w in range(4):
        g.finish(w)
    for i in range(7):
        frm = vecs.at[(c - i - 1 + 8) % 8]
        remote(frm, frm, vs.at[i], vr.at[i], others[i]).wait_recv()
    total = vecs[0]
    for i in range(1, 8):
        total = total + vecs[i]
    o_gs[...] = total
    for cp in copies:
        cp.wait_send()


def reduce_call(po, pn, gin, gexp, gcon, gout, tok, cot, gains):
    bf, f4 = jnp.bfloat16, jnp.float32
    VM = pl.BlockSpec(memory_space=pltpu.VMEM)
    V = pltpu.VMEM
    D = pltpu.SemaphoreType.DMA
    S = jax.ShapeDtypeStruct
    ANY = pl.BlockSpec(memory_space=pl.ANY)
    return pl.pallas_call(
        reduce_kernel,
        out_shape=[S((2, 256, 2048), bf), S((2, 256, 2048), f4), S((8, 256), f4), S((3, 256, 512), bf), S((256, 2048), bf), S((2048, 256), bf), S((512, 256), bf)],
        in_specs=[ANY] * 6 + [VM] * 3,
        out_specs=[ANY, VM, VM] + [ANY] * 4,
        scratch_shapes=[V((2, 256, 2048), bf), V((2, 8, 2048), f4), V((8, 8, 256), f4), V((8, 8, 256), f4), D((7,)), D((7,))] + (reduce_bufs() + reduce_sems()) * 2 + grad_bufs() + grad_sems(),
        compiler_params=pltpu.CompilerParams(collective_id=1, has_side_effects=True, vmem_limit_bytes=56 * MB),
        name="reduce",
    )(po, pn, gin, gexp, gcon, gout, tok, cot, gains)


NT = (((1,), (1,)), ((), ()))


def dot(a, b):
    return jnp.dot(a, b, preferred_element_type=jnp.float32)


def turn(v, tab):
    cos, lo, hi = tab
    return v * cos + pltpu.roll(v, 112, 1) * lo + pltpu.roll(v, 16, 1) * hi


def turn_back(v, tab):
    cos, lo, hi = tab
    return v * cos - pltpu.roll(v, 112, 1) * lo - pltpu.roll(v, 16, 1) * hi


def angle_table(within, block, b):
    cr, sr = within[0], within[1]
    cb, sb = block[0, pl.ds(b, 1)], block[1, pl.ds(b, 1)]
    cos, sin = cb * cr - sb * sr, sb * cr + cb * sr
    entry = lax.broadcasted_iota(jnp.int32, cos.shape, 1) % 64
    return cos, jnp.where(entry < 16, -sin, 0.0), jnp.where(entry < 16, 0.0, sin)


def angles(rows, step):
    frequency = (10000.0 ** (-2.0 * np.arange(16) / 32)).astype(np.float32).astype(np.float64)
    lanes = np.concatenate([frequency, frequency, np.zeros(32)] * 2)
    angle = step * np.arange(rows)[:, None] * lanes
    return np.stack([np.cos(angle), np.sin(angle)]).astype(np.float32)


def attention_kernel(inv, proj, do, within, block, mixed, pg, q, k, v, qt, kt, vt, dos, dot_, ot, dqt, dk, dv):
    n = q.shape[1]
    nb = n // 128
    half = nb // 2

    def source(b):
        pair = jnp.where(b < half, b, nb - 1 - b)
        return pl.multiple_of(inv[pair] * 256 + jnp.where(b < half, 0, 128), 128)

    @pl.loop(0, nb)
    def _(b):
        src = pl.ds(source(b), 128)
        here = pl.ds(pl.multiple_of(b * 128, 128), 128)
        t = angle_table(within, block, b)
        rq = turn(proj[0, src], t).astype(jnp.bfloat16) * jnp.bfloat16(0.125)
        rk = turn(proj[1, src], t).astype(jnp.bfloat16)
        rv = proj[2, src].astype(jnp.bfloat16)
        g = do[src]
        qT, kT, vT, gT = (a.astype(jnp.float32).T.astype(jnp.bfloat16) for a in (rq, rk, rv, g))
        for h in range(2):
            at = slice(64 * h, 64 * h + 64)
            q[h, here], k[h, here], v[h, here], dos[h, here] = rq[:, at], rk[:, at], rv[:, at], g[:, at]
            qt[h, :, here], kt[h, :, here], vt[h, :, here], dot_[h, :, here] = qT[at], kT[at], vT[at], gT[at]

    dk[...] = jnp.zeros_like(dk)
    dv[...] = jnp.zeros_like(dv)

    @pl.loop(0, 2)
    def _(h):
        for i in range(n // 256):
            kr = 256 * (i + 1)
            here = pl.ds(256 * i, 256)
            gT = dot_[h, :, here]
            st = dot(k[h, :kr], qt[h, :, here])
            row = lax.broadcasted_iota(jnp.int32, (256, 256), 0)
            column = lax.broadcasted_iota(jnp.int32, (256, 256), 1)
            last = jnp.where(row <= column, st[kr - 256:], -1e30)
            st = last if i == 0 else jnp.concatenate([st[:kr - 256], last], axis=0)
            peak = jnp.max(st, axis=0, keepdims=True)
            p = jnp.exp(st - peak)
            p = p * (1.0 / jnp.sum(p, axis=0, keepdims=True))
            low = p.astype(jnp.bfloat16)
            o = dot(vt[h, :, :kr], low)
            ot[h, :, here] = o
            delta = jnp.sum(o * gT.astype(jnp.float32), axis=0, keepdims=True)
            ds = (p * (dot(v[h, :kr], gT) - delta)).astype(jnp.bfloat16)
            dv[h, :kr] += dot(low, dos[h, here])
            dk[h, :kr] += dot(ds, q[h, here])
            dqt[h, :, here] = dot(kt[h, :, :kr], ds) * 0.125

    @pl.loop(0, nb)
    def _(b):
        dst = pl.ds(source(b), 128)
        here = pl.ds(pl.multiple_of(b * 128, 128), 128)
        t = angle_table(within, block, b)
        mixed[dst] = jnp.concatenate([ot[0, :, here], ot[1, :, here]], axis=0).T.astype(jnp.bfloat16)
        gq = jnp.concatenate([dqt[0, :, here], dqt[1, :, here]], axis=0).T
        gk = jnp.concatenate([dk[0, here], dk[1, here]], axis=1)
        gv = jnp.concatenate([dv[0, here], dv[1, here]], axis=1)
        pg[0, dst] = turn_back(gq, t).astype(jnp.bfloat16)
        pg[1, dst] = turn_back(gk, t).astype(jnp.bfloat16)
        pg[2, dst] = gv.astype(jnp.bfloat16)


def attention_call(inv, proj, do):
    n = proj.shape[1]
    bf, f4 = jnp.bfloat16, jnp.float32
    S = jax.ShapeDtypeStruct
    VM = pl.BlockSpec(memory_space=pltpu.VMEM)
    V = pltpu.VMEM
    return pl.pallas_call(
        attention_kernel,
        out_shape=[S((n, 128), bf), S((3, n, 128), bf)],
        in_specs=[pl.BlockSpec(memory_space=pltpu.SMEM)] + [VM] * 4,
        out_specs=[VM] * 2,
        scratch_shapes=[V((2, n, 64), bf)] * 3 + [V((2, 64, n), bf)] * 3 + [V((2, n, 64), bf), V((2, 64, n), bf)]
        + [V((2, 64, n), f4)] * 2 + [V((2, n, 64), f4)] * 2,
        compiler_params=pltpu.CompilerParams(vmem_limit_bytes=56 * MB),
        name="attention",
    )(inv, proj, do, jnp.asarray(angles(128, 1)), jnp.asarray(angles(n // 128, 128)))

def own_local(tokens, pair_index, norm_gain, norm_shift, w_attention_in, w_attention_out, w_expand, w_contract, cotangent):
    f4, bf = jnp.float32, jnp.bfloat16
    dots = functools.partial(jnp.einsum, preferred_element_type=f4)
    x = lax.axis_index("ctx") % 2
    pairs = lax.dynamic_index_in_dim(pair_index, x, 0, False)
    which = jnp.arange(8, dtype=jnp.int32)
    inverse = jnp.sum(jnp.where(pairs[None, :] == which[:, None], which[None, :], 0), axis=1).astype(jnp.int32)
    gs = jnp.concatenate([norm_gain[None], norm_shift[None], jnp.zeros((6, 256), bf)], axis=0).astype(f4)
    xn, ct, win, wout, wexp, wcon, gs_all = gather_call(tokens, gs, cotangent, w_attention_in, w_attention_out, w_expand, w_contract)
    xn, ct = xn.reshape(2048, 2048), ct.reshape(2048, 2048)
    win, wexp = win.reshape(3, 2048, 128), wexp.reshape(2048, 512)
    proj = dots("td,kde->kte", xn, win)
    mixed_grad = dots("td,ed->te", ct, wout).astype(bf)
    mixed, pg = attention_call(inverse, proj, mixed_grad)
    hidden = dots("td,df->tf", xn, wexp)
    activated_full, pull = jax.vjp(gelu_tanh, hidden)
    activated = activated_full.astype(bf)
    out_part = (dots("te,ed->td", mixed, wout) + dots("tf,fd->td", activated, wcon)).astype(bf)
    gcon = dots("tf,td->fd", activated, ct).astype(bf)
    hidden_grad = pull(dots("td,fd->tf", ct, wcon))[0].astype(bf)
    gout = dots("te,td->ed", mixed, ct).astype(bf)
    gexp = dots("td,tf->df", xn, hidden_grad).astype(bf)
    gin = dots("td,kte->kde", xn, pg).astype(bf)
    ng_part = (dots("kte,kde->td", pg, win) + dots("tf,df->td", hidden_grad, wexp)).astype(bf)
    out_sum, input_grad, vectors, gin, gexp, gcon, gout = reduce_call(
        out_part.reshape(4, 2, 256, 2048), ng_part.reshape(4, 2, 256, 2048),
        gin.reshape(3, 4, 2, 256, 128), gexp.reshape(4, 2, 256, 512), gcon, gout, tokens, cotangent, gs_all)
    output = (tokens.astype(f4) + out_sum.astype(f4)).astype(bf)
    return (output, input_grad, vectors[0], vectors[1],
            gin.astype(f4), gout.astype(f4), gexp.astype(f4), gcon.astype(f4))


def local(tokens, pair_index, norm_gain, norm_shift, w_attention_in, w_attention_out, w_expand, w_contract, cotangent):
    args = (tokens, pair_index, norm_gain, norm_shift, w_attention_in, w_attention_out, w_expand, w_contract, cotangent)
    sizes = (lax.axis_size("ctx"), lax.axis_size("tp")) + tokens.shape + w_attention_in.shape[2:] + w_expand.shape[1:]
    if sizes == (8, 4, 2, 256, 2048, 512, 2048):
        return own_local(*args)
    return general_local(*args)


def solution(mesh):
    in_specs = (
        P(None, "ctx", None),
        P(),
        P("ctx"),
        P("ctx"),
        P(None, "ctx", "tp"),
        P("tp", "ctx"),
        P("ctx", "tp"),
        P("tp", "ctx"),
        P(None, "ctx", None),
    )
    out_specs = (
        P(None, "ctx", None),
        P(None, "ctx", None),
        P("ctx"),
        P("ctx"),
        P(None, "ctx", "tp"),
        P("tp", "ctx"),
        P("ctx", "tp"),
        P("tp", "ctx"),
    )
    return jax.shard_map(local, mesh=mesh, in_specs=in_specs, out_specs=out_specs, check_vma=False)
```

```python
import itertools

import jax
import jax.numpy as jnp
import numpy as np
from jax import lax
from jax.experimental import pallas as pl
from jax.experimental.pallas import tpu as pltpu
from jax.sharding import PartitionSpec as P

HEAD_DIM = 64
ROT = 32


epsilon = 1e-05


def position_table(pair_index, shard_rows):
    pair_count = pair_index.shape[1]
    half_rows = shard_rows // 2
    token_index = jnp.arange(shard_rows * pair_count, dtype=jnp.int32)
    owning = token_index // shard_rows
    within = token_index % shard_rows
    picked = (owning[:, None] == jnp.arange(pair_count, dtype=jnp.int32)[None, :]).astype(jnp.int32)
    chosen = jnp.sum(picked[None, :, :] * pair_index[:, None, :], axis=2)
    first_half = chosen * half_rows + within[None, :]
    second = (2 * pair_count - 1 - chosen) * half_rows + within[None, :] - half_rows
    return jnp.where(within[None, :] < half_rows, first_half, second)


def rotate(tensor, positions):
    half_rot = ROT // 2
    frequency = 10000.0 ** (-2.0 * jnp.arange(half_rot, dtype=jnp.float32) / ROT)
    angles = positions.astype(jnp.float32)[..., None] * frequency
    cosine = jnp.cos(angles)[..., None, :]
    sine_part = jnp.sin(angles)[..., None, :]
    leading = tensor[..., :half_rot]
    trailing = tensor[..., half_rot:ROT]
    return jnp.concatenate(
        [
            leading * cosine - trailing * sine_part,
            trailing * cosine + leading * sine_part,
            tensor[..., ROT:],
        ],
        axis=-1,
    )


def gelu_tanh(values_in):
    return (
        0.5
        * values_in
        * (
            1.0
            + jnp.tanh(
                0.7978845608028654 * (values_in + 0.044715 * values_in * values_in * values_in)
            )
        )
    )


def layer_norm(inputs, gain_full, shift_full):
    centred = inputs - jnp.mean(inputs, axis=-1, keepdims=True)
    spread = jnp.mean(centred * centred, axis=-1, keepdims=True)
    return centred * lax.rsqrt(spread + epsilon) * gain_full + shift_full


def block_probs(queries, keys_block, log_total, query_pos, key_pos):
    raw_scores = jnp.einsum(
        "sqhe,skhe->shqk", queries, keys_block, preferred_element_type=jnp.float32
    )
    allowed = key_pos[:, None, None, :] <= query_pos[:, None, :, None]
    return jnp.where(allowed, jnp.exp(raw_scores * HEAD_DIM ** (-0.5) - log_total[..., None]), 0.0)


def score_grads(
    queries, keys_block, values_block, log_total, row_delta, out_grad, query_pos, key_pos
):
    probs_full = block_probs(queries, keys_block, log_total, query_pos, key_pos)
    prob_grad = jnp.einsum(
        "sqhe,skhe->shqk", out_grad, values_block, preferred_element_type=jnp.float32
    )
    score_grad = (probs_full * (prob_grad - row_delta[..., None]) * HEAD_DIM ** (-0.5)).astype(
        jnp.bfloat16
    )
    return (probs_full.astype(jnp.bfloat16), score_grad)


def key_slice(keys_all, offset, key_rows, head_count):
    seq_count = keys_all.shape[0]
    return lax.dynamic_slice_in_dim(keys_all, offset, key_rows, 1).reshape(
        seq_count, key_rows, head_count, HEAD_DIM
    )


def log_totals(queries, keys_all, query_pos, pos_table, key_rows):
    seq_count, query_rows, head_count, head_size = queries.shape
    turn_count = keys_all.shape[1] // key_rows

    def log_one_turn(turn_index, state_in):
        running_max, running_sum = state_in
        offset = turn_index * key_rows
        keys_block = key_slice(keys_all, offset, key_rows, head_count)
        key_pos = lax.dynamic_slice_in_dim(pos_table, offset, key_rows, 1)
        raw_scores = jnp.einsum(
            "sqhe,skhe->shqk", queries, keys_block, preferred_element_type=jnp.float32
        ) * HEAD_DIM ** (-0.5)
        allowed = key_pos[:, None, None, :] <= query_pos[:, None, :, None]
        masked = jnp.where(allowed, raw_scores, -1e30)
        new_max = jnp.maximum(running_max, jnp.max(masked, axis=-1))
        kept_terms = jnp.where(allowed, jnp.exp(masked - new_max[..., None]), 0.0)
        return (
            new_max,
            running_sum * jnp.exp(running_max - new_max) + jnp.sum(kept_terms, axis=-1),
        )

    initial = (
        jnp.full((seq_count, head_count, query_rows), -1e30, jnp.float32),
        jnp.zeros((seq_count, head_count, query_rows), jnp.float32),
    )
    final_max, final_sum = lax.fori_loop(0, turn_count, log_one_turn, initial)
    return final_max + jnp.log(final_sum)


def attend_values(queries, keys_all, values_all, log_total, query_pos, pos_table, key_rows):
    head_count = queries.shape[2]
    turn_count = keys_all.shape[1] // key_rows

    def attend_one_turn(turn_index, running):
        offset = turn_index * key_rows
        keys_block = key_slice(keys_all, offset, key_rows, head_count)
        values_block = key_slice(values_all, offset, key_rows, head_count)
        key_pos = lax.dynamic_slice_in_dim(pos_table, offset, key_rows, 1)
        weights_low = block_probs(queries, keys_block, log_total, query_pos, key_pos).astype(
            jnp.bfloat16
        )
        return running + jnp.einsum(
            "shqk,skhe->sqhe", weights_low, values_block, preferred_element_type=jnp.float32
        )

    return lax.fori_loop(0, turn_count, attend_one_turn, jnp.zeros(queries.shape, jnp.float32))


def full_grads(
    queries, keys_all, values_all, log_total, row_delta, out_grad, query_pos, pos_table, key_rows
):
    seq_count, query_rows, head_count, head_size = queries.shape
    turn_count = keys_all.shape[1] // key_rows

    def full_one_turn(turn_index, state_in):
        query_grad, key_terms, value_terms = state_in
        offset = turn_index * key_rows
        keys_block = key_slice(keys_all, offset, key_rows, head_count)
        values_block = key_slice(values_all, offset, key_rows, head_count)
        key_pos = lax.dynamic_slice_in_dim(pos_table, offset, key_rows, 1)
        weights_low, score_grad = score_grads(
            queries, keys_block, values_block, log_total, row_delta, out_grad, query_pos, key_pos
        )
        query_grad = query_grad + jnp.einsum(
            "shqk,skhe->sqhe", score_grad, keys_block, preferred_element_type=jnp.float32
        )
        key_part = jnp.einsum(
            "shqk,sqhe->skhe", score_grad, queries, preferred_element_type=jnp.float32
        ).reshape(seq_count, key_rows, head_count * head_size)
        value_part = jnp.einsum(
            "shqk,sqhe->skhe", weights_low, out_grad, preferred_element_type=jnp.float32
        ).reshape(seq_count, key_rows, head_count * head_size)
        key_terms = lax.dynamic_update_slice_in_dim(key_terms, key_part, offset, 1)
        value_terms = lax.dynamic_update_slice_in_dim(value_terms, value_part, offset, 1)
        return (query_grad, key_terms, value_terms)

    initial = (
        jnp.zeros(queries.shape, jnp.float32),
        jnp.zeros(keys_all.shape, jnp.float32),
        jnp.zeros(values_all.shape, jnp.float32),
    )
    return lax.fori_loop(0, turn_count, full_one_turn, initial)


def general_local(
    tokens,
    pair_index,
    norm_gain,
    norm_shift,
    w_attention_in,
    w_attention_out,
    w_expand,
    w_contract,
    cotangent,
):
    seq_count, shard_rows, model_width = tokens.shape
    gain_full, shift_full, attention_in, attention_out, expand_full, contract_full = (
        lax.all_gather(norm_gain, "ctx", axis=0, tiled=True),
        lax.all_gather(norm_shift, "ctx", axis=0, tiled=True),
        lax.all_gather(w_attention_in, "ctx", axis=1, tiled=True),
        lax.all_gather(w_attention_out, "ctx", axis=1, tiled=True),
        lax.all_gather(w_expand, "ctx", axis=0, tiled=True),
        lax.all_gather(w_contract, "ctx", axis=1, tiled=True),
    )
    local_width = attention_in.shape[2]
    head_count = local_width // HEAD_DIM
    flat_rows = seq_count * shard_rows
    pos_table = position_table(pair_index, shard_rows)
    total_rows = pos_table.shape[1]
    own_pos = lax.dynamic_slice_in_dim(pos_table, lax.axis_index("ctx") * shard_rows, shard_rows, 1)
    key_rows = min(total_rows, 1024)
    inputs = tokens.astype(jnp.float32)
    normed_full, norm_pull = jax.vjp(
        layer_norm, inputs, gain_full.astype(jnp.float32), shift_full.astype(jnp.float32)
    )
    normed = normed_full.astype(jnp.bfloat16).reshape(flat_rows, model_width)
    projected = jnp.einsum("td,kde->kte", normed, attention_in, preferred_element_type=jnp.float32)
    split_heads = projected.reshape(3, seq_count, shard_rows, head_count, HEAD_DIM)
    rotated, rotate_pull = jax.vjp(lambda pair_part: rotate(pair_part, own_pos), split_heads[:2])
    queries = rotated[0].astype(jnp.bfloat16)
    own_keys = rotated[1].astype(jnp.bfloat16)
    own_values = split_heads[2].astype(jnp.bfloat16)
    keys_all, values_all = (
        lax.all_gather(
            own_keys.reshape(seq_count, shard_rows, local_width), "ctx", axis=1, tiled=True
        ),
        lax.all_gather(
            own_values.reshape(seq_count, shard_rows, local_width), "ctx", axis=1, tiled=True
        ),
    )
    log_total = log_totals(queries, keys_all, own_pos, pos_table, key_rows)
    attended = attend_values(queries, keys_all, values_all, log_total, own_pos, pos_table, key_rows)
    mixed = attended.reshape(flat_rows, local_width).astype(jnp.bfloat16)
    hidden_pre = jnp.dot(normed, expand_full, preferred_element_type=jnp.float32)
    activated_full, gelu_pull = jax.vjp(gelu_tanh, hidden_pre)
    activated = activated_full.astype(jnp.bfloat16)
    branch = jnp.dot(mixed, attention_out, preferred_element_type=jnp.float32) + jnp.dot(
        activated, contract_full, preferred_element_type=jnp.float32
    )
    branch = lax.psum(branch.astype(jnp.bfloat16), "tp").astype(jnp.float32)
    output = (inputs + branch.reshape(seq_count, shard_rows, model_width)).astype(jnp.bfloat16)
    upstream = cotangent.reshape(flat_rows, model_width)
    contract_grad = jnp.einsum("tf,td->fd", activated, upstream, preferred_element_type=jnp.float32)
    (gelu_grad,) = gelu_pull(
        jnp.einsum("td,fd->tf", upstream, contract_full, preferred_element_type=jnp.float32)
    )
    hidden_grad = gelu_grad.astype(jnp.bfloat16)
    expand_grad = jnp.einsum("td,tf->df", normed, hidden_grad, preferred_element_type=jnp.float32)
    mixed_grad = jnp.einsum(
        "td,ed->te", upstream, attention_out, preferred_element_type=jnp.float32
    ).astype(jnp.bfloat16)
    attention_out_grad = jnp.einsum(
        "te,td->ed", mixed, upstream, preferred_element_type=jnp.float32
    )
    out_grad = mixed_grad.reshape(seq_count, shard_rows, head_count, HEAD_DIM)
    row_delta = jnp.sum(out_grad.astype(jnp.float32) * attended, axis=-1).transpose(0, 2, 1)
    query_grad, key_terms, value_terms = full_grads(
        queries, keys_all, values_all, log_total, row_delta, out_grad, own_pos, pos_table, key_rows
    )
    key_grad, value_grad = (
        lax.psum_scatter(
            key_terms.astype(jnp.bfloat16), "ctx", scatter_dimension=1, tiled=True
        ).astype(jnp.float32),
        lax.psum_scatter(
            value_terms.astype(jnp.bfloat16), "ctx", scatter_dimension=1, tiled=True
        ).astype(jnp.float32),
    )
    key_grad = key_grad.reshape(seq_count, shard_rows, head_count, HEAD_DIM)
    value_grad = value_grad.reshape(seq_count, shard_rows, head_count, HEAD_DIM)
    (rotated_grad,) = rotate_pull(jnp.stack([query_grad, key_grad]))
    projected_grad = (
        jnp.concatenate([rotated_grad, value_grad[None]], axis=0)
        .reshape(3, flat_rows, local_width)
        .astype(jnp.bfloat16)
    )
    attention_in_grad = jnp.einsum(
        "td,kte->kde", normed, projected_grad, preferred_element_type=jnp.float32
    )
    normed_grad = jnp.einsum(
        "kte,kde->td", projected_grad, attention_in, preferred_element_type=jnp.float32
    )
    normed_grad = normed_grad + jnp.einsum(
        "tf,df->td", hidden_grad, expand_full, preferred_element_type=jnp.float32
    )
    normed_grad = lax.psum(normed_grad.astype(jnp.bfloat16), "tp").astype(jnp.float32)
    input_part, gain_grad, shift_grad = norm_pull(
        normed_grad.reshape(seq_count, shard_rows, model_width)
    )
    input_grad = input_part + cotangent.astype(jnp.float32)
    reduced = (
        lax.psum_scatter(
            gain_grad.astype(jnp.bfloat16), "ctx", scatter_dimension=0, tiled=True
        ).astype(jnp.float32),
        lax.psum_scatter(
            shift_grad.astype(jnp.bfloat16), "ctx", scatter_dimension=0, tiled=True
        ).astype(jnp.float32),
        lax.psum_scatter(
            attention_in_grad.astype(jnp.bfloat16), "ctx", scatter_dimension=1, tiled=True
        ).astype(jnp.float32),
        lax.psum_scatter(
            attention_out_grad.astype(jnp.bfloat16), "ctx", scatter_dimension=1, tiled=True
        ).astype(jnp.float32),
        lax.psum_scatter(
            expand_grad.astype(jnp.bfloat16), "ctx", scatter_dimension=0, tiled=True
        ).astype(jnp.float32),
        lax.psum_scatter(
            contract_grad.astype(jnp.bfloat16), "ctx", scatter_dimension=1, tiled=True
        ).astype(jnp.float32),
    )
    return (
        output,
        input_grad,
        reduced[0],
        reduced[1],
        reduced[2],
        reduced[3],
        reduced[4],
        reduced[5],
    )


MESH = pl.DeviceIdType.MESH
MB = 1 << 20
EPS = 1e-05
BF = jnp.bfloat16
F4 = jnp.float32
NT = (((1,), (1,)), ((), ()))
FAR = (2, 3, 1, 0)


def place():
    c = lax.axis_index("ctx")
    t = lax.axis_index("tp")
    return c // 2, c % 2, t // 2, t % 2


def device(z, x, y, k):
    return (z * 2 + x, y * 2 + k)


def remote(src, dst, send_sem, recv_sem, target):
    return pltpu.make_async_remote_copy(
        src_ref=src, dst_ref=dst, send_sem=send_sem, recv_sem=recv_sem,
        device_id=target, device_id_type=MESH,
    )


def meet(peers):
    barrier = pltpu.get_barrier_semaphore()
    for peer in peers:
        pl.semaphore_signal(barrier, inc=1, device_id=peer, device_id_type=MESH)
    pl.semaphore_wait(barrier, len(peers))


def peers_of(z, x, y, k):
    c = z * 2 + x
    others = [((c + i) % 8, lax.axis_index("tp")) for i in range(1, 8)]
    return others, others + [device(z, x, 1 - y, k), device(z, x, y, 1 - k)]


def columns(n, i):
    return pl.ds(pl.multiple_of(n * i, n), n)


def dot(a, b):
    return jnp.dot(a, b, preferred_element_type=F4)


def dot_t(a, b):
    return lax.dot_general(a, b, NT, preferred_element_type=F4)


def far_first(z, i):
    return (3 * (1 - z // 2), z // 2 + 2 * (1 - z % 2), 1 + z % 2, z)[i]


def add_into(dst, src):
    lead, rows = dst.shape[:-2], dst.shape[-2]
    for idx in itertools.product(*(range(n) for n in lead)):
        @pl.loop(0, rows // 16)
        def _(i):
            at = idx + (pl.ds(pl.multiple_of(16 * i, 16), 16), slice(None))
            dst[at] = (dst[at].astype(F4) + src[at].astype(F4)).astype(BF)


class TokenGather:
    def __init__(self, whole, sems):
        self.whole = whole
        self.xs, self.xr, self.zs, self.zr, self.ys, self.yr, self.cs, self.cr = sems
        self.z, self.x, self.y, self.k = place()
        self.q = 2 * self.y + self.k

    def chunk(self, zz, s, q):
        xx = self.x if s == 0 else 1 - self.x
        return self.whole.at[zz, xx, pl.ds(64 * q, 64), :]

    def send_x(self, src):
        z, x, y, k = self.z, self.x, self.y, self.k
        return remote(src, self.whole.at[z, x, pl.ds(64 * self.q, 64), :], self.xs, self.xr, device(z, 1 - x, y, k))

    def send_up(self, zz, s, src):
        return remote(src, self.chunk(zz, s, self.q), self.zs.at[zz, s, 0], self.zr.at[zz, s],
                      device(jnp.minimum(self.z + 1, 3), self.x, self.y, self.k))

    def send_down(self, zz, s, src):
        return remote(src, self.chunk(zz, s, self.q), self.zs.at[zz, s, 1], self.zr.at[zz, s],
                      device(jnp.maximum(self.z - 1, 0), self.x, self.y, self.k))

    def send_y(self, zz, s):
        c = self.chunk(zz, s, self.q)
        return remote(c, c, self.ys.at[zz, s], self.yr.at[zz, s], device(self.z, self.x, 1 - self.y, self.k))

    def send_core(self, zz, s, j):
        yy = self.y if j == 0 else 1 - self.y
        c = self.chunk(zz, s, 2 * yy + self.k)
        return remote(c, c, self.cs.at[zz, s, j], self.cr.at[zz, s, j], device(self.z, self.x, self.y, 1 - self.k))

    def both_ways(self, s, src):
        z = self.z

        @pl.when(z < 3)
        def _():
            self.send_up(z, s, src).start()

        @pl.when(z > 0)
        def _():
            self.send_down(z, s, src).start()

    def start(self, own_quarter, other_quarter):
        self.send_x(other_quarter).start()
        self.both_ways(0, own_quarter)

    def after_x(self):
        c = self.chunk(self.z, 1, self.q)
        remote(c, c, self.xs, self.xr, device(self.z, 1 - self.x, self.y, self.k)).wait_recv()
        self.both_ways(1, c)
        self.send_y(self.z, 1).start()
        self.send_core(self.z, 1, 0).start()

    def hop(self, d, s):
        z = self.z

        @pl.when(z >= d)
        def _():
            zz = z - d
            c = self.chunk(zz, s, self.q)
            self.send_down(zz, s, c).wait_recv()

            @pl.when(z < 3)
            def _():
                self.send_up(zz, s, c).start()

            self.send_y(zz, s).start()
            self.send_core(zz, s, 0).start()

        @pl.when(z + d <= 3)
        def _():
            zz = z + d
            c = self.chunk(zz, s, self.q)
            self.send_up(zz, s, c).wait_recv()

            @pl.when(z > 0)
            def _():
                self.send_down(zz, s, c).start()

            self.send_y(zz, s).start()
            self.send_core(zz, s, 0).start()

    def y_in(self, zz, s):
        c = self.chunk(zz, s, 2 * (1 - self.y) + self.k)
        remote(c, c, self.ys.at[zz, s], self.yr.at[zz, s], device(self.z, self.x, 1 - self.y, self.k)).wait_recv()
        self.send_core(zz, s, 1).start()

    def y_hop(self, d, s):
        z = self.z
        if d == 0:
            self.y_in(z, s)
            return

        @pl.when(z >= d)
        def _():
            self.y_in(z - d, s)

        @pl.when(z + d <= 3)
        def _():
            self.y_in(z + d, s)

    def landed(self, zz):
        def rest(s):
            for j in range(2):
                yy = self.y if j == 0 else 1 - self.y
                c = self.chunk(zz, s, 2 * yy + 1 - self.k)
                remote(c, c, self.cs.at[zz, s, j], self.cr.at[zz, s, j], device(self.z, self.x, self.y, 1 - self.k)).wait_recv()

        pl.when(self.z != zz)(lambda: rest(0))
        rest(1)

    def finish(self, other_quarter):
        z = self.z
        self.send_x(other_quarter).wait_send()
        for zz in range(4):
            for s in range(2):
                def rest():
                    self.send_y(zz, s).wait_send()
                    for j in range(2):
                        self.send_core(zz, s, j).wait_send()
                if s == 0:
                    pl.when(z != zz)(rest)
                else:
                    rest()
                c = self.chunk(zz, s, self.q)

                @pl.when((z < 3) & (zz <= z))
                def _():
                    self.send_up(zz, s, c).wait_send()

                @pl.when((z > 0) & (zz >= z))
                def _():
                    self.send_down(zz, s, c).wait_send()


def token_sems():
    D = pltpu.SemaphoreType.DMA
    return [D, D, D((4, 2, 2)), D((4, 2)), D((4, 2)), D((4, 2)), D((4, 2, 2)), D((4, 2, 2))]


class WeightGather:
    def __init__(self, pairs, sems):
        self.pairs = pairs
        self.zs, self.zr, self.xs, self.xr, self.loc = sems
        self.z, self.x, self.y, self.k = place()

    def z_send(self, d, w):
        src, dst = self.pairs[w]
        to = (self.z + d) % 4
        return remote(src(to), dst(self.z, self.x), self.zs.at[d, w], self.zr.at[d, w], device(to, self.x, self.y, self.k))

    def z_recv(self, d, w):
        dst = self.pairs[w][1]
        frm = (self.z - d + 4) % 4
        return remote(dst(frm, self.x), dst(frm, self.x), self.zs.at[d, w], self.zr.at[d, w], device(frm, self.x, self.y, self.k))

    def x_send(self, d, w):
        src, dst = self.pairs[w]
        frm = (self.z - d + 4) % 4
        s = src(self.z) if d == 0 else dst(frm, self.x)
        return remote(s, dst(frm, self.x), self.xs.at[d, w], self.xr.at[d, w], device(self.z, 1 - self.x, self.y, self.k))

    def x_recv(self, d, w):
        frm = (self.z - d + 4) % 4
        r = self.pairs[w][1](frm, 1 - self.x)
        return remote(r, r, self.xs.at[d, w], self.xr.at[d, w], device(self.z, 1 - self.x, self.y, self.k))

    def local(self, w):
        src, dst = self.pairs[w]
        return pltpu.make_async_copy(src(self.z), dst(self.z, self.x), self.loc.at[w])

    def start(self, *ws):
        for w in ws:
            for d in (2, 3, 1):
                self.z_send(d, w).start()
            self.x_send(0, w).start()
            self.local(w).start()

    def forward(self, w, d):
        self.z_recv(d, w).wait_recv()
        self.x_send(d, w).start()

    def landed(self, w):
        self.local(w).wait()
        for d in range(4):
            self.x_recv(d, w).wait_recv()

    def finish(self, w):
        for d in range(4):
            if d:
                self.z_send(d, w).wait_send()
            self.x_send(d, w).wait_send()


def weight_sems(n):
    D = pltpu.SemaphoreType.DMA
    return [D((4, n)), D((4, n)), D((4, n)), D((4, n)), D((n,))]


class TokenReduce:
    def __init__(self, out, bufs, sems):
        self.out = out
        self.A, self.S, self.r1, self.r2, self.rz, self.rf = bufs
        (self.cs, self.cr, self.ys, self.yr, self.zs, self.zr, self.xs, self.xr,
         self.fl, self.fys, self.fyr, self.fcs, self.fcr) = sems
        self.z, self.x, self.y, self.k = place()
        self.q = 2 * self.y + self.k

    def core(self, i):
        zz = far_first(self.z, i)
        return remote(self.S.at[i % 2], self.r1.at[zz], self.cs.at[zz], self.cr.at[zz], device(self.z, self.x, self.y, 1 - self.k))

    def yex(self, zz):
        return remote(self.r1.at[zz, 1 - self.y], self.r2.at[zz], self.ys.at[zz], self.yr.at[zz],
                      device(self.z, self.x, 1 - self.y, self.k))

    def up(self, zz):
        return remote(self.r1.at[zz, self.y], self.rz.at[zz], self.zs.at[zz], self.zr.at[zz],
                      device(jnp.minimum(self.z + 1, 3), self.x, self.y, self.k))

    def down(self, zz):
        slot = jnp.where(zz == self.z - 1, 4, zz)
        return remote(self.r1.at[zz, self.y], self.rz.at[slot], self.zs.at[zz], self.zr.at[slot],
                      device(jnp.maximum(self.z - 1, 0), self.x, self.y, self.k))

    def arrived(self, slot):
        remote(self.rz.at[slot], self.rz.at[slot], self.zs.at[0], self.zr.at[slot],
               device(self.z, self.x, self.y, 1 - self.k)).wait_recv()

    def xex(self):
        return remote(self.r1.at[self.z, self.y, 1 - self.x], self.rf, self.xs, self.xr,
                      device(self.z, 1 - self.x, self.y, self.k))

    def fill(self, i, lhs, rhs, free):
        zz = far_first(self.z, i)
        free()

        def rows(kk):
            return jnp.concatenate([lhs(zz, xx, 64 * (2 * yy + kk)) for yy in range(2) for xx in range(2)], axis=0)

        for kk, dst in ((1 - self.k, self.S.at[i % 2]), (self.k, self.A.at[i % 2])):
            a = rows(kk)

            @pl.loop(0, 4)
            def _(j):
                at = columns(512, j)
                dst[:, :, :, at] = rhs(a, at).astype(BF).reshape(2, 2, 64, 512)
            if kk is not self.k:
                self.core(i).start()

    def after_core(self, i):
        zz = far_first(self.z, i)
        self.core(i).wait_recv()
        add_into(self.r1.at[zz], self.A.at[i % 2])
        self.yex(zz).start()

    def after_y(self, i):
        zz = far_first(self.z, i)
        self.yex(zz).wait_recv()
        add_into(self.r1.at[zz, self.y], self.r2.at[zz])

    def line(self, i):
        z = self.z
        zz = far_first(z, i)
        mine = self.r1.at[zz, self.y]
        if i < 3:
            @pl.when(zz > z)
            def _():
                @pl.when(z > 0)
                def _():
                    self.arrived(zz)
                    add_into(mine, self.rz.at[zz])
                self.up(zz).start()

            @pl.when(zz < z)
            def _():
                @pl.when(z < 3)
                def _():
                    self.arrived(zz)
                    add_into(mine, self.rz.at[zz])
                self.down(zz).start()
        else:
            @pl.when(z > 0)
            def _():
                self.arrived(z)
                add_into(mine, self.rz.at[z])

            @pl.when(z < 3)
            def _():
                self.arrived(4)
                add_into(mine, self.rz.at[4])
            self.xex().start()

    def spot(self, s, q):
        return self.out.at[s, pl.ds(64 * q, 64), :]

    def fin(self, s):
        return (self.r1.at[self.z, self.y, self.x], self.x) if s == 0 else (self.rf, 1 - self.x)

    def fin_copies(self, s):
        src, seq = self.fin(s)
        here = self.spot(seq, self.q)
        return (pltpu.make_async_copy(src, here, self.fl.at[s]),
                remote(src, here, self.fys.at[s], self.fyr.at[s], device(self.z, self.x, 1 - self.y, self.k)),
                remote(src, here, self.fcs.at[s, 0], self.fcr.at[s, 0], device(self.z, self.x, self.y, 1 - self.k)))

    def relay(self, s):
        seq = self.x if s == 0 else 1 - self.x
        r = self.spot(seq, 2 * (1 - self.y) + self.k)
        return remote(r, r, self.fcs.at[s, 1], self.fcr.at[s, 1], device(self.z, self.x, self.y, 1 - self.k))

    def spread(self, s):
        if s == 1:
            self.xex().wait_recv()
        for cp in self.fin_copies(s):
            cp.start()

    def spread_y(self, s):
        seq = self.x if s == 0 else 1 - self.x
        r = self.spot(seq, 2 * (1 - self.y) + self.k)
        remote(r, r, self.fys.at[s], self.fyr.at[s], device(self.z, self.x, 1 - self.y, self.k)).wait_recv()
        self.relay(s).start()

    def finish(self):
        z = self.z
        for zz in range(4):
            self.yex(zz).wait_send()

            @pl.when(z != zz)
            def _():
                self.up(zz).wait_send()
        self.xex().wait_send()
        for s in range(2):
            seq = self.x if s == 0 else 1 - self.x
            a, b, c = self.fin_copies(s)
            a.wait()
            b.wait_send()
            c.wait_send()
            self.relay(s).wait_send()
            for j, yy in ((0, self.y), (1, 1 - self.y)):
                r = self.spot(seq, 2 * yy + 1 - self.k)
                remote(r, r, self.fcs.at[s, j], self.fcr.at[s, j], device(self.z, self.x, self.y, 1 - self.k)).wait_recv()


def reduce_sems():
    D = pltpu.SemaphoreType.DMA
    return [D((4,)), D((4,)), D((4,)), D((4,)), D((4,)), D((5,)), D, D,
            D((2,)), D((2,)), D((2,)), D((2, 2)), D((2, 2))]


def reduce_bufs():
    V = lambda *s: pltpu.VMEM(s, BF)
    return [V(4, 2, 2, 64, 2048), V(4, 2, 64, 2048), V(5, 2, 64, 2048), V(64, 2048)]


def ring_bufs():
    return [pltpu.VMEM((2, 2, 2, 64, 2048), BF)] * 2


class GradReduce:
    def __init__(self, out, own, away, got, sems):
        self.out, self.own, self.away, self.got = out, own, away, got
        self.xs, self.xr, self.zs, self.zr = sems
        self.z, self.x, self.y, self.k = place()

    def x_send(self, d):
        return remote(self.away.at[FAR.index(d) % 2], self.got.at[d], self.xs.at[d], self.xr.at[d], device(self.z, 1 - self.x, self.y, self.k))

    def z_send(self, d):
        here = self.out.at[self.z]
        if d == 0:
            return pltpu.make_async_copy(self.own.at[0], here, self.zs.at[0])
        return remote(self.own.at[d], here, self.zs.at[d], self.zr.at[d], device((self.z + d) % 4, self.x, self.y, self.k))

    def give(self, d, terms):
        i = FAR.index(d)
        if i >= 2:
            self.x_send(FAR[i - 2]).wait_send()
        self.away[i % 2] = terms.astype(BF)
        self.x_send(d).start()

    def keep(self, d, terms):
        self.x_send(d).wait_recv()
        self.own[d] = (terms + self.got[d].astype(F4)).astype(BF)
        self.z_send(d).start()

    def finish(self):
        self.z_send(0).wait()
        for d in FAR[2:]:
            self.x_send(d).wait_send()
        for d in range(4):
            if d:
                self.z_send(d).wait_send()
                frm = (self.z - d + 4) % 4
                r = self.out.at[frm]
                remote(r, r, self.zs.at[d], self.zr.at[d], device(frm, self.x, self.y, self.k)).wait_recv()


def grad_scratch(block):
    D = pltpu.SemaphoreType.DMA
    V = pltpu.VMEM
    return [V((4,) + block, BF), V((2,) + block, BF), V((4,) + block, BF)] + [D((4,))] * 4


def norm_rows(rows, gain, shift):
    v = rows.astype(F4)
    centred = v - jnp.mean(v, axis=-1, keepdims=True)
    spread = jnp.mean(centred * centred, axis=-1, keepdims=True)
    return (centred * lax.rsqrt(spread + EPS) * gain + shift).astype(BF)


def turn(v, tab):
    cos, lo, hi = tab
    return v * cos + pltpu.roll(v, 112, 1) * lo + pltpu.roll(v, 16, 1) * hi


def turn_back(v, tab):
    cos, lo, hi = tab
    return v * cos - pltpu.roll(v, 112, 1) * lo - pltpu.roll(v, 16, 1) * hi


def angle_table(within, block, b):
    cr, sr = within[0], within[1]
    cb, sb = block[0, pl.ds(b, 1)], block[1, pl.ds(b, 1)]
    cos, sin = cb * cr - sb * sr, sb * cr + cb * sr
    entry = lax.broadcasted_iota(jnp.int32, cos.shape, 1) % 64
    return cos, jnp.where(entry < 16, -sin, 0.0), jnp.where(entry < 16, 0.0, sin)


def angles(rows, step):
    frequency = (10000.0 ** (-2.0 * np.arange(16) / 32)).astype(np.float32).astype(np.float64)
    lanes = np.concatenate([frequency, frequency, np.zeros(32)] * 2)
    angle = step * np.arange(rows)[:, None] * lanes
    return np.stack([np.cos(angle), np.sin(angle)]).astype(np.float32)


def pick(index, parts):
    chosen = parts(0)
    for j in range(1, 8):
        chosen = jnp.where(index == j, parts(j), chosen)
    return chosen


def one_head(v, h, axis):
    entry = lax.broadcasted_iota(jnp.int32, v.shape, axis)
    return jnp.where((entry < 64) == (h == 0), v, jnp.zeros_like(v))


def masked(st, kr):
    row = lax.broadcasted_iota(jnp.int32, (256, 256), 0)
    column = lax.broadcasted_iota(jnp.int32, (256, 256), 1)
    last = jnp.where(row <= column, st[kr - 256:], -1e30)
    return last if kr == 256 else jnp.concatenate([st[:kr - 256], last], axis=0)


def flip(v):
    return v.astype(F4).T.astype(BF)


def front_kernel(order, tok, gs, within, block, cot, win, wout, wexp, wcon,
                 xn_out, ct_out, wx_out, wco, am_out, amt_out, dgelu_out, pg_out, gs_all,
                 xn, ct, xo, wx, wo, proj, am, amt, dgelu, pg, qkv, qt, kt, vt, ot, logs, gt, gpos, dqt, dk, dv,
                 osem, csem, gsem_s, gsem_r, *sems):
    z, x, y, k = place()
    c, q = z * 2 + x, 2 * y + k
    nt = len(token_sems())
    tx = TokenGather(xn, sems[:nt])
    tc = TokenGather(ct, sems[nt:2 * nt])
    pairs = [
        (lambda zz, j=j: win.at[j, :, columns(128, zz)], lambda zz, xx, j=j: wx.at[zz, xx, :, pl.ds(512 + 128 * j, 128)])
        for j in range(3)
    ] + [
        (lambda zz: wexp.at[:, columns(512, zz)], lambda zz, xx: wx.at[zz, xx, :, pl.ds(0, 512)]),
        (lambda zz: wcon.at[columns(512, zz), :], lambda zz, xx: wco.at[pl.ds(0, 512), columns(256, zz * 2 + xx)]),
        (lambda zz: wout.at[columns(128, zz), :], lambda zz, xx: wo.at[:, columns(256, zz * 2 + xx)]),
    ]
    wg = WeightGather(pairs, sems[2 * nt:])
    others, everyone = peers_of(z, x, y, k)
    meet(everyone)
    gcopies = [remote(gs, gs_all.at[c], gsem_s.at[i], gsem_r.at[i], others[i]) for i in range(7)]
    for g in gcopies:
        g.start()
    gs_all[c] = gs[...]
    wg.start(0, 1, 2)
    own_slot = pltpu.make_async_copy(cot.at[x], ct.at[z, x], csem)
    own_slot.start()
    for i in range(7):
        frm = gs_all.at[(c - i - 1 + 8) % 8]
        remote(frm, frm, gsem_s.at[i], gsem_r.at[i], others[i]).wait_recv()
    gain = jnp.concatenate([gs_all[i, 0:1, :] for i in range(8)], axis=1)
    shift = jnp.concatenate([gs_all[i, 1:2, :] for i in range(8)], axis=1)

    @pl.loop(0, 2)
    def _(i):
        xo[pl.ds(32 * i, 32)] = norm_rows(tok[1 - x, pl.ds(64 * q + 32 * i, 32)], gain, shift)

    @pl.loop(0, 8)
    def _(i):
        xn[z, x, pl.ds(32 * i, 32)] = norm_rows(tok[x, pl.ds(32 * i, 32)], gain, shift)

    cot_other = cot.at[1 - x, pl.ds(64 * q, 64)]
    tx.start(tx.chunk(z, 0, q), xo)
    tx.after_x()
    tc.start(cot.at[x, pl.ds(64 * q, 64)], cot_other)
    wg.start(5, 3)

    def project(i):
        zz = far_first(z, 3 - i)
        tx.landed(zz)

        @pl.loop(0, 2)
        def _(xx):
            row = pl.multiple_of(512 * zz + 256 * xx, 256)
            proj[pl.ds(row, 256)] = dot(xn[zz, xx], wx[:, :, :, pl.ds(512, 384)].reshape(2048, 384))

    tx.hop(1, 0)
    tx.hop(1, 1)
    for w in range(3):
        for d in (1, 2, 3):
            wg.forward(w, d)
    tx.y_hop(0, 1)
    tx.hop(2, 0)
    tx.hop(2, 1)
    tc.after_x()
    for s in range(2):
        tx.y_hop(1, s)
    for s in range(2):
        tx.hop(3, s)
    for s in range(2):
        tx.y_hop(2, s)
    wg.start(4)
    for s in range(2):
        tc.hop(1, s)
    for s in range(2):
        tx.y_hop(3, s)
    tc.y_hop(0, 1)
    for d in (1, 2, 3):
        wg.forward(5, d)
    for w in range(3):
        wg.landed(w)
    project(0)
    project(1)
    for s in range(2):
        tc.hop(2, s)
    for s in range(2):
        tc.y_hop(1, s)
    project(2)
    project(3)
    out_xn = pltpu.make_async_copy(xn, xn_out, osem.at[0])
    out_xn.start()
    for s in range(2):
        tc.hop(3, s)
    for s in range(2):
        tc.y_hop(2, s)

    @pl.loop(0, 16)
    def _(b):
        half = b // 8
        pair = b + half * (15 - 2 * b)
        here = pl.ds(pl.multiple_of(b * 128, 128), 128)
        t = angle_table(within, block, b)
        three = pick(order[0, pair], lambda j: proj[pl.ds(pl.multiple_of(256 * j + 128 * half, 128), 128)])
        rq = turn(three[:, 0:128], t).astype(BF) * BF(0.125)
        rk = turn(three[:, 128:256], t).astype(BF)
        rv = three[:, 256:384].astype(BF)
        qkv[0, here], qkv[1, here], qkv[2, here] = rq, rk, rv
        qt[:, here], kt[:, here], vt[:, here] = flip(rq), flip(rk), flip(rv)

    for i in range(8):
        kr, here = 256 * (i + 1), pl.ds(256 * i, 256)
        for h in range(2):
            st = masked(dot(qkv[1, :kr], one_head(qt[:, here], h, 0)), kr)
            peak = jnp.max(st, axis=0, keepdims=True)
            p = jnp.exp(st - peak)
            total = jnp.sum(p, axis=0, keepdims=True)
            o = dot(vt[:, :kr], p.astype(BF)) * (1.0 / total)
            ot[pl.ds(64 * h, 64), here] = o[64 * h:64 * h + 64]
            logs[pl.ds(h, 1), here] = peak + jnp.log(total)
        if i in (3, 5, 6):
            wg.forward(3, {3: 1, 5: 2, 6: 3}[i])
    for s in range(2):
        tc.y_hop(3, s)

    @pl.loop(0, 16)
    def _(b):
        here = pl.ds(pl.multiple_of(b * 128, 128), 128)
        gpos[here] = ot[:, here].T

    def by_rows(c2, half):
        p = order[1, c2]
        return lambda ref: pick(p, lambda j: ref[pl.ds(128 * (j if half == 0 else 15 - j), 128)])

    for half in range(2):
        @pl.loop(0, 8)
        def _(c2):
            row = pl.ds(pl.multiple_of(256 * c2 + 128 * half, 128), 128)
            am[row, pl.ds(512, 128)] = by_rows(c2, half)(gpos).astype(BF)

    own_slot.wait()
    wg.landed(5)

    @pl.loop(0, 4)
    def _(zz):
        tc.landed(zz)
        for xx in range(2):
            row = pl.multiple_of(512 * zz + 256 * xx, 256)
            proj[pl.ds(row, 256), pl.ds(0, 128)] = dot_t(ct[zz, xx], wo[...])

    out_ct = pltpu.make_async_copy(ct, ct_out, osem.at[1])
    out_ct.start()

    @pl.loop(0, 16)
    def _(b):
        half = b // 8
        pair = b + half * (15 - 2 * b)
        here = pl.ds(pl.multiple_of(b * 128, 128), 128)
        g = pick(order[0, pair], lambda j: proj[pl.ds(pl.multiple_of(256 * j + 128 * half, 128), 128), pl.ds(0, 128)])
        gpos[here] = g
        gt[:, here] = flip(g)

    dk[...] = jnp.zeros_like(dk)
    dv[...] = jnp.zeros_like(dv)
    for i in range(8):
        kr, here = 256 * (i + 1), pl.ds(256 * i, 256)
        for h in range(2):
            gT = gt[:, here]
            st = masked(dot(qkv[1, :kr], one_head(qt[:, here], h, 0)), kr)
            p = jnp.exp(st - logs[pl.ds(h, 1), here])
            low = p.astype(BF)
            at = pl.ds(64 * h, 64)
            delta = jnp.sum(ot[at, here] * gt[at, here].astype(F4), axis=0, keepdims=True)
            ds = (p * (dot(qkv[2, :kr], one_head(gT, h, 0)) - delta)).astype(BF)
            dv[:kr] += dot(low, one_head(gpos[here].astype(BF), h, 1))
            dk[:kr] += dot(ds, one_head(qkv[0, here], h, 1))
            dqt[at, here] = dot(kt[:, :kr], ds)[64 * h:64 * h + 64] * 0.125
        if i in (3, 5, 6):
            wg.forward(4, {3: 1, 5: 2, 6: 3}[i])

    @pl.loop(0, 16)
    def _(b):
        here = pl.ds(pl.multiple_of(b * 128, 128), 128)
        t = angle_table(within, block, b)
        gpos[here] = turn_back(dqt[:, here].T, t)
        dk[here] = turn_back(dk[here], t)

    for half in range(2):
        @pl.loop(0, 8)
        def _(c2):
            row = pl.ds(pl.multiple_of(256 * c2 + 128 * half, 128), 128)
            for j, ref in enumerate((gpos, dk, dv)):
                pg[row, pl.ds(128 * j, 128)] = by_rows(c2, half)(ref).astype(BF)

    outs = [pltpu.make_async_copy(pg, pg_out, osem.at[2])]
    outs[0].start()
    wg.landed(3)
    outs.append(pltpu.make_async_copy(wx, wx_out, osem.at[3]))
    outs[1].start()
    outs.append(pltpu.make_async_copy(wo, wco.at[pl.ds(512, 128)], osem.at[4]))
    outs[2].start()

    @pl.loop(0, 8)
    def _(i):
        at = pl.ds(pl.multiple_of(256 * i, 256), 256)
        u = dot(xn[i // 2, i % 2], wx[:, :, :, pl.ds(0, 512)].reshape(2048, 512))
        square = u * u
        t = jnp.tanh(0.7978845608028654 * (u + 0.044715 * u * square))
        half = 0.5 * (1.0 + t)
        am[at, pl.ds(0, 512)] = (u * half).astype(BF)
        dgelu[at] = half + 0.5 * u * (1.0 - t * t) * (0.7978845608028654 * (1.0 + 3 * 0.044715 * square))
        amt[:, at] = flip(am[at])

    for j, (src, dst) in enumerate(((am, am_out), (amt, amt_out), (dgelu, dgelu_out))):
        outs.append(pltpu.make_async_copy(src, dst, osem.at[5 + j]))
        outs[-1].start()
    wg.landed(4)
    tx.finish(xo)
    tc.finish(cot_other)
    for w in range(6):
        wg.finish(w)
    for g in gcopies:
        g.wait_send()
    for o in [out_xn, out_ct] + outs:
        o.wait()


def front_call(order, tokens, gs, cot, win, wout, wexp, wcon):
    S = jax.ShapeDtypeStruct
    ANY = pl.BlockSpec(memory_space=pl.ANY)
    VM = pl.BlockSpec(memory_space=pltpu.VMEM)
    D = pltpu.SemaphoreType.DMA
    V = pltpu.VMEM
    rows = (4, 2, 256, 2048)
    return pl.pallas_call(
        front_kernel,
        out_shape=[S(rows, BF), S(rows, BF), S((4, 2, 256, 896), BF), S((640, 2048), BF), S((2048, 640), BF), S((640, 2048), BF),
                   S((2048, 512), F4), S((2048, 384), BF), S((8, 8, 256), F4)],
        in_specs=[pl.BlockSpec(memory_space=pltpu.SMEM)] + [VM] * 4 + [ANY] * 5,
        out_specs=[ANY] * 8 + [VM],
        scratch_shapes=[V(rows, BF), V(rows, BF), V((64, 2048), BF), V((4, 2, 256, 896), BF), V((128, 2048), BF), V((2048, 384), F4),
                        V((2048, 640), BF), V((640, 2048), BF), V((2048, 512), F4), V((2048, 384), BF),
                        V((3, 2048, 128), BF), V((128, 2048), BF), V((128, 2048), BF), V((128, 2048), BF),
                        V((128, 2048), F4), V((8, 2048), F4), V((128, 2048), BF), V((2048, 128), F4), V((128, 2048), F4),
                        V((2048, 128), F4), V((2048, 128), F4), D((8,)), D, D((7,)), D((7,))]
        + token_sems() * 2 + weight_sems(6),
        compiler_params=pltpu.CompilerParams(collective_id=0, has_side_effects=True, vmem_limit_bytes=60 * MB),
        name="front",
    )(order, tokens, gs, jnp.asarray(angles(128, 1)), jnp.asarray(angles(16, 128)), cot, win, wout, wexp, wcon)


def norm_backward(tok, cot, ng, gains, out, stage, ssem, sums):
    gain = jnp.concatenate([gains[i, 0:1, :] for i in range(8)], axis=1)
    sums[...] = jnp.zeros_like(sums)

    def store(i):
        return pltpu.make_async_copy(stage.at[i % 2], out.at[i // 8, pl.ds(pl.multiple_of(32 * (i % 8), 32), 32)], ssem.at[i % 2])

    @pl.loop(0, 16)
    def _(i):
        s, at = i // 8, pl.ds(pl.multiple_of(32 * (i % 8), 32), 32)
        v = tok[s, at].astype(F4)
        centred = v - jnp.mean(v, axis=-1, keepdims=True)
        scale = lax.rsqrt(jnp.mean(centred * centred, axis=-1, keepdims=True) + EPS)
        xhat = centred * scale
        n = ng[s, at].astype(F4)
        g = n * gain
        along = jnp.mean(g * xhat, axis=-1, keepdims=True)

        @pl.when(i >= 2)
        def _():
            store(i - 2).wait()
        stage[i % 2] = cot[s, at].astype(F4) + (g - jnp.mean(g, axis=-1, keepdims=True) - xhat * along) * scale
        store(i).start()
        both = n * xhat
        sums[0] += both[:8] + both[8:16] + both[16:24] + both[24:]
        sums[1] += n[:8] + n[8:16] + n[16:24] + n[24:]

    store(14).wait()
    store(15).wait()


def back_kernel(am, amt, wco, wx, gains, ct, xn, dgelu, pg, tok, cot,
                out, ig, vectors, o1, o2,
                hp, ctr, col, dg, ng, stage, sums, vec, vecs, psem, rsem, csem, dsem, tsem, ssem, vs, vr, *rest):
    z, x, y, k = place()
    c = z * 2 + x
    rest = list(rest)
    take = lambda n: [rest.pop(0) for _ in range(n)]
    ring = take(2)
    nb, ns = len(reduce_bufs()), len(reduce_sems())
    tn = TokenReduce(ng, ring + take(nb), take(ns))
    to = TokenReduce(out, ring + take(nb), take(ns))
    g1 = GradReduce(o1, *take(3), take(4))
    g2 = GradReduce(o2, *take(3), take(4))
    others, everyone = peers_of(z, x, y, k)
    load_pg = pltpu.make_async_copy(pg, hp.at[:, pl.ds(512, 384)], psem)
    load_pg.start()

    def chunk_loads(i):
        zz = far_first(z, i)
        return (pltpu.make_async_copy(ct.at[zz], ctr.at[i % 2], rsem.at[i % 2]),
                pltpu.make_async_copy(dgelu.at[pl.ds(pl.multiple_of(512 * zz, 512), 512)], dg.at[i % 2], dsem.at[i % 2]))

    blocks = [(src, d, xx) for xx in (1 - x, x) for src in (ct, xn) for d in FAR]

    def block_load(n):
        src, d, xx = blocks[n]
        return pltpu.make_async_copy(src.at[:, :, :, columns(256, 2 * ((z + d) % 4) + xx)], col.at[n % 3], csem.at[n % 3])

    for i in range(2):
        for cp in chunk_loads(i):
            cp.start()
    for n in range(3):
        block_load(n).start()
    meet(everyone)

    def pull(i):
        zz = far_first(z, i)
        for cp in chunk_loads(i):
            cp.wait()
        for xx in range(2):
            row = pl.multiple_of(512 * zz + 256 * xx, 256)
            g = dot_t(ctr[i % 2, xx], wco[pl.ds(0, 512)])
            hp[pl.ds(row, 256), pl.ds(0, 512)] = (g * dg[i % 2, pl.ds(256 * xx, 256)]).astype(BF)
        if i < 2:
            for cp in chunk_loads(i + 2):
                cp.start()

    def fill_n(i):
        tn.fill(i, lambda zz, xx, r: hp[pl.ds(pl.multiple_of(512 * zz + 256 * xx + r, 64), 64)], lambda a, at: dot_t(a, wx[at]),
                lambda: tn.core(i - 2).wait_send() if i >= 2 else None)

    def fill_o(i):
        to.fill(i, lambda zz, xx, r: am[pl.ds(pl.multiple_of(512 * zz + 256 * xx + r, 64), 64)], lambda a, at: dot(a, wco[:, at]),
                lambda: (to.core(i - 2) if i >= 2 else tn.core(i + 2)).wait_send())

    def grad(n):
        block_load(n).wait()
        v = col[n % 3].reshape(2048, 256)
        terms = dot(amt[...], v) if n // 4 % 2 == 0 else dot(flip(v), hp[...])
        g = (g1, g2)[n // 4 % 2]
        (g.give if n < 8 else g.keep)(blocks[n][1], terms)
        if n + 3 < 16:
            block_load(n + 3).start()

    pull(0)
    load_pg.wait()
    fill_n(0)
    pull(1)
    fill_n(1)
    tn.after_core(0)
    pull(2)
    fill_n(2)
    tn.after_core(1)
    pull(3)
    fill_n(3)
    tn.after_core(2)
    grad(0)
    tn.after_core(3)
    tn.after_y(0)
    tn.line(0)
    fill_o(0)
    grad(1)
    fill_o(1)
    tn.after_y(1)
    tn.line(1)
    to.after_core(0)
    grad(2)
    grad(3)
    fill_o(2)
    to.after_core(1)
    grad(4)
    tn.after_y(2)
    tn.line(2)
    grad(5)
    fill_o(3)
    to.after_core(2)
    grad(6)
    grad(7)
    to.after_core(3)
    grad(8)
    tn.after_y(3)
    tn.line(3)
    loads = [pltpu.make_async_copy(tok, ctr.at[0], tsem.at[0]), pltpu.make_async_copy(cot, ctr.at[1], tsem.at[1])]
    for cp in loads:
        cp.start()
    grad(9)
    grad(10)
    grad(11)
    to.after_y(0)
    to.line(0)
    tn.spread(0)
    tn.spread(1)
    grad(12)
    grad(13)
    tn.spread_y(0)
    tn.spread_y(1)
    to.after_y(1)
    to.line(1)
    grad(14)
    grad(15)
    tn.finish()
    for cp in loads:
        cp.wait()
    to.after_y(2)
    to.line(2)
    norm_backward(ctr.at[0], ctr.at[1], ng, gains, ig, stage, ssem, sums)
    for i in range(8):
        at = slice(256 * i, 256 * i + 256)
        for j in range(2):
            vec[i, j:j + 1, :] = jnp.sum(sums[j, :, at], axis=0, keepdims=True)
        vec[i, 2:8, :] = jnp.zeros((6, 256), F4)
    vecs[c] = vec[c]
    copies = [remote(vec.at[(c + i + 1) % 8], vecs.at[c], vs.at[i], vr.at[i], others[i]) for i in range(7)]
    for cp in copies:
        cp.start()
    to.after_y(3)
    to.line(3)
    to.spread(0)
    to.spread(1)
    to.spread_y(0)
    to.spread_y(1)
    for i in range(7):
        frm = vecs.at[(c - i - 1 + 8) % 8]
        remote(frm, frm, vs.at[i], vr.at[i], others[i]).wait_recv()
    total = vecs[0]
    for i in range(1, 8):
        total = total + vecs[i]
    vectors[...] = total
    to.core(2).wait_send()
    to.core(3).wait_send()
    to.finish()
    g1.finish()
    g2.finish()
    for cp in copies:
        cp.wait_send()


def back_call(am, amt, wco, wx, gains, ct, xn, dgelu, pg, tok, cot):
    S = jax.ShapeDtypeStruct
    ANY = pl.BlockSpec(memory_space=pl.ANY)
    VM = pl.BlockSpec(memory_space=pltpu.VMEM)
    D = pltpu.SemaphoreType.DMA
    V = pltpu.VMEM
    b1, b2 = (640, 256), (256, 896)
    return pl.pallas_call(
        back_kernel,
        out_shape=[S((2, 256, 2048), BF), S((2, 256, 2048), F4), S((8, 256), F4), S((4,) + b1, BF), S((4,) + b2, BF)],
        in_specs=[VM] * 5 + [ANY] * 6,
        out_specs=[ANY, ANY, VM, ANY, ANY],
        scratch_shapes=[V((2048, 896), BF), V((2, 2, 256, 2048), BF), V((3, 4, 2, 256, 256), BF), V((2, 512, 512), F4),
                        V((2, 256, 2048), BF), V((2, 32, 2048), F4), V((2, 8, 2048), F4), V((8, 8, 256), F4), V((8, 8, 256), F4),
                        D, D((2,)), D((3,)), D((2,)), D((2,)), D((2,)), D((7,)), D((7,))]
        + ring_bufs() + (reduce_bufs() + reduce_sems()) * 2 + grad_scratch(b1) + grad_scratch(b2),
        compiler_params=pltpu.CompilerParams(collective_id=1, has_side_effects=True, vmem_limit_bytes=62 * MB),
        name="back",
    )(am, amt, wco, wx.reshape(2048, 896), gains, ct, xn, dgelu, pg, tok, cot)


def own_local(tokens, pair_index, norm_gain, norm_shift, w_attention_in, w_attention_out, w_expand, w_contract, cotangent):
    x = lax.axis_index("ctx") % 2
    pairs = lax.dynamic_index_in_dim(pair_index, x, 0, False)
    which = jnp.arange(8, dtype=jnp.int32)
    inverse = jnp.sum(jnp.where(pairs[None, :] == which[:, None], which[None, :], 0), axis=1).astype(jnp.int32)
    gs = jnp.concatenate([norm_gain[None], norm_shift[None], jnp.zeros((6, 256), BF)], axis=0).astype(F4)
    xn, ct, wx, wco, am, amt, dgelu, pg, gains = front_call(
        jnp.stack([inverse, pairs]), tokens, gs, cotangent, w_attention_in, w_attention_out, w_expand, w_contract)
    out_sum, input_grad, vectors, o1, o2 = back_call(am, amt, wco, wx, gains, ct, xn, dgelu, pg, tokens, cotangent)
    output = (tokens.astype(F4) + out_sum.astype(F4)).astype(BF)
    gcon = o1[:, :512].reshape(2048, 256).astype(F4)
    gout = o1[:, 512:].reshape(512, 256).astype(F4)
    gexp = o2[:, :, :512].transpose(1, 0, 2).reshape(256, 2048).astype(F4)
    gin = o2[:, :, 512:].reshape(4, 256, 3, 128).transpose(2, 1, 0, 3).reshape(3, 256, 512).astype(F4)
    return (output, input_grad, vectors[0], vectors[1], gin, gout, gexp, gcon)


def local(tokens, pair_index, norm_gain, norm_shift, w_attention_in, w_attention_out, w_expand, w_contract, cotangent):
    args = (tokens, pair_index, norm_gain, norm_shift, w_attention_in, w_attention_out, w_expand, w_contract, cotangent)
    sizes = (lax.axis_size("ctx"), lax.axis_size("tp")) + tokens.shape + w_attention_in.shape[2:] + w_expand.shape[1:]
    if sizes == (8, 4, 2, 256, 2048, 512, 2048):
        return own_local(*args)
    return general_local(*args)


def solution(mesh):
    in_specs = (
        P(None, "ctx", None),
        P(),
        P("ctx"),
        P("ctx"),
        P(None, "ctx", "tp"),
        P("tp", "ctx"),
        P("ctx", "tp"),
        P("tp", "ctx"),
        P(None, "ctx", None),
    )
    out_specs = (
        P(None, "ctx", None),
        P(None, "ctx", None),
        P("ctx"),
        P("ctx"),
        P(None, "ctx", "tp"),
        P("tp", "ctx"),
        P("ctx", "tp"),
        P("tp", "ctx"),
    )
    return jax.shard_map(local, mesh=mesh, in_specs=in_specs, out_specs=out_specs, check_vma=False)
```

```python
import itertools

import jax
import jax.numpy as jnp
import numpy as np
from jax import lax
from jax.experimental import pallas as pl
from jax.experimental.pallas import tpu as pltpu
from jax.sharding import PartitionSpec as P

HEAD_DIM = 64
ROT = 32


epsilon = 1e-05


def position_table(pair_index, shard_rows):
    pair_count = pair_index.shape[1]
    half_rows = shard_rows // 2
    token_index = jnp.arange(shard_rows * pair_count, dtype=jnp.int32)
    owning = token_index // shard_rows
    within = token_index % shard_rows
    picked = (owning[:, None] == jnp.arange(pair_count, dtype=jnp.int32)[None, :]).astype(jnp.int32)
    chosen = jnp.sum(picked[None, :, :] * pair_index[:, None, :], axis=2)
    first_half = chosen * half_rows + within[None, :]
    second = (2 * pair_count - 1 - chosen) * half_rows + within[None, :] - half_rows
    return jnp.where(within[None, :] < half_rows, first_half, second)


def rotate(tensor, positions):
    half_rot = ROT // 2
    frequency = 10000.0 ** (-2.0 * jnp.arange(half_rot, dtype=jnp.float32) / ROT)
    angles = positions.astype(jnp.float32)[..., None] * frequency
    cosine = jnp.cos(angles)[..., None, :]
    sine_part = jnp.sin(angles)[..., None, :]
    leading = tensor[..., :half_rot]
    trailing = tensor[..., half_rot:ROT]
    return jnp.concatenate(
        [
            leading * cosine - trailing * sine_part,
            trailing * cosine + leading * sine_part,
            tensor[..., ROT:],
        ],
        axis=-1,
    )


def gelu_tanh(values_in):
    return (
        0.5
        * values_in
        * (
            1.0
            + jnp.tanh(
                0.7978845608028654 * (values_in + 0.044715 * values_in * values_in * values_in)
            )
        )
    )


def layer_norm(inputs, gain_full, shift_full):
    centred = inputs - jnp.mean(inputs, axis=-1, keepdims=True)
    spread = jnp.mean(centred * centred, axis=-1, keepdims=True)
    return centred * lax.rsqrt(spread + epsilon) * gain_full + shift_full


def block_probs(queries, keys_block, log_total, query_pos, key_pos):
    raw_scores = jnp.einsum(
        "sqhe,skhe->shqk", queries, keys_block, preferred_element_type=jnp.float32
    )
    allowed = key_pos[:, None, None, :] <= query_pos[:, None, :, None]
    return jnp.where(allowed, jnp.exp(raw_scores * HEAD_DIM ** (-0.5) - log_total[..., None]), 0.0)


def score_grads(
    queries, keys_block, values_block, log_total, row_delta, out_grad, query_pos, key_pos
):
    probs_full = block_probs(queries, keys_block, log_total, query_pos, key_pos)
    prob_grad = jnp.einsum(
        "sqhe,skhe->shqk", out_grad, values_block, preferred_element_type=jnp.float32
    )
    score_grad = (probs_full * (prob_grad - row_delta[..., None]) * HEAD_DIM ** (-0.5)).astype(
        jnp.bfloat16
    )
    return (probs_full.astype(jnp.bfloat16), score_grad)


def key_slice(keys_all, offset, key_rows, head_count):
    seq_count = keys_all.shape[0]
    return lax.dynamic_slice_in_dim(keys_all, offset, key_rows, 1).reshape(
        seq_count, key_rows, head_count, HEAD_DIM
    )


def log_totals(queries, keys_all, query_pos, pos_table, key_rows):
    seq_count, query_rows, head_count, head_size = queries.shape
    turn_count = keys_all.shape[1] // key_rows

    def log_one_turn(turn_index, state_in):
        running_max, running_sum = state_in
        offset = turn_index * key_rows
        keys_block = key_slice(keys_all, offset, key_rows, head_count)
        key_pos = lax.dynamic_slice_in_dim(pos_table, offset, key_rows, 1)
        raw_scores = jnp.einsum(
            "sqhe,skhe->shqk", queries, keys_block, preferred_element_type=jnp.float32
        ) * HEAD_DIM ** (-0.5)
        allowed = key_pos[:, None, None, :] <= query_pos[:, None, :, None]
        masked = jnp.where(allowed, raw_scores, -1e30)
        new_max = jnp.maximum(running_max, jnp.max(masked, axis=-1))
        kept_terms = jnp.where(allowed, jnp.exp(masked - new_max[..., None]), 0.0)
        return (
            new_max,
            running_sum * jnp.exp(running_max - new_max) + jnp.sum(kept_terms, axis=-1),
        )

    initial = (
        jnp.full((seq_count, head_count, query_rows), -1e30, jnp.float32),
        jnp.zeros((seq_count, head_count, query_rows), jnp.float32),
    )
    final_max, final_sum = lax.fori_loop(0, turn_count, log_one_turn, initial)
    return final_max + jnp.log(final_sum)


def attend_values(queries, keys_all, values_all, log_total, query_pos, pos_table, key_rows):
    head_count = queries.shape[2]
    turn_count = keys_all.shape[1] // key_rows

    def attend_one_turn(turn_index, running):
        offset = turn_index * key_rows
        keys_block = key_slice(keys_all, offset, key_rows, head_count)
        values_block = key_slice(values_all, offset, key_rows, head_count)
        key_pos = lax.dynamic_slice_in_dim(pos_table, offset, key_rows, 1)
        weights_low = block_probs(queries, keys_block, log_total, query_pos, key_pos).astype(
            jnp.bfloat16
        )
        return running + jnp.einsum(
            "shqk,skhe->sqhe", weights_low, values_block, preferred_element_type=jnp.float32
        )

    return lax.fori_loop(0, turn_count, attend_one_turn, jnp.zeros(queries.shape, jnp.float32))


def full_grads(
    queries, keys_all, values_all, log_total, row_delta, out_grad, query_pos, pos_table, key_rows
):
    seq_count, query_rows, head_count, head_size = queries.shape
    turn_count = keys_all.shape[1] // key_rows

    def full_one_turn(turn_index, state_in):
        query_grad, key_terms, value_terms = state_in
        offset = turn_index * key_rows
        keys_block = key_slice(keys_all, offset, key_rows, head_count)
        values_block = key_slice(values_all, offset, key_rows, head_count)
        key_pos = lax.dynamic_slice_in_dim(pos_table, offset, key_rows, 1)
        weights_low, score_grad = score_grads(
            queries, keys_block, values_block, log_total, row_delta, out_grad, query_pos, key_pos
        )
        query_grad = query_grad + jnp.einsum(
            "shqk,skhe->sqhe", score_grad, keys_block, preferred_element_type=jnp.float32
        )
        key_part = jnp.einsum(
            "shqk,sqhe->skhe", score_grad, queries, preferred_element_type=jnp.float32
        ).reshape(seq_count, key_rows, head_count * head_size)
        value_part = jnp.einsum(
            "shqk,sqhe->skhe", weights_low, out_grad, preferred_element_type=jnp.float32
        ).reshape(seq_count, key_rows, head_count * head_size)
        key_terms = lax.dynamic_update_slice_in_dim(key_terms, key_part, offset, 1)
        value_terms = lax.dynamic_update_slice_in_dim(value_terms, value_part, offset, 1)
        return (query_grad, key_terms, value_terms)

    initial = (
        jnp.zeros(queries.shape, jnp.float32),
        jnp.zeros(keys_all.shape, jnp.float32),
        jnp.zeros(values_all.shape, jnp.float32),
    )
    return lax.fori_loop(0, turn_count, full_one_turn, initial)


def general_local(
    tokens,
    pair_index,
    norm_gain,
    norm_shift,
    w_attention_in,
    w_attention_out,
    w_expand,
    w_contract,
    cotangent,
):
    seq_count, shard_rows, model_width = tokens.shape
    gain_full, shift_full, attention_in, attention_out, expand_full, contract_full = (
        lax.all_gather(norm_gain, "ctx", axis=0, tiled=True),
        lax.all_gather(norm_shift, "ctx", axis=0, tiled=True),
        lax.all_gather(w_attention_in, "ctx", axis=1, tiled=True),
        lax.all_gather(w_attention_out, "ctx", axis=1, tiled=True),
        lax.all_gather(w_expand, "ctx", axis=0, tiled=True),
        lax.all_gather(w_contract, "ctx", axis=1, tiled=True),
    )
    local_width = attention_in.shape[2]
    head_count = local_width // HEAD_DIM
    flat_rows = seq_count * shard_rows
    pos_table = position_table(pair_index, shard_rows)
    total_rows = pos_table.shape[1]
    own_pos = lax.dynamic_slice_in_dim(pos_table, lax.axis_index("ctx") * shard_rows, shard_rows, 1)
    key_rows = min(total_rows, 1024)
    inputs = tokens.astype(jnp.float32)
    normed_full, norm_pull = jax.vjp(
        layer_norm, inputs, gain_full.astype(jnp.float32), shift_full.astype(jnp.float32)
    )
    normed = normed_full.astype(jnp.bfloat16).reshape(flat_rows, model_width)
    projected = jnp.einsum("td,kde->kte", normed, attention_in, preferred_element_type=jnp.float32)
    split_heads = projected.reshape(3, seq_count, shard_rows, head_count, HEAD_DIM)
    rotated, rotate_pull = jax.vjp(lambda pair_part: rotate(pair_part, own_pos), split_heads[:2])
    queries = rotated[0].astype(jnp.bfloat16)
    own_keys = rotated[1].astype(jnp.bfloat16)
    own_values = split_heads[2].astype(jnp.bfloat16)
    keys_all, values_all = (
        lax.all_gather(
            own_keys.reshape(seq_count, shard_rows, local_width), "ctx", axis=1, tiled=True
        ),
        lax.all_gather(
            own_values.reshape(seq_count, shard_rows, local_width), "ctx", axis=1, tiled=True
        ),
    )
    log_total = log_totals(queries, keys_all, own_pos, pos_table, key_rows)
    attended = attend_values(queries, keys_all, values_all, log_total, own_pos, pos_table, key_rows)
    mixed = attended.reshape(flat_rows, local_width).astype(jnp.bfloat16)
    hidden_pre = jnp.dot(normed, expand_full, preferred_element_type=jnp.float32)
    activated_full, gelu_pull = jax.vjp(gelu_tanh, hidden_pre)
    activated = activated_full.astype(jnp.bfloat16)
    branch = jnp.dot(mixed, attention_out, preferred_element_type=jnp.float32) + jnp.dot(
        activated, contract_full, preferred_element_type=jnp.float32
    )
    branch = lax.psum(branch.astype(jnp.bfloat16), "tp").astype(jnp.float32)
    output = (inputs + branch.reshape(seq_count, shard_rows, model_width)).astype(jnp.bfloat16)
    upstream = cotangent.reshape(flat_rows, model_width)
    contract_grad = jnp.einsum("tf,td->fd", activated, upstream, preferred_element_type=jnp.float32)
    (gelu_grad,) = gelu_pull(
        jnp.einsum("td,fd->tf", upstream, contract_full, preferred_element_type=jnp.float32)
    )
    hidden_grad = gelu_grad.astype(jnp.bfloat16)
    expand_grad = jnp.einsum("td,tf->df", normed, hidden_grad, preferred_element_type=jnp.float32)
    mixed_grad = jnp.einsum(
        "td,ed->te", upstream, attention_out, preferred_element_type=jnp.float32
    ).astype(jnp.bfloat16)
    attention_out_grad = jnp.einsum(
        "te,td->ed", mixed, upstream, preferred_element_type=jnp.float32
    )
    out_grad = mixed_grad.reshape(seq_count, shard_rows, head_count, HEAD_DIM)
    row_delta = jnp.sum(out_grad.astype(jnp.float32) * attended, axis=-1).transpose(0, 2, 1)
    query_grad, key_terms, value_terms = full_grads(
        queries, keys_all, values_all, log_total, row_delta, out_grad, own_pos, pos_table, key_rows
    )
    key_grad, value_grad = (
        lax.psum_scatter(
            key_terms.astype(jnp.bfloat16), "ctx", scatter_dimension=1, tiled=True
        ).astype(jnp.float32),
        lax.psum_scatter(
            value_terms.astype(jnp.bfloat16), "ctx", scatter_dimension=1, tiled=True
        ).astype(jnp.float32),
    )
    key_grad = key_grad.reshape(seq_count, shard_rows, head_count, HEAD_DIM)
    value_grad = value_grad.reshape(seq_count, shard_rows, head_count, HEAD_DIM)
    (rotated_grad,) = rotate_pull(jnp.stack([query_grad, key_grad]))
    projected_grad = (
        jnp.concatenate([rotated_grad, value_grad[None]], axis=0)
        .reshape(3, flat_rows, local_width)
        .astype(jnp.bfloat16)
    )
    attention_in_grad = jnp.einsum(
        "td,kte->kde", normed, projected_grad, preferred_element_type=jnp.float32
    )
    normed_grad = jnp.einsum(
        "kte,kde->td", projected_grad, attention_in, preferred_element_type=jnp.float32
    )
    normed_grad = normed_grad + jnp.einsum(
        "tf,df->td", hidden_grad, expand_full, preferred_element_type=jnp.float32
    )
    normed_grad = lax.psum(normed_grad.astype(jnp.bfloat16), "tp").astype(jnp.float32)
    input_part, gain_grad, shift_grad = norm_pull(
        normed_grad.reshape(seq_count, shard_rows, model_width)
    )
    input_grad = input_part + cotangent.astype(jnp.float32)
    reduced = (
        lax.psum_scatter(
            gain_grad.astype(jnp.bfloat16), "ctx", scatter_dimension=0, tiled=True
        ).astype(jnp.float32),
        lax.psum_scatter(
            shift_grad.astype(jnp.bfloat16), "ctx", scatter_dimension=0, tiled=True
        ).astype(jnp.float32),
        lax.psum_scatter(
            attention_in_grad.astype(jnp.bfloat16), "ctx", scatter_dimension=1, tiled=True
        ).astype(jnp.float32),
        lax.psum_scatter(
            attention_out_grad.astype(jnp.bfloat16), "ctx", scatter_dimension=1, tiled=True
        ).astype(jnp.float32),
        lax.psum_scatter(
            expand_grad.astype(jnp.bfloat16), "ctx", scatter_dimension=0, tiled=True
        ).astype(jnp.float32),
        lax.psum_scatter(
            contract_grad.astype(jnp.bfloat16), "ctx", scatter_dimension=1, tiled=True
        ).astype(jnp.float32),
    )
    return (
        output,
        input_grad,
        reduced[0],
        reduced[1],
        reduced[2],
        reduced[3],
        reduced[4],
        reduced[5],
    )


MESH = pl.DeviceIdType.MESH
MB = 1 << 20
EPS = 1e-05
BF = jnp.bfloat16
F4 = jnp.float32
NT = (((1,), (1,)), ((), ()))
FAR = (2, 3, 1, 0)


def place():
    c = lax.axis_index("ctx")
    t = lax.axis_index("tp")
    return c // 2, c % 2, t // 2, t % 2


def device(z, x, y, k):
    return (z * 2 + x, y * 2 + k)


def remote(src, dst, send_sem, recv_sem, target):
    return pltpu.make_async_remote_copy(
        src_ref=src, dst_ref=dst, send_sem=send_sem, recv_sem=recv_sem,
        device_id=target, device_id_type=MESH,
    )


def meet(peers):
    barrier = pltpu.get_barrier_semaphore()
    for peer in peers:
        pl.semaphore_signal(barrier, inc=1, device_id=peer, device_id_type=MESH)
    pl.semaphore_wait(barrier, len(peers))


def peers_of(z, x, y, k):
    c = z * 2 + x
    others = [((c + i) % 8, lax.axis_index("tp")) for i in range(1, 8)]
    return others, others + [device(z, x, 1 - y, k), device(z, x, y, 1 - k)]


def columns(n, i):
    return pl.ds(pl.multiple_of(n * i, n), n)


def dot(a, b):
    return jnp.dot(a, b, preferred_element_type=F4)


def dot_t(a, b):
    return lax.dot_general(a, b, NT, preferred_element_type=F4)


def far_first(z, i):
    return (3 * (1 - z // 2), z // 2 + 2 * (1 - z % 2), 1 + z % 2, z)[i]


def add_into(dst, src):
    lead, rows = dst.shape[:-2], dst.shape[-2]
    for idx in itertools.product(*(range(n) for n in lead)):
        @pl.loop(0, rows // 16)
        def _(i):
            at = idx + (pl.ds(pl.multiple_of(16 * i, 16), 16), slice(None))
            dst[at] = (dst[at].astype(F4) + src[at].astype(F4)).astype(BF)


class TokenGather:
    def __init__(self, whole, sems):
        self.whole = whole
        self.xs, self.xr, self.zs, self.zr, self.ys, self.yr, self.cs, self.cr = sems
        self.z, self.x, self.y, self.k = place()
        self.q = 2 * self.y + self.k

    def chunk(self, zz, s, q):
        xx = self.x if s == 0 else 1 - self.x
        return self.whole.at[zz, xx, pl.ds(64 * q, 64), :]

    def send_x(self, src):
        z, x, y, k = self.z, self.x, self.y, self.k
        return remote(src, self.whole.at[z, x, pl.ds(64 * self.q, 64), :], self.xs, self.xr, device(z, 1 - x, y, k))

    def send_up(self, zz, s, src):
        return remote(src, self.chunk(zz, s, self.q), self.zs.at[zz, s, 0], self.zr.at[zz, s],
                      device(jnp.minimum(self.z + 1, 3), self.x, self.y, self.k))

    def send_down(self, zz, s, src):
        return remote(src, self.chunk(zz, s, self.q), self.zs.at[zz, s, 1], self.zr.at[zz, s],
                      device(jnp.maximum(self.z - 1, 0), self.x, self.y, self.k))

    def send_y(self, zz, s):
        c = self.chunk(zz, s, self.q)
        return remote(c, c, self.ys.at[zz, s], self.yr.at[zz, s], device(self.z, self.x, 1 - self.y, self.k))

    def send_core(self, zz, s, j):
        yy = self.y if j == 0 else 1 - self.y
        c = self.chunk(zz, s, 2 * yy + self.k)
        return remote(c, c, self.cs.at[zz, s, j], self.cr.at[zz, s, j], device(self.z, self.x, self.y, 1 - self.k))

    def both_ways(self, s, src):
        z = self.z

        @pl.when(z < 3)
        def _():
            self.send_up(z, s, src).start()

        @pl.when(z > 0)
        def _():
            self.send_down(z, s, src).start()

    def start(self, own_quarter, other_quarter):
        self.send_x(other_quarter).start()
        self.both_ways(0, own_quarter)

    def after_x(self):
        c = self.chunk(self.z, 1, self.q)
        remote(c, c, self.xs, self.xr, device(self.z, 1 - self.x, self.y, self.k)).wait_recv()
        self.both_ways(1, c)
        self.send_y(self.z, 1).start()
        self.send_core(self.z, 1, 0).start()

    def hop(self, d, s):
        z = self.z

        @pl.when(z >= d)
        def _():
            zz = z - d
            c = self.chunk(zz, s, self.q)
            self.send_down(zz, s, c).wait_recv()

            @pl.when(z < 3)
            def _():
                self.send_up(zz, s, c).start()

            self.send_y(zz, s).start()
            self.send_core(zz, s, 0).start()

        @pl.when(z + d <= 3)
        def _():
            zz = z + d
            c = self.chunk(zz, s, self.q)
            self.send_up(zz, s, c).wait_recv()

            @pl.when(z > 0)
            def _():
                self.send_down(zz, s, c).start()

            self.send_y(zz, s).start()
            self.send_core(zz, s, 0).start()

    def y_in(self, zz, s):
        c = self.chunk(zz, s, 2 * (1 - self.y) + self.k)
        remote(c, c, self.ys.at[zz, s], self.yr.at[zz, s], device(self.z, self.x, 1 - self.y, self.k)).wait_recv()
        self.send_core(zz, s, 1).start()

    def y_hop(self, d):
        z = self.z
        if d == 0:
            self.y_in(z, 1)
            return
        for s in range(2):
            pl.when(z >= d)(lambda: self.y_in(z - d, s))
            pl.when(z + d <= 3)(lambda: self.y_in(z + d, s))

    def landed(self, zz):
        def rest(s):
            for j in range(2):
                yy = self.y if j == 0 else 1 - self.y
                c = self.chunk(zz, s, 2 * yy + 1 - self.k)
                remote(c, c, self.cs.at[zz, s, j], self.cr.at[zz, s, j], device(self.z, self.x, self.y, 1 - self.k)).wait_recv()

        pl.when(self.z != zz)(lambda: rest(0))
        rest(1)

    def finish(self, other_quarter):
        z = self.z
        self.send_x(other_quarter).wait_send()
        for zz in range(4):
            for s in range(2):
                def rest():
                    self.send_y(zz, s).wait_send()
                    for j in range(2):
                        self.send_core(zz, s, j).wait_send()
                if s == 0:
                    pl.when(z != zz)(rest)
                else:
                    rest()
                c = self.chunk(zz, s, self.q)

                @pl.when((z < 3) & (zz <= z))
                def _():
                    self.send_up(zz, s, c).wait_send()

                @pl.when((z > 0) & (zz >= z))
                def _():
                    self.send_down(zz, s, c).wait_send()


def token_sems():
    D = pltpu.SemaphoreType.DMA
    return [D, D, D((4, 2, 2)), D((4, 2)), D((4, 2)), D((4, 2)), D((4, 2, 2)), D((4, 2, 2))]


class WeightGather:
    def __init__(self, pairs, sems):
        self.pairs = pairs
        self.zs, self.zr, self.xs, self.xr, self.loc = sems
        self.z, self.x, self.y, self.k = place()

    def z_send(self, d, w):
        src, dst = self.pairs[w]
        to = (self.z + d) % 4
        return remote(src(to), dst(self.z, self.x), self.zs.at[d, w], self.zr.at[d, w], device(to, self.x, self.y, self.k))

    def z_recv(self, d, w):
        dst = self.pairs[w][1]
        frm = (self.z - d + 4) % 4
        return remote(dst(frm, self.x), dst(frm, self.x), self.zs.at[d, w], self.zr.at[d, w], device(frm, self.x, self.y, self.k))

    def x_send(self, d, w):
        src, dst = self.pairs[w]
        frm = (self.z - d + 4) % 4
        s = src(self.z) if d == 0 else dst(frm, self.x)
        return remote(s, dst(frm, self.x), self.xs.at[d, w], self.xr.at[d, w], device(self.z, 1 - self.x, self.y, self.k))

    def x_recv(self, d, w):
        frm = (self.z - d + 4) % 4
        r = self.pairs[w][1](frm, 1 - self.x)
        return remote(r, r, self.xs.at[d, w], self.xr.at[d, w], device(self.z, 1 - self.x, self.y, self.k))

    def local(self, w):
        src, dst = self.pairs[w]
        return pltpu.make_async_copy(src(self.z), dst(self.z, self.x), self.loc.at[w])

    def send(self, ws, *ds):
        for d in ds:
            for w in ws:
                if d:
                    self.z_send(d, w).start()
                else:
                    self.x_send(0, w).start()
                    self.local(w).start()

    def forward(self, ws, *ds):
        for d in ds:
            for w in ws:
                self.z_recv(d, w).wait_recv()
                self.x_send(d, w).start()

    def landed(self, w):
        self.local(w).wait()
        for d in range(4):
            self.x_recv(d, w).wait_recv()

    def finish(self, w):
        for d in range(4):
            if d:
                self.z_send(d, w).wait_send()
            self.x_send(d, w).wait_send()


def weight_sems(n):
    D = pltpu.SemaphoreType.DMA
    return [D((4, n)), D((4, n)), D((4, n)), D((4, n)), D((n,))]


class TokenReduce:
    def __init__(self, out, bufs, sems):
        self.out = out
        self.S, self.A, self.r1, self.r2, self.rz, self.rf = bufs
        (self.cs, self.cr, self.ys, self.yr, self.zs, self.zr, self.xs, self.xr,
         self.fl, self.fys, self.fyr, self.fcs, self.fcr) = sems
        self.z, self.x, self.y, self.k = place()
        self.q = 2 * self.y + self.k

    def slot(self, s):
        return self.x if s == 0 else 1 - self.x

    def core(self, i):
        zz = far_first(self.z, i)
        return remote(self.S.at[i % 2], self.r1.at[zz], self.cs.at[zz], self.cr.at[zz], device(self.z, self.x, self.y, 1 - self.k))

    def yex(self, zz, s):
        xx = self.slot(s)
        return remote(self.r1.at[zz, 1 - self.y, xx], self.r2.at[zz, xx], self.ys.at[zz, s], self.yr.at[zz, s],
                      device(self.z, self.x, 1 - self.y, self.k))

    def mine(self, zz, s):
        return self.r1.at[zz, self.y, self.slot(s)]

    def up(self, zz, s):
        return remote(self.mine(zz, s), self.rz.at[zz, s], self.zs.at[zz, s], self.zr.at[zz, s],
                      device(jnp.minimum(self.z + 1, 3), self.x, self.y, self.k))

    def down(self, zz, s):
        slot = jnp.where(zz == self.z - 1, 4, zz)
        return remote(self.mine(zz, s), self.rz.at[slot, s], self.zs.at[zz, s], self.zr.at[slot, s],
                      device(jnp.maximum(self.z - 1, 0), self.x, self.y, self.k))

    def arrive(self, zz, s, slot):
        r = self.rz.at[slot, s]
        remote(r, r, self.zs.at[0, s], self.zr.at[slot, s], device(self.z, self.x, self.y, 1 - self.k)).wait_recv()
        add_into(self.mine(zz, s), r)

    def xex(self):
        return remote(self.mine(self.z, 1), self.rf, self.xs, self.xr, device(self.z, 1 - self.x, self.y, self.k))

    def fill(self, i, lhs, rhs, free):
        zz = far_first(self.z, i)
        free()

        def rows(kk):
            return jnp.concatenate([lhs(zz, xx, 64 * (2 * yy + kk)) for yy in range(2) for xx in range(2)], axis=0)

        for kk, dst in ((1 - self.k, self.S.at[i % 2]), (self.k, self.A.at[i % 2])):
            a = rows(kk)

            @pl.loop(0, 4)
            def _(j):
                at = columns(512, j)
                dst[:, :, :, at] = rhs(a, at).astype(BF).reshape(2, 2, 64, 512)
            if kk is not self.k:
                self.core(i).start()

    def after_core(self, i):
        zz = far_first(self.z, i)
        self.core(i).wait_recv()
        add_into(self.r1.at[zz, 1 - self.y], self.A.at[i % 2, 1 - self.y])
        for s in (1, 0):
            self.yex(zz, s).start()
        add_into(self.r1.at[zz, self.y], self.A.at[i % 2, self.y])

    def line(self, i, s):
        z = self.z
        zz = far_first(z, i)
        self.yex(zz, s).wait_recv()
        add_into(self.mine(zz, s), self.r2.at[zz, self.slot(s)])
        if i < 3:
            @pl.when(zz > z)
            def _():
                pl.when(z > 0)(lambda: self.arrive(zz, s, zz))
                self.up(zz, s).start()

            @pl.when(zz < z)
            def _():
                pl.when(z < 3)(lambda: self.arrive(zz, s, zz))
                self.down(zz, s).start()
        else:
            pl.when(z > 0)(lambda: self.arrive(z, s, z))
            pl.when(z < 3)(lambda: self.arrive(z, s, 4))
            if s == 1:
                self.xex().start()

    def spot(self, s, q):
        return self.out.at[self.slot(s), pl.ds(64 * q, 64), :]

    def fin_copies(self, s):
        src = self.mine(self.z, 0) if s == 0 else self.rf
        here = self.spot(s, self.q)
        return (pltpu.make_async_copy(src, here, self.fl.at[s]),
                remote(src, here, self.fys.at[s], self.fyr.at[s], device(self.z, self.x, 1 - self.y, self.k)),
                remote(src, here, self.fcs.at[s, 0], self.fcr.at[s, 0], device(self.z, self.x, self.y, 1 - self.k)))

    def relay(self, s):
        r = self.spot(s, 2 * (1 - self.y) + self.k)
        return remote(r, r, self.fcs.at[s, 1], self.fcr.at[s, 1], device(self.z, self.x, self.y, 1 - self.k))

    def spread(self, s, base=None):
        if s == 1:
            self.xex().wait_recv()
        if base is not None:
            add_into(self.mine(self.z, 0) if s == 0 else self.rf, base(self.slot(s), pl.ds(64 * self.q, 64)))
        for cp in self.fin_copies(s):
            cp.start()

    def spread_y(self, s):
        r = self.spot(s, 2 * (1 - self.y) + self.k)
        remote(r, r, self.fys.at[s], self.fyr.at[s], device(self.z, self.x, 1 - self.y, self.k)).wait_recv()
        self.relay(s).start()

    def finish(self):
        z = self.z
        for zz in range(4):
            for s in range(2):
                self.yex(zz, s).wait_send()
                pl.when(z != zz)(lambda: self.up(zz, s).wait_send())
        self.xex().wait_send()
        for s in range(2):
            a, b, c = self.fin_copies(s)
            a.wait()
            b.wait_send()
            c.wait_send()
            self.relay(s).wait_send()
            for j, yy in ((0, self.y), (1, 1 - self.y)):
                r = self.spot(s, 2 * yy + 1 - self.k)
                remote(r, r, self.fcs.at[s, j], self.fcr.at[s, j], device(self.z, self.x, self.y, 1 - self.k)).wait_recv()


def reduce_sems():
    D = pltpu.SemaphoreType.DMA
    return [D((4,)), D((4,)), D((4, 2)), D((4, 2)), D((4, 2)), D((5, 2)), D, D,
            D((2,)), D((2,)), D((2,)), D((2, 2)), D((2, 2))]


def reduce_bufs():
    V = lambda *s: pltpu.VMEM(s, BF)
    return [V(4, 2, 2, 64, 2048), V(4, 2, 64, 2048), V(5, 2, 64, 2048), V(64, 2048)]


def ring_bufs():
    return [pltpu.VMEM((2, 2, 2, 64, 2048), BF)] * 2


class GradReduce:
    def __init__(self, parts, own, away, got, sems):
        self.parts, self.own, self.away, self.got = parts, own, away, got
        self.xs, self.xr, self.zs, self.zr = sems
        self.z, self.x, self.y, self.k = place()

    def x_send(self, d):
        return remote(self.away.at[FAR.index(d) % 2], self.got.at[d], self.xs.at[d], self.xr.at[d], device(self.z, 1 - self.x, self.y, self.k))

    def z_sends(self, d):
        for i, (part, there) in enumerate(self.parts):
            src, dst = self.own.at[(d,) + part], there(self.z)
            if d == 0:
                yield pltpu.make_async_copy(src, dst, self.zs.at[0, i])
            else:
                yield remote(src, dst, self.zs.at[d, i], self.zr.at[d, i], device((self.z + d) % 4, self.x, self.y, self.k))

    def give(self, d, terms):
        i = FAR.index(d)
        if i >= 2:
            self.x_send(FAR[i - 2]).wait_send()
        self.away[i % 2] = terms.astype(BF)
        self.x_send(d).start()

    def keep(self, d, terms):
        self.x_send(d).wait_recv()
        self.own[d] = (terms + self.got[d].astype(F4)).astype(BF)
        for cp in self.z_sends(d):
            cp.start()

    def finish(self):
        for cp in self.z_sends(0):
            cp.wait()
        for d in FAR[2:]:
            self.x_send(d).wait_send()
        for d in range(1, 4):
            frm = (self.z - d + 4) % 4
            for cp in self.z_sends(d):
                cp.wait_send()
            for i, (part, there) in enumerate(self.parts):
                r = there(frm)
                remote(r, r, self.zs.at[d, i], self.zr.at[d, i], device(frm, self.x, self.y, self.k)).wait_recv()


def grad_scratch(block, parts):
    D = pltpu.SemaphoreType.DMA
    V = pltpu.VMEM
    return [V((4,) + block, BF), V((2,) + block, BF), V((4,) + block, BF)] + [D((4,))] * 2 + [D((4, parts))] * 2


def norm_rows(rows, gain, shift):
    v = rows.astype(F4)
    centred = v - jnp.mean(v, axis=-1, keepdims=True)
    spread = jnp.mean(centred * centred, axis=-1, keepdims=True)
    return (centred * lax.rsqrt(spread + EPS) * gain + shift).astype(BF)


def turn(v, tab):
    cos, lo, hi = tab
    return v * cos + pltpu.roll(v, 112, 1) * lo + pltpu.roll(v, 16, 1) * hi


def turn_back(v, tab):
    cos, lo, hi = tab
    return v * cos - pltpu.roll(v, 112, 1) * lo - pltpu.roll(v, 16, 1) * hi


def angle_table(within, block, b):
    cr, sr = within[0], within[1]
    cb, sb = block[0, pl.ds(b, 1)], block[1, pl.ds(b, 1)]
    cos, sin = cb * cr - sb * sr, sb * cr + cb * sr
    entry = lax.broadcasted_iota(jnp.int32, cos.shape, 1) % 64
    return cos, jnp.where(entry < 16, -sin, 0.0), jnp.where(entry < 16, 0.0, sin)


def angles(rows, step):
    frequency = (10000.0 ** (-2.0 * np.arange(16) / 32)).astype(np.float32).astype(np.float64)
    lanes = np.concatenate([frequency, frequency, np.zeros(32)] * 2)
    angle = step * np.arange(rows)[:, None] * lanes
    return np.stack([np.cos(angle), np.sin(angle)]).astype(np.float32)


def pick(index, parts):
    chosen = parts(0)
    for j in range(1, 8):
        chosen = jnp.where(index == j, parts(j), chosen)
    return chosen


def one_head(v, h, axis):
    entry = lax.broadcasted_iota(jnp.int32, v.shape, axis)
    return jnp.where((entry < 64) == (h == 0), v, jnp.zeros_like(v))


def masked(st, kr):
    row = lax.broadcasted_iota(jnp.int32, (256, 256), 0)
    column = lax.broadcasted_iota(jnp.int32, (256, 256), 1)
    last = jnp.where(row <= column, st[kr - 256:], -1e30)
    return last if kr == 256 else jnp.concatenate([st[:kr - 256], last], axis=0)


def flip(v):
    return v.astype(F4).T.astype(BF)


def front_kernel(order, tok, gs, within, block, cot, win, wout, wexp, wcon,
                 xn_out, ct_out, wx_out, wco, am_out, amt_out, dgelu_out, pg_out, gs_all,
                 xn, ct, xo, wx, wo, proj, am, amt, dgelu, pg, qkv, qt, kt, vt, ot, logs, gt, gpos, dqt, dk, dv,
                 osem, csem, gsem_s, gsem_r, *sems):
    z, x, y, k = place()
    c, q = z * 2 + x, 2 * y + k
    nt = len(token_sems())
    tx = TokenGather(xn, sems[:nt])
    tc = TokenGather(ct, sems[nt:2 * nt])
    pairs = [
        (lambda zz, j=j: win.at[j, :, columns(128, zz)], lambda zz, xx, j=j: wx.at[zz, xx, :, pl.ds(512 + 128 * j, 128)])
        for j in range(3)
    ] + [
        (lambda zz: wexp.at[:, columns(512, zz)], lambda zz, xx: wx.at[zz, xx, :, pl.ds(0, 512)]),
        (lambda zz: wcon.at[columns(512, zz), :], lambda zz, xx: wco.at[pl.ds(0, 512), columns(256, zz * 2 + xx)]),
        (lambda zz: wout.at[columns(128, zz), :], lambda zz, xx: wo.at[:, columns(256, zz * 2 + xx)]),
    ]
    wg = WeightGather(pairs, sems[2 * nt:])
    others, everyone = peers_of(z, x, y, k)
    meet(everyone)
    gcopies = [remote(gs, gs_all.at[c], gsem_s.at[i], gsem_r.at[i], others[i]) for i in range(7)]
    for g in gcopies:
        g.start()
    gs_all[c] = gs[...]
    UA, UB, UC = (0, 1, 2, 5), (3,), (4,)
    wg.send(UA, 2, 3, 1, 0)
    own_slot = pltpu.make_async_copy(cot.at[x], ct.at[z, x], csem)
    own_slot.start()
    for i in range(7):
        frm = gs_all.at[(c - i - 1 + 8) % 8]
        remote(frm, frm, gsem_s.at[i], gsem_r.at[i], others[i]).wait_recv()
    gain = jnp.concatenate([gs_all[i, 0:1, :] for i in range(8)], axis=1)
    shift = jnp.concatenate([gs_all[i, 1:2, :] for i in range(8)], axis=1)

    @pl.loop(0, 2)
    def _(i):
        xo[pl.ds(32 * i, 32)] = norm_rows(tok[1 - x, pl.ds(64 * q + 32 * i, 32)], gain, shift)

    @pl.loop(0, 8)
    def _(i):
        xn[z, x, pl.ds(32 * i, 32)] = norm_rows(tok[x, pl.ds(32 * i, 32)], gain, shift)

    cot_other = cot.at[1 - x, pl.ds(64 * q, 64)]
    def project(i):
        zz = far_first(z, 3 - i)
        tx.landed(zz)

        @pl.loop(0, 2)
        def _(xx):
            row = pl.multiple_of(512 * zz + 256 * xx, 256)
            proj[pl.ds(row, 256)] = dot(xn[zz, xx], wx[:, :, :, pl.ds(512, 384)].reshape(2048, 384))

    tx.start(tx.chunk(z, 0, q), xo)
    tx.after_x()
    tc.start(cot.at[x, pl.ds(64 * q, 64)], cot_other)
    tx.hop(1, 0)
    tx.hop(1, 1)
    tc.after_x()
    tx.y_hop(0)
    wg.forward(UA, 2, 3, 1)
    tx.hop(2, 0)
    tx.hop(2, 1)
    tx.y_hop(1)
    tc.hop(1, 0)
    tc.hop(1, 1)
    tx.hop(3, 0)
    tx.hop(3, 1)
    wg.send(UB, 2)
    tx.y_hop(2)
    tc.y_hop(0)
    tc.hop(2, 0)
    tc.hop(2, 1)
    wg.send(UB, 3, 1, 0)
    tx.y_hop(3)
    tc.y_hop(1)
    for w in range(3):
        wg.landed(w)
    project(0)
    tc.hop(3, 0)
    project(1)
    tc.hop(3, 1)
    wg.send(UC, 2, 3, 1, 0)
    project(2)
    project(3)
    out_xn = pltpu.make_async_copy(xn, xn_out, osem.at[0])
    out_xn.start()
    tc.y_hop(2)

    @pl.loop(0, 16)
    def _(b):
        half = b // 8
        pair = b + half * (15 - 2 * b)
        here = pl.ds(pl.multiple_of(b * 128, 128), 128)
        t = angle_table(within, block, b)
        three = pick(order[0, pair], lambda j: proj[pl.ds(pl.multiple_of(256 * j + 128 * half, 128), 128)])
        rq = turn(three[:, 0:128], t).astype(BF) * BF(0.125)
        rk = turn(three[:, 128:256], t).astype(BF)
        rv = three[:, 256:384].astype(BF)
        qkv[0, here], qkv[1, here], qkv[2, here] = rq, rk, rv
        qt[:, here], kt[:, here], vt[:, here] = flip(rq), flip(rk), flip(rv)

    steps = [(i, h) for i in range(8) for h in range(2)]

    def score(i, h):
        kr = 256 * (i + 1)
        return masked(dot(qkv[1, :kr], one_head(qt[:, pl.ds(256 * i, 256)], h, 0)), kr)

    ahead = score(0, 0)
    for n, (i, h) in enumerate(steps):
        kr, here, st = 256 * (i + 1), pl.ds(256 * i, 256), ahead
        if n < 15:
            ahead = score(*steps[n + 1])
        peak = jnp.max(st, axis=0, keepdims=True)
        p = jnp.exp(st - peak)
        total = jnp.sum(p, axis=0, keepdims=True)
        o = dot(vt[:, :kr], p.astype(BF)) * (1.0 / total)
        ot[pl.ds(64 * h, 64), here] = o[64 * h:64 * h + 64]
        logs[pl.ds(h, 1), here] = peak + jnp.log(total)
        if (i, h) == (4, 1):
            tc.y_hop(3)

    @pl.loop(0, 16)
    def _(b):
        here = pl.ds(pl.multiple_of(b * 128, 128), 128)
        gpos[here] = ot[:, here].T

    def by_rows(c2, half):
        p = order[1, c2]
        return lambda ref: pick(p, lambda j: ref[pl.ds(128 * (j if half == 0 else 15 - j), 128)])

    for half in range(2):
        @pl.loop(0, 8)
        def _(c2):
            row = pl.ds(pl.multiple_of(256 * c2 + 128 * half, 128), 128)
            am[row, pl.ds(512, 128)] = by_rows(c2, half)(gpos).astype(BF)

    outs = []
    own_slot.wait()
    wg.landed(5)
    outs.append(pltpu.make_async_copy(wo, wco.at[pl.ds(512, 128)], osem.at[4]))
    outs[-1].start()

    @pl.loop(0, 4)
    def _(zz):
        tc.landed(zz)
        for xx in range(2):
            row = pl.multiple_of(512 * zz + 256 * xx, 256)
            proj[pl.ds(row, 256), pl.ds(0, 128)] = dot_t(ct[zz, xx], wo[...])

    out_ct = pltpu.make_async_copy(ct, ct_out, osem.at[1])
    out_ct.start()
    wg.forward(UB, 2, 3, 1)

    @pl.loop(0, 16)
    def _(b):
        half = b // 8
        pair = b + half * (15 - 2 * b)
        here = pl.ds(pl.multiple_of(b * 128, 128), 128)
        g = pick(order[0, pair], lambda j: proj[pl.ds(pl.multiple_of(256 * j + 128 * half, 128), 128), pl.ds(0, 128)])
        gpos[here] = g
        gt[:, here] = flip(g)

    dk[...] = jnp.zeros_like(dk)
    dv[...] = jnp.zeros_like(dv)
    for i in range(8):
        kr, here = 256 * (i + 1), pl.ds(256 * i, 256)
        for h in range(2):
            gT = gt[:, here]
            st = masked(dot(qkv[1, :kr], one_head(qt[:, here], h, 0)), kr)
            p = jnp.exp(st - logs[pl.ds(h, 1), here])
            low = p.astype(BF)
            at = pl.ds(64 * h, 64)
            delta = jnp.sum(ot[at, here] * gt[at, here].astype(F4), axis=0, keepdims=True)
            ds = (p * (dot(qkv[2, :kr], one_head(gT, h, 0)) - delta)).astype(BF)
            dv[:kr] += dot(low, one_head(gpos[here].astype(BF), h, 1))
            dk[:kr] += dot(ds, one_head(qkv[0, here], h, 1))
            dqt[at, here] = dot(kt[:, :kr], ds)[64 * h:64 * h + 64] * 0.125
        if i in (4, 6):
            wg.forward(UC, *((2,) if i == 4 else (3, 1)))

    @pl.loop(0, 16)
    def _(b):
        here = pl.ds(pl.multiple_of(b * 128, 128), 128)
        t = angle_table(within, block, b)
        gpos[here] = turn_back(dqt[:, here].T, t)
        dk[here] = turn_back(dk[here], t)

    for half in range(2):
        @pl.loop(0, 8)
        def _(c2):
            row = pl.ds(pl.multiple_of(256 * c2 + 128 * half, 128), 128)
            for j, ref in enumerate((gpos, dk, dv)):
                pg[row, pl.ds(128 * j, 128)] = by_rows(c2, half)(ref).astype(BF)

    outs.append(pltpu.make_async_copy(pg, pg_out, osem.at[2]))
    outs[-1].start()
    wg.landed(3)
    outs.append(pltpu.make_async_copy(wx, wx_out, osem.at[3]))
    outs[-1].start()

    @pl.loop(0, 8)
    def _(i):
        at = pl.ds(pl.multiple_of(256 * i, 256), 256)
        u = dot(xn[i // 2, i % 2], wx[:, :, :, pl.ds(0, 512)].reshape(2048, 512))
        square = u * u
        t = jnp.tanh(0.7978845608028654 * (u + 0.044715 * u * square))
        half = 0.5 * (1.0 + t)
        am[at, pl.ds(0, 512)] = (u * half).astype(BF)
        dgelu[at] = half + 0.5 * u * (1.0 - t * t) * (0.7978845608028654 * (1.0 + 3 * 0.044715 * square))
        amt[:, at] = flip(am[at])

    for j, (src, dst) in enumerate(((am, am_out), (amt, amt_out), (dgelu, dgelu_out))):
        outs.append(pltpu.make_async_copy(src, dst, osem.at[5 + j]))
        outs[-1].start()
    wg.landed(4)
    tx.finish(xo)
    tc.finish(cot_other)
    for w in range(6):
        wg.finish(w)
    for g in gcopies:
        g.wait_send()
    for o in [out_xn, out_ct] + outs:
        o.wait()


def front_call(order, tokens, gs, cot, win, wout, wexp, wcon):
    S = jax.ShapeDtypeStruct
    ANY = pl.BlockSpec(memory_space=pl.ANY)
    VM = pl.BlockSpec(memory_space=pltpu.VMEM)
    D = pltpu.SemaphoreType.DMA
    V = pltpu.VMEM
    rows = (4, 2, 256, 2048)
    return pl.pallas_call(
        front_kernel,
        out_shape=[S(rows, BF), S(rows, BF), S((4, 2, 256, 896), BF), S((640, 2048), BF), S((2048, 640), BF), S((640, 2048), BF),
                   S((2048, 512), F4), S((2048, 384), BF), S((8, 8, 256), F4)],
        in_specs=[pl.BlockSpec(memory_space=pltpu.SMEM)] + [VM] * 4 + [ANY] * 5,
        out_specs=[ANY] * 8 + [VM],
        scratch_shapes=[V(rows, BF), V(rows, BF), V((64, 2048), BF), V((4, 2, 256, 896), BF), V((128, 2048), BF), V((2048, 384), F4),
                        V((2048, 640), BF), V((640, 2048), BF), V((2048, 512), F4), V((2048, 384), BF),
                        V((3, 2048, 128), BF), V((128, 2048), BF), V((128, 2048), BF), V((128, 2048), BF),
                        V((128, 2048), F4), V((8, 2048), F4), V((128, 2048), BF), V((2048, 128), F4), V((128, 2048), F4),
                        V((2048, 128), F4), V((2048, 128), F4), D((8,)), D, D((7,)), D((7,))]
        + token_sems() * 2 + weight_sems(6),
        compiler_params=pltpu.CompilerParams(collective_id=0, has_side_effects=True, vmem_limit_bytes=60 * MB),
        name="front",
    )(order, tokens, gs, jnp.asarray(angles(128, 1)), jnp.asarray(angles(16, 128)), cot, win, wout, wexp, wcon)


def norm_backward(tok, cot, ng, gains, out, stage, ssem, sums):
    gain = jnp.concatenate([gains[i, 0:1, :] for i in range(8)], axis=1)
    sums[...] = jnp.zeros_like(sums)

    def store(i):
        return pltpu.make_async_copy(stage.at[i % 2], out.at[i // 8, pl.ds(pl.multiple_of(32 * (i % 8), 32), 32)], ssem.at[i % 2])

    @pl.loop(0, 16)
    def _(i):
        s, at = i // 8, pl.ds(pl.multiple_of(32 * (i % 8), 32), 32)
        v = tok[s, at].astype(F4)
        centred = v - jnp.mean(v, axis=-1, keepdims=True)
        scale = lax.rsqrt(jnp.mean(centred * centred, axis=-1, keepdims=True) + EPS)
        xhat = centred * scale
        n = ng[s, at].astype(F4)
        g = n * gain
        along = jnp.mean(g * xhat, axis=-1, keepdims=True)

        @pl.when(i >= 2)
        def _():
            store(i - 2).wait()
        stage[i % 2] = cot[s, at].astype(F4) + (g - jnp.mean(g, axis=-1, keepdims=True) - xhat * along) * scale
        store(i).start()
        both = n * xhat
        sums[0] += both[:8] + both[8:16] + both[16:24] + both[24:]
        sums[1] += n[:8] + n[8:16] + n[16:24] + n[24:]

    store(14).wait()
    store(15).wait()


def back_kernel(am, amt, wco, wx, gains, ct, xn, dgelu, pg, tok, cot,
                out, ig, vectors, gin, gout, gexp, gcon,
                hp, ctr, col, dg, ng, stage, sums, vec, vecs, psem, rsem, csem, dsem, tsem, ssem, vs, vr, *rest):
    z, x, y, k = place()
    c = z * 2 + x
    rest = list(rest)
    take = lambda n: [rest.pop(0) for _ in range(n)]
    ring = take(2)
    nb, ns = len(reduce_bufs()), len(reduce_sems())
    tn = TokenReduce(ng, ring + take(nb), take(ns))
    to = TokenReduce(out, ring + take(nb), take(ns))
    whole = slice(None)
    g1 = GradReduce([((pl.ds(0, 512), whole), lambda zz: gcon.at[columns(512, zz), :]),
                     ((pl.ds(512, 128), whole), lambda zz: gout.at[columns(128, zz), :])], *take(3), take(4))
    g2 = GradReduce([((whole, pl.ds(0, 512)), lambda zz: gexp.at[:, columns(512, zz)])]
                    + [((whole, pl.ds(512 + 128 * j, 128)), lambda zz, j=j: gin.at[j, :, columns(128, zz)]) for j in range(3)],
                    *take(3), take(4))
    others, everyone = peers_of(z, x, y, k)
    load_pg = pltpu.make_async_copy(pg, hp.at[:, pl.ds(512, 384)], psem)
    load_pg.start()

    def chunk_loads(i):
        zz = far_first(z, i)
        return (pltpu.make_async_copy(ct.at[zz], ctr.at[i % 2], rsem.at[i % 2]),
                pltpu.make_async_copy(dgelu.at[pl.ds(pl.multiple_of(512 * zz, 512), 512)], dg.at[i % 2], dsem.at[i % 2]))

    plan = [(0, 2, 1), (0, 3, 1), (0, 1, 1), (1, 2, 1), (1, 3, 1), (0, 2, 0), (1, 1, 1), (0, 3, 0),
            (0, 0, 1), (0, 1, 0), (1, 0, 1), (1, 2, 0), (1, 3, 0), (1, 1, 0), (0, 0, 0), (1, 0, 0)]

    def block_load(n):
        j, d, away = plan[n]
        xx = 1 - x if away else x
        return pltpu.make_async_copy((ct, xn)[j].at[:, :, :, columns(256, 2 * ((z + d) % 4) + xx)], col.at[n % 3], csem.at[n % 3])

    for i in range(2):
        for cp in chunk_loads(i):
            cp.start()
    for n in range(3):
        block_load(n).start()
    meet(everyone)

    def pull(i):
        zz = far_first(z, i)
        for cp in chunk_loads(i):
            cp.wait()
        for xx in range(2):
            row = pl.multiple_of(512 * zz + 256 * xx, 256)
            g = dot_t(ctr[i % 2, xx], wco[pl.ds(0, 512)])
            hp[pl.ds(row, 256), pl.ds(0, 512)] = (g * dg[i % 2, pl.ds(256 * xx, 256)]).astype(BF)
        if i < 2:
            for cp in chunk_loads(i + 2):
                cp.start()

    def fill_n(i):
        tn.fill(i, lambda zz, xx, r: hp[pl.ds(pl.multiple_of(512 * zz + 256 * xx + r, 64), 64)], lambda a, at: dot_t(a, wx[at]),
                lambda: tn.core(i - 2).wait_send() if i >= 2 else None)

    def fill_o(i):
        to.fill(i, lambda zz, xx, r: am[pl.ds(pl.multiple_of(512 * zz + 256 * xx + r, 64), 64)], lambda a, at: dot(a, wco[:, at]),
                lambda: (to.core(i - 2) if i >= 2 else tn.core(i + 2)).wait_send())

    def grad(n):
        j, d, away = plan[n]
        block_load(n).wait()
        v = col[n % 3].reshape(2048, 256)
        terms = dot(flip(v), hp[...]) if j else dot(amt[...], v)
        g = (g1, g2)[j]
        (g.give if away else g.keep)(d, terms)
        if n + 3 < 16:
            block_load(n + 3).start()

    def line(t, i):
        t.line(i, 1)
        t.line(i, 0)

    pull(0)
    load_pg.wait()
    fill_n(0)
    pull(1)
    tn.after_core(0)
    fill_n(1)
    grad(0)
    tn.after_core(1)
    pull(2)
    fill_n(2)
    grad(1)
    tn.after_core(2)
    pull(3)
    fill_n(3)
    loads = [pltpu.make_async_copy(tok, ctr.at[0], tsem.at[0]), pltpu.make_async_copy(cot, ctr.at[1], tsem.at[1])]
    for cp in loads:
        cp.start()
    grad(2)
    tn.after_core(3)
    grad(3)
    fill_o(0)
    line(tn, 0)
    grad(4)
    to.after_core(0)
    fill_o(1)
    line(tn, 1)
    grad(5)
    to.after_core(1)
    grad(6)
    fill_o(2)
    line(tn, 2)
    grad(7)
    to.after_core(2)
    grad(8)
    fill_o(3)
    line(tn, 3)
    to.after_core(3)
    tn.spread(0)
    tn.spread(1)
    grad(9)
    grad(10)
    line(to, 0)
    grad(11)
    tn.spread_y(0)
    tn.spread_y(1)
    line(to, 1)
    grad(12)
    tn.finish()
    for cp in loads:
        cp.wait()
    line(to, 2)
    grad(13)
    norm_backward(ctr.at[0], ctr.at[1], ng, gains, ig, stage, ssem, sums)
    for i in range(8):
        at = slice(256 * i, 256 * i + 256)
        for j in range(2):
            vec[i, j:j + 1, :] = jnp.sum(sums[j, :, at], axis=0, keepdims=True)
        vec[i, 2:8, :] = jnp.zeros((6, 256), F4)
    vecs[c] = vec[c]
    copies = [remote(vec.at[(c + i + 1) % 8], vecs.at[c], vs.at[i], vr.at[i], others[i]) for i in range(7)]
    for cp in copies:
        cp.start()
    line(to, 3)
    base = lambda seq, rows: ctr.at[0, seq, rows]
    to.spread(0, base)
    to.spread(1, base)
    grad(14)
    grad(15)
    to.spread_y(0)
    to.spread_y(1)
    for i in range(7):
        frm = vecs.at[(c - i - 1 + 8) % 8]
        remote(frm, frm, vs.at[i], vr.at[i], others[i]).wait_recv()
    total = vecs[0]
    for i in range(1, 8):
        total = total + vecs[i]
    vectors[...] = total
    to.core(2).wait_send()
    to.core(3).wait_send()
    to.finish()
    g1.finish()
    g2.finish()
    for cp in copies:
        cp.wait_send()


def back_call(am, amt, wco, wx, gains, ct, xn, dgelu, pg, tok, cot):
    S = jax.ShapeDtypeStruct
    ANY = pl.BlockSpec(memory_space=pl.ANY)
    VM = pl.BlockSpec(memory_space=pltpu.VMEM)
    D = pltpu.SemaphoreType.DMA
    V = pltpu.VMEM
    b1, b2 = (640, 256), (256, 896)
    return pl.pallas_call(
        back_kernel,
        out_shape=[S((2, 256, 2048), BF), S((2, 256, 2048), F4), S((8, 256), F4),
                   S((3, 256, 512), BF), S((512, 256), BF), S((256, 2048), BF), S((2048, 256), BF)],
        in_specs=[VM] * 5 + [ANY] * 6,
        out_specs=[ANY, ANY, VM] + [ANY] * 4,
        scratch_shapes=[V((2048, 896), BF), V((2, 2, 256, 2048), BF), V((3, 4, 2, 256, 256), BF), V((2, 512, 512), F4),
                        V((2, 256, 2048), BF), V((2, 32, 2048), F4), V((2, 8, 2048), F4), V((8, 8, 256), F4), V((8, 8, 256), F4),
                        D, D((2,)), D((3,)), D((2,)), D((2,)), D((2,)), D((7,)), D((7,))]
        + ring_bufs() + (reduce_bufs() + reduce_sems()) * 2 + grad_scratch(b1, 2) + grad_scratch(b2, 4),
        compiler_params=pltpu.CompilerParams(collective_id=1, has_side_effects=True, vmem_limit_bytes=62 * MB),
        name="back",
    )(am, amt, wco, wx.reshape(2048, 896), gains, ct, xn, dgelu, pg, tok, cot)


def own_local(tokens, pair_index, norm_gain, norm_shift, w_attention_in, w_attention_out, w_expand, w_contract, cotangent):
    x = lax.axis_index("ctx") % 2
    pairs = lax.dynamic_index_in_dim(pair_index, x, 0, False)
    which = jnp.arange(8, dtype=jnp.int32)
    inverse = jnp.sum(jnp.where(pairs[None, :] == which[:, None], which[None, :], 0), axis=1).astype(jnp.int32)
    gs = jnp.concatenate([norm_gain[None], norm_shift[None], jnp.zeros((6, 256), BF)], axis=0).astype(F4)
    xn, ct, wx, wco, am, amt, dgelu, pg, gains = front_call(
        jnp.stack([inverse, pairs]), tokens, gs, cotangent, w_attention_in, w_attention_out, w_expand, w_contract)
    output, input_grad, vectors, *grads = back_call(am, amt, wco, wx, gains, ct, xn, dgelu, pg, tokens, cotangent)
    return (output, input_grad, vectors[0], vectors[1], *(g.astype(F4) for g in grads))


def local(tokens, pair_index, norm_gain, norm_shift, w_attention_in, w_attention_out, w_expand, w_contract, cotangent):
    args = (tokens, pair_index, norm_gain, norm_shift, w_attention_in, w_attention_out, w_expand, w_contract, cotangent)
    sizes = (lax.axis_size("ctx"), lax.axis_size("tp")) + tokens.shape + w_attention_in.shape[2:] + w_expand.shape[1:]
    if sizes == (8, 4, 2, 256, 2048, 512, 2048):
        return own_local(*args)
    return general_local(*args)


def solution(mesh):
    in_specs = (
        P(None, "ctx", None),
        P(),
        P("ctx"),
        P("ctx"),
        P(None, "ctx", "tp"),
        P("tp", "ctx"),
        P("ctx", "tp"),
        P("tp", "ctx"),
        P(None, "ctx", None),
    )
    out_specs = (
        P(None, "ctx", None),
        P(None, "ctx", None),
        P("ctx"),
        P("ctx"),
        P(None, "ctx", "tp"),
        P("tp", "ctx"),
        P("ctx", "tp"),
        P("tp", "ctx"),
    )
    return jax.shard_map(local, mesh=mesh, in_specs=in_specs, out_specs=out_specs, check_vma=False)
```

```python
import functools
import itertools

import jax
import jax.numpy as jnp
import numpy as np
from jax import lax
from jax.experimental import pallas as pl
from jax.experimental.pallas import tpu as pltpu
from jax.sharding import PartitionSpec as P

HEAD_DIM = 64
ROT = 32


epsilon = 1e-05


def position_table(pair_index, shard_rows):
    pair_count = pair_index.shape[1]
    half_rows = shard_rows // 2
    token_index = jnp.arange(shard_rows * pair_count, dtype=jnp.int32)
    owning = token_index // shard_rows
    within = token_index % shard_rows
    picked = (owning[:, None] == jnp.arange(pair_count, dtype=jnp.int32)[None, :]).astype(jnp.int32)
    chosen = jnp.sum(picked[None, :, :] * pair_index[:, None, :], axis=2)
    first_half = chosen * half_rows + within[None, :]
    second = (2 * pair_count - 1 - chosen) * half_rows + within[None, :] - half_rows
    return jnp.where(within[None, :] < half_rows, first_half, second)


def rotate(tensor, positions):
    half_rot = ROT // 2
    frequency = 10000.0 ** (-2.0 * jnp.arange(half_rot, dtype=jnp.float32) / ROT)
    angles = positions.astype(jnp.float32)[..., None] * frequency
    cosine = jnp.cos(angles)[..., None, :]
    sine_part = jnp.sin(angles)[..., None, :]
    leading = tensor[..., :half_rot]
    trailing = tensor[..., half_rot:ROT]
    return jnp.concatenate(
        [
            leading * cosine - trailing * sine_part,
            trailing * cosine + leading * sine_part,
            tensor[..., ROT:],
        ],
        axis=-1,
    )


def gelu_tanh(values_in):
    return (
        0.5
        * values_in
        * (
            1.0
            + jnp.tanh(
                0.7978845608028654 * (values_in + 0.044715 * values_in * values_in * values_in)
            )
        )
    )


def layer_norm(inputs, gain_full, shift_full):
    centred = inputs - jnp.mean(inputs, axis=-1, keepdims=True)
    spread = jnp.mean(centred * centred, axis=-1, keepdims=True)
    return centred * lax.rsqrt(spread + epsilon) * gain_full + shift_full


def block_probs(queries, keys_block, log_total, query_pos, key_pos):
    raw_scores = jnp.einsum(
        "sqhe,skhe->shqk", queries, keys_block, preferred_element_type=jnp.float32
    )
    allowed = key_pos[:, None, None, :] <= query_pos[:, None, :, None]
    return jnp.where(allowed, jnp.exp(raw_scores * HEAD_DIM ** (-0.5) - log_total[..., None]), 0.0)


def score_grads(
    queries, keys_block, values_block, log_total, row_delta, out_grad, query_pos, key_pos
):
    probs_full = block_probs(queries, keys_block, log_total, query_pos, key_pos)
    prob_grad = jnp.einsum(
        "sqhe,skhe->shqk", out_grad, values_block, preferred_element_type=jnp.float32
    )
    score_grad = (probs_full * (prob_grad - row_delta[..., None]) * HEAD_DIM ** (-0.5)).astype(
        jnp.bfloat16
    )
    return (probs_full.astype(jnp.bfloat16), score_grad)


def key_slice(keys_all, offset, key_rows, head_count):
    seq_count = keys_all.shape[0]
    return lax.dynamic_slice_in_dim(keys_all, offset, key_rows, 1).reshape(
        seq_count, key_rows, head_count, HEAD_DIM
    )


def log_totals(queries, keys_all, query_pos, pos_table, key_rows):
    seq_count, query_rows, head_count, head_size = queries.shape
    turn_count = keys_all.shape[1] // key_rows

    def log_one_turn(turn_index, state_in):
        running_max, running_sum = state_in
        offset = turn_index * key_rows
        keys_block = key_slice(keys_all, offset, key_rows, head_count)
        key_pos = lax.dynamic_slice_in_dim(pos_table, offset, key_rows, 1)
        raw_scores = jnp.einsum(
            "sqhe,skhe->shqk", queries, keys_block, preferred_element_type=jnp.float32
        ) * HEAD_DIM ** (-0.5)
        allowed = key_pos[:, None, None, :] <= query_pos[:, None, :, None]
        masked = jnp.where(allowed, raw_scores, -1e30)
        new_max = jnp.maximum(running_max, jnp.max(masked, axis=-1))
        kept_terms = jnp.where(allowed, jnp.exp(masked - new_max[..., None]), 0.0)
        return (
            new_max,
            running_sum * jnp.exp(running_max - new_max) + jnp.sum(kept_terms, axis=-1),
        )

    initial = (
        jnp.full((seq_count, head_count, query_rows), -1e30, jnp.float32),
        jnp.zeros((seq_count, head_count, query_rows), jnp.float32),
    )
    final_max, final_sum = lax.fori_loop(0, turn_count, log_one_turn, initial)
    return final_max + jnp.log(final_sum)


def attend_values(queries, keys_all, values_all, log_total, query_pos, pos_table, key_rows):
    head_count = queries.shape[2]
    turn_count = keys_all.shape[1] // key_rows

    def attend_one_turn(turn_index, running):
        offset = turn_index * key_rows
        keys_block = key_slice(keys_all, offset, key_rows, head_count)
        values_block = key_slice(values_all, offset, key_rows, head_count)
        key_pos = lax.dynamic_slice_in_dim(pos_table, offset, key_rows, 1)
        weights_low = block_probs(queries, keys_block, log_total, query_pos, key_pos).astype(
            jnp.bfloat16
        )
        return running + jnp.einsum(
            "shqk,skhe->sqhe", weights_low, values_block, preferred_element_type=jnp.float32
        )

    return lax.fori_loop(0, turn_count, attend_one_turn, jnp.zeros(queries.shape, jnp.float32))


def full_grads(
    queries, keys_all, values_all, log_total, row_delta, out_grad, query_pos, pos_table, key_rows
):
    seq_count, query_rows, head_count, head_size = queries.shape
    turn_count = keys_all.shape[1] // key_rows

    def full_one_turn(turn_index, state_in):
        query_grad, key_terms, value_terms = state_in
        offset = turn_index * key_rows
        keys_block = key_slice(keys_all, offset, key_rows, head_count)
        values_block = key_slice(values_all, offset, key_rows, head_count)
        key_pos = lax.dynamic_slice_in_dim(pos_table, offset, key_rows, 1)
        weights_low, score_grad = score_grads(
            queries, keys_block, values_block, log_total, row_delta, out_grad, query_pos, key_pos
        )
        query_grad = query_grad + jnp.einsum(
            "shqk,skhe->sqhe", score_grad, keys_block, preferred_element_type=jnp.float32
        )
        key_part = jnp.einsum(
            "shqk,sqhe->skhe", score_grad, queries, preferred_element_type=jnp.float32
        ).reshape(seq_count, key_rows, head_count * head_size)
        value_part = jnp.einsum(
            "shqk,sqhe->skhe", weights_low, out_grad, preferred_element_type=jnp.float32
        ).reshape(seq_count, key_rows, head_count * head_size)
        key_terms = lax.dynamic_update_slice_in_dim(key_terms, key_part, offset, 1)
        value_terms = lax.dynamic_update_slice_in_dim(value_terms, value_part, offset, 1)
        return (query_grad, key_terms, value_terms)

    initial = (
        jnp.zeros(queries.shape, jnp.float32),
        jnp.zeros(keys_all.shape, jnp.float32),
        jnp.zeros(values_all.shape, jnp.float32),
    )
    return lax.fori_loop(0, turn_count, full_one_turn, initial)


def general_local(
    tokens,
    pair_index,
    norm_gain,
    norm_shift,
    w_attention_in,
    w_attention_out,
    w_expand,
    w_contract,
    cotangent,
):
    seq_count, shard_rows, model_width = tokens.shape
    gain_full, shift_full, attention_in, attention_out, expand_full, contract_full = (
        lax.all_gather(norm_gain, "ctx", axis=0, tiled=True),
        lax.all_gather(norm_shift, "ctx", axis=0, tiled=True),
        lax.all_gather(w_attention_in, "ctx", axis=1, tiled=True),
        lax.all_gather(w_attention_out, "ctx", axis=1, tiled=True),
        lax.all_gather(w_expand, "ctx", axis=0, tiled=True),
        lax.all_gather(w_contract, "ctx", axis=1, tiled=True),
    )
    local_width = attention_in.shape[2]
    head_count = local_width // HEAD_DIM
    flat_rows = seq_count * shard_rows
    pos_table = position_table(pair_index, shard_rows)
    total_rows = pos_table.shape[1]
    own_pos = lax.dynamic_slice_in_dim(pos_table, lax.axis_index("ctx") * shard_rows, shard_rows, 1)
    key_rows = min(total_rows, 1024)
    inputs = tokens.astype(jnp.float32)
    normed_full, norm_pull = jax.vjp(
        layer_norm, inputs, gain_full.astype(jnp.float32), shift_full.astype(jnp.float32)
    )
    normed = normed_full.astype(jnp.bfloat16).reshape(flat_rows, model_width)
    projected = jnp.einsum("td,kde->kte", normed, attention_in, preferred_element_type=jnp.float32)
    split_heads = projected.reshape(3, seq_count, shard_rows, head_count, HEAD_DIM)
    rotated, rotate_pull = jax.vjp(lambda pair_part: rotate(pair_part, own_pos), split_heads[:2])
    queries = rotated[0].astype(jnp.bfloat16)
    own_keys = rotated[1].astype(jnp.bfloat16)
    own_values = split_heads[2].astype(jnp.bfloat16)
    keys_all, values_all = (
        lax.all_gather(
            own_keys.reshape(seq_count, shard_rows, local_width), "ctx", axis=1, tiled=True
        ),
        lax.all_gather(
            own_values.reshape(seq_count, shard_rows, local_width), "ctx", axis=1, tiled=True
        ),
    )
    log_total = log_totals(queries, keys_all, own_pos, pos_table, key_rows)
    attended = attend_values(queries, keys_all, values_all, log_total, own_pos, pos_table, key_rows)
    mixed = attended.reshape(flat_rows, local_width).astype(jnp.bfloat16)
    hidden_pre = jnp.dot(normed, expand_full, preferred_element_type=jnp.float32)
    activated_full, gelu_pull = jax.vjp(gelu_tanh, hidden_pre)
    activated = activated_full.astype(jnp.bfloat16)
    branch = jnp.dot(mixed, attention_out, preferred_element_type=jnp.float32) + jnp.dot(
        activated, contract_full, preferred_element_type=jnp.float32
    )
    branch = lax.psum(branch.astype(jnp.bfloat16), "tp").astype(jnp.float32)
    output = (inputs + branch.reshape(seq_count, shard_rows, model_width)).astype(jnp.bfloat16)
    upstream = cotangent.reshape(flat_rows, model_width)
    contract_grad = jnp.einsum("tf,td->fd", activated, upstream, preferred_element_type=jnp.float32)
    (gelu_grad,) = gelu_pull(
        jnp.einsum("td,fd->tf", upstream, contract_full, preferred_element_type=jnp.float32)
    )
    hidden_grad = gelu_grad.astype(jnp.bfloat16)
    expand_grad = jnp.einsum("td,tf->df", normed, hidden_grad, preferred_element_type=jnp.float32)
    mixed_grad = jnp.einsum(
        "td,ed->te", upstream, attention_out, preferred_element_type=jnp.float32
    ).astype(jnp.bfloat16)
    attention_out_grad = jnp.einsum(
        "te,td->ed", mixed, upstream, preferred_element_type=jnp.float32
    )
    out_grad = mixed_grad.reshape(seq_count, shard_rows, head_count, HEAD_DIM)
    row_delta = jnp.sum(out_grad.astype(jnp.float32) * attended, axis=-1).transpose(0, 2, 1)
    query_grad, key_terms, value_terms = full_grads(
        queries, keys_all, values_all, log_total, row_delta, out_grad, own_pos, pos_table, key_rows
    )
    key_grad, value_grad = (
        lax.psum_scatter(
            key_terms.astype(jnp.bfloat16), "ctx", scatter_dimension=1, tiled=True
        ).astype(jnp.float32),
        lax.psum_scatter(
            value_terms.astype(jnp.bfloat16), "ctx", scatter_dimension=1, tiled=True
        ).astype(jnp.float32),
    )
    key_grad = key_grad.reshape(seq_count, shard_rows, head_count, HEAD_DIM)
    value_grad = value_grad.reshape(seq_count, shard_rows, head_count, HEAD_DIM)
    (rotated_grad,) = rotate_pull(jnp.stack([query_grad, key_grad]))
    projected_grad = (
        jnp.concatenate([rotated_grad, value_grad[None]], axis=0)
        .reshape(3, flat_rows, local_width)
        .astype(jnp.bfloat16)
    )
    attention_in_grad = jnp.einsum(
        "td,kte->kde", normed, projected_grad, preferred_element_type=jnp.float32
    )
    normed_grad = jnp.einsum(
        "kte,kde->td", projected_grad, attention_in, preferred_element_type=jnp.float32
    )
    normed_grad = normed_grad + jnp.einsum(
        "tf,df->td", hidden_grad, expand_full, preferred_element_type=jnp.float32
    )
    normed_grad = lax.psum(normed_grad.astype(jnp.bfloat16), "tp").astype(jnp.float32)
    input_part, gain_grad, shift_grad = norm_pull(
        normed_grad.reshape(seq_count, shard_rows, model_width)
    )
    input_grad = input_part + cotangent.astype(jnp.float32)
    reduced = (
        lax.psum_scatter(
            gain_grad.astype(jnp.bfloat16), "ctx", scatter_dimension=0, tiled=True
        ).astype(jnp.float32),
        lax.psum_scatter(
            shift_grad.astype(jnp.bfloat16), "ctx", scatter_dimension=0, tiled=True
        ).astype(jnp.float32),
        lax.psum_scatter(
            attention_in_grad.astype(jnp.bfloat16), "ctx", scatter_dimension=1, tiled=True
        ).astype(jnp.float32),
        lax.psum_scatter(
            attention_out_grad.astype(jnp.bfloat16), "ctx", scatter_dimension=1, tiled=True
        ).astype(jnp.float32),
        lax.psum_scatter(
            expand_grad.astype(jnp.bfloat16), "ctx", scatter_dimension=0, tiled=True
        ).astype(jnp.float32),
        lax.psum_scatter(
            contract_grad.astype(jnp.bfloat16), "ctx", scatter_dimension=1, tiled=True
        ).astype(jnp.float32),
    )
    return (
        output,
        input_grad,
        reduced[0],
        reduced[1],
        reduced[2],
        reduced[3],
        reduced[4],
        reduced[5],
    )


MESH = pl.DeviceIdType.MESH
MB = 1 << 20
EPS = 1e-05
BF = jnp.bfloat16
F4 = jnp.float32
NT = (((1,), (1,)), ((), ()))
FAR = (1, 2, 3, 0)


def place():
    c = lax.axis_index("ctx")
    t = lax.axis_index("tp")
    return c // 2, c % 2, t // 2, t % 2


def device(z, x, y, k):
    return (z * 2 + x, y * 2 + k)


def remote(src, dst, send_sem, recv_sem, target):
    return pltpu.make_async_remote_copy(
        src_ref=src, dst_ref=dst, send_sem=send_sem, recv_sem=recv_sem,
        device_id=target, device_id_type=MESH,
    )


def meet(peers):
    barrier = pltpu.get_barrier_semaphore()
    for peer in peers:
        pl.semaphore_signal(barrier, inc=1, device_id=peer, device_id_type=MESH)
    pl.semaphore_wait(barrier, len(peers))


def peers_of(z, x, y, k):
    c = z * 2 + x
    others = [((c + i) % 8, lax.axis_index("tp")) for i in range(1, 8)]
    return others, others + [device(z, x, 1 - y, k), device(z, x, y, 1 - k)]


def columns(n, i):
    return pl.ds(pl.multiple_of(n * i, n), n)


def dot(a, b):
    return jnp.dot(a, b, preferred_element_type=F4)


def dot_t(a, b):
    return lax.dot_general(a, b, NT, preferred_element_type=F4)


def mirrored(z, e):
    return jnp.where(z < 2, 4 - e, e) if e in (1, 3) else e


def far_first(z, i):
    return (3 * (1 - z // 2), z // 2 + 2 * (1 - z % 2), 1 + z % 2, z)[i]


def add_into(dst, src):
    lead, rows = dst.shape[:-2], dst.shape[-2]
    for idx in itertools.product(*(range(n) for n in lead)):
        @pl.loop(0, rows // 16)
        def _(i):
            at = idx + (pl.ds(pl.multiple_of(16 * i, 16), 16), slice(None))
            dst[at] = (dst[at].astype(F4) + src[at].astype(F4)).astype(BF)


class TokenGather:
    def __init__(self, whole, sems):
        self.whole = whole
        self.xs, self.xr, self.zs, self.zr, self.ys, self.yr, self.cs, self.cr = sems
        self.z, self.x, self.y, self.k = place()
        self.q = 2 * self.y + self.k

    def chunk(self, zz, s, q):
        xx = self.x if s == 0 else 1 - self.x
        return self.whole.at[zz, xx, pl.ds(64 * q, 64), :]

    def send_x(self, src):
        z, x, y, k = self.z, self.x, self.y, self.k
        return remote(src, self.whole.at[z, x, pl.ds(64 * self.q, 64), :], self.xs, self.xr, device(z, 1 - x, y, k))

    def send_up(self, zz, s, src):
        return remote(src, self.chunk(zz, s, self.q), self.zs.at[zz, s, 0], self.zr.at[zz, s],
                      device(jnp.minimum(self.z + 1, 3), self.x, self.y, self.k))

    def send_down(self, zz, s, src):
        return remote(src, self.chunk(zz, s, self.q), self.zs.at[zz, s, 1], self.zr.at[zz, s],
                      device(jnp.maximum(self.z - 1, 0), self.x, self.y, self.k))

    def send_y(self, zz, s):
        c = self.chunk(zz, s, self.q)
        return remote(c, c, self.ys.at[zz, s], self.yr.at[zz, s], device(self.z, self.x, 1 - self.y, self.k))

    def send_core(self, zz, s, j):
        yy = self.y if j == 0 else 1 - self.y
        c = self.chunk(zz, s, 2 * yy + self.k)
        return remote(c, c, self.cs.at[zz, s, j], self.cr.at[zz, s, j], device(self.z, self.x, self.y, 1 - self.k))

    def both_ways(self, s, src):
        z = self.z

        @pl.when(z < 3)
        def _():
            self.send_up(z, s, src).start()

        @pl.when(z > 0)
        def _():
            self.send_down(z, s, src).start()

    def start(self, own_quarter, other_quarter):
        self.send_x(other_quarter).start()
        self.both_ways(0, own_quarter)

    def after_x(self):
        c = self.chunk(self.z, 1, self.q)
        remote(c, c, self.xs, self.xr, device(self.z, 1 - self.x, self.y, self.k)).wait_recv()
        self.both_ways(1, c)
        self.send_y(self.z, 1).start()
        self.send_core(self.z, 1, 0).start()

    def hop(self, d, s):
        z = self.z

        @pl.when(z >= d)
        def _():
            zz = z - d
            c = self.chunk(zz, s, self.q)
            self.send_down(zz, s, c).wait_recv()

            @pl.when(z < 3)
            def _():
                self.send_up(zz, s, c).start()

            self.send_y(zz, s).start()
            self.send_core(zz, s, 0).start()

        @pl.when(z + d <= 3)
        def _():
            zz = z + d
            c = self.chunk(zz, s, self.q)
            self.send_up(zz, s, c).wait_recv()

            @pl.when(z > 0)
            def _():
                self.send_down(zz, s, c).start()

            self.send_y(zz, s).start()
            self.send_core(zz, s, 0).start()

    def y_in(self, zz, s):
        c = self.chunk(zz, s, 2 * (1 - self.y) + self.k)
        remote(c, c, self.ys.at[zz, s], self.yr.at[zz, s], device(self.z, self.x, 1 - self.y, self.k)).wait_recv()
        self.send_core(zz, s, 1).start()

    def y_hop(self, d):
        z = self.z
        if d == 0:
            self.y_in(z, 1)
            return
        for s in range(2):
            pl.when(z >= d)(lambda: self.y_in(z - d, s))
            pl.when(z + d <= 3)(lambda: self.y_in(z + d, s))

    def landed(self, zz):
        def rest(s):
            for j in range(2):
                yy = self.y if j == 0 else 1 - self.y
                c = self.chunk(zz, s, 2 * yy + 1 - self.k)
                remote(c, c, self.cs.at[zz, s, j], self.cr.at[zz, s, j], device(self.z, self.x, self.y, 1 - self.k)).wait_recv()

        pl.when(self.z != zz)(lambda: rest(0))
        rest(1)

    def sent_own(self, own_quarter, other_quarter):
        z = self.z
        self.send_x(other_quarter).wait_send()
        pl.when(z < 3)(lambda: self.send_up(z, 0, own_quarter).wait_send())
        pl.when(z > 0)(lambda: self.send_down(z, 0, own_quarter).wait_send())

    def finish(self):
        z = self.z
        for zz in range(4):
            for s in range(2):
                def rest():
                    self.send_y(zz, s).wait_send()
                    for j in range(2):
                        self.send_core(zz, s, j).wait_send()
                if s == 0:
                    pl.when(z != zz)(rest)
                else:
                    rest()
                c = self.chunk(zz, s, self.q)

                pl.when((z < 3) & (zz < z + s))(lambda: self.send_up(zz, s, c).wait_send())
                pl.when((z > 0) & (zz > z - s))(lambda: self.send_down(zz, s, c).wait_send())


def token_sems():
    D = pltpu.SemaphoreType.DMA
    return [D, D, D((4, 2, 2)), D((4, 2)), D((4, 2)), D((4, 2)), D((4, 2, 2)), D((4, 2, 2))]


class WeightGather:
    def __init__(self, pairs, sems):
        self.pairs = pairs
        self.zs, self.zr, self.xs, self.xr, self.loc = sems
        self.z, self.x, self.y, self.k = place()

    def z_send(self, d, w):
        src, dst = self.pairs[w]
        to = (self.z + d) % 4
        return remote(src(to), dst(self.z, self.x), self.zs.at[d, w], self.zr.at[d, w], device(to, self.x, self.y, self.k))

    def z_recv(self, d, w):
        dst = self.pairs[w][1]
        frm = (self.z - d + 4) % 4
        return remote(dst(frm, self.x), dst(frm, self.x), self.zs.at[d, w], self.zr.at[d, w], device(frm, self.x, self.y, self.k))

    def x_send(self, d, w):
        src, dst = self.pairs[w]
        frm = (self.z - d + 4) % 4
        s = src(self.z) if isinstance(d, int) and d == 0 else dst(frm, self.x)
        return remote(s, dst(frm, self.x), self.xs.at[d, w], self.xr.at[d, w], device(self.z, 1 - self.x, self.y, self.k))

    def x_recv(self, d, w):
        frm = (self.z - d + 4) % 4
        r = self.pairs[w][1](frm, 1 - self.x)
        return remote(r, r, self.xs.at[d, w], self.xr.at[d, w], device(self.z, 1 - self.x, self.y, self.k))

    def local(self, w):
        src, dst = self.pairs[w]
        return pltpu.make_async_copy(src(self.z), dst(self.z, self.x), self.loc.at[w])

    def send(self, ws, e):
        d = mirrored(self.z, e)
        for w in ws:
            if e:
                self.z_send(d, w).start()
            else:
                self.x_send(0, w).start()
                self.local(w).start()

    def forward(self, ws, e):
        d = mirrored(self.z, e)
        for w in ws:
            self.z_recv(d, w).wait_recv()
            self.x_send(d, w).start()

    def landed(self, w):
        self.local(w).wait()
        for d in range(4):
            self.x_recv(d, w).wait_recv()

    def finish(self, w):
        for d in range(4):
            if d:
                self.z_send(d, w).wait_send()
            self.x_send(d, w).wait_send()


def weight_sems(n):
    D = pltpu.SemaphoreType.DMA
    return [D((4, n)), D((4, n)), D((4, n)), D((4, n)), D((n,))]


class TokenReduce:
    def __init__(self, out, bufs, sems):
        self.out = out
        self.S, self.r1, self.r2, self.rz, self.rf = bufs
        (self.cs, self.cr, self.ys, self.yr, self.zs, self.zr, self.xs, self.xr,
         self.fl, self.fys, self.fyr, self.fcs, self.fcr) = sems
        self.z, self.x, self.y, self.k = place()
        self.q = 2 * self.y + self.k

    def slot(self, s):
        return self.x if s == 0 else 1 - self.x

    def core(self, i, slot=0):
        zz = far_first(self.z, i)
        return remote(self.S.at[slot], self.r1.at[zz], self.cs.at[zz], self.cr.at[zz], device(self.z, self.x, self.y, 1 - self.k))

    def yex(self, zz, s):
        xx = self.slot(s)
        return remote(self.r1.at[zz, 1 - self.y, xx], self.r2.at[zz, xx], self.ys.at[zz, s], self.yr.at[zz, s],
                      device(self.z, self.x, 1 - self.y, self.k))

    def mine(self, zz, s):
        return self.r1.at[zz, self.y, self.slot(s)]

    def up(self, zz, s):
        return remote(self.mine(zz, s), self.rz.at[zz, s], self.zs.at[zz, s], self.zr.at[zz, s],
                      device(jnp.minimum(self.z + 1, 3), self.x, self.y, self.k))

    def down(self, zz, s):
        slot = jnp.where(zz == self.z - 1, 4, zz)
        return remote(self.mine(zz, s), self.rz.at[slot, s], self.zs.at[zz, s], self.zr.at[slot, s],
                      device(jnp.maximum(self.z - 1, 0), self.x, self.y, self.k))

    def arrive(self, zz, s, slot):
        r = self.rz.at[slot, s]
        remote(r, r, self.zs.at[0, s], self.zr.at[slot, s], device(self.z, self.x, self.y, 1 - self.k)).wait_recv()
        add_into(self.mine(zz, s), r)

    def xex(self):
        return remote(self.mine(self.z, 1), self.rf, self.xs, self.xr, device(self.z, 1 - self.x, self.y, self.k))

    def rows(self, i, kk, lhs):
        zz = far_first(self.z, i)
        return jnp.concatenate([lhs(zz, xx, 64 * (2 * yy + kk)) for yy in range(2) for xx in range(2)], axis=0)

    def fill(self, i, slot, lhs, rhs):
        a = self.rows(i, 1 - self.k, lhs)

        @pl.loop(0, 4)
        def _(j):
            at = columns(512, j)
            self.S[slot, :, :, :, at] = rhs(a, j).astype(BF).reshape(2, 2, 64, 512)
        self.core(i, slot).start()

    def after_core(self, i, lhs, rhs):
        zz = far_first(self.z, i)
        a = self.rows(i, self.k, lhs)
        self.core(i).wait_recv()

        @pl.loop(0, 4)
        def _(j):
            at = columns(512, j)
            got = self.r1[zz, :, :, :, at].reshape(256, 512).astype(F4)
            self.r1[zz, :, :, :, at] = (rhs(a, j) + got).astype(BF).reshape(2, 2, 64, 512)
        for s in (1, 0):
            self.yex(zz, s).start()

    def line(self, i, s):
        z = self.z
        zz = far_first(z, i)
        self.yex(zz, s).wait_recv()
        add_into(self.mine(zz, s), self.r2.at[zz, self.slot(s)])
        if i < 3:
            @pl.when(zz > z)
            def _():
                pl.when(z > 0)(lambda: self.arrive(zz, s, zz))
                self.up(zz, s).start()

            @pl.when(zz < z)
            def _():
                pl.when(z < 3)(lambda: self.arrive(zz, s, zz))
                self.down(zz, s).start()
        else:
            pl.when(z > 0)(lambda: self.arrive(z, s, z))
            pl.when(z < 3)(lambda: self.arrive(z, s, 4))
            if s == 1:
                self.xex().start()

    def spot(self, s, q):
        return self.out.at[self.slot(s), pl.ds(64 * q, 64), :]

    def fin_copies(self, s):
        src = self.mine(self.z, 0) if s == 0 else self.rf
        here = self.spot(s, self.q)
        return (pltpu.make_async_copy(src, here, self.fl.at[s]),
                remote(src, here, self.fys.at[s], self.fyr.at[s], device(self.z, self.x, 1 - self.y, self.k)),
                remote(src, here, self.fcs.at[s, 0], self.fcr.at[s, 0], device(self.z, self.x, self.y, 1 - self.k)))

    def relay(self, s):
        r = self.spot(s, 2 * (1 - self.y) + self.k)
        return remote(r, r, self.fcs.at[s, 1], self.fcr.at[s, 1], device(self.z, self.x, self.y, 1 - self.k))

    def spread(self, s, base=None):
        if s == 1:
            self.xex().wait_recv()
        if base is not None:
            add_into(self.mine(self.z, 0) if s == 0 else self.rf, base(self.slot(s), pl.ds(64 * self.q, 64)))
        for cp in self.fin_copies(s):
            cp.start()

    def spread_y(self, s):
        r = self.spot(s, 2 * (1 - self.y) + self.k)
        remote(r, r, self.fys.at[s], self.fyr.at[s], device(self.z, self.x, 1 - self.y, self.k)).wait_recv()
        self.relay(s).start()

    def finish(self):
        z = self.z
        for zz in range(4):
            for s in range(2):
                self.yex(zz, s).wait_send()
                pl.when(z != zz)(lambda: self.up(zz, s).wait_send())
        self.xex().wait_send()
        for s in range(2):
            a, b, c = self.fin_copies(s)
            a.wait()
            b.wait_send()
            c.wait_send()
            self.relay(s).wait_send()
            for j, yy in ((0, self.y), (1, 1 - self.y)):
                r = self.spot(s, 2 * yy + 1 - self.k)
                remote(r, r, self.fcs.at[s, j], self.fcr.at[s, j], device(self.z, self.x, self.y, 1 - self.k)).wait_recv()


def reduce_sems():
    D = pltpu.SemaphoreType.DMA
    return [D((4,)), D((4,)), D((4, 2)), D((4, 2)), D((4, 2)), D((5, 2)), D, D,
            D((2,)), D((2,)), D((2,)), D((2, 2)), D((2, 2))]


def reduce_bufs():
    V = lambda *s: pltpu.VMEM(s, BF)
    return [V(4, 2, 2, 64, 2048), V(4, 2, 64, 2048), V(5, 2, 64, 2048), V(64, 2048)]


class GradReduce:
    def __init__(self, parts, away, got, sems):
        self.parts, self.away, self.got = parts, away, got
        self.xs, self.xr, self.zs, self.zr = sems
        self.z, self.x, self.y, self.k = place()

    def x_send(self, e):
        i = FAR.index(e)
        return remote(self.away.at[i % 2], self.got.at[i], self.xs.at[i], self.xr.at[i], device(self.z, 1 - self.x, self.y, self.k))

    def z_sends(self, e):
        d = mirrored(self.z, e)
        for i, (part, there) in enumerate(self.parts):
            src, dst = self.got.at[(FAR.index(e),) + part], there(self.z)
            if e == 0:
                yield pltpu.make_async_copy(src, dst, self.zs.at[0, i])
            else:
                yield remote(src, dst, self.zs.at[d, i], self.zr.at[d, i], device((self.z + d) % 4, self.x, self.y, self.k))

    def give(self, e, terms):
        i = FAR.index(e)
        if i >= 2:
            self.x_send(FAR[i - 2]).wait_send()
        self.away[i % 2] = terms.astype(BF)
        self.x_send(e).start()

    def keep(self, e, terms):
        i = FAR.index(e)
        self.x_send(e).wait_recv()
        self.got[i] = (terms + self.got[i].astype(F4)).astype(BF)
        for cp in self.z_sends(e):
            cp.start()

    def finish(self):
        for cp in self.z_sends(0):
            cp.wait()
        for e in FAR[2:]:
            self.x_send(e).wait_send()
        for d in range(1, 4):
            frm = (self.z - d + 4) % 4
            for cp in self.z_sends(d):
                cp.wait_send()
            for i, (part, there) in enumerate(self.parts):
                r = there(frm)
                remote(r, r, self.zs.at[d, i], self.zr.at[d, i], device(frm, self.x, self.y, self.k)).wait_recv()


def grad_scratch(block, parts):
    D = pltpu.SemaphoreType.DMA
    V = pltpu.VMEM
    return [V((2,) + block, BF), V((4,) + block, BF)] + [D((4,))] * 2 + [D((4, parts))] * 2


def norm_rows(rows, gain, shift):
    v = rows.astype(F4)
    centred = v - jnp.mean(v, axis=-1, keepdims=True)
    spread = jnp.mean(centred * centred, axis=-1, keepdims=True)
    return (centred * lax.rsqrt(spread + EPS) * gain + shift).astype(BF)


def turn(v, tab):
    cos, lo, hi = tab
    return v * cos + pltpu.roll(v, 112, 1) * lo + pltpu.roll(v, 16, 1) * hi


def turn_back(v, tab):
    cos, lo, hi = tab
    return v * cos - pltpu.roll(v, 112, 1) * lo - pltpu.roll(v, 16, 1) * hi


def angle_table(within, cb, sb):
    cr, sr = within[0], within[1]
    cos, sin = cb * cr - sb * sr, sb * cr + cb * sr
    entry = lax.broadcasted_iota(jnp.int32, cos.shape, 1) % 64
    return cos, jnp.where(entry < 16, -sin, 0.0), jnp.where(entry < 16, 0.0, sin)


def angles(rows, step):
    frequency = (10000.0 ** (-2.0 * np.arange(16) / 32)).astype(np.float32).astype(np.float64)
    lanes = np.concatenate([frequency, frequency, np.zeros(32)] * 2)
    angle = step * np.arange(rows)[:, None] * lanes
    return np.stack([np.cos(angle), np.sin(angle)]).astype(np.float32)


def pick(index, parts):
    chosen = parts(0)
    for j in range(1, 8):
        chosen = jnp.where(index == j, parts(j), chosen)
    return chosen


def one_head(v, h, axis):
    entry = lax.broadcasted_iota(jnp.int32, v.shape, axis)
    return jnp.where((entry < 64) == (h == 0), v, jnp.zeros_like(v))


def masked(st, kr):
    row = lax.broadcasted_iota(jnp.int32, (256, 256), 0)
    column = lax.broadcasted_iota(jnp.int32, (256, 256), 1)
    last = jnp.where(row <= column, st[kr - 256:], -1e30)
    return last if kr == 256 else jnp.concatenate([st[:kr - 256], last], axis=0)


def flip(v):
    return v.astype(F4).T.astype(BF)


def norm_backward(tok, cot, ng, gains, out, stage, ssem, sums):
    gain = jnp.concatenate([gains[i, 0:1, :] for i in range(8)], axis=1)
    sums[...] = jnp.zeros_like(sums)

    def store(i):
        return pltpu.make_async_copy(stage.at[i % 2], out.at[i // 8, pl.ds(pl.multiple_of(32 * (i % 8), 32), 32)], ssem.at[i % 2])

    @pl.loop(0, 16)
    def _(i):
        s, at = i // 8, pl.ds(pl.multiple_of(32 * (i % 8), 32), 32)
        v = tok[s, at].astype(F4)
        centred = v - jnp.mean(v, axis=-1, keepdims=True)
        scale = lax.rsqrt(jnp.mean(centred * centred, axis=-1, keepdims=True) + EPS)
        xhat = centred * scale
        n = ng[s, at].astype(F4)
        g = n * gain
        along = jnp.mean(g * xhat, axis=-1, keepdims=True)

        @pl.when(i >= 2)
        def _():
            store(i - 2).wait()
        stage[i % 2] = cot[s, at].astype(F4) + (g - jnp.mean(g, axis=-1, keepdims=True) - xhat * along) * scale
        store(i).start()
        both = n * xhat
        sums[0] += both[:8] + both[8:16] + both[16:24] + both[24:]
        sums[1] += n[:8] + n[8:16] + n[16:24] + n[24:]

    store(14).wait()
    store(15).wait()


ORDER = (
    "start", "WB1", "WB2", "ln", "sx", "WB3", "WB0", "hx10", "FB3", "ax", "WA1", "hx20", "WA0", "FB1", "hx11", "WC0", "WA2", "WA3",
    "hx21", "FA1", "WC3", "yx0", "WC1", "FA2", "yx1", "sc", "hx31", "yx2", "FA3", "hx30", "ac", "FB2", "yx3", "WC2", "hc10", "lwin",
    "P0", "FC1", "P1", "P2", "P3", "FC3", "rope", "hc11", "f0", "f1", "f2", "lwexp", "hid0", "hid1", "hc20", "hid2", "f3", "yc0", "FC2",
    "yc1", "f4", "hc21", "f5", "f6", "f7", "hc30", "lwout", "lwcon", "mix", "fillo0", "fillo1", "fillo2", "yc2", "hc31", "hid3",
    "coreo0", "mg0", "coreo1", "yc3", "mg1", "fillo3", "mg2", "coreo2", "mg3", "gflip", "b0", "b1", "lo01", "coreo3", "b2", "b3", "b4",
    "lo00", "b5", "b6", "lo11", "b7", "pg", "lo10", "g01", "lo21", "pull0", "lo20", "g02", "filln0", "pull1", "g03", "pull2", "k01",
    "g00", "coren0", "filln1", "lo30", "filln2", "k02", "pull3", "g11", "coren1", "ln01", "g12", "g13", "k03", "g10", "coren2", "ln00",
    "ln11", "ln21", "lo31", "filln3", "spo0", "ln10", "k12", "coren3", "ln20", "ln31", "k11", "k00", "ln30", "spn0", "spn1", "syn1",
    "syn0", "syo0", "spo1", "k13", "finn", "norm", "k10", "syo1", "fino", "gf",
)


def block_kernel(order, gs, within, block, tok, cot, win, wout, wexp, wcon,
                 out, ig, vectors, gin, gout, gexp, gcon, xn, ct,
                 wx, wco, hp, am, S, ctr, ng, gs_all, vec, vecs,
                 gsem_s, gsem_r, lsem, rsem, csem, ssem, vs, vr, *rest):
    z, x, y, k = place()
    c, q = z * 2 + x, 2 * y + k
    rest = list(rest)
    take = lambda n: [rest.pop(0) for _ in range(n)]
    nt, nb, ns = len(token_sems()), len(reduce_bufs()), len(reduce_sems())
    tx = TokenGather(xn, take(nt))
    tc = TokenGather(ct, take(nt))
    pairs = [
        (lambda zz, j=j: win.at[j, :, columns(128, zz)], lambda zz, xx, j=j: wx.at[zz, xx, :, pl.ds(512 + 128 * j, 128)])
        for j in range(3)
    ] + [
        (lambda zz: wexp.at[:, columns(512, zz)], lambda zz, xx: wx.at[zz, xx, :, pl.ds(0, 512)]),
        (lambda zz: wcon.at[columns(512, zz), :], lambda zz, xx: wco.at[pl.ds(0, 512), columns(256, zz * 2 + xx)]),
        (lambda zz: wout.at[columns(128, zz), :], lambda zz, xx: wco.at[pl.ds(512, 128), columns(256, zz * 2 + xx)]),
    ]
    wg = WeightGather(pairs, take(len(weight_sems(6))))
    tn = TokenReduce(ng, [S] + take(nb), take(ns))
    to = TokenReduce(out, [S] + take(nb), take(ns))
    whole = slice(None)
    g1 = GradReduce([((pl.ds(0, 512), whole), lambda zz: gcon.at[columns(512, zz), :]),
                     ((pl.ds(512, 128), whole), lambda zz: gout.at[columns(128, zz), :])], *take(2), take(4))
    g2 = GradReduce([((whole, pl.ds(0, 512)), lambda zz: gexp.at[:, columns(512, zz)])]
                    + [((whole, pl.ds(512 + 128 * j, 128)), lambda zz, j=j: gin.at[j, :, columns(128, zz)]) for j in range(3)],
                    *take(2), take(4))
    others, everyone = peers_of(z, x, y, k)

    V = pltpu.VMEM
    steps = {}
    flags = set()
    U = {"A": (0, 1, 2, 5), "B": (3,), "C": (4,)}
    load_tok = lambda: pltpu.make_async_copy(tok, ctr.at[0], lsem.at[0])
    load_cot = lambda: pltpu.make_async_copy(cot, ctr.at[1], lsem.at[1])
    own_cot = lambda: pltpu.make_async_copy(cot.at[x], ct.at[z, x], lsem.at[2])
    xl, xo = ctr.at[1, 0], ctr.at[1, 1, pl.ds(0, 64)]
    own_xn = lambda: pltpu.make_async_copy(xl, xn.at[z, x], lsem.at[3])
    gcopies = lambda: [remote(gs, gs_all.at[c], gsem_s.at[i], gsem_r.at[i], others[i]) for i in range(7)]
    mine, cot_mine = xl.at[pl.ds(64 * q, 64)], cot.at[x, pl.ds(64 * q, 64)]
    cot_other = cot.at[1 - x, pl.ds(64 * q, 64)]

    def once(name, act):
        if name not in flags:
            flags.add(name)
            act()

    users = [n for n in ORDER if n[:-1] in ("P", "mg", "hid", "pull")]

    def rows_in(n, xx):
        name = users[n]
        i = int(name[-1])
        zz = far_first(z, i if name[:-1] in ("hid", "pull") else 3 - i)
        src = xn if name[:-1] in ("P", "hid") else ct
        return zz, pltpu.make_async_copy(src.at[zz, xx], ctr.at[n % 2, xx], rsem.at[n % 2, xx])

    def begin_rows(n):
        flags.add(n)
        for xx in range(2):
            rows_in(n, xx)[1].start()

    def each_half(name, act):
        n = users.index(name)
        if n not in flags:
            begin_rows(n)
        for xx in range(2):
            zz, cp = rows_in(n, xx)
            cp.wait()
            act(zz, xx, ctr.at[n % 2, xx], pl.multiple_of(512 * zz + 256 * xx, 256))
        flags.add(name)
        for m in (n + 1, n + 2):
            if m < len(users) and m not in flags and {"hid": "P3", "pull": "mg3"}.get(users[m][:-1]) in flags:
                begin_rows(m)
        if n + 1 == len(users):
            load_tok().start()
            load_cot().start()

    def start():
        load_tok().start()
        meet(everyone)
        for g in gcopies():
            g.start()
        gs_all[c] = gs[...]
        own_cot().start()

    def norm():
        for i in range(7):
            frm = gs_all.at[(c - i - 1 + 8) % 8]
            remote(frm, frm, gsem_s.at[i], gsem_r.at[i], others[i]).wait_recv()
        gain = jnp.concatenate([gs_all[i, 0:1, :] for i in range(8)], axis=1)
        shift = jnp.concatenate([gs_all[i, 1:2, :] for i in range(8)], axis=1)
        load_tok().wait()

        @pl.loop(0, 2)
        def _(i):
            xo[pl.ds(32 * i, 32)] = norm_rows(ctr[0, 1 - x, pl.ds(64 * q + 32 * i, 32)], gain, shift)

        @pl.loop(0, 8)
        def _(i):
            xl[pl.ds(32 * i, 32)] = norm_rows(ctr[0, x, pl.ds(32 * i, 32)], gain, shift)

        own_xn().start()

    steps["start"], steps["ln"] = start, norm
    for u, ws in U.items():
        for d in range(4):
            steps[f"W{u}{d}"] = functools.partial(wg.send, ws, d)
            steps[f"F{u}{d}"] = functools.partial(wg.forward, ws, d)
    for name, ws in (("lwin", (0, 1, 2)), ("lwout", (5,)), ("lwexp", (3,)), ("lwcon", (4,))):
        steps[name] = functools.partial(lambda ws: [wg.landed(w) for w in ws], ws)
    steps["sx"] = lambda: tx.start(mine, xo)
    steps["sc"] = lambda: tc.start(cot_mine, cot_other)
    for name, t in (("x", tx), ("c", tc)):
        steps["a" + name] = t.after_x
        for d in range(4):
            steps[f"y{name}{d}"] = functools.partial(t.y_hop, d)
            for s in range(2):
                steps[f"h{name}{d}{s}"] = functools.partial(t.hop, d, s)

    def hidden(zz, xx, rows, row):
        at = pl.ds(row, 256)
        u = dot(rows[...], wx[:, :, :, pl.ds(0, 512)].reshape(2048, 512))
        square = u * u
        t = jnp.tanh(0.7978845608028654 * (u + 0.044715 * u * square))
        half = 0.5 * (1.0 + t)
        am[at, pl.ds(0, 512)] = (u * half).astype(BF)
        hp[at, pl.ds(0, 512)] = (half + 0.5 * u * (1.0 - t * t) * (0.7978845608028654 * (1.0 + 3 * 0.044715 * square))).astype(BF)

    def pull(zz, xx, rows, row):
        at = (pl.ds(row, 256), pl.ds(0, 512))
        hp[at] = (dot_t(rows[...], wco[pl.ds(0, 512)]) * hp[at].astype(F4)).astype(BF)

    for i in range(4):
        steps[f"hid{i}"] = functools.partial(each_half, f"hid{i}", hidden)
        steps[f"pull{i}"] = functools.partial(each_half, f"pull{i}", pull)

    def piece(ref):
        return lambda zz, xx, r: ref[pl.ds(pl.multiple_of(512 * zz + 256 * xx + r, 64), 64)]

    of = {"n": (piece(hp), lambda a, j: dot_t(a, wx[j].reshape(512, 896))),
          "o": (piece(am), lambda a, j: dot(a, wco[:, columns(512, j)]))}
    filled = []

    def fill(name, t, i):
        if len(filled) >= 2:
            sent(filled[-2])
        filled.append((t, i))
        t.fill(i, (len(filled) - 1) % 2, *of[name])

    def sent(one):
        one[0].core(one[1]).wait_send()

    def to_base(seq, rows):
        once("tok", lambda: load_tok().wait())
        return ctr.at[0, seq, rows]

    for name, t in (("n", tn), ("o", to)):
        for i in range(4):
            steps[f"fill{name}{i}"] = functools.partial(fill, name, t, i)
            steps[f"core{name}{i}"] = functools.partial(t.after_core, i, *of[name])
            for s in range(2):
                steps[f"l{name}{i}{s}"] = functools.partial(t.line, i, s)
        for s in range(2):
            steps[f"sp{name}{s}"] = functools.partial(t.spread, s, to_base if t is to else None)
            steps[f"sy{name}{s}"] = functools.partial(t.spread_y, s)
        steps["fin" + name] = t.finish

    def by_block(zz, xx, half):
        p = order[1, 2 * zz + xx]
        return [pick(p, lambda j: block[i, pl.ds(j if half == 0 else 15 - j, 1)]) for i in range(2)]

    cut = ORDER.index("pg") + 1

    def attention(ps, qkv, qt, kt, vt, gt, ot, logs, gpos, dqt, dk, dv):
        def project(zz, xx, rows, row):
            three = dot(rows[...], wx[:, :, :, pl.ds(512, 384)].reshape(2048, 384))
            for half in range(2):
                v = three[128 * half:128 * half + 128]
                t = angle_table(within, *by_block(zz, xx, half))
                at = pl.ds(row + 128 * half, 128)
                ps[at, pl.ds(0, 128)] = turn(v[:, 0:128], t).astype(BF) * BF(0.125)
                ps[at, pl.ds(128, 128)] = turn(v[:, 128:256], t).astype(BF)
                ps[at, pl.ds(256, 128)] = v[:, 256:384].astype(BF)

        def slope(zz, xx, rows, row):
            ps[pl.ds(row, 256), pl.ds(0, 128)] = dot_t(rows[...], wco[pl.ds(512, 128)]).astype(BF)

        def landed(i, name, t, own, act):
            once("own" + name, own)
            t.landed(far_first(z, 3 - i))
            each_half(f"{name}{i}", act)

        def own_rows():
            own_xn().wait()
            tx.sent_own(mine, xo)

        for i in range(4):
            steps[f"P{i}"] = functools.partial(landed, i, "P", tx, own_rows, project)
            steps[f"mg{i}"] = functools.partial(landed, i, "mg", tc, lambda: own_cot().wait(), slope)

        def by_position(b, cols):
            half = b // 8
            pair = b + half * (15 - 2 * b)
            return pick(order[0, pair], lambda j: ps[pl.ds(pl.multiple_of(256 * j + 128 * half, 128), 128), cols].astype(F4))

        def by_rows(c2, half):
            p = order[1, c2]
            return lambda ref: pick(p, lambda j: ref[pl.ds(128 * (j if half == 0 else 15 - j), 128)])

        def blocks(act):
            @pl.loop(0, 16)
            def _(b):
                act(b, pl.ds(pl.multiple_of(b * 128, 128), 128))

        def slots(act):
            for half in range(2):
                @pl.loop(0, 8)
                def _(c2):
                    act(by_rows(c2, half), pl.ds(pl.multiple_of(256 * c2 + 128 * half, 128), 128))

        def rope():
            def act(b, here):
                three = by_position(b, slice(None))
                for j, ref in enumerate((qt, kt, vt)):
                    v = three[:, 128 * j:128 * j + 128]
                    qkv[j, here] = v.astype(BF)
                    ref[:, here] = v.T.astype(BF)
            blocks(act)

        def score(i, h):
            kr = 256 * (i + 1)
            return masked(dot(qkv[1, :kr], one_head(qt[:, pl.ds(256 * i, 256)], h, 0)), kr)

        ahead = []

        def forward(i):
            kr, here = 256 * (i + 1), pl.ds(256 * i, 256)
            for h in range(2):
                st = ahead.pop() if ahead else score(0, 0)
                if (i, h) != (7, 1):
                    ahead.append(score(i + h, 1 - h))
                peak = jnp.max(st, axis=0, keepdims=True)
                p = jnp.exp(st - peak)
                total = jnp.sum(p, axis=0, keepdims=True)
                o = dot(vt[:, :kr], p.astype(BF)) * (1.0 / total)
                ot[pl.ds(64 * h, 64), here] = o[64 * h:64 * h + 64]
                logs[pl.ds(h, 1), here] = peak + jnp.log(total)

        def mix():
            def turned(b, here):
                gpos[here] = ot[:, here].T

            def placed(pos, row):
                am[row, pl.ds(512, 128)] = pos(gpos).astype(BF)
            blocks(turned)
            slots(placed)

        def gflip():
            def act(b, here):
                g = by_position(b, pl.ds(0, 128))
                gpos[here] = g
                gt[:, here] = g.T.astype(BF)
            blocks(act)
            dk[...] = jnp.zeros_like(dk)
            dv[...] = jnp.zeros_like(dv)

        def backward(i):
            kr, here = 256 * (i + 1), pl.ds(256 * i, 256)
            for h in range(2):
                p = jnp.exp(score(i, h) - logs[pl.ds(h, 1), here])
                low = p.astype(BF)
                at = pl.ds(64 * h, 64)
                delta = jnp.sum(ot[at, here] * gt[at, here].astype(F4), axis=0, keepdims=True)
                ds = (p * (dot(qkv[2, :kr], one_head(gt[:, here], h, 0)) - delta)).astype(BF)
                dv[:kr] += dot(low, one_head(gpos[here].astype(BF), h, 1))
                dk[:kr] += dot(ds, one_head(qkv[0, here], h, 1))
                dqt[at, here] = dot(kt[:, :kr], ds)[64 * h:64 * h + 64] * 0.125

        def gradients():
            def turned(b, here):
                t = angle_table(within, block[0, pl.ds(b, 1)], block[1, pl.ds(b, 1)])
                gpos[here] = turn_back(dqt[:, here].T, t)
                dk[here] = turn_back(dk[here], t)

            def placed(pos, row):
                for j, ref in enumerate((gpos, dk, dv)):
                    hp[row, pl.ds(512 + 128 * j, 128)] = pos(ref).astype(BF)
            blocks(turned)
            slots(placed)

        steps.update(rope=rope, mix=mix, gflip=gflip, pg=gradients)
        for i in range(8):
            steps[f"f{i}"] = functools.partial(forward, i)
            steps[f"b{i}"] = functools.partial(backward, i)
        for name in ORDER[:cut]:
            steps[name]()

    pl.run_scoped(
        attention, V((2048, 384), BF), V((3, 2048, 128), BF), V((128, 2048), BF), V((128, 2048), BF), V((128, 2048), BF),
        V((128, 2048), BF), V((128, 2048), F4), V((8, 2048), F4), V((2048, 128), F4), V((128, 2048), F4),
        V((2048, 128), F4), V((2048, 128), F4))

    def rest_of(col, stage, sums):
        plan = [n for n in ORDER if len(n) == 3 and n[0] in "gk" and n[1:].isdigit()]

        def block_load(n):
            xx = 1 - x if plan[n][0] == "g" else x
            src, d = (ct, xn)[int(plan[n][1])], mirrored(z, int(plan[n][2]))
            return pltpu.make_async_copy(src.at[:, :, :, columns(256, 2 * ((z + d) % 4) + xx)], col.at[n % 3], csem.at[n % 3])

        def grad(n):
            j, e = int(plan[n][1]), int(plan[n][2])
            block_load(n).wait()
            terms = dot(flip(col[n % 3].reshape(2048, 256)), (am, hp)[j][...])
            g = (g1, g2)[j]
            (g.give if plan[n][0] == "g" else g.keep)(e, terms if j else terms.T)
            if n + 3 < len(plan):
                block_load(n + 3).start()

        for n in range(3):
            block_load(n).start()
        copies = [remote(vec.at[(c + i + 1) % 8], vecs.at[c], vs.at[i], vr.at[i], others[i]) for i in range(7)]

        def normed_gradient():
            once("tok", lambda: load_tok().wait())
            load_cot().wait()
            norm_backward(ctr.at[0], ctr.at[1], ng, gs_all, ig, stage, ssem, sums)
            for i in range(8):
                at = slice(256 * i, 256 * i + 256)
                for j in range(2):
                    vec[i, j:j + 1, :] = jnp.sum(sums[j, :, at], axis=0, keepdims=True)
                vec[i, 2:8, :] = jnp.zeros((6, 256), F4)
            vecs[c] = vec[c]
            for cp in copies:
                cp.start()

        def gradients():
            g1.finish()
            g2.finish()

        steps["norm"], steps["gf"] = normed_gradient, gradients
        for n, name in enumerate(plan):
            steps[name] = functools.partial(grad, n)
        for name in ORDER[cut:]:
            steps[name]()
        for i in range(7):
            frm = vecs.at[(c - i - 1 + 8) % 8]
            remote(frm, frm, vs.at[i], vr.at[i], others[i]).wait_recv()
        total = vecs[0]
        for i in range(1, 8):
            total = total + vecs[i]
        vectors[...] = total
        for cp in copies:
            cp.wait_send()

    pl.run_scoped(rest_of, V((3, 4, 2, 256, 256), BF), V((2, 32, 2048), F4), V((2, 8, 2048), F4))
    for one in filled[-2:]:
        sent(one)
    tx.finish()
    tc.sent_own(cot_mine, cot_other)
    tc.finish()
    for w in range(6):
        wg.finish(w)
    for g in gcopies():
        g.wait_send()


def block_call(order, gs, tok, cot, win, wout, wexp, wcon):
    S = jax.ShapeDtypeStruct
    ANY = pl.BlockSpec(memory_space=pl.ANY)
    VM = pl.BlockSpec(memory_space=pltpu.VMEM)
    D = pltpu.SemaphoreType.DMA
    V = pltpu.VMEM
    rows = (4, 2, 256, 2048)
    return pl.pallas_call(
        block_kernel,
        out_shape=[S((2, 256, 2048), BF), S((2, 256, 2048), F4), S((8, 256), F4),
                   S((3, 256, 512), BF), S((512, 256), BF), S((256, 2048), BF), S((2048, 256), BF), S(rows, BF), S(rows, BF)],
        in_specs=[pl.BlockSpec(memory_space=pltpu.SMEM)] + [VM] * 3 + [ANY] * 6,
        out_specs=[ANY, ANY, VM] + [ANY] * 6,
        scratch_shapes=[V((4, 2, 256, 896), BF), V((640, 2048), BF), V((2048, 896), BF), V((2048, 640), BF), V((2, 2, 2, 64, 2048), BF),
                        V((2, 2, 256, 2048), BF), V((2, 256, 2048), BF), V((8, 8, 256), F4), V((8, 8, 256), F4), V((8, 8, 256), F4),
                        D((7,)), D((7,)), D((4,)), D((2, 2)), D((3,)), D((2,)), D((7,)), D((7,))]
        + token_sems() * 2 + weight_sems(6) + (reduce_bufs() + reduce_sems()) * 2 + grad_scratch((640, 256), 2) + grad_scratch((256, 896), 4),
        compiler_params=pltpu.CompilerParams(collective_id=0, has_side_effects=True, vmem_limit_bytes=63 * MB),
        name="block",
    )(order, gs, jnp.asarray(angles(128, 1)), jnp.asarray(angles(16, 128)), tok, cot, win, wout, wexp, wcon)


def own_local(tokens, pair_index, norm_gain, norm_shift, w_attention_in, w_attention_out, w_expand, w_contract, cotangent):
    x = lax.axis_index("ctx") % 2
    pairs = lax.dynamic_index_in_dim(pair_index, x, 0, False)
    which = jnp.arange(8, dtype=jnp.int32)
    inverse = jnp.sum(jnp.where(pairs[None, :] == which[:, None], which[None, :], 0), axis=1).astype(jnp.int32)
    gs = jnp.concatenate([norm_gain[None], norm_shift[None], jnp.zeros((6, 256), BF)], axis=0).astype(F4)
    output, input_grad, vectors, *grads = block_call(
        jnp.stack([inverse, pairs]), gs, tokens, cotangent, w_attention_in, w_attention_out, w_expand, w_contract)
    return (output, input_grad, vectors[0], vectors[1], *(g.astype(F4) for g in grads[:4]))


def local(tokens, pair_index, norm_gain, norm_shift, w_attention_in, w_attention_out, w_expand, w_contract, cotangent):
    args = (tokens, pair_index, norm_gain, norm_shift, w_attention_in, w_attention_out, w_expand, w_contract, cotangent)
    sizes = (lax.axis_size("ctx"), lax.axis_size("tp")) + tokens.shape + w_attention_in.shape[2:] + w_expand.shape[1:]
    if sizes == (8, 4, 2, 256, 2048, 512, 2048):
        return own_local(*args)
    return general_local(*args)


def solution(mesh):
    in_specs = (
        P(None, "ctx", None),
        P(),
        P("ctx"),
        P("ctx"),
        P(None, "ctx", "tp"),
        P("tp", "ctx"),
        P("ctx", "tp"),
        P("tp", "ctx"),
        P(None, "ctx", None),
    )
    out_specs = (
        P(None, "ctx", None),
        P(None, "ctx", None),
        P("ctx"),
        P("ctx"),
        P(None, "ctx", "tp"),
        P("tp", "ctx"),
        P("ctx", "tp"),
        P("tp", "ctx"),
    )
    return jax.shard_map(local, mesh=mesh, in_specs=in_specs, out_specs=out_specs, check_vma=False)
```

```python
import functools
import itertools

import jax
import jax.numpy as jnp
import numpy as np
from jax import lax
from jax.experimental import pallas as pl
from jax.experimental.pallas import tpu as pltpu
from jax.sharding import PartitionSpec as P

HEAD_DIM = 64
ROT = 32


epsilon = 1e-05


def position_table(pair_index, shard_rows):
    pair_count = pair_index.shape[1]
    half_rows = shard_rows // 2
    token_index = jnp.arange(shard_rows * pair_count, dtype=jnp.int32)
    owning = token_index // shard_rows
    within = token_index % shard_rows
    picked = (owning[:, None] == jnp.arange(pair_count, dtype=jnp.int32)[None, :]).astype(jnp.int32)
    chosen = jnp.sum(picked[None, :, :] * pair_index[:, None, :], axis=2)
    first_half = chosen * half_rows + within[None, :]
    second = (2 * pair_count - 1 - chosen) * half_rows + within[None, :] - half_rows
    return jnp.where(within[None, :] < half_rows, first_half, second)


def rotate(tensor, positions):
    half_rot = ROT // 2
    frequency = 10000.0 ** (-2.0 * jnp.arange(half_rot, dtype=jnp.float32) / ROT)
    angles = positions.astype(jnp.float32)[..., None] * frequency
    cosine = jnp.cos(angles)[..., None, :]
    sine_part = jnp.sin(angles)[..., None, :]
    leading = tensor[..., :half_rot]
    trailing = tensor[..., half_rot:ROT]
    return jnp.concatenate(
        [
            leading * cosine - trailing * sine_part,
            trailing * cosine + leading * sine_part,
            tensor[..., ROT:],
        ],
        axis=-1,
    )


def gelu_tanh(values_in):
    return (
        0.5
        * values_in
        * (
            1.0
            + jnp.tanh(
                0.7978845608028654 * (values_in + 0.044715 * values_in * values_in * values_in)
            )
        )
    )


def layer_norm(inputs, gain_full, shift_full):
    centred = inputs - jnp.mean(inputs, axis=-1, keepdims=True)
    spread = jnp.mean(centred * centred, axis=-1, keepdims=True)
    return centred * lax.rsqrt(spread + epsilon) * gain_full + shift_full


def block_probs(queries, keys_block, log_total, query_pos, key_pos):
    raw_scores = jnp.einsum(
        "sqhe,skhe->shqk", queries, keys_block, preferred_element_type=jnp.float32
    )
    allowed = key_pos[:, None, None, :] <= query_pos[:, None, :, None]
    return jnp.where(allowed, jnp.exp(raw_scores * HEAD_DIM ** (-0.5) - log_total[..., None]), 0.0)


def score_grads(
    queries, keys_block, values_block, log_total, row_delta, out_grad, query_pos, key_pos
):
    probs_full = block_probs(queries, keys_block, log_total, query_pos, key_pos)
    prob_grad = jnp.einsum(
        "sqhe,skhe->shqk", out_grad, values_block, preferred_element_type=jnp.float32
    )
    score_grad = (probs_full * (prob_grad - row_delta[..., None]) * HEAD_DIM ** (-0.5)).astype(
        jnp.bfloat16
    )
    return (probs_full.astype(jnp.bfloat16), score_grad)


def key_slice(keys_all, offset, key_rows, head_count):
    seq_count = keys_all.shape[0]
    return lax.dynamic_slice_in_dim(keys_all, offset, key_rows, 1).reshape(
        seq_count, key_rows, head_count, HEAD_DIM
    )


def log_totals(queries, keys_all, query_pos, pos_table, key_rows):
    seq_count, query_rows, head_count, head_size = queries.shape
    turn_count = keys_all.shape[1] // key_rows

    def log_one_turn(turn_index, state_in):
        running_max, running_sum = state_in
        offset = turn_index * key_rows
        keys_block = key_slice(keys_all, offset, key_rows, head_count)
        key_pos = lax.dynamic_slice_in_dim(pos_table, offset, key_rows, 1)
        raw_scores = jnp.einsum(
            "sqhe,skhe->shqk", queries, keys_block, preferred_element_type=jnp.float32
        ) * HEAD_DIM ** (-0.5)
        allowed = key_pos[:, None, None, :] <= query_pos[:, None, :, None]
        masked = jnp.where(allowed, raw_scores, -1e30)
        new_max = jnp.maximum(running_max, jnp.max(masked, axis=-1))
        kept_terms = jnp.where(allowed, jnp.exp(masked - new_max[..., None]), 0.0)
        return (
            new_max,
            running_sum * jnp.exp(running_max - new_max) + jnp.sum(kept_terms, axis=-1),
        )

    initial = (
        jnp.full((seq_count, head_count, query_rows), -1e30, jnp.float32),
        jnp.zeros((seq_count, head_count, query_rows), jnp.float32),
    )
    final_max, final_sum = lax.fori_loop(0, turn_count, log_one_turn, initial)
    return final_max + jnp.log(final_sum)


def attend_values(queries, keys_all, values_all, log_total, query_pos, pos_table, key_rows):
    head_count = queries.shape[2]
    turn_count = keys_all.shape[1] // key_rows

    def attend_one_turn(turn_index, running):
        offset = turn_index * key_rows
        keys_block = key_slice(keys_all, offset, key_rows, head_count)
        values_block = key_slice(values_all, offset, key_rows, head_count)
        key_pos = lax.dynamic_slice_in_dim(pos_table, offset, key_rows, 1)
        weights_low = block_probs(queries, keys_block, log_total, query_pos, key_pos).astype(
            jnp.bfloat16
        )
        return running + jnp.einsum(
            "shqk,skhe->sqhe", weights_low, values_block, preferred_element_type=jnp.float32
        )

    return lax.fori_loop(0, turn_count, attend_one_turn, jnp.zeros(queries.shape, jnp.float32))


def full_grads(
    queries, keys_all, values_all, log_total, row_delta, out_grad, query_pos, pos_table, key_rows
):
    seq_count, query_rows, head_count, head_size = queries.shape
    turn_count = keys_all.shape[1] // key_rows

    def full_one_turn(turn_index, state_in):
        query_grad, key_terms, value_terms = state_in
        offset = turn_index * key_rows
        keys_block = key_slice(keys_all, offset, key_rows, head_count)
        values_block = key_slice(values_all, offset, key_rows, head_count)
        key_pos = lax.dynamic_slice_in_dim(pos_table, offset, key_rows, 1)
        weights_low, score_grad = score_grads(
            queries, keys_block, values_block, log_total, row_delta, out_grad, query_pos, key_pos
        )
        query_grad = query_grad + jnp.einsum(
            "shqk,skhe->sqhe", score_grad, keys_block, preferred_element_type=jnp.float32
        )
        key_part = jnp.einsum(
            "shqk,sqhe->skhe", score_grad, queries, preferred_element_type=jnp.float32
        ).reshape(seq_count, key_rows, head_count * head_size)
        value_part = jnp.einsum(
            "shqk,sqhe->skhe", weights_low, out_grad, preferred_element_type=jnp.float32
        ).reshape(seq_count, key_rows, head_count * head_size)
        key_terms = lax.dynamic_update_slice_in_dim(key_terms, key_part, offset, 1)
        value_terms = lax.dynamic_update_slice_in_dim(value_terms, value_part, offset, 1)
        return (query_grad, key_terms, value_terms)

    initial = (
        jnp.zeros(queries.shape, jnp.float32),
        jnp.zeros(keys_all.shape, jnp.float32),
        jnp.zeros(values_all.shape, jnp.float32),
    )
    return lax.fori_loop(0, turn_count, full_one_turn, initial)


def general_local(
    tokens,
    pair_index,
    norm_gain,
    norm_shift,
    w_attention_in,
    w_attention_out,
    w_expand,
    w_contract,
    cotangent,
):
    seq_count, shard_rows, model_width = tokens.shape
    gain_full, shift_full, attention_in, attention_out, expand_full, contract_full = (
        lax.all_gather(norm_gain, "ctx", axis=0, tiled=True),
        lax.all_gather(norm_shift, "ctx", axis=0, tiled=True),
        lax.all_gather(w_attention_in, "ctx", axis=1, tiled=True),
        lax.all_gather(w_attention_out, "ctx", axis=1, tiled=True),
        lax.all_gather(w_expand, "ctx", axis=0, tiled=True),
        lax.all_gather(w_contract, "ctx", axis=1, tiled=True),
    )
    local_width = attention_in.shape[2]
    head_count = local_width // HEAD_DIM
    flat_rows = seq_count * shard_rows
    pos_table = position_table(pair_index, shard_rows)
    total_rows = pos_table.shape[1]
    own_pos = lax.dynamic_slice_in_dim(pos_table, lax.axis_index("ctx") * shard_rows, shard_rows, 1)
    key_rows = min(total_rows, 1024)
    inputs = tokens.astype(jnp.float32)
    normed_full, norm_pull = jax.vjp(
        layer_norm, inputs, gain_full.astype(jnp.float32), shift_full.astype(jnp.float32)
    )
    normed = normed_full.astype(jnp.bfloat16).reshape(flat_rows, model_width)
    projected = jnp.einsum("td,kde->kte", normed, attention_in, preferred_element_type=jnp.float32)
    split_heads = projected.reshape(3, seq_count, shard_rows, head_count, HEAD_DIM)
    rotated, rotate_pull = jax.vjp(lambda pair_part: rotate(pair_part, own_pos), split_heads[:2])
    queries = rotated[0].astype(jnp.bfloat16)
    own_keys = rotated[1].astype(jnp.bfloat16)
    own_values = split_heads[2].astype(jnp.bfloat16)
    keys_all, values_all = (
        lax.all_gather(
            own_keys.reshape(seq_count, shard_rows, local_width), "ctx", axis=1, tiled=True
        ),
        lax.all_gather(
            own_values.reshape(seq_count, shard_rows, local_width), "ctx", axis=1, tiled=True
        ),
    )
    log_total = log_totals(queries, keys_all, own_pos, pos_table, key_rows)
    attended = attend_values(queries, keys_all, values_all, log_total, own_pos, pos_table, key_rows)
    mixed = attended.reshape(flat_rows, local_width).astype(jnp.bfloat16)
    hidden_pre = jnp.dot(normed, expand_full, preferred_element_type=jnp.float32)
    activated_full, gelu_pull = jax.vjp(gelu_tanh, hidden_pre)
    activated = activated_full.astype(jnp.bfloat16)
    branch = jnp.dot(mixed, attention_out, preferred_element_type=jnp.float32) + jnp.dot(
        activated, contract_full, preferred_element_type=jnp.float32
    )
    branch = lax.psum(branch.astype(jnp.bfloat16), "tp").astype(jnp.float32)
    output = (inputs + branch.reshape(seq_count, shard_rows, model_width)).astype(jnp.bfloat16)
    upstream = cotangent.reshape(flat_rows, model_width)
    contract_grad = jnp.einsum("tf,td->fd", activated, upstream, preferred_element_type=jnp.float32)
    (gelu_grad,) = gelu_pull(
        jnp.einsum("td,fd->tf", upstream, contract_full, preferred_element_type=jnp.float32)
    )
    hidden_grad = gelu_grad.astype(jnp.bfloat16)
    expand_grad = jnp.einsum("td,tf->df", normed, hidden_grad, preferred_element_type=jnp.float32)
    mixed_grad = jnp.einsum(
        "td,ed->te", upstream, attention_out, preferred_element_type=jnp.float32
    ).astype(jnp.bfloat16)
    attention_out_grad = jnp.einsum(
        "te,td->ed", mixed, upstream, preferred_element_type=jnp.float32
    )
    out_grad = mixed_grad.reshape(seq_count, shard_rows, head_count, HEAD_DIM)
    row_delta = jnp.sum(out_grad.astype(jnp.float32) * attended, axis=-1).transpose(0, 2, 1)
    query_grad, key_terms, value_terms = full_grads(
        queries, keys_all, values_all, log_total, row_delta, out_grad, own_pos, pos_table, key_rows
    )
    key_grad, value_grad = (
        lax.psum_scatter(
            key_terms.astype(jnp.bfloat16), "ctx", scatter_dimension=1, tiled=True
        ).astype(jnp.float32),
        lax.psum_scatter(
            value_terms.astype(jnp.bfloat16), "ctx", scatter_dimension=1, tiled=True
        ).astype(jnp.float32),
    )
    key_grad = key_grad.reshape(seq_count, shard_rows, head_count, HEAD_DIM)
    value_grad = value_grad.reshape(seq_count, shard_rows, head_count, HEAD_DIM)
    (rotated_grad,) = rotate_pull(jnp.stack([query_grad, key_grad]))
    projected_grad = (
        jnp.concatenate([rotated_grad, value_grad[None]], axis=0)
        .reshape(3, flat_rows, local_width)
        .astype(jnp.bfloat16)
    )
    attention_in_grad = jnp.einsum(
        "td,kte->kde", normed, projected_grad, preferred_element_type=jnp.float32
    )
    normed_grad = jnp.einsum(
        "kte,kde->td", projected_grad, attention_in, preferred_element_type=jnp.float32
    )
    normed_grad = normed_grad + jnp.einsum(
        "tf,df->td", hidden_grad, expand_full, preferred_element_type=jnp.float32
    )
    normed_grad = lax.psum(normed_grad.astype(jnp.bfloat16), "tp").astype(jnp.float32)
    input_part, gain_grad, shift_grad = norm_pull(
        normed_grad.reshape(seq_count, shard_rows, model_width)
    )
    input_grad = input_part + cotangent.astype(jnp.float32)
    reduced = (
        lax.psum_scatter(
            gain_grad.astype(jnp.bfloat16), "ctx", scatter_dimension=0, tiled=True
        ).astype(jnp.float32),
        lax.psum_scatter(
            shift_grad.astype(jnp.bfloat16), "ctx", scatter_dimension=0, tiled=True
        ).astype(jnp.float32),
        lax.psum_scatter(
            attention_in_grad.astype(jnp.bfloat16), "ctx", scatter_dimension=1, tiled=True
        ).astype(jnp.float32),
        lax.psum_scatter(
            attention_out_grad.astype(jnp.bfloat16), "ctx", scatter_dimension=1, tiled=True
        ).astype(jnp.float32),
        lax.psum_scatter(
            expand_grad.astype(jnp.bfloat16), "ctx", scatter_dimension=0, tiled=True
        ).astype(jnp.float32),
        lax.psum_scatter(
            contract_grad.astype(jnp.bfloat16), "ctx", scatter_dimension=1, tiled=True
        ).astype(jnp.float32),
    )
    return (
        output,
        input_grad,
        reduced[0],
        reduced[1],
        reduced[2],
        reduced[3],
        reduced[4],
        reduced[5],
    )


MESH = pl.DeviceIdType.MESH
MB = 1 << 20
EPS = 1e-05
BF = jnp.bfloat16
F4 = jnp.float32
NT = (((1,), (1,)), ((), ()))
FAR = (1, 2, 3, 0)


def place():
    c = lax.axis_index("ctx")
    t = lax.axis_index("tp")
    return c // 2, c % 2, t // 2, t % 2


def device(z, x, y, k):
    return (z * 2 + x, y * 2 + k)


def remote(src, dst, send_sem, recv_sem, target):
    return pltpu.make_async_remote_copy(
        src_ref=src, dst_ref=dst, send_sem=send_sem, recv_sem=recv_sem,
        device_id=target, device_id_type=MESH,
    )


def meet(peers):
    barrier = pltpu.get_barrier_semaphore()
    for peer in peers:
        pl.semaphore_signal(barrier, inc=1, device_id=peer, device_id_type=MESH)
    pl.semaphore_wait(barrier, len(peers))


def peers_of(z, x, y, k):
    c = z * 2 + x
    others = [((c + i) % 8, lax.axis_index("tp")) for i in range(1, 8)]
    return others, others + [device(z, x, 1 - y, k), device(z, x, y, 1 - k)]


def columns(n, i):
    return pl.ds(pl.multiple_of(n * i, n), n)


def dot(a, b):
    return jnp.dot(a, b, preferred_element_type=F4)


def dot_t(a, b):
    return lax.dot_general(a, b, NT, preferred_element_type=F4)


def mirrored(z, e):
    return jnp.where(z < 2, 4 - e, e) if e in (1, 3) else e


def far_first(z, i):
    return (3 * (1 - z // 2), z // 2 + 2 * (1 - z % 2), 1 + z % 2, z)[i]


def add_into(dst, src):
    lead, rows = dst.shape[:-2], dst.shape[-2]
    for idx in itertools.product(*(range(n) for n in lead)):
        @pl.loop(0, rows // 16)
        def _(i):
            at = idx + (pl.ds(pl.multiple_of(16 * i, 16), 16), slice(None))
            dst[at] = (dst[at].astype(F4) + src[at].astype(F4)).astype(BF)


class TokenGather:
    def __init__(self, whole, sems):
        self.whole = whole
        self.xs, self.xr, self.zs, self.zr, self.ys, self.yr, self.cs, self.cr = sems
        self.z, self.x, self.y, self.k = place()
        self.q = 2 * self.y + self.k

    def chunk(self, zz, s, q):
        xx = self.x if s == 0 else 1 - self.x
        return self.whole.at[zz, xx, pl.ds(64 * q, 64), :]

    def send_x(self, src):
        z, x, y, k = self.z, self.x, self.y, self.k
        return remote(src, self.whole.at[z, x, pl.ds(64 * self.q, 64), :], self.xs, self.xr, device(z, 1 - x, y, k))

    def send_up(self, zz, s, src):
        return remote(src, self.chunk(zz, s, self.q), self.zs.at[zz, s, 0], self.zr.at[zz, s],
                      device(jnp.minimum(self.z + 1, 3), self.x, self.y, self.k))

    def send_down(self, zz, s, src):
        return remote(src, self.chunk(zz, s, self.q), self.zs.at[zz, s, 1], self.zr.at[zz, s],
                      device(jnp.maximum(self.z - 1, 0), self.x, self.y, self.k))

    def send_y(self, zz, s):
        c = self.chunk(zz, s, self.q)
        return remote(c, c, self.ys.at[zz, s], self.yr.at[zz, s], device(self.z, self.x, 1 - self.y, self.k))

    def send_core(self, zz, s, j):
        yy = self.y if j == 0 else 1 - self.y
        c = self.chunk(zz, s, 2 * yy + self.k)
        return remote(c, c, self.cs.at[zz, s, j], self.cr.at[zz, s, j], device(self.z, self.x, self.y, 1 - self.k))

    def both_ways(self, s, src):
        z = self.z

        @pl.when(z < 3)
        def _():
            self.send_up(z, s, src).start()

        @pl.when(z > 0)
        def _():
            self.send_down(z, s, src).start()

    def start(self, own_quarter, other_quarter):
        self.send_x(other_quarter).start()
        self.both_ways(0, own_quarter)

    def after_x(self):
        c = self.chunk(self.z, 1, self.q)
        remote(c, c, self.xs, self.xr, device(self.z, 1 - self.x, self.y, self.k)).wait_recv()
        self.both_ways(1, c)
        self.send_y(self.z, 1).start()
        self.send_core(self.z, 1, 0).start()

    def hop(self, d, s):
        z = self.z

        @pl.when(z >= d)
        def _():
            zz = z - d
            c = self.chunk(zz, s, self.q)
            self.send_down(zz, s, c).wait_recv()

            @pl.when(z < 3)
            def _():
                self.send_up(zz, s, c).start()

            self.send_y(zz, s).start()
            self.send_core(zz, s, 0).start()

        @pl.when(z + d <= 3)
        def _():
            zz = z + d
            c = self.chunk(zz, s, self.q)
            self.send_up(zz, s, c).wait_recv()

            @pl.when(z > 0)
            def _():
                self.send_down(zz, s, c).start()

            self.send_y(zz, s).start()
            self.send_core(zz, s, 0).start()

    def y_in(self, zz, s):
        c = self.chunk(zz, s, 2 * (1 - self.y) + self.k)
        remote(c, c, self.ys.at[zz, s], self.yr.at[zz, s], device(self.z, self.x, 1 - self.y, self.k)).wait_recv()
        self.send_core(zz, s, 1).start()

    def y_hop(self, d):
        z = self.z
        if d == 0:
            self.y_in(z, 1)
            return
        for s in range(2):
            pl.when(z >= d)(lambda: self.y_in(z - d, s))
            pl.when(z + d <= 3)(lambda: self.y_in(z + d, s))

    def landed(self, zz):
        def rest(s):
            for j in range(2):
                yy = self.y if j == 0 else 1 - self.y
                c = self.chunk(zz, s, 2 * yy + 1 - self.k)
                remote(c, c, self.cs.at[zz, s, j], self.cr.at[zz, s, j], device(self.z, self.x, self.y, 1 - self.k)).wait_recv()

        pl.when(self.z != zz)(lambda: rest(0))
        rest(1)

    def sent_own(self, own_quarter, other_quarter):
        z = self.z
        self.send_x(other_quarter).wait_send()
        pl.when(z < 3)(lambda: self.send_up(z, 0, own_quarter).wait_send())
        pl.when(z > 0)(lambda: self.send_down(z, 0, own_quarter).wait_send())

    def finish(self):
        z = self.z
        for zz in range(4):
            for s in range(2):
                def rest():
                    self.send_y(zz, s).wait_send()
                    for j in range(2):
                        self.send_core(zz, s, j).wait_send()
                if s == 0:
                    pl.when(z != zz)(rest)
                else:
                    rest()
                c = self.chunk(zz, s, self.q)

                pl.when((z < 3) & (zz < z + s))(lambda: self.send_up(zz, s, c).wait_send())
                pl.when((z > 0) & (zz > z - s))(lambda: self.send_down(zz, s, c).wait_send())


def token_sems():
    D = pltpu.SemaphoreType.DMA
    return [D, D, D((4, 2, 2)), D((4, 2)), D((4, 2)), D((4, 2)), D((4, 2, 2)), D((4, 2, 2))]


class WeightGather:
    def __init__(self, pairs, sems):
        self.pairs = pairs
        self.zs, self.zr, self.xs, self.xr, self.loc = sems
        self.z, self.x, self.y, self.k = place()

    def z_send(self, d, w):
        src, dst = self.pairs[w]
        to = (self.z + d) % 4
        return remote(src(to), dst(self.z, self.x), self.zs.at[d, w], self.zr.at[d, w], device(to, self.x, self.y, self.k))

    def z_recv(self, d, w):
        dst = self.pairs[w][1]
        frm = (self.z - d + 4) % 4
        return remote(dst(frm, self.x), dst(frm, self.x), self.zs.at[d, w], self.zr.at[d, w], device(frm, self.x, self.y, self.k))

    def x_send(self, d, w):
        src, dst = self.pairs[w]
        frm = (self.z - d + 4) % 4
        s = src(self.z) if isinstance(d, int) and d == 0 else dst(frm, self.x)
        return remote(s, dst(frm, self.x), self.xs.at[d, w], self.xr.at[d, w], device(self.z, 1 - self.x, self.y, self.k))

    def x_recv(self, d, w):
        frm = (self.z - d + 4) % 4
        r = self.pairs[w][1](frm, 1 - self.x)
        return remote(r, r, self.xs.at[d, w], self.xr.at[d, w], device(self.z, 1 - self.x, self.y, self.k))

    def local(self, w):
        src, dst = self.pairs[w]
        return pltpu.make_async_copy(src(self.z), dst(self.z, self.x), self.loc.at[w])

    def send(self, ws, e):
        d = mirrored(self.z, e)
        for w in ws:
            if e:
                self.z_send(d, w).start()
            else:
                self.x_send(0, w).start()
                self.local(w).start()

    def forward(self, ws, e):
        d = mirrored(self.z, e)
        for w in ws:
            self.z_recv(d, w).wait_recv()
            self.x_send(d, w).start()

    def landed(self, w):
        self.local(w).wait()
        for d in range(4):
            self.x_recv(d, w).wait_recv()

    def finish(self, w):
        for d in range(4):
            if d:
                self.z_send(d, w).wait_send()
            self.x_send(d, w).wait_send()


def weight_sems(n):
    D = pltpu.SemaphoreType.DMA
    return [D((4, n)), D((4, n)), D((4, n)), D((4, n)), D((n,))]


class TokenReduce:
    def __init__(self, out, bufs, sems):
        self.out = out
        self.S, self.r1, self.r2, self.rz, self.rf = bufs
        (self.cs, self.cr, self.ys, self.yr, self.zs, self.zr, self.xs, self.xr,
         self.fl, self.fys, self.fyr, self.fcs, self.fcr) = sems
        self.z, self.x, self.y, self.k = place()
        self.q = 2 * self.y + self.k

    def slot(self, s):
        return self.x if s == 0 else 1 - self.x

    def core(self, i, slot=0):
        zz = far_first(self.z, i)
        return remote(self.S.at[slot], self.r1.at[zz], self.cs.at[zz], self.cr.at[zz], device(self.z, self.x, self.y, 1 - self.k))

    def yex(self, zz, s):
        xx = self.slot(s)
        return remote(self.r1.at[zz, 1 - self.y, xx], self.r2.at[zz, xx], self.ys.at[zz, s], self.yr.at[zz, s],
                      device(self.z, self.x, 1 - self.y, self.k))

    def mine(self, zz, s):
        return self.r1.at[zz, self.y, self.slot(s)]

    def up(self, zz, s):
        return remote(self.mine(zz, s), self.rz.at[zz, s], self.zs.at[zz, s], self.zr.at[zz, s],
                      device(jnp.minimum(self.z + 1, 3), self.x, self.y, self.k))

    def down(self, zz, s):
        slot = jnp.where(zz == self.z - 1, 4, zz)
        return remote(self.mine(zz, s), self.rz.at[slot, s], self.zs.at[zz, s], self.zr.at[slot, s],
                      device(jnp.maximum(self.z - 1, 0), self.x, self.y, self.k))

    def arrive(self, zz, s, slot):
        r = self.rz.at[slot, s]
        remote(r, r, self.zs.at[0, s], self.zr.at[slot, s], device(self.z, self.x, self.y, 1 - self.k)).wait_recv()
        add_into(self.mine(zz, s), r)

    def xex(self):
        return remote(self.mine(self.z, 1), self.rf, self.xs, self.xr, device(self.z, 1 - self.x, self.y, self.k))

    def rows(self, i, kk, lhs):
        zz = far_first(self.z, i)
        return jnp.concatenate([lhs(zz, xx, 64 * (2 * yy + kk)) for yy in range(2) for xx in range(2)], axis=0)

    def fill(self, i, slot, lhs, rhs):
        a = self.rows(i, 1 - self.k, lhs)

        @pl.loop(0, 4)
        def _(j):
            at = columns(512, j)
            self.S[slot, :, :, :, at] = rhs(a, j).astype(BF).reshape(2, 2, 64, 512)
        self.core(i, slot).start()

    def after_core(self, i, lhs, rhs):
        zz = far_first(self.z, i)
        a = self.rows(i, self.k, lhs)
        self.core(i).wait_recv()

        @pl.loop(0, 4)
        def _(j):
            at = columns(512, j)
            got = self.r1[zz, :, :, :, at].reshape(256, 512).astype(F4)
            self.r1[zz, :, :, :, at] = (rhs(a, j) + got).astype(BF).reshape(2, 2, 64, 512)
        for s in (1, 0):
            self.yex(zz, s).start()

    def line(self, i, s):
        z = self.z
        zz = far_first(z, i)
        self.yex(zz, s).wait_recv()
        add_into(self.mine(zz, s), self.r2.at[zz, self.slot(s)])
        if i < 3:
            @pl.when(zz > z)
            def _():
                pl.when(z > 0)(lambda: self.arrive(zz, s, zz))
                self.up(zz, s).start()

            @pl.when(zz < z)
            def _():
                pl.when(z < 3)(lambda: self.arrive(zz, s, zz))
                self.down(zz, s).start()
        else:
            pl.when(z > 0)(lambda: self.arrive(z, s, z))
            pl.when(z < 3)(lambda: self.arrive(z, s, 4))
            if s == 1:
                self.xex().start()

    def spot(self, s, q):
        return self.out.at[self.slot(s), pl.ds(64 * q, 64), :]

    def fin_copies(self, s):
        src = self.mine(self.z, 0) if s == 0 else self.rf
        here = self.spot(s, self.q)
        return (pltpu.make_async_copy(src, here, self.fl.at[s]),
                remote(src, here, self.fys.at[s], self.fyr.at[s], device(self.z, self.x, 1 - self.y, self.k)),
                remote(src, here, self.fcs.at[s, 0], self.fcr.at[s, 0], device(self.z, self.x, self.y, 1 - self.k)))

    def relay(self, s):
        r = self.spot(s, 2 * (1 - self.y) + self.k)
        return remote(r, r, self.fcs.at[s, 1], self.fcr.at[s, 1], device(self.z, self.x, self.y, 1 - self.k))

    def spread(self, s, base=None):
        if s == 1:
            self.xex().wait_recv()
        if base is not None:
            add_into(self.mine(self.z, 0) if s == 0 else self.rf, base(self.slot(s), pl.ds(64 * self.q, 64)))
        for cp in self.fin_copies(s):
            cp.start()

    def spread_y(self, s):
        r = self.spot(s, 2 * (1 - self.y) + self.k)
        remote(r, r, self.fys.at[s], self.fyr.at[s], device(self.z, self.x, 1 - self.y, self.k)).wait_recv()
        self.relay(s).start()

    def finish(self):
        z = self.z
        for zz in range(4):
            for s in range(2):
                self.yex(zz, s).wait_send()
                pl.when(z != zz)(lambda: self.up(zz, s).wait_send())
        self.xex().wait_send()
        for s in range(2):
            for copy in self.fin_copies(s)[1:]:
                copy.wait_send()
            self.relay(s).wait_send()

    def landed(self, s):
        self.fin_copies(s)[0].wait()
        for j, yy in ((0, self.y), (1, 1 - self.y)):
            r = self.spot(s, 2 * yy + 1 - self.k)
            remote(r, r, self.fcs.at[s, j], self.fcr.at[s, j], device(self.z, self.x, self.y, 1 - self.k)).wait_recv()


def reduce_sems():
    D = pltpu.SemaphoreType.DMA
    return [D((4,)), D((4,)), D((4, 2)), D((4, 2)), D((4, 2)), D((5, 2)), D, D,
            D((2,)), D((2,)), D((2,)), D((2, 2)), D((2, 2))]


def reduce_bufs():
    V = lambda *s: pltpu.VMEM(s, BF)
    return [V(4, 2, 2, 64, 2048), V(4, 2, 64, 2048), V(5, 2, 64, 2048), V(64, 2048)]


class GradReduce:
    def __init__(self, parts, away, got, sems):
        self.parts, self.away, self.got = parts, away, got
        self.xs, self.xr, self.zs, self.zr = sems
        self.z, self.x, self.y, self.k = place()

    def x_send(self, e):
        i = FAR.index(e)
        return remote(self.away.at[i % 2], self.got.at[i], self.xs.at[i], self.xr.at[i], device(self.z, 1 - self.x, self.y, self.k))

    def z_sends(self, e):
        d = mirrored(self.z, e)
        for i, (part, there) in enumerate(self.parts):
            src, dst = self.got.at[(FAR.index(e),) + part], there(self.z)
            if e == 0:
                yield pltpu.make_async_copy(src, dst, self.zs.at[0, i])
            else:
                yield remote(src, dst, self.zs.at[d, i], self.zr.at[d, i], device((self.z + d) % 4, self.x, self.y, self.k))

    def give(self, e, terms):
        i = FAR.index(e)
        if i >= 2:
            self.x_send(FAR[i - 2]).wait_send()
        self.away[i % 2] = terms.astype(BF)
        self.x_send(e).start()

    def keep(self, e, terms):
        i = FAR.index(e)
        self.x_send(e).wait_recv()
        self.got[i] = (terms + self.got[i].astype(F4)).astype(BF)
        for cp in self.z_sends(e):
            cp.start()

    def finish(self):
        for cp in self.z_sends(0):
            cp.wait()
        for e in FAR[2:]:
            self.x_send(e).wait_send()
        for d in range(1, 4):
            frm = (self.z - d + 4) % 4
            for cp in self.z_sends(d):
                cp.wait_send()
            for i, (part, there) in enumerate(self.parts):
                r = there(frm)
                remote(r, r, self.zs.at[d, i], self.zr.at[d, i], device(frm, self.x, self.y, self.k)).wait_recv()


def grad_scratch(block, parts):
    D = pltpu.SemaphoreType.DMA
    V = pltpu.VMEM
    return [V((2,) + block, BF), V((4,) + block, BF)] + [D((4,))] * 2 + [D((4, parts))] * 2


def norm_rows(rows, gain, shift):
    v = rows.astype(F4)
    centred = v - jnp.mean(v, axis=-1, keepdims=True)
    spread = jnp.mean(centred * centred, axis=-1, keepdims=True)
    return (centred * lax.rsqrt(spread + EPS) * gain + shift).astype(BF)


def turn(v, tab):
    cos, lo, hi = tab
    return v * cos + pltpu.roll(v, 112, 1) * lo + pltpu.roll(v, 16, 1) * hi


def turn_back(v, tab):
    cos, lo, hi = tab
    return v * cos - pltpu.roll(v, 112, 1) * lo - pltpu.roll(v, 16, 1) * hi


def angle_table(within, cb, sb):
    cr, sr = within[0], within[1]
    cos, sin = cb * cr - sb * sr, sb * cr + cb * sr
    entry = lax.broadcasted_iota(jnp.int32, cos.shape, 1) % 64
    return cos, jnp.where(entry < 16, -sin, 0.0), jnp.where(entry < 16, 0.0, sin)


def angles(rows, step):
    frequency = (10000.0 ** (-2.0 * np.arange(16) / 32)).astype(np.float32).astype(np.float64)
    lanes = np.concatenate([frequency, frequency, np.zeros(32)] * 2)
    angle = step * np.arange(rows)[:, None] * lanes
    return np.stack([np.cos(angle), np.sin(angle)]).astype(np.float32)


def pick(index, parts):
    chosen = parts(0)
    for j in range(1, 8):
        chosen = jnp.where(index == j, parts(j), chosen)
    return chosen


def one_head(v, h, axis):
    entry = lax.broadcasted_iota(jnp.int32, v.shape, axis)
    return jnp.where((entry < 64) == (h == 0), v, jnp.zeros_like(v))


def masked(st, kr):
    row = lax.broadcasted_iota(jnp.int32, (256, 256), 0)
    column = lax.broadcasted_iota(jnp.int32, (256, 256), 1)
    last = jnp.where(row <= column, st[kr - 256:], -1e30)
    return last if kr == 256 else jnp.concatenate([st[:kr - 256], last], axis=0)


def flip(v):
    return v.astype(F4).T.astype(BF)


def norm_backward(s, tok, cot, ng, gains, out, stage, ssem, sums):
    gain = jnp.concatenate([gains[i, 0:1, :] for i in range(8)], axis=1)

    def store(i):
        return pltpu.make_async_copy(stage.at[i % 2], out.at[s, pl.ds(pl.multiple_of(32 * i, 32), 32)], ssem.at[i % 2])

    @pl.loop(0, 8)
    def _(i):
        at = pl.ds(pl.multiple_of(32 * i, 32), 32)
        v = tok[s, at].astype(F4)
        centred = v - jnp.mean(v, axis=-1, keepdims=True)
        scale = lax.rsqrt(jnp.mean(centred * centred, axis=-1, keepdims=True) + EPS)
        xhat = centred * scale
        n = ng[s, at].astype(F4)
        g = n * gain
        along = jnp.mean(g * xhat, axis=-1, keepdims=True)

        @pl.when(i >= 2)
        def _():
            store(i - 2).wait()
        stage[i % 2] = cot[s, at].astype(F4) + (g - jnp.mean(g, axis=-1, keepdims=True) - xhat * along) * scale
        store(i).start()
        both = n * xhat
        sums[0] += both[:8] + both[8:16] + both[16:24] + both[24:]
        sums[1] += n[:8] + n[8:16] + n[16:24] + n[24:]

    store(6).wait()
    store(7).wait()


(
    START, NORM, SEND, PASS, HAVE, OPEN, CROSS, HOP, TWIN, PROJECT, ARRANGE, ATTEND, MIX, SLOPE, TURN, RETURN, PROJECTED, HIDDEN,
    PULL, FILL, CORE, LINE, SPREAD, RELAY, DONE, GIVE, KEEP, LAST, GRADIENTS,
) = range(29)
ORDER = (
    (START,), (SEND, 1, 1), (SEND, 0, 1), (SEND, 0, 3), (SEND, 0, 2), (PASS, 0, 1), (SEND, 1, 0), (NORM,), (OPEN, 0), (CROSS, 0),
    (SEND, 2, 3), (HOP, 0, 1, 0), (HOP, 0, 1, 1), (PASS, 0, 3), (SEND, 1, 3), (HOP, 0, 2, 0), (HOP, 0, 2, 1), (SEND, 0, 0),
    (HOP, 0, 3, 0), (HOP, 0, 3, 1), (TWIN, 0, 0), (TWIN, 0, 1), (SEND, 1, 2), (OPEN, 1), (PASS, 0, 2), (TWIN, 0, 3), (TWIN, 0, 2),
    (HAVE, 0), (SEND, 2, 1), (SEND, 2, 2), (SEND, 2, 0), (CROSS, 1), (PASS, 1, 1), (HOP, 1, 1, 0), (PASS, 1, 3), (PROJECT, 0),
    (PROJECT, 1), (PASS, 1, 2), (PROJECT, 2), (PROJECT, 3), (ARRANGE,), (ATTEND, 0), (ATTEND, 1), (ATTEND, 2), (ATTEND, 3),
    (HOP, 1, 1, 1), (ATTEND, 4), (HAVE, 3), (PASS, 2, 1), (HAVE, 1), (HIDDEN, 0), (ATTEND, 5), (PASS, 2, 3), (ATTEND, 6),
    (TWIN, 1, 0), (HOP, 1, 2, 0), (HIDDEN, 1), (HOP, 1, 2, 1), (TWIN, 1, 1), (PASS, 2, 2), (HIDDEN, 2), (ATTEND, 7), (MIX,),
    (HOP, 1, 3, 0), (HOP, 1, 3, 1), (HAVE, 2), (FILL, 1, 0), (FILL, 1, 1), (TWIN, 1, 2), (SLOPE, 0), (FILL, 1, 2), (CORE, 1, 0),
    (CORE, 1, 1), (HIDDEN, 3), (LINE, 1, 0, 1), (TWIN, 1, 3), (SLOPE, 1), (SLOPE, 2), (CORE, 1, 2), (SLOPE, 3), (TURN,), (RETURN, 0),
    (RETURN, 1), (LINE, 1, 0, 0), (RETURN, 2), (RETURN, 3), (RETURN, 4), (LINE, 1, 1, 1), (RETURN, 5), (RETURN, 6), (LINE, 1, 1, 0),
    (RETURN, 7), (PROJECTED,), (GIVE, 0, 1), (GIVE, 0, 2), (PULL, 0), (FILL, 0, 0), (LINE, 1, 2, 0), (GIVE, 0, 3), (FILL, 1, 3),
    (KEEP, 0, 1), (CORE, 0, 0), (CORE, 1, 3), (GIVE, 0, 0), (LINE, 1, 2, 1), (PULL, 1), (LINE, 0, 0, 1), (PULL, 2), (PULL, 3),
    (GIVE, 1, 1), (FILL, 0, 1), (FILL, 0, 2), (KEEP, 0, 2), (CORE, 0, 1), (FILL, 0, 3), (GIVE, 1, 2), (LINE, 0, 0, 0),
    (LINE, 1, 3, 1), (CORE, 0, 2), (KEEP, 1, 1), (GIVE, 1, 3), (LINE, 0, 1, 1), (KEEP, 0, 3), (CORE, 0, 3), (LINE, 0, 1, 0),
    (LINE, 0, 2, 1), (LINE, 0, 2, 0), (KEEP, 1, 3), (LINE, 0, 3, 1), (LINE, 1, 3, 0), (SPREAD, 1, 0), (LINE, 0, 3, 0), (KEEP, 1, 2),
    (SPREAD, 1, 1), (RELAY, 1, 0), (GIVE, 1, 0), (SPREAD, 0, 0), (SPREAD, 0, 1), (RELAY, 0, 0), (RELAY, 1, 1), (DONE, 1, 1),
    (DONE, 1, 0), (DONE, 0, 0), (LAST, 0), (RELAY, 0, 1), (KEEP, 1, 0), (DONE, 0, 1), (LAST, 1), (KEEP, 0, 0), (GRADIENTS,),
)


def block_kernel(pairs_of, gains, within, block, tok, cot, win, wout, wexp, wcon,
                 out, ig, vectors, gin, gout, gexp, gcon, xn, ct,
                 wx, wco, hp, am, S, ctr, ng, gs, gs_all, vec, vecs,
                 gsem_s, gsem_r, lsem, rsem, csem, ssem, vs, vr, *rest):
    z, x, y, k = place()
    c, q = z * 2 + x, 2 * y + k
    rest = list(rest)
    take = lambda n: [rest.pop(0) for _ in range(n)]
    nt, nb, ns = len(token_sems()), len(reduce_bufs()), len(reduce_sems())
    tx = TokenGather(xn, take(nt))
    tc = TokenGather(ct, take(nt))
    pairs = [
        (lambda zz, j=j: win.at[j, :, columns(128, zz)], lambda zz, xx, j=j: wx.at[zz, xx, :, pl.ds(512 + 128 * j, 128)])
        for j in range(3)
    ] + [
        (lambda zz: wexp.at[:, columns(512, zz)], lambda zz, xx: wx.at[zz, xx, :, pl.ds(0, 512)]),
        (lambda zz: wcon.at[columns(512, zz), :], lambda zz, xx: wco.at[pl.ds(0, 512), columns(256, zz * 2 + xx)]),
        (lambda zz: wout.at[columns(128, zz), :], lambda zz, xx: wco.at[pl.ds(512, 128), columns(256, zz * 2 + xx)]),
    ]
    wg = WeightGather(pairs, take(len(weight_sems(6))))
    tn = TokenReduce(ng, [S] + take(nb), take(ns))
    to = TokenReduce(out, [S] + take(nb), take(ns))
    whole = slice(None)
    g1 = GradReduce([((pl.ds(0, 512), whole), lambda zz: gcon.at[columns(512, zz), :]),
                     ((pl.ds(512, 128), whole), lambda zz: gout.at[columns(128, zz), :])], *take(2), take(4))
    g2 = GradReduce([((whole, pl.ds(0, 512)), lambda zz: gexp.at[:, columns(512, zz)])]
                    + [((whole, pl.ds(512 + 128 * j, 128)), lambda zz, j=j: gin.at[j, :, columns(128, zz)]) for j in range(3)],
                    *take(2), take(4))
    others, everyone = peers_of(z, x, y, k)

    def pair_at(slot):
        return pairs_of[x, slot]

    def slot_of(pair):
        found = jnp.int32(0)
        for j in range(8):
            found = jnp.where(pairs_of[x, j] == pair, j, found)
        return found


    V = pltpu.VMEM
    steps = {}
    flags = set()
    load_tok = lambda: pltpu.make_async_copy(tok, ctr.at[0], lsem.at[0])
    load_cot = lambda: pltpu.make_async_copy(cot, ctr.at[1], lsem.at[1])
    xl, xo, cl = ctr.at[1, 0], S.at[0, 0, 0], ctr.at[1, 1]
    near_cot = lambda: pltpu.make_async_copy(cot.at[x], cl, lsem.at[1])
    own_cot = lambda: pltpu.make_async_copy(cl, ct.at[z, x], lsem.at[2])
    own_xn = lambda: pltpu.make_async_copy(xl, xn.at[z, x], lsem.at[3])
    gcopies = lambda: [remote(gs, gs_all.at[c], gsem_s.at[i], gsem_r.at[i], others[i]) for i in range(7)]
    mine, cot_mine = xl.at[pl.ds(64 * q, 64)], cot.at[x, pl.ds(64 * q, 64)]
    cot_other = cot.at[1 - x, pl.ds(64 * q, 64)]

    def once(name, act):
        if name not in flags:
            flags.add(name)
            act()

    users = [n for n in ORDER if n[0] in (PROJECT, SLOPE, HIDDEN, PULL)]

    def rows_in(n, xx):
        kind, i = users[n]
        zz = far_first(z, i if kind in (HIDDEN, PULL) else 3 - i)
        src = xn if kind in (PROJECT, HIDDEN) else ct
        return zz, pltpu.make_async_copy(src.at[zz, xx], ctr.at[n % 2, xx], rsem.at[n % 2, xx])

    def begin_rows(n):
        flags.add(n)
        for xx in range(2):
            rows_in(n, xx)[1].start()

    def each_half(name, act):
        n = users.index(name)
        if n not in flags:
            begin_rows(n)
        for xx in range(2):
            zz, cp = rows_in(n, xx)
            cp.wait()
            act(zz, xx, ctr.at[n % 2, xx], pl.multiple_of(512 * zz + 256 * xx, 256))
        flags.add(name)
        for m in (n + 1, n + 2):
            if m < len(users) and m not in flags and {HIDDEN: (PROJECT, 3), PULL: (SLOPE, 3)}.get(users[m][0]) in flags:
                begin_rows(m)
        if n + 1 == len(users):
            load_tok().start()
            load_cot().start()

    def start():
        load_tok().start()
        gs[...] = jnp.zeros_like(gs)
        gs[0:2, :] = gains[...]
        meet(everyone)
        for g in gcopies():
            g.start()
        gs_all[c] = gs[...]
        near_cot().start()

    def norm():
        for i in range(7):
            frm = gs_all.at[(c - i - 1 + 8) % 8]
            remote(frm, frm, gsem_s.at[i], gsem_r.at[i], others[i]).wait_recv()
        gain = jnp.concatenate([gs_all[i, 0:1, :] for i in range(8)], axis=1)
        shift = jnp.concatenate([gs_all[i, 1:2, :] for i in range(8)], axis=1)
        load_tok().wait()

        @pl.loop(0, 2)
        def _(i):
            xo[pl.ds(32 * i, 32)] = norm_rows(ctr[0, 1 - x, pl.ds(64 * q + 32 * i, 32)], gain, shift)

        @pl.loop(0, 8)
        def _(i):
            xl[pl.ds(32 * i, 32)] = norm_rows(ctr[0, x, pl.ds(32 * i, 32)], gain, shift)

        own_xn().start()
        near_cot().wait()
        own_cot().start()

    steps[START,], steps[NORM,] = start, norm
    for u, ws in enumerate(((0, 1, 2, 5), (3,), (4,))):
        for d in range(4):
            steps[SEND, u, d] = functools.partial(wg.send, ws, d)
            steps[PASS, u, d] = functools.partial(wg.forward, ws, d)
    for u, ws in enumerate(((0, 1, 2), (3,), (4,), (5,))):
        steps[HAVE, u] = functools.partial(lambda ws: [wg.landed(w) for w in ws], ws)
    steps[OPEN, 0] = lambda: tx.start(mine, xo)
    steps[OPEN, 1] = lambda: tc.start(cot_mine, cot_other)
    for name, t in enumerate((tx, tc)):
        steps[CROSS, name] = t.after_x
        for d in range(4):
            steps[TWIN, name, d] = functools.partial(t.y_hop, d)
            for s in range(2):
                steps[HOP, name, d, s] = functools.partial(t.hop, d, s)

    def hidden(zz, xx, rows, row):
        at = pl.ds(row, 256)
        u = dot(rows[...], wx[:, :, :, pl.ds(0, 512)].reshape(2048, 512))
        square = u * u
        t = jnp.tanh(0.7978845608028654 * (u + 0.044715 * u * square))
        half = 0.5 * (1.0 + t)
        am[at, pl.ds(0, 512)] = (u * half).astype(BF)
        hp[at, pl.ds(0, 512)] = (half + 0.5 * u * (1.0 - t * t) * (0.7978845608028654 * (1.0 + 3 * 0.044715 * square))).astype(BF)

    def pull(zz, xx, rows, row):
        at = (pl.ds(row, 256), pl.ds(0, 512))
        hp[at] = (dot_t(rows[...], wco[pl.ds(0, 512)]) * hp[at].astype(F4)).astype(BF)

    for i in range(4):
        steps[HIDDEN, i] = functools.partial(each_half, (HIDDEN, i), hidden)
        steps[PULL, i] = functools.partial(each_half, (PULL, i), pull)

    def piece(ref):
        return lambda zz, xx, r: ref[pl.ds(pl.multiple_of(512 * zz + 256 * xx + r, 64), 64)]

    of = ((piece(hp), lambda a, j: dot_t(a, wx[j].reshape(512, 896))), (piece(am), lambda a, j: dot(a, wco[:, columns(512, j)])))
    filled = []

    def fill(name, t, i):
        if len(filled) >= 2:
            sent(filled[-2])
        filled.append((t, i))
        t.fill(i, (len(filled) - 1) % 2, *of[name])

    def sent(one):
        one[0].core(one[1]).wait_send()

    def to_base(seq, rows):
        once(load_tok, lambda: load_tok().wait())
        return ctr.at[0, seq, rows]

    for name, t in enumerate((tn, to)):
        for i in range(4):
            steps[FILL, name, i] = functools.partial(fill, name, t, i)
            steps[CORE, name, i] = functools.partial(t.after_core, i, *of[name])
            for s in range(2):
                steps[LINE, name, i, s] = functools.partial(t.line, i, s)
        for s in range(2):
            steps[SPREAD, name, s] = functools.partial(t.spread, s, to_base if t is to else None)
            steps[RELAY, name, s] = functools.partial(t.spread_y, s)
            steps[DONE, name, s] = functools.partial(t.landed, s)

    def by_block(zz, xx, half):
        p = pair_at(2 * zz + xx)
        return [pick(p, lambda j: block[i, pl.ds(j if half == 0 else 15 - j, 1)]) for i in range(2)]

    cut = ORDER.index((PROJECTED,)) + 1

    def attention(ps, qkv, qt, kt, vt, gt, ot, logs, gpos, dqt, dk, dv):
        def project(zz, xx, rows, row):
            three = dot(rows[...], wx[:, :, :, pl.ds(512, 384)].reshape(2048, 384))
            for half in range(2):
                v = three[128 * half:128 * half + 128]
                t = angle_table(within, *by_block(zz, xx, half))
                at = pl.ds(row + 128 * half, 128)
                ps[at, pl.ds(0, 128)] = turn(v[:, 0:128], t).astype(BF) * BF(0.125)
                ps[at, pl.ds(128, 128)] = turn(v[:, 128:256], t).astype(BF)
                ps[at, pl.ds(256, 128)] = v[:, 256:384].astype(BF)

        def slope(zz, xx, rows, row):
            ps[pl.ds(row, 256), pl.ds(0, 128)] = dot_t(rows[...], wco[pl.ds(512, 128)]).astype(BF)

        def landed(i, kind, t, act):
            once(own_rows, own_rows)
            t.landed(far_first(z, 3 - i))
            each_half((kind, i), act)

        def own_rows():
            own_xn().wait()
            own_cot().wait()
            tx.sent_own(mine, xo)

        for i in range(4):
            steps[PROJECT, i] = functools.partial(landed, i, PROJECT, tx, project)
            steps[SLOPE, i] = functools.partial(landed, i, SLOPE, tc, slope)

        def by_position(b, cols):
            half = b // 8
            pair = b + half * (15 - 2 * b)
            return pick(slot_of(pair), lambda j: ps[pl.ds(pl.multiple_of(256 * j + 128 * half, 128), 128), cols].astype(F4))

        def by_rows(c2, half):
            p = pair_at(c2)
            return lambda ref: pick(p, lambda j: ref[pl.ds(128 * (j if half == 0 else 15 - j), 128)])

        def blocks(act):
            @pl.loop(0, 16)
            def _(b):
                act(b, pl.ds(pl.multiple_of(b * 128, 128), 128))

        def slots(act):
            for half in range(2):
                @pl.loop(0, 8)
                def _(c2):
                    act(by_rows(c2, half), pl.ds(pl.multiple_of(256 * c2 + 128 * half, 128), 128))

        def rope():
            def act(b, here):
                three = by_position(b, slice(None))
                for j, ref in enumerate((qt, kt, vt)):
                    v = three[:, 128 * j:128 * j + 128]
                    qkv[j, here] = v.astype(BF)
                    ref[:, here] = v.T.astype(BF)
            blocks(act)

        def score(i, h):
            kr = 256 * (i + 1)
            return masked(dot(qkv[1, :kr], one_head(qt[:, pl.ds(256 * i, 256)], h, 0)), kr)

        ahead = []

        def forward(i):
            kr, here = 256 * (i + 1), pl.ds(256 * i, 256)
            for h in range(2):
                st = ahead.pop() if ahead else score(0, 0)
                if (i, h) != (7, 1):
                    ahead.append(score(i + h, 1 - h))
                peak = jnp.max(st, axis=0, keepdims=True)
                p = jnp.exp(st - peak)
                total = jnp.sum(p, axis=0, keepdims=True)
                o = dot(vt[:, :kr], p.astype(BF)) * (1.0 / total)
                ot[pl.ds(64 * h, 64), here] = o[64 * h:64 * h + 64]
                logs[pl.ds(h, 1), here] = peak + jnp.log(total)

        def mix():
            def turned(b, here):
                gpos[here] = ot[:, here].T

            def placed(pos, row):
                am[row, pl.ds(512, 128)] = pos(gpos).astype(BF)
            blocks(turned)
            slots(placed)

        def gflip():
            def act(b, here):
                g = by_position(b, pl.ds(0, 128))
                gpos[here] = g
                gt[:, here] = g.T.astype(BF)
            blocks(act)
            dk[...] = jnp.zeros_like(dk)
            dv[...] = jnp.zeros_like(dv)

        def backward(i):
            kr, here = 256 * (i + 1), pl.ds(256 * i, 256)
            for h in range(2):
                p = jnp.exp(score(i, h) - logs[pl.ds(h, 1), here])
                low = p.astype(BF)
                at = pl.ds(64 * h, 64)
                delta = jnp.sum(ot[at, here] * gt[at, here].astype(F4), axis=0, keepdims=True)
                ds = (p * (dot(qkv[2, :kr], one_head(gt[:, here], h, 0)) - delta)).astype(BF)
                dv[:kr] += dot(low, one_head(gpos[here].astype(BF), h, 1))
                dk[:kr] += dot(ds, one_head(qkv[0, here], h, 1))
                dqt[at, here] = dot(kt[:, :kr], ds)[64 * h:64 * h + 64] * 0.125

        def gradients():
            def turned(b, here):
                t = angle_table(within, block[0, pl.ds(b, 1)], block[1, pl.ds(b, 1)])
                gpos[here] = turn_back(dqt[:, here].T, t)
                dk[here] = turn_back(dk[here], t)

            def placed(pos, row):
                for j, ref in enumerate((gpos, dk, dv)):
                    hp[row, pl.ds(512 + 128 * j, 128)] = pos(ref).astype(BF)
            blocks(turned)
            slots(placed)

        steps[ARRANGE,], steps[MIX,], steps[TURN,], steps[PROJECTED,] = rope, mix, gflip, gradients
        for i in range(8):
            steps[ATTEND, i] = functools.partial(forward, i)
            steps[RETURN, i] = functools.partial(backward, i)
        for name in ORDER[:cut]:
            steps[name]()

    pl.run_scoped(
        attention, V((2048, 384), BF), V((3, 2048, 128), BF), V((128, 2048), BF), V((128, 2048), BF), V((128, 2048), BF),
        V((128, 2048), BF), V((128, 2048), F4), V((8, 2048), F4), V((2048, 128), F4), V((128, 2048), F4),
        V((2048, 128), F4), V((2048, 128), F4))

    def rest_of(col, stage, sums):
        plan = [n for n in ORDER if n[0] in (GIVE, KEEP)]

        def block_load(n):
            kind, j, e = plan[n]
            src, d, xx = (ct, xn)[j], mirrored(z, e), 1 - x if kind == GIVE else x
            return pltpu.make_async_copy(src.at[:, :, :, columns(256, 2 * ((z + d) % 4) + xx)], col.at[n % 3], csem.at[n % 3])

        def grad(n):
            kind, j, e = plan[n]
            block_load(n).wait()
            terms = dot(flip(col[n % 3].reshape(2048, 256)), (am, hp)[j][...])
            g = (g1, g2)[j]
            (g.give if kind == GIVE else g.keep)(e, terms if j else terms.T)
            if n + 3 < len(plan):
                block_load(n + 3).start()

        for n in range(3):
            block_load(n).start()
        copies = [remote(vec.at[(c + i + 1) % 8], vecs.at[c], vs.at[i], vr.at[i], others[i]) for i in range(7)]

        def normed_gradient(s):
            once(load_tok, lambda: load_tok().wait())
            once(load_cot, lambda: load_cot().wait())
            if s == 0:
                sums[...] = jnp.zeros_like(sums)
            norm_backward(x if s == 0 else 1 - x, ctr.at[0], ctr.at[1], ng, gs_all, ig, stage, ssem, sums)
            if s == 0:
                return
            for i in range(8):
                at = slice(256 * i, 256 * i + 256)
                for j in range(2):
                    vec[i, j:j + 1, :] = jnp.sum(sums[j, :, at], axis=0, keepdims=True)
                vec[i, 2:8, :] = jnp.zeros((6, 256), F4)
            vecs[c] = vec[c]
            for cp in copies:
                cp.start()

        def gradients():
            g1.finish()
            g2.finish()

        steps[GRADIENTS,] = gradients
        for s in range(2):
            steps[LAST, s] = functools.partial(normed_gradient, s)
        for n, name in enumerate(plan):
            steps[name] = functools.partial(grad, n)
        for name in ORDER[cut:]:
            steps[name]()
        for i in range(7):
            frm = vecs.at[(c - i - 1 + 8) % 8]
            remote(frm, frm, vs.at[i], vr.at[i], others[i]).wait_recv()
        total = vecs[0]
        for i in range(1, 8):
            total = total + vecs[i]
        vectors[...] = total
        for cp in copies:
            cp.wait_send()

    pl.run_scoped(rest_of, V((3, 4, 2, 256, 256), BF), V((2, 32, 2048), F4), V((2, 8, 2048), F4))
    for one in filled[-2:]:
        sent(one)
    tn.finish()
    to.finish()
    tx.finish()
    tc.sent_own(cot_mine, cot_other)
    tc.finish()
    for w in range(6):
        wg.finish(w)
    for g in gcopies():
        g.wait_send()


def block_call(pairs_of, gains, tok, cot, win, wout, wexp, wcon):
    S = jax.ShapeDtypeStruct
    ANY = pl.BlockSpec(memory_space=pl.ANY)
    VM = pl.BlockSpec(memory_space=pltpu.VMEM)
    D = pltpu.SemaphoreType.DMA
    V = pltpu.VMEM
    rows = (4, 2, 256, 2048)
    return pl.pallas_call(
        block_kernel,
        out_shape=[S((2, 256, 2048), BF), S((2, 256, 2048), F4), S((8, 256), F4),
                   S((3, 256, 512), BF), S((512, 256), BF), S((256, 2048), BF), S((2048, 256), BF), S(rows, BF), S(rows, BF)],
        in_specs=[pl.BlockSpec(memory_space=pltpu.SMEM)] + [VM] * 3 + [ANY] * 6,
        out_specs=[ANY, ANY, VM] + [ANY] * 6,
        scratch_shapes=[V((4, 2, 256, 896), BF), V((640, 2048), BF), V((2048, 896), BF), V((2048, 640), BF), V((2, 2, 2, 64, 2048), BF),
                        V((2, 2, 256, 2048), BF), V((2, 256, 2048), BF), V((8, 256), F4), V((8, 8, 256), F4), V((8, 8, 256), F4), V((8, 8, 256), F4),
                        D((7,)), D((7,)), D((4,)), D((2, 2)), D((3,)), D((2,)), D((7,)), D((7,))]
        + token_sems() * 2 + weight_sems(6) + (reduce_bufs() + reduce_sems()) * 2 + grad_scratch((640, 256), 2) + grad_scratch((256, 896), 4),
        compiler_params=pltpu.CompilerParams(collective_id=0, has_side_effects=True, vmem_limit_bytes=63 * MB),
        name="block",
    )(pairs_of, gains, jnp.asarray(angles(128, 1)), jnp.asarray(angles(16, 128)), tok, cot, win, wout, wexp, wcon)


def finish_kernel(out, ig, gin, gout, gexp, gcon, out_to, ig_to, gin_to, gout_to, gexp_to, gcon_to,
                  vin, vout, vexp, vcon, fin, fout, fexp, fcon, through, wide, isem, osem):
    work = ((gexp, vexp, fexp, gexp_to), (gcon, vcon, fcon, gcon_to), (gin, vin, fin, gin_to), (gout, vout, fout, gout_to),
            (ig, wide, wide, ig_to), (out, through, through, out_to))
    loads = [pltpu.make_async_copy(w[0], w[1], isem.at[i]) for i, w in enumerate(work)]
    stores = [pltpu.make_async_copy(w[2], w[3], osem.at[i]) for i, w in enumerate(work)]
    for copy in loads:
        copy.start()
    for (_, low, full, _), load, store in zip(work, loads, stores):
        load.wait()
        if low is not full:
            rows = low.shape[-2]
            for j in range(low.shape[0] if len(low.shape) == 3 else 1):
                @pl.loop(0, rows // 128)
                def _(i):
                    at = (pl.ds(pl.multiple_of(128 * i, 128), 128),)
                    at = (j,) + at if len(low.shape) == 3 else at
                    full[at] = low[at].astype(F4)
        store.start()
    for copy in stores:
        copy.wait()


def finish_call(out, ig, *grads):
    S = jax.ShapeDtypeStruct
    ANY = pl.BlockSpec(memory_space=pl.ANY)
    D = pltpu.SemaphoreType.DMA
    V = pltpu.VMEM
    shapes = [g.shape for g in grads]
    return pl.pallas_call(
        finish_kernel,
        out_shape=[S(out.shape, BF), S(ig.shape, F4)] + [S(s, F4) for s in shapes],
        in_specs=[ANY] * 6,
        out_specs=[ANY] * 6,
        scratch_shapes=[V(s, BF) for s in shapes] + [V(s, F4) for s in shapes] + [V(out.shape, BF), V(ig.shape, F4), D((6,)), D((6,))],
        compiler_params=pltpu.CompilerParams(vmem_limit_bytes=60 * MB),
        name="finish",
    )(out, ig, *grads)


def own_local(tokens, pair_index, norm_gain, norm_shift, w_attention_in, w_attention_out, w_expand, w_contract, cotangent):
    gains = jnp.stack([norm_gain, norm_shift]).astype(F4)
    output, input_grad, vectors, *grads = block_call(
        pair_index, gains, tokens, cotangent, w_attention_in, w_attention_out, w_expand, w_contract)
    output, input_grad, *grads = finish_call(output, input_grad, *grads[:4])
    return (output, input_grad, vectors[0], vectors[1], *grads)


def local(tokens, pair_index, norm_gain, norm_shift, w_attention_in, w_attention_out, w_expand, w_contract, cotangent):
    args = (tokens, pair_index, norm_gain, norm_shift, w_attention_in, w_attention_out, w_expand, w_contract, cotangent)
    sizes = (lax.axis_size("ctx"), lax.axis_size("tp")) + tokens.shape + w_attention_in.shape[2:] + w_expand.shape[1:]
    if sizes == (8, 4, 2, 256, 2048, 512, 2048):
        return own_local(*args)
    return general_local(*args)


def solution(mesh):
    in_specs = (
        P(None, "ctx", None),
        P(),
        P("ctx"),
        P("ctx"),
        P(None, "ctx", "tp"),
        P("tp", "ctx"),
        P("ctx", "tp"),
        P("tp", "ctx"),
        P(None, "ctx", None),
    )
    out_specs = (
        P(None, "ctx", None),
        P(None, "ctx", None),
        P("ctx"),
        P("ctx"),
        P(None, "ctx", "tp"),
        P("tp", "ctx"),
        P("ctx", "tp"),
        P("tp", "ctx"),
    )
    return jax.shard_map(local, mesh=mesh, in_specs=in_specs, out_specs=out_specs, check_vma=False)
```

```python
import functools
import itertools

import jax
import jax.numpy as jnp
import numpy as np
from jax import lax
from jax.experimental import pallas as pl
from jax.experimental.pallas import tpu as pltpu
from jax.sharding import PartitionSpec as P

HEAD_DIM = 64
ROT = 32


epsilon = 1e-05


def position_table(pair_index, shard_rows):
    pair_count = pair_index.shape[1]
    half_rows = shard_rows // 2
    token_index = jnp.arange(shard_rows * pair_count, dtype=jnp.int32)
    owning = token_index // shard_rows
    within = token_index % shard_rows
    picked = (owning[:, None] == jnp.arange(pair_count, dtype=jnp.int32)[None, :]).astype(jnp.int32)
    chosen = jnp.sum(picked[None, :, :] * pair_index[:, None, :], axis=2)
    first_half = chosen * half_rows + within[None, :]
    second = (2 * pair_count - 1 - chosen) * half_rows + within[None, :] - half_rows
    return jnp.where(within[None, :] < half_rows, first_half, second)


def rotate(tensor, positions):
    half_rot = ROT // 2
    frequency = 10000.0 ** (-2.0 * jnp.arange(half_rot, dtype=jnp.float32) / ROT)
    angles = positions.astype(jnp.float32)[..., None] * frequency
    cosine = jnp.cos(angles)[..., None, :]
    sine_part = jnp.sin(angles)[..., None, :]
    leading = tensor[..., :half_rot]
    trailing = tensor[..., half_rot:ROT]
    return jnp.concatenate(
        [
            leading * cosine - trailing * sine_part,
            trailing * cosine + leading * sine_part,
            tensor[..., ROT:],
        ],
        axis=-1,
    )


def gelu_tanh(values_in):
    return (
        0.5
        * values_in
        * (
            1.0
            + jnp.tanh(
                0.7978845608028654 * (values_in + 0.044715 * values_in * values_in * values_in)
            )
        )
    )


def layer_norm(inputs, gain_full, shift_full):
    centred = inputs - jnp.mean(inputs, axis=-1, keepdims=True)
    spread = jnp.mean(centred * centred, axis=-1, keepdims=True)
    return centred * lax.rsqrt(spread + epsilon) * gain_full + shift_full


def block_probs(queries, keys_block, log_total, query_pos, key_pos):
    raw_scores = jnp.einsum(
        "sqhe,skhe->shqk", queries, keys_block, preferred_element_type=jnp.float32
    )
    allowed = key_pos[:, None, None, :] <= query_pos[:, None, :, None]
    return jnp.where(allowed, jnp.exp(raw_scores * HEAD_DIM ** (-0.5) - log_total[..., None]), 0.0)


def score_grads(
    queries, keys_block, values_block, log_total, row_delta, out_grad, query_pos, key_pos
):
    probs_full = block_probs(queries, keys_block, log_total, query_pos, key_pos)
    prob_grad = jnp.einsum(
        "sqhe,skhe->shqk", out_grad, values_block, preferred_element_type=jnp.float32
    )
    score_grad = (probs_full * (prob_grad - row_delta[..., None]) * HEAD_DIM ** (-0.5)).astype(
        jnp.bfloat16
    )
    return (probs_full.astype(jnp.bfloat16), score_grad)


def key_slice(keys_all, offset, key_rows, head_count):
    seq_count = keys_all.shape[0]
    return lax.dynamic_slice_in_dim(keys_all, offset, key_rows, 1).reshape(
        seq_count, key_rows, head_count, HEAD_DIM
    )


def log_totals(queries, keys_all, query_pos, pos_table, key_rows):
    seq_count, query_rows, head_count, head_size = queries.shape
    turn_count = keys_all.shape[1] // key_rows

    def log_one_turn(turn_index, state_in):
        running_max, running_sum = state_in
        offset = turn_index * key_rows
        keys_block = key_slice(keys_all, offset, key_rows, head_count)
        key_pos = lax.dynamic_slice_in_dim(pos_table, offset, key_rows, 1)
        raw_scores = jnp.einsum(
            "sqhe,skhe->shqk", queries, keys_block, preferred_element_type=jnp.float32
        ) * HEAD_DIM ** (-0.5)
        allowed = key_pos[:, None, None, :] <= query_pos[:, None, :, None]
        masked = jnp.where(allowed, raw_scores, -1e30)
        new_max = jnp.maximum(running_max, jnp.max(masked, axis=-1))
        kept_terms = jnp.where(allowed, jnp.exp(masked - new_max[..., None]), 0.0)
        return (
            new_max,
            running_sum * jnp.exp(running_max - new_max) + jnp.sum(kept_terms, axis=-1),
        )

    initial = (
        jnp.full((seq_count, head_count, query_rows), -1e30, jnp.float32),
        jnp.zeros((seq_count, head_count, query_rows), jnp.float32),
    )
    final_max, final_sum = lax.fori_loop(0, turn_count, log_one_turn, initial)
    return final_max + jnp.log(final_sum)


def attend_values(queries, keys_all, values_all, log_total, query_pos, pos_table, key_rows):
    head_count = queries.shape[2]
    turn_count = keys_all.shape[1] // key_rows

    def attend_one_turn(turn_index, running):
        offset = turn_index * key_rows
        keys_block = key_slice(keys_all, offset, key_rows, head_count)
        values_block = key_slice(values_all, offset, key_rows, head_count)
        key_pos = lax.dynamic_slice_in_dim(pos_table, offset, key_rows, 1)
        weights_low = block_probs(queries, keys_block, log_total, query_pos, key_pos).astype(
            jnp.bfloat16
        )
        return running + jnp.einsum(
            "shqk,skhe->sqhe", weights_low, values_block, preferred_element_type=jnp.float32
        )

    return lax.fori_loop(0, turn_count, attend_one_turn, jnp.zeros(queries.shape, jnp.float32))


def full_grads(
    queries, keys_all, values_all, log_total, row_delta, out_grad, query_pos, pos_table, key_rows
):
    seq_count, query_rows, head_count, head_size = queries.shape
    turn_count = keys_all.shape[1] // key_rows

    def full_one_turn(turn_index, state_in):
        query_grad, key_terms, value_terms = state_in
        offset = turn_index * key_rows
        keys_block = key_slice(keys_all, offset, key_rows, head_count)
        values_block = key_slice(values_all, offset, key_rows, head_count)
        key_pos = lax.dynamic_slice_in_dim(pos_table, offset, key_rows, 1)
        weights_low, score_grad = score_grads(
            queries, keys_block, values_block, log_total, row_delta, out_grad, query_pos, key_pos
        )
        query_grad = query_grad + jnp.einsum(
            "shqk,skhe->sqhe", score_grad, keys_block, preferred_element_type=jnp.float32
        )
        key_part = jnp.einsum(
            "shqk,sqhe->skhe", score_grad, queries, preferred_element_type=jnp.float32
        ).reshape(seq_count, key_rows, head_count * head_size)
        value_part = jnp.einsum(
            "shqk,sqhe->skhe", weights_low, out_grad, preferred_element_type=jnp.float32
        ).reshape(seq_count, key_rows, head_count * head_size)
        key_terms = lax.dynamic_update_slice_in_dim(key_terms, key_part, offset, 1)
        value_terms = lax.dynamic_update_slice_in_dim(value_terms, value_part, offset, 1)
        return (query_grad, key_terms, value_terms)

    initial = (
        jnp.zeros(queries.shape, jnp.float32),
        jnp.zeros(keys_all.shape, jnp.float32),
        jnp.zeros(values_all.shape, jnp.float32),
    )
    return lax.fori_loop(0, turn_count, full_one_turn, initial)


def general_local(
    tokens,
    pair_index,
    norm_gain,
    norm_shift,
    w_attention_in,
    w_attention_out,
    w_expand,
    w_contract,
    cotangent,
):
    seq_count, shard_rows, model_width = tokens.shape
    gain_full, shift_full, attention_in, attention_out, expand_full, contract_full = (
        lax.all_gather(norm_gain, "ctx", axis=0, tiled=True),
        lax.all_gather(norm_shift, "ctx", axis=0, tiled=True),
        lax.all_gather(w_attention_in, "ctx", axis=1, tiled=True),
        lax.all_gather(w_attention_out, "ctx", axis=1, tiled=True),
        lax.all_gather(w_expand, "ctx", axis=0, tiled=True),
        lax.all_gather(w_contract, "ctx", axis=1, tiled=True),
    )
    local_width = attention_in.shape[2]
    head_count = local_width // HEAD_DIM
    flat_rows = seq_count * shard_rows
    pos_table = position_table(pair_index, shard_rows)
    total_rows = pos_table.shape[1]
    own_pos = lax.dynamic_slice_in_dim(pos_table, lax.axis_index("ctx") * shard_rows, shard_rows, 1)
    key_rows = min(total_rows, 1024)
    inputs = tokens.astype(jnp.float32)
    normed_full, norm_pull = jax.vjp(
        layer_norm, inputs, gain_full.astype(jnp.float32), shift_full.astype(jnp.float32)
    )
    normed = normed_full.astype(jnp.bfloat16).reshape(flat_rows, model_width)
    projected = jnp.einsum("td,kde->kte", normed, attention_in, preferred_element_type=jnp.float32)
    split_heads = projected.reshape(3, seq_count, shard_rows, head_count, HEAD_DIM)
    rotated, rotate_pull = jax.vjp(lambda pair_part: rotate(pair_part, own_pos), split_heads[:2])
    queries = rotated[0].astype(jnp.bfloat16)
    own_keys = rotated[1].astype(jnp.bfloat16)
    own_values = split_heads[2].astype(jnp.bfloat16)
    keys_all, values_all = (
        lax.all_gather(
            own_keys.reshape(seq_count, shard_rows, local_width), "ctx", axis=1, tiled=True
        ),
        lax.all_gather(
            own_values.reshape(seq_count, shard_rows, local_width), "ctx", axis=1, tiled=True
        ),
    )
    log_total = log_totals(queries, keys_all, own_pos, pos_table, key_rows)
    attended = attend_values(queries, keys_all, values_all, log_total, own_pos, pos_table, key_rows)
    mixed = attended.reshape(flat_rows, local_width).astype(jnp.bfloat16)
    hidden_pre = jnp.dot(normed, expand_full, preferred_element_type=jnp.float32)
    activated_full, gelu_pull = jax.vjp(gelu_tanh, hidden_pre)
    activated = activated_full.astype(jnp.bfloat16)
    branch = jnp.dot(mixed, attention_out, preferred_element_type=jnp.float32) + jnp.dot(
        activated, contract_full, preferred_element_type=jnp.float32
    )
    branch = lax.psum(branch.astype(jnp.bfloat16), "tp").astype(jnp.float32)
    output = (inputs + branch.reshape(seq_count, shard_rows, model_width)).astype(jnp.bfloat16)
    upstream = cotangent.reshape(flat_rows, model_width)
    contract_grad = jnp.einsum("tf,td->fd", activated, upstream, preferred_element_type=jnp.float32)
    (gelu_grad,) = gelu_pull(
        jnp.einsum("td,fd->tf", upstream, contract_full, preferred_element_type=jnp.float32)
    )
    hidden_grad = gelu_grad.astype(jnp.bfloat16)
    expand_grad = jnp.einsum("td,tf->df", normed, hidden_grad, preferred_element_type=jnp.float32)
    mixed_grad = jnp.einsum(
        "td,ed->te", upstream, attention_out, preferred_element_type=jnp.float32
    ).astype(jnp.bfloat16)
    attention_out_grad = jnp.einsum(
        "te,td->ed", mixed, upstream, preferred_element_type=jnp.float32
    )
    out_grad = mixed_grad.reshape(seq_count, shard_rows, head_count, HEAD_DIM)
    row_delta = jnp.sum(out_grad.astype(jnp.float32) * attended, axis=-1).transpose(0, 2, 1)
    query_grad, key_terms, value_terms = full_grads(
        queries, keys_all, values_all, log_total, row_delta, out_grad, own_pos, pos_table, key_rows
    )
    key_grad, value_grad = (
        lax.psum_scatter(
            key_terms.astype(jnp.bfloat16), "ctx", scatter_dimension=1, tiled=True
        ).astype(jnp.float32),
        lax.psum_scatter(
            value_terms.astype(jnp.bfloat16), "ctx", scatter_dimension=1, tiled=True
        ).astype(jnp.float32),
    )
    key_grad = key_grad.reshape(seq_count, shard_rows, head_count, HEAD_DIM)
    value_grad = value_grad.reshape(seq_count, shard_rows, head_count, HEAD_DIM)
    (rotated_grad,) = rotate_pull(jnp.stack([query_grad, key_grad]))
    projected_grad = (
        jnp.concatenate([rotated_grad, value_grad[None]], axis=0)
        .reshape(3, flat_rows, local_width)
        .astype(jnp.bfloat16)
    )
    attention_in_grad = jnp.einsum(
        "td,kte->kde", normed, projected_grad, preferred_element_type=jnp.float32
    )
    normed_grad = jnp.einsum(
        "kte,kde->td", projected_grad, attention_in, preferred_element_type=jnp.float32
    )
    normed_grad = normed_grad + jnp.einsum(
        "tf,df->td", hidden_grad, expand_full, preferred_element_type=jnp.float32
    )
    normed_grad = lax.psum(normed_grad.astype(jnp.bfloat16), "tp").astype(jnp.float32)
    input_part, gain_grad, shift_grad = norm_pull(
        normed_grad.reshape(seq_count, shard_rows, model_width)
    )
    input_grad = input_part + cotangent.astype(jnp.float32)
    reduced = (
        lax.psum_scatter(
            gain_grad.astype(jnp.bfloat16), "ctx", scatter_dimension=0, tiled=True
        ).astype(jnp.float32),
        lax.psum_scatter(
            shift_grad.astype(jnp.bfloat16), "ctx", scatter_dimension=0, tiled=True
        ).astype(jnp.float32),
        lax.psum_scatter(
            attention_in_grad.astype(jnp.bfloat16), "ctx", scatter_dimension=1, tiled=True
        ).astype(jnp.float32),
        lax.psum_scatter(
            attention_out_grad.astype(jnp.bfloat16), "ctx", scatter_dimension=1, tiled=True
        ).astype(jnp.float32),
        lax.psum_scatter(
            expand_grad.astype(jnp.bfloat16), "ctx", scatter_dimension=0, tiled=True
        ).astype(jnp.float32),
        lax.psum_scatter(
            contract_grad.astype(jnp.bfloat16), "ctx", scatter_dimension=1, tiled=True
        ).astype(jnp.float32),
    )
    return (
        output,
        input_grad,
        reduced[0],
        reduced[1],
        reduced[2],
        reduced[3],
        reduced[4],
        reduced[5],
    )


MESH = pl.DeviceIdType.MESH
MB = 1 << 20
EPS = 1e-05
BF = jnp.bfloat16
F4 = jnp.float32
NT = (((1,), (1,)), ((), ()))
FAR = (1, 2, 3, 0)


def place():
    c = lax.axis_index("ctx")
    t = lax.axis_index("tp")
    return c // 2, c % 2, t // 2, t % 2


def device(z, x, y, k):
    return (z * 2 + x, y * 2 + k)


def remote(src, dst, send_sem, recv_sem, target):
    return pltpu.make_async_remote_copy(
        src_ref=src, dst_ref=dst, send_sem=send_sem, recv_sem=recv_sem,
        device_id=target, device_id_type=MESH,
    )


def meet(peers):
    barrier = pltpu.get_barrier_semaphore()
    for peer in peers:
        pl.semaphore_signal(barrier, inc=1, device_id=peer, device_id_type=MESH)
    pl.semaphore_wait(barrier, len(peers))


def peers_of(z, x, y, k):
    c = z * 2 + x
    others = [((c + i) % 8, lax.axis_index("tp")) for i in range(1, 8)]
    return others, others + [device(z, x, 1 - y, k), device(z, x, y, 1 - k)]


def columns(n, i):
    return pl.ds(pl.multiple_of(n * i, n), n)


def dot(a, b):
    return jnp.dot(a, b, preferred_element_type=F4)


def dot_t(a, b):
    return lax.dot_general(a, b, NT, preferred_element_type=F4)


def mirrored(z, e):
    return jnp.where(z < 2, 4 - e, e) if e in (1, 3) else e


def far_first(z, i):
    return (3 * (1 - z // 2), z // 2 + 2 * (1 - z % 2), 1 + z % 2, z)[i]


def add_into(dst, src):
    lead, rows = dst.shape[:-2], dst.shape[-2]
    for idx in itertools.product(*(range(n) for n in lead)):
        @pl.loop(0, rows // 16)
        def _(i):
            at = idx + (pl.ds(pl.multiple_of(16 * i, 16), 16), slice(None))
            dst[at] = (dst[at].astype(F4) + src[at].astype(F4)).astype(BF)


class TokenGather:
    def __init__(self, whole, sems):
        self.whole = whole
        self.xs, self.xr, self.zs, self.zr, self.ys, self.yr, self.cs, self.cr = sems
        self.z, self.x, self.y, self.k = place()
        self.q = 2 * self.y + self.k

    def chunk(self, zz, s, q):
        xx = self.x if s == 0 else 1 - self.x
        return self.whole.at[zz, xx, pl.ds(64 * q, 64), :]

    def send_x(self, src):
        z, x, y, k = self.z, self.x, self.y, self.k
        return remote(src, self.whole.at[z, x, pl.ds(64 * self.q, 64), :], self.xs, self.xr, device(z, 1 - x, y, k))

    def send_up(self, zz, s, src):
        return remote(src, self.chunk(zz, s, self.q), self.zs.at[zz, s, 0], self.zr.at[zz, s],
                      device(jnp.minimum(self.z + 1, 3), self.x, self.y, self.k))

    def send_down(self, zz, s, src):
        return remote(src, self.chunk(zz, s, self.q), self.zs.at[zz, s, 1], self.zr.at[zz, s],
                      device(jnp.maximum(self.z - 1, 0), self.x, self.y, self.k))

    def send_y(self, zz, s):
        c = self.chunk(zz, s, self.q)
        return remote(c, c, self.ys.at[zz, s], self.yr.at[zz, s], device(self.z, self.x, 1 - self.y, self.k))

    def send_core(self, zz, s, j):
        yy = self.y if j == 0 else 1 - self.y
        c = self.chunk(zz, s, 2 * yy + self.k)
        return remote(c, c, self.cs.at[zz, s, j], self.cr.at[zz, s, j], device(self.z, self.x, self.y, 1 - self.k))

    def both_ways(self, s, src):
        z = self.z

        @pl.when(z < 3)
        def _():
            self.send_up(z, s, src).start()

        @pl.when(z > 0)
        def _():
            self.send_down(z, s, src).start()

    def start(self, own_quarter, other_quarter):
        self.send_x(other_quarter).start()
        self.both_ways(0, own_quarter)

    def after_x(self):
        c = self.chunk(self.z, 1, self.q)
        remote(c, c, self.xs, self.xr, device(self.z, 1 - self.x, self.y, self.k)).wait_recv()
        self.both_ways(1, c)
        self.send_y(self.z, 1).start()
        self.send_core(self.z, 1, 0).start()

    def hop(self, d, s):
        z = self.z

        @pl.when(z >= d)
        def _():
            zz = z - d
            c = self.chunk(zz, s, self.q)
            self.send_down(zz, s, c).wait_recv()

            @pl.when(z < 3)
            def _():
                self.send_up(zz, s, c).start()

            self.send_y(zz, s).start()
            self.send_core(zz, s, 0).start()

        @pl.when(z + d <= 3)
        def _():
            zz = z + d
            c = self.chunk(zz, s, self.q)
            self.send_up(zz, s, c).wait_recv()

            @pl.when(z > 0)
            def _():
                self.send_down(zz, s, c).start()

            self.send_y(zz, s).start()
            self.send_core(zz, s, 0).start()

    def y_in(self, zz, s):
        c = self.chunk(zz, s, 2 * (1 - self.y) + self.k)
        remote(c, c, self.ys.at[zz, s], self.yr.at[zz, s], device(self.z, self.x, 1 - self.y, self.k)).wait_recv()
        self.send_core(zz, s, 1).start()

    def y_hop(self, d):
        z = self.z
        if d == 0:
            self.y_in(z, 1)
            return
        for s in range(2):
            pl.when(z >= d)(lambda: self.y_in(z - d, s))
            pl.when(z + d <= 3)(lambda: self.y_in(z + d, s))

    def landed(self, zz):
        def rest(s):
            for j in range(2):
                yy = self.y if j == 0 else 1 - self.y
                c = self.chunk(zz, s, 2 * yy + 1 - self.k)
                remote(c, c, self.cs.at[zz, s, j], self.cr.at[zz, s, j], device(self.z, self.x, self.y, 1 - self.k)).wait_recv()

        pl.when(self.z != zz)(lambda: rest(0))
        rest(1)

    def sent_own(self, own_quarter, other_quarter):
        z = self.z
        self.send_x(other_quarter).wait_send()
        pl.when(z < 3)(lambda: self.send_up(z, 0, own_quarter).wait_send())
        pl.when(z > 0)(lambda: self.send_down(z, 0, own_quarter).wait_send())

    def finish(self):
        z = self.z
        for zz in range(4):
            for s in range(2):
                def rest():
                    self.send_y(zz, s).wait_send()
                    for j in range(2):
                        self.send_core(zz, s, j).wait_send()
                if s == 0:
                    pl.when(z != zz)(rest)
                else:
                    rest()
                c = self.chunk(zz, s, self.q)

                pl.when((z < 3) & (zz < z + s))(lambda: self.send_up(zz, s, c).wait_send())
                pl.when((z > 0) & (zz > z - s))(lambda: self.send_down(zz, s, c).wait_send())


def token_sems():
    D = pltpu.SemaphoreType.DMA
    return [D, D, D((4, 2, 2)), D((4, 2)), D((4, 2)), D((4, 2)), D((4, 2, 2)), D((4, 2, 2))]


class WeightGather:
    def __init__(self, pairs, sems):
        self.pairs = pairs
        self.zs, self.zr, self.xs, self.xr, self.loc = sems
        self.z, self.x, self.y, self.k = place()

    def z_send(self, d, w):
        src, dst = self.pairs[w]
        to = (self.z + d) % 4
        return remote(src(to), dst(self.z, self.x), self.zs.at[d, w], self.zr.at[d, w], device(to, self.x, self.y, self.k))

    def z_recv(self, d, w):
        dst = self.pairs[w][1]
        frm = (self.z - d + 4) % 4
        return remote(dst(frm, self.x), dst(frm, self.x), self.zs.at[d, w], self.zr.at[d, w], device(frm, self.x, self.y, self.k))

    def x_send(self, d, w):
        src, dst = self.pairs[w]
        frm = (self.z - d + 4) % 4
        s = src(self.z) if isinstance(d, int) and d == 0 else dst(frm, self.x)
        return remote(s, dst(frm, self.x), self.xs.at[d, w], self.xr.at[d, w], device(self.z, 1 - self.x, self.y, self.k))

    def x_recv(self, d, w):
        frm = (self.z - d + 4) % 4
        r = self.pairs[w][1](frm, 1 - self.x)
        return remote(r, r, self.xs.at[d, w], self.xr.at[d, w], device(self.z, 1 - self.x, self.y, self.k))

    def local(self, w):
        src, dst = self.pairs[w]
        return pltpu.make_async_copy(src(self.z), dst(self.z, self.x), self.loc.at[w])

    def send(self, ws, e):
        d = mirrored(self.z, e)
        for w in ws:
            if e:
                self.z_send(d, w).start()
            else:
                self.x_send(0, w).start()
                self.local(w).start()

    def forward(self, ws, e):
        d = mirrored(self.z, e)
        for w in ws:
            self.z_recv(d, w).wait_recv()
            self.x_send(d, w).start()

    def landed(self, w):
        self.local(w).wait()
        for d in range(4):
            self.x_recv(d, w).wait_recv()

    def finish(self, w):
        for d in range(4):
            if d:
                self.z_send(d, w).wait_send()
            self.x_send(d, w).wait_send()


def weight_sems(n):
    D = pltpu.SemaphoreType.DMA
    return [D((4, n)), D((4, n)), D((4, n)), D((4, n)), D((n,))]


class TokenReduce:
    def __init__(self, out, bufs, sems):
        self.out = out
        self.S, self.r1, self.r2, self.rz, self.rf = bufs
        (self.cs, self.cr, self.ys, self.yr, self.zs, self.zr, self.xs, self.xr,
         self.fl, self.fys, self.fyr, self.fcs, self.fcr) = sems
        self.z, self.x, self.y, self.k = place()
        self.q = 2 * self.y + self.k

    def slot(self, s):
        return self.x if s == 0 else 1 - self.x

    def core(self, i, slot=0):
        zz = far_first(self.z, i)
        return remote(self.S.at[slot], self.r1.at[zz], self.cs.at[zz], self.cr.at[zz], device(self.z, self.x, self.y, 1 - self.k))

    def yex(self, zz, s):
        xx = self.slot(s)
        return remote(self.r1.at[zz, 1 - self.y, xx], self.r2.at[zz, xx], self.ys.at[zz, s], self.yr.at[zz, s],
                      device(self.z, self.x, 1 - self.y, self.k))

    def mine(self, zz, s):
        return self.r1.at[zz, self.y, self.slot(s)]

    def up(self, zz, s):
        return remote(self.mine(zz, s), self.rz.at[zz, s], self.zs.at[zz, s], self.zr.at[zz, s],
                      device(jnp.minimum(self.z + 1, 3), self.x, self.y, self.k))

    def down(self, zz, s):
        slot = jnp.where(zz == self.z - 1, 4, zz)
        return remote(self.mine(zz, s), self.rz.at[slot, s], self.zs.at[zz, s], self.zr.at[slot, s],
                      device(jnp.maximum(self.z - 1, 0), self.x, self.y, self.k))

    def arrive(self, zz, s, slot):
        r = self.rz.at[slot, s]
        remote(r, r, self.zs.at[0, s], self.zr.at[slot, s], device(self.z, self.x, self.y, 1 - self.k)).wait_recv()
        add_into(self.mine(zz, s), r)

    def xex(self):
        return remote(self.mine(self.z, 1), self.rf, self.xs, self.xr, device(self.z, 1 - self.x, self.y, self.k))

    def rows(self, i, kk, lhs):
        zz = far_first(self.z, i)
        return jnp.concatenate([lhs(zz, xx, 64 * (2 * yy + kk)) for yy in range(2) for xx in range(2)], axis=0)

    def fill(self, i, slot, lhs, rhs):
        a = self.rows(i, 1 - self.k, lhs)

        @pl.loop(0, 4)
        def _(j):
            at = columns(512, j)
            self.S[slot, :, :, :, at] = rhs(a, j).astype(BF).reshape(2, 2, 64, 512)
        self.core(i, slot).start()

    def after_core(self, i, lhs, rhs):
        zz = far_first(self.z, i)
        a = self.rows(i, self.k, lhs)
        self.core(i).wait_recv()

        @pl.loop(0, 4)
        def _(j):
            at = columns(512, j)
            got = self.r1[zz, :, :, :, at].reshape(256, 512).astype(F4)
            self.r1[zz, :, :, :, at] = (rhs(a, j) + got).astype(BF).reshape(2, 2, 64, 512)
        for s in (1, 0):
            self.yex(zz, s).start()

    def line(self, i, s):
        z = self.z
        zz = far_first(z, i)
        self.yex(zz, s).wait_recv()
        add_into(self.mine(zz, s), self.r2.at[zz, self.slot(s)])
        if i < 3:
            @pl.when(zz > z)
            def _():
                pl.when(z > 0)(lambda: self.arrive(zz, s, zz))
                self.up(zz, s).start()

            @pl.when(zz < z)
            def _():
                pl.when(z < 3)(lambda: self.arrive(zz, s, zz))
                self.down(zz, s).start()
        else:
            pl.when(z > 0)(lambda: self.arrive(z, s, z))
            pl.when(z < 3)(lambda: self.arrive(z, s, 4))
            if s == 1:
                self.xex().start()

    def spot(self, s, q):
        return self.out.at[self.slot(s), pl.ds(64 * q, 64), :]

    def fin_copies(self, s):
        src = self.mine(self.z, 0) if s == 0 else self.rf
        here = self.spot(s, self.q)
        return (pltpu.make_async_copy(src, here, self.fl.at[s]),
                remote(src, here, self.fys.at[s], self.fyr.at[s], device(self.z, self.x, 1 - self.y, self.k)),
                remote(src, here, self.fcs.at[s, 0], self.fcr.at[s, 0], device(self.z, self.x, self.y, 1 - self.k)))

    def relay(self, s):
        r = self.spot(s, 2 * (1 - self.y) + self.k)
        return remote(r, r, self.fcs.at[s, 1], self.fcr.at[s, 1], device(self.z, self.x, self.y, 1 - self.k))

    def spread(self, s, base=None):
        if s == 1:
            self.xex().wait_recv()
        if base is not None:
            add_into(self.mine(self.z, 0) if s == 0 else self.rf, base(self.slot(s), pl.ds(64 * self.q, 64)))
        for cp in self.fin_copies(s):
            cp.start()

    def spread_y(self, s):
        r = self.spot(s, 2 * (1 - self.y) + self.k)
        remote(r, r, self.fys.at[s], self.fyr.at[s], device(self.z, self.x, 1 - self.y, self.k)).wait_recv()
        self.relay(s).start()

    def finish(self):
        z = self.z
        for zz in range(4):
            for s in range(2):
                self.yex(zz, s).wait_send()
                pl.when(z != zz)(lambda: self.up(zz, s).wait_send())
        self.xex().wait_send()
        for s in range(2):
            for copy in self.fin_copies(s)[1:]:
                copy.wait_send()
            self.relay(s).wait_send()

    def landed(self, s):
        self.fin_copies(s)[0].wait()
        for j, yy in ((0, self.y), (1, 1 - self.y)):
            r = self.spot(s, 2 * yy + 1 - self.k)
            remote(r, r, self.fcs.at[s, j], self.fcr.at[s, j], device(self.z, self.x, self.y, 1 - self.k)).wait_recv()


def reduce_sems():
    D = pltpu.SemaphoreType.DMA
    return [D((4,)), D((4,)), D((4, 2)), D((4, 2)), D((4, 2)), D((5, 2)), D, D,
            D((2,)), D((2,)), D((2,)), D((2, 2)), D((2, 2))]


def reduce_bufs():
    V = lambda *s: pltpu.VMEM(s, BF)
    return [V(4, 2, 2, 64, 2048), V(4, 2, 64, 2048), V(5, 2, 64, 2048), V(64, 2048)]


class GradReduce:
    def __init__(self, parts, away, got, sems):
        self.parts, self.away, self.got = parts, away, got
        self.xs, self.xr, self.zs, self.zr = sems
        self.z, self.x, self.y, self.k = place()

    def x_send(self, e):
        i = FAR.index(e)
        return remote(self.away.at[i % 2], self.got.at[i], self.xs.at[i], self.xr.at[i], device(self.z, 1 - self.x, self.y, self.k))

    def z_sends(self, e):
        d = mirrored(self.z, e)
        for i, (part, there) in enumerate(self.parts):
            src, dst = self.got.at[(FAR.index(e),) + part], there(self.z)
            if e == 0:
                yield pltpu.make_async_copy(src, dst, self.zs.at[0, i])
            else:
                yield remote(src, dst, self.zs.at[d, i], self.zr.at[d, i], device((self.z + d) % 4, self.x, self.y, self.k))

    def give(self, e, terms):
        i = FAR.index(e)
        if i >= 2:
            self.x_send(FAR[i - 2]).wait_send()
        self.away[i % 2] = terms.astype(BF)
        self.x_send(e).start()

    def keep(self, e, terms):
        i = FAR.index(e)
        self.x_send(e).wait_recv()
        self.got[i] = (terms + self.got[i].astype(F4)).astype(BF)
        for cp in self.z_sends(e):
            cp.start()

    def finish(self):
        for cp in self.z_sends(0):
            cp.wait()
        for e in FAR[2:]:
            self.x_send(e).wait_send()
        for d in range(1, 4):
            frm = (self.z - d + 4) % 4
            for cp in self.z_sends(d):
                cp.wait_send()
            for i, (part, there) in enumerate(self.parts):
                r = there(frm)
                remote(r, r, self.zs.at[d, i], self.zr.at[d, i], device(frm, self.x, self.y, self.k)).wait_recv()


def grad_scratch(block, parts):
    D = pltpu.SemaphoreType.DMA
    V = pltpu.VMEM
    return [V((2,) + block, BF), V((4,) + block, BF)] + [D((4,))] * 2 + [D((4, parts))] * 2


def norm_rows(rows, gain, shift):
    v = rows.astype(F4)
    centred = v - jnp.mean(v, axis=-1, keepdims=True)
    spread = jnp.mean(centred * centred, axis=-1, keepdims=True)
    return (centred * lax.rsqrt(spread + EPS) * gain + shift).astype(BF)


def turn(v, tab):
    cos, lo, hi = tab
    return v * cos + pltpu.roll(v, 112, 1) * lo + pltpu.roll(v, 16, 1) * hi


def turn_back(v, tab):
    cos, lo, hi = tab
    return v * cos - pltpu.roll(v, 112, 1) * lo - pltpu.roll(v, 16, 1) * hi


def angle_table(within, cb, sb):
    cr, sr = within[0], within[1]
    cos, sin = cb * cr - sb * sr, sb * cr + cb * sr
    entry = lax.broadcasted_iota(jnp.int32, cos.shape, 1) % 64
    return cos, jnp.where(entry < 16, -sin, 0.0), jnp.where(entry < 16, 0.0, sin)


def angles(rows, step):
    frequency = (10000.0 ** (-2.0 * np.arange(16) / 32)).astype(np.float32).astype(np.float64)
    lanes = np.concatenate([frequency, frequency, np.zeros(32)] * 2)
    angle = step * np.arange(rows)[:, None] * lanes
    return np.stack([np.cos(angle), np.sin(angle)]).astype(np.float32)


def pick(index, parts):
    chosen = parts(0)
    for j in range(1, 8):
        chosen = jnp.where(index == j, parts(j), chosen)
    return chosen


def one_head(v, h, axis):
    entry = lax.broadcasted_iota(jnp.int32, v.shape, axis)
    return jnp.where((entry < 64) == (h == 0), v, jnp.zeros_like(v))


def masked(st, kr):
    row = lax.broadcasted_iota(jnp.int32, (256, 256), 0)
    column = lax.broadcasted_iota(jnp.int32, (256, 256), 1)
    last = jnp.where(row <= column, st[kr - 256:], -1e30)
    return last if kr == 256 else jnp.concatenate([st[:kr - 256], last], axis=0)


def flip(v):
    return v.astype(F4).T.astype(BF)


def norm_backward(s, tok, cot, ng, gains, out, stage, ssem, sums):
    gain = jnp.concatenate([gains[i, 0:1, :] for i in range(8)], axis=1)

    def store(i):
        return pltpu.make_async_copy(stage.at[i % 2], out.at[s, pl.ds(pl.multiple_of(32 * i, 32), 32)], ssem.at[i % 2])

    @pl.loop(0, 8)
    def _(i):
        at = pl.ds(pl.multiple_of(32 * i, 32), 32)
        v = tok[s, at].astype(F4)
        centred = v - jnp.mean(v, axis=-1, keepdims=True)
        scale = lax.rsqrt(jnp.mean(centred * centred, axis=-1, keepdims=True) + EPS)
        xhat = centred * scale
        n = ng[s, at].astype(F4)
        g = n * gain
        along = jnp.mean(g * xhat, axis=-1, keepdims=True)

        @pl.when(i >= 2)
        def _():
            store(i - 2).wait()
        stage[i % 2] = cot[s, at].astype(F4) + (g - jnp.mean(g, axis=-1, keepdims=True) - xhat * along) * scale
        store(i).start()
        both = n * xhat
        sums[0] += both[:8] + both[8:16] + both[16:24] + both[24:]
        sums[1] += n[:8] + n[8:16] + n[16:24] + n[24:]

    store(6).wait()
    store(7).wait()


(
    START, NORM, SEND, PASS, HAVE, OPEN, CROSS, HOP, TWIN, PROJECT, ARRANGE, ATTEND, MIX, SLOPE, TURN, RETURN, PROJECTED, HIDDEN,
    PULL, FILL, CORE, LINE, SPREAD, RELAY, DONE, GIVE, KEEP, LAST, GRADIENTS,
) = range(29)
ORDER = (
    (START,), (SEND, 0, 2), (SEND, 0, 3), (SEND, 0, 1), (SEND, 0, 0), (SEND, 1, 1), (NORM,), (OPEN, 0), (SEND, 1, 0), (CROSS, 0),
    (SEND, 2, 0), (PASS, 0, 1), (TWIN, 0, 0), (HOP, 0, 1, 0), (PASS, 0, 2), (HOP, 0, 1, 1), (HOP, 0, 2, 0), (SEND, 1, 2), (OPEN, 1),
    (HOP, 0, 2, 1), (SEND, 1, 3), (PASS, 0, 3), (CROSS, 1), (SEND, 2, 3), (SEND, 2, 2), (TWIN, 0, 1), (HOP, 0, 3, 0), (HOP, 0, 3, 1),
    (PASS, 1, 3), (HOP, 1, 1, 0), (SEND, 2, 1), (TWIN, 0, 3), (TWIN, 0, 2), (PASS, 1, 2), (HAVE, 0), (PROJECT, 0), (PROJECT, 1),
    (PASS, 1, 1), (PROJECT, 2), (PROJECT, 3), (ARRANGE,), (HAVE, 1), (HIDDEN, 0), (HIDDEN, 1), (TWIN, 1, 0), (PASS, 2, 3),
    (HOP, 1, 1, 1), (PASS, 2, 2), (HAVE, 3), (PASS, 2, 1), (ATTEND, 0), (ATTEND, 1), (ATTEND, 2), (ATTEND, 3), (HOP, 1, 2, 0),
    (HIDDEN, 2), (HOP, 1, 2, 1), (ATTEND, 4), (TWIN, 1, 1), (ATTEND, 5), (ATTEND, 6), (ATTEND, 7), (MIX,), (HOP, 1, 3, 1), (HAVE, 2),
    (FILL, 1, 0), (SLOPE, 0), (TWIN, 1, 2), (HOP, 1, 3, 0), (FILL, 1, 1), (CORE, 1, 0), (SLOPE, 1), (SLOPE, 2), (HIDDEN, 3),
    (TWIN, 1, 3), (FILL, 1, 2), (FILL, 1, 3), (CORE, 1, 1), (SLOPE, 3), (TURN,), (RETURN, 0), (PULL, 0), (RETURN, 1), (LINE, 1, 0, 0),
    (RETURN, 2), (RETURN, 3), (RETURN, 4), (CORE, 1, 2), (LINE, 1, 0, 1), (RETURN, 5), (RETURN, 6), (LINE, 1, 1, 0), (RETURN, 7),
    (LINE, 1, 1, 1), (PROJECTED,), (GIVE, 0, 1), (GIVE, 0, 2), (LINE, 1, 2, 0), (PULL, 1), (LINE, 1, 2, 1), (FILL, 0, 0),
    (FILL, 0, 1), (CORE, 0, 0), (KEEP, 0, 1), (GIVE, 0, 3), (CORE, 0, 1), (KEEP, 0, 2), (PULL, 2), (CORE, 1, 3), (PULL, 3),
    (LINE, 0, 0, 1), (GIVE, 1, 1), (FILL, 0, 2), (FILL, 0, 3), (LINE, 0, 0, 0), (GIVE, 1, 2), (CORE, 0, 2), (KEEP, 1, 1),
    (LINE, 1, 3, 0), (GIVE, 1, 3), (LINE, 0, 1, 1), (LINE, 0, 2, 1), (CORE, 0, 3), (LINE, 0, 1, 0), (LINE, 1, 3, 1), (KEEP, 0, 3),
    (LINE, 0, 3, 1), (LINE, 0, 2, 0), (SPREAD, 1, 1), (KEEP, 1, 3), (LINE, 0, 3, 0), (RELAY, 1, 1), (SPREAD, 0, 0), (GIVE, 0, 0),
    (KEEP, 1, 2), (SPREAD, 0, 1), (GIVE, 1, 0), (RELAY, 0, 0), (SPREAD, 1, 0), (RELAY, 0, 1), (DONE, 0, 0), (LAST, 0), (DONE, 1, 1),
    (DONE, 0, 1), (RELAY, 1, 0), (LAST, 1), (DONE, 1, 0), (KEEP, 1, 0), (KEEP, 0, 0), (GRADIENTS,),
)


def block_kernel(pairs_of, gains, within, block, tok, cot, win, wout, wexp, wcon,
                 out, ig, vectors, gin, gout, gexp, gcon, xn, ct,
                 wx, wco, hp, am, S, ctr, ng, gs, gs_all, vec, vecs,
                 gsem_s, gsem_r, lsem, rsem, csem, ssem, vs, vr, *rest):
    z, x, y, k = place()
    c, q = z * 2 + x, 2 * y + k
    rest = list(rest)
    take = lambda n: [rest.pop(0) for _ in range(n)]
    nt, nb, ns = len(token_sems()), len(reduce_bufs()), len(reduce_sems())
    tx = TokenGather(xn, take(nt))
    tc = TokenGather(ct, take(nt))
    pairs = [
        (lambda zz, j=j: win.at[j, :, columns(128, zz)], lambda zz, xx, j=j: wx.at[zz, xx, :, pl.ds(512 + 128 * j, 128)])
        for j in range(3)
    ] + [
        (lambda zz: wexp.at[:, columns(512, zz)], lambda zz, xx: wx.at[zz, xx, :, pl.ds(0, 512)]),
        (lambda zz: wcon.at[columns(512, zz), :], lambda zz, xx: wco.at[pl.ds(0, 512), columns(256, zz * 2 + xx)]),
        (lambda zz: wout.at[columns(128, zz), :], lambda zz, xx: wco.at[pl.ds(512, 128), columns(256, zz * 2 + xx)]),
    ]
    wg = WeightGather(pairs, take(len(weight_sems(6))))
    tn = TokenReduce(ng, [S] + take(nb), take(ns))
    to = TokenReduce(out, [S] + take(nb), take(ns))
    whole = slice(None)
    g1 = GradReduce([((pl.ds(0, 512), whole), lambda zz: gcon.at[columns(512, zz), :]),
                     ((pl.ds(512, 128), whole), lambda zz: gout.at[columns(128, zz), :])], *take(2), take(4))
    g2 = GradReduce([((whole, pl.ds(0, 512)), lambda zz: gexp.at[:, columns(512, zz)])]
                    + [((whole, pl.ds(512 + 128 * j, 128)), lambda zz, j=j: gin.at[j, :, columns(128, zz)]) for j in range(3)],
                    *take(2), take(4))
    others, everyone = peers_of(z, x, y, k)

    def pair_at(slot):
        return pairs_of[x, slot]

    def slot_of(pair):
        found = jnp.int32(0)
        for j in range(8):
            found = jnp.where(pairs_of[x, j] == pair, j, found)
        return found


    V = pltpu.VMEM
    steps = {}
    flags = set()
    load_tok = lambda: pltpu.make_async_copy(tok, ctr.at[0], lsem.at[0])
    load_cot = lambda: pltpu.make_async_copy(cot, ctr.at[1], lsem.at[1])
    xl, xo, cl = ctr.at[1, 0], S.at[0, 0, 0], ctr.at[1, 1]
    near_cot = lambda: pltpu.make_async_copy(cot.at[x], cl, lsem.at[1])
    own_cot = lambda: pltpu.make_async_copy(cl, ct.at[z, x], lsem.at[2])
    own_xn = lambda: pltpu.make_async_copy(xl, xn.at[z, x], lsem.at[3])
    gcopies = lambda: [remote(gs, gs_all.at[c], gsem_s.at[i], gsem_r.at[i], others[i]) for i in range(7)]
    mine, cot_mine = xl.at[pl.ds(64 * q, 64)], cot.at[x, pl.ds(64 * q, 64)]
    cot_other = cot.at[1 - x, pl.ds(64 * q, 64)]

    def once(name, act):
        if name not in flags:
            flags.add(name)
            act()

    users = [n for n in ORDER if n[0] in (PROJECT, SLOPE, HIDDEN, PULL)]

    def rows_in(n, xx):
        kind, i = users[n]
        zz = far_first(z, i if kind in (HIDDEN, PULL) else 3 - i)
        src = xn if kind in (PROJECT, HIDDEN) else ct
        return zz, pltpu.make_async_copy(src.at[zz, xx], ctr.at[n % 2, xx], rsem.at[n % 2, xx])

    def begin_rows(n):
        flags.add(n)
        for xx in range(2):
            rows_in(n, xx)[1].start()

    def each_half(name, act):
        n = users.index(name)
        if n not in flags:
            begin_rows(n)
        for xx in range(2):
            zz, cp = rows_in(n, xx)
            cp.wait()
            if name[0] in (PROJECT, SLOPE):
                act(zz, xx, ctr.at[n % 2, xx], pl.multiple_of(512 * zz + 256 * xx, 256))
        if name[0] in (HIDDEN, PULL):
            act(ctr.at[n % 2], pl.multiple_of(512 * zz, 512))
        flags.add(name)
        for m in (n + 1, n + 2):
            if m < len(users) and m not in flags and {HIDDEN: (PROJECT, 3), PULL: (SLOPE, 3)}.get(users[m][0]) in flags:
                begin_rows(m)
        if n + 1 == len(users):
            load_tok().start()
            load_cot().start()

    def start():
        load_tok().start()
        gs[...] = jnp.zeros_like(gs)
        gs[0:2, :] = gains[...]
        meet(everyone)
        for g in gcopies():
            g.start()
        gs_all[c] = gs[...]
        near_cot().start()

    def norm():
        for i in range(7):
            frm = gs_all.at[(c - i - 1 + 8) % 8]
            remote(frm, frm, gsem_s.at[i], gsem_r.at[i], others[i]).wait_recv()
        gain = jnp.concatenate([gs_all[i, 0:1, :] for i in range(8)], axis=1)
        shift = jnp.concatenate([gs_all[i, 1:2, :] for i in range(8)], axis=1)
        load_tok().wait()

        @pl.loop(0, 2)
        def _(i):
            xo[pl.ds(32 * i, 32)] = norm_rows(ctr[0, 1 - x, pl.ds(64 * q + 32 * i, 32)], gain, shift)

        @pl.loop(0, 8)
        def _(i):
            xl[pl.ds(32 * i, 32)] = norm_rows(ctr[0, x, pl.ds(32 * i, 32)], gain, shift)

        own_xn().start()
        near_cot().wait()
        own_cot().start()

    steps[START,], steps[NORM,] = start, norm
    for u, ws in enumerate(((0, 1, 2, 5), (3,), (4,))):
        for d in range(4):
            steps[SEND, u, d] = functools.partial(wg.send, ws, d)
            steps[PASS, u, d] = functools.partial(wg.forward, ws, d)
    for u, ws in enumerate(((0, 1, 2), (3,), (4,), (5,))):
        steps[HAVE, u] = functools.partial(lambda ws: [wg.landed(w) for w in ws], ws)
    steps[OPEN, 0] = lambda: tx.start(mine, xo)
    steps[OPEN, 1] = lambda: tc.start(cot_mine, cot_other)
    for name, t in enumerate((tx, tc)):
        steps[CROSS, name] = t.after_x
        for d in range(4):
            steps[TWIN, name, d] = functools.partial(t.y_hop, d)
            for s in range(2):
                steps[HOP, name, d, s] = functools.partial(t.hop, d, s)

    def hidden(rows, row):
        at = pl.ds(row, 512)
        u = dot(rows[...].reshape(512, 2048), wx[:, :, :, pl.ds(0, 512)].reshape(2048, 512))
        square = u * u
        t = jnp.tanh(0.7978845608028654 * (u + 0.044715 * u * square))
        half = 0.5 * (1.0 + t)
        am[at, pl.ds(0, 512)] = (u * half).astype(BF)
        hp[at, pl.ds(0, 512)] = (half + 0.5 * u * (1.0 - t * t) * (0.7978845608028654 * (1.0 + 3 * 0.044715 * square))).astype(BF)

    def pull(rows, row):
        at = (pl.ds(row, 512), pl.ds(0, 512))
        hp[at] = (dot_t(rows[...].reshape(512, 2048), wco[pl.ds(0, 512)]) * hp[at].astype(F4)).astype(BF)

    for i in range(4):
        steps[HIDDEN, i] = functools.partial(each_half, (HIDDEN, i), hidden)
        steps[PULL, i] = functools.partial(each_half, (PULL, i), pull)

    def piece(ref):
        return lambda zz, xx, r: ref[pl.ds(pl.multiple_of(512 * zz + 256 * xx + r, 64), 64)]

    of = ((piece(hp), lambda a, j: dot_t(a, wx[j].reshape(512, 896))), (piece(am), lambda a, j: dot(a, wco[:, columns(512, j)])))
    filled = []

    def fill(name, t, i):
        if len(filled) >= 2:
            sent(filled[-2])
        filled.append((t, i))
        t.fill(i, (len(filled) - 1) % 2, *of[name])

    def sent(one):
        one[0].core(one[1]).wait_send()

    def to_base(seq, rows):
        once(load_tok, lambda: load_tok().wait())
        return ctr.at[0, seq, rows]

    for name, t in enumerate((tn, to)):
        for i in range(4):
            steps[FILL, name, i] = functools.partial(fill, name, t, i)
            steps[CORE, name, i] = functools.partial(t.after_core, i, *of[name])
            for s in range(2):
                steps[LINE, name, i, s] = functools.partial(t.line, i, s)
        for s in range(2):
            steps[SPREAD, name, s] = functools.partial(t.spread, s, to_base if t is to else None)
            steps[RELAY, name, s] = functools.partial(t.spread_y, s)
            steps[DONE, name, s] = functools.partial(t.landed, s)

    def by_block(zz, xx, half):
        p = pair_at(2 * zz + xx)
        return [pick(p, lambda j: block[i, pl.ds(j if half == 0 else 15 - j, 1)]) for i in range(2)]

    cut = ORDER.index((PROJECTED,)) + 1

    def attention(ps, qkv, qt, kt, vt, gt, ot, logs, gpos, dqt, dk, dv):
        def project(zz, xx, rows, row):
            three = dot(rows[...], wx[:, :, :, pl.ds(512, 384)].reshape(2048, 384))
            for half in range(2):
                v = three[128 * half:128 * half + 128]
                t = angle_table(within, *by_block(zz, xx, half))
                at = pl.ds(row + 128 * half, 128)
                ps[at, pl.ds(0, 128)] = turn(v[:, 0:128], t).astype(BF) * BF(0.125)
                ps[at, pl.ds(128, 128)] = turn(v[:, 128:256], t).astype(BF)
                ps[at, pl.ds(256, 128)] = v[:, 256:384].astype(BF)

        def slope(zz, xx, rows, row):
            ps[pl.ds(row, 256), pl.ds(0, 128)] = dot_t(rows[...], wco[pl.ds(512, 128)]).astype(BF)

        def landed(i, kind, t, act):
            once(own_rows, own_rows)
            t.landed(far_first(z, 3 - i))
            each_half((kind, i), act)

        def own_rows():
            own_xn().wait()
            own_cot().wait()
            tx.sent_own(mine, xo)

        for i in range(4):
            steps[PROJECT, i] = functools.partial(landed, i, PROJECT, tx, project)
            steps[SLOPE, i] = functools.partial(landed, i, SLOPE, tc, slope)

        def by_position(b, cols):
            half = b // 8
            pair = b + half * (15 - 2 * b)
            return pick(slot_of(pair), lambda j: ps[pl.ds(pl.multiple_of(256 * j + 128 * half, 128), 128), cols].astype(F4))

        def by_rows(c2, half):
            p = pair_at(c2)
            return lambda ref: pick(p, lambda j: ref[pl.ds(128 * (j if half == 0 else 15 - j), 128)])

        def blocks(act):
            @pl.loop(0, 16)
            def _(b):
                act(b, pl.ds(pl.multiple_of(b * 128, 128), 128))

        def slots(act):
            for half in range(2):
                @pl.loop(0, 8)
                def _(c2):
                    act(by_rows(c2, half), pl.ds(pl.multiple_of(256 * c2 + 128 * half, 128), 128))

        def rope():
            def act(b, here):
                three = by_position(b, slice(None))
                for j, ref in enumerate((qt, kt, vt)):
                    v = three[:, 128 * j:128 * j + 128]
                    qkv[j, here] = v.astype(BF)
                    ref[:, here] = v.T.astype(BF)
            blocks(act)

        def score(i, h):
            kr = 256 * (i + 1)
            return masked(dot(qkv[1, :kr], one_head(qt[:, pl.ds(256 * i, 256)], h, 0)), kr)

        ahead = []

        def forward(i):
            kr, here = 256 * (i + 1), pl.ds(256 * i, 256)
            for h in range(2):
                st = ahead.pop() if ahead else score(0, 0)
                if (i, h) != (7, 1):
                    ahead.append(score(i + h, 1 - h))
                peak = jnp.max(st, axis=0, keepdims=True)
                p = jnp.exp(st - peak)
                total = jnp.sum(p, axis=0, keepdims=True)
                o = dot(vt[:, :kr], p.astype(BF)) * (1.0 / total)
                ot[pl.ds(64 * h, 64), here] = o[64 * h:64 * h + 64]
                logs[pl.ds(h, 1), here] = peak + jnp.log(total)

        def mix():
            def turned(b, here):
                gpos[here] = ot[:, here].T

            def placed(pos, row):
                am[row, pl.ds(512, 128)] = pos(gpos).astype(BF)
            blocks(turned)
            slots(placed)

        def gflip():
            def act(b, here):
                g = by_position(b, pl.ds(0, 128))
                gpos[here] = g
                gt[:, here] = g.T.astype(BF)
            blocks(act)
            dk[...] = jnp.zeros_like(dk)
            dv[...] = jnp.zeros_like(dv)

        def backward(i):
            kr, here = 256 * (i + 1), pl.ds(256 * i, 256)
            for h in range(2):
                p = jnp.exp(score(i, h) - logs[pl.ds(h, 1), here])
                low = p.astype(BF)
                at = pl.ds(64 * h, 64)
                delta = jnp.sum(ot[at, here] * gt[at, here].astype(F4), axis=0, keepdims=True)
                ds = (p * (dot(qkv[2, :kr], one_head(gt[:, here], h, 0)) - delta)).astype(BF)
                dv[:kr] += dot(low, one_head(gpos[here].astype(BF), h, 1))
                dk[:kr] += dot(ds, one_head(qkv[0, here], h, 1))
                dqt[at, here] = dot(kt[:, :kr], ds)[64 * h:64 * h + 64] * 0.125

        def gradients():
            def turned(b, here):
                t = angle_table(within, block[0, pl.ds(b, 1)], block[1, pl.ds(b, 1)])
                gpos[here] = turn_back(dqt[:, here].T, t)
                dk[here] = turn_back(dk[here], t)

            def placed(pos, row):
                for j, ref in enumerate((gpos, dk, dv)):
                    hp[row, pl.ds(512 + 128 * j, 128)] = pos(ref).astype(BF)
            blocks(turned)
            slots(placed)

        steps[ARRANGE,], steps[MIX,], steps[TURN,], steps[PROJECTED,] = rope, mix, gflip, gradients
        for i in range(8):
            steps[ATTEND, i] = functools.partial(forward, i)
            steps[RETURN, i] = functools.partial(backward, i)
        for name in ORDER[:cut]:
            steps[name]()

    pl.run_scoped(
        attention, V((2048, 384), BF), V((3, 2048, 128), BF), V((128, 2048), BF), V((128, 2048), BF), V((128, 2048), BF),
        V((128, 2048), BF), V((128, 2048), F4), V((8, 2048), F4), V((2048, 128), F4), V((128, 2048), F4),
        V((2048, 128), F4), V((2048, 128), F4))

    def rest_of(col, stage, sums):
        plan = [n for n in ORDER if n[0] in (GIVE, KEEP)]

        def block_load(n):
            kind, j, e = plan[n]
            src, d, xx = (ct, xn)[j], mirrored(z, e), 1 - x if kind == GIVE else x
            return pltpu.make_async_copy(src.at[:, :, :, columns(256, 2 * ((z + d) % 4) + xx)], col.at[n % 3], csem.at[n % 3])

        def grad(n):
            kind, j, e = plan[n]
            block_load(n).wait()
            terms = dot(flip(col[n % 3].reshape(2048, 256)), (am, hp)[j][...])
            g = (g1, g2)[j]
            (g.give if kind == GIVE else g.keep)(e, terms if j else terms.T)
            if n + 3 < len(plan):
                block_load(n + 3).start()

        for n in range(3):
            block_load(n).start()
        copies = [remote(vec.at[(c + i + 1) % 8], vecs.at[c], vs.at[i], vr.at[i], others[i]) for i in range(7)]

        def normed_gradient(s):
            once(load_tok, lambda: load_tok().wait())
            once(load_cot, lambda: load_cot().wait())
            if s == 0:
                sums[...] = jnp.zeros_like(sums)
            norm_backward(x if s == 0 else 1 - x, ctr.at[0], ctr.at[1], ng, gs_all, ig, stage, ssem, sums)
            if s == 0:
                return
            for i in range(8):
                at = slice(256 * i, 256 * i + 256)
                for j in range(2):
                    vec[i, j:j + 1, :] = jnp.sum(sums[j, :, at], axis=0, keepdims=True)
                vec[i, 2:8, :] = jnp.zeros((6, 256), F4)
            vecs[c] = vec[c]
            for cp in copies:
                cp.start()

        def gradients():
            g1.finish()
            g2.finish()

        steps[GRADIENTS,] = gradients
        for s in range(2):
            steps[LAST, s] = functools.partial(normed_gradient, s)
        for n, name in enumerate(plan):
            steps[name] = functools.partial(grad, n)
        for name in ORDER[cut:]:
            steps[name]()
        for i in range(7):
            frm = vecs.at[(c - i - 1 + 8) % 8]
            remote(frm, frm, vs.at[i], vr.at[i], others[i]).wait_recv()
        total = vecs[0]
        for i in range(1, 8):
            total = total + vecs[i]
        vectors[...] = total
        for cp in copies:
            cp.wait_send()

    pl.run_scoped(rest_of, V((3, 4, 2, 256, 256), BF), V((2, 32, 2048), F4), V((2, 8, 2048), F4))
    for one in filled[-2:]:
        sent(one)
    tn.finish()
    to.finish()
    tx.finish()
    tc.sent_own(cot_mine, cot_other)
    tc.finish()
    for w in range(6):
        wg.finish(w)
    for g in gcopies():
        g.wait_send()


def block_call(pairs_of, gains, tok, cot, win, wout, wexp, wcon):
    S = jax.ShapeDtypeStruct
    ANY = pl.BlockSpec(memory_space=pl.ANY)
    VM = pl.BlockSpec(memory_space=pltpu.VMEM)
    D = pltpu.SemaphoreType.DMA
    V = pltpu.VMEM
    rows = (4, 2, 256, 2048)
    return pl.pallas_call(
        block_kernel,
        out_shape=[S((2, 256, 2048), BF), S((2, 256, 2048), F4), S((8, 256), F4),
                   S((3, 256, 512), BF), S((512, 256), BF), S((256, 2048), BF), S((2048, 256), BF), S(rows, BF), S(rows, BF)],
        in_specs=[pl.BlockSpec(memory_space=pltpu.SMEM)] + [VM] * 3 + [ANY] * 6,
        out_specs=[ANY, ANY, VM] + [ANY] * 6,
        scratch_shapes=[V((4, 2, 256, 896), BF), V((640, 2048), BF), V((2048, 896), BF), V((2048, 640), BF), V((2, 2, 2, 64, 2048), BF),
                        V((2, 2, 256, 2048), BF), V((2, 256, 2048), BF), V((8, 256), F4), V((8, 8, 256), F4), V((8, 8, 256), F4), V((8, 8, 256), F4),
                        D((7,)), D((7,)), D((4,)), D((2, 2)), D((3,)), D((2,)), D((7,)), D((7,))]
        + token_sems() * 2 + weight_sems(6) + (reduce_bufs() + reduce_sems()) * 2 + grad_scratch((640, 256), 2) + grad_scratch((256, 896), 4),
        compiler_params=pltpu.CompilerParams(collective_id=0, has_side_effects=True, vmem_limit_bytes=63 * MB),
        name="block",
    )(pairs_of, gains, jnp.asarray(angles(128, 1)), jnp.asarray(angles(16, 128)), tok, cot, win, wout, wexp, wcon)


def finish_kernel(out, ig, gin, gout, gexp, gcon, out_to, ig_to, gin_to, gout_to, gexp_to, gcon_to,
                  vin, vout, vexp, vcon, fin, fout, fexp, fcon, through, wide, isem, osem):
    work = ((gexp, vexp, fexp, gexp_to), (gcon, vcon, fcon, gcon_to), (gin, vin, fin, gin_to), (gout, vout, fout, gout_to),
            (ig, wide, wide, ig_to), (out, through, through, out_to))
    loads = [pltpu.make_async_copy(w[0], w[1], isem.at[i]) for i, w in enumerate(work)]
    stores = [pltpu.make_async_copy(w[2], w[3], osem.at[i]) for i, w in enumerate(work)]
    for copy in loads:
        copy.start()
    for (_, low, full, _), load, store in zip(work, loads, stores):
        load.wait()
        if low is not full:
            rows = low.shape[-2]
            for j in range(low.shape[0] if len(low.shape) == 3 else 1):
                @pl.loop(0, rows // 128)
                def _(i):
                    at = (pl.ds(pl.multiple_of(128 * i, 128), 128),)
                    at = (j,) + at if len(low.shape) == 3 else at
                    full[at] = low[at].astype(F4)
        store.start()
    for copy in stores:
        copy.wait()


def finish_call(out, ig, *grads):
    S = jax.ShapeDtypeStruct
    ANY = pl.BlockSpec(memory_space=pl.ANY)
    D = pltpu.SemaphoreType.DMA
    V = pltpu.VMEM
    shapes = [g.shape for g in grads]
    return pl.pallas_call(
        finish_kernel,
        out_shape=[S(out.shape, BF), S(ig.shape, F4)] + [S(s, F4) for s in shapes],
        in_specs=[ANY] * 6,
        out_specs=[ANY] * 6,
        scratch_shapes=[V(s, BF) for s in shapes] + [V(s, F4) for s in shapes] + [V(out.shape, BF), V(ig.shape, F4), D((6,)), D((6,))],
        compiler_params=pltpu.CompilerParams(vmem_limit_bytes=60 * MB),
        name="finish",
    )(out, ig, *grads)


def own_local(tokens, pair_index, norm_gain, norm_shift, w_attention_in, w_attention_out, w_expand, w_contract, cotangent):
    gains = jnp.stack([norm_gain, norm_shift]).astype(F4)
    output, input_grad, vectors, *grads = block_call(
        pair_index, gains, tokens, cotangent, w_attention_in, w_attention_out, w_expand, w_contract)
    output, input_grad, *grads = finish_call(output, input_grad, *grads[:4])
    return (output, input_grad, vectors[0], vectors[1], *grads)


def local(tokens, pair_index, norm_gain, norm_shift, w_attention_in, w_attention_out, w_expand, w_contract, cotangent):
    args = (tokens, pair_index, norm_gain, norm_shift, w_attention_in, w_attention_out, w_expand, w_contract, cotangent)
    sizes = (lax.axis_size("ctx"), lax.axis_size("tp")) + tokens.shape + w_attention_in.shape[2:] + w_expand.shape[1:]
    if sizes == (8, 4, 2, 256, 2048, 512, 2048):
        return own_local(*args)
    return general_local(*args)


def solution(mesh):
    in_specs = (
        P(None, "ctx", None),
        P(),
        P("ctx"),
        P("ctx"),
        P(None, "ctx", "tp"),
        P("tp", "ctx"),
        P("ctx", "tp"),
        P("tp", "ctx"),
        P(None, "ctx", None),
    )
    out_specs = (
        P(None, "ctx", None),
        P(None, "ctx", None),
        P("ctx"),
        P("ctx"),
        P(None, "ctx", "tp"),
        P("tp", "ctx"),
        P("ctx", "tp"),
        P("tp", "ctx"),
    )
    return jax.shard_map(local, mesh=mesh, in_specs=in_specs, out_specs=out_specs, check_vma=False)
```

```python
import functools
import itertools

import jax
import jax.numpy as jnp
import numpy as np
from jax import lax
from jax.experimental import pallas as pl
from jax.experimental.pallas import tpu as pltpu
from jax.sharding import PartitionSpec as P

HEAD_DIM = 64
ROT = 32


epsilon = 1e-05


def position_table(pair_index, shard_rows):
    pair_count = pair_index.shape[1]
    half_rows = shard_rows // 2
    token_index = jnp.arange(shard_rows * pair_count, dtype=jnp.int32)
    owning = token_index // shard_rows
    within = token_index % shard_rows
    picked = (owning[:, None] == jnp.arange(pair_count, dtype=jnp.int32)[None, :]).astype(jnp.int32)
    chosen = jnp.sum(picked[None, :, :] * pair_index[:, None, :], axis=2)
    first_half = chosen * half_rows + within[None, :]
    second = (2 * pair_count - 1 - chosen) * half_rows + within[None, :] - half_rows
    return jnp.where(within[None, :] < half_rows, first_half, second)


def rotate(tensor, positions):
    half_rot = ROT // 2
    frequency = 10000.0 ** (-2.0 * jnp.arange(half_rot, dtype=jnp.float32) / ROT)
    angles = positions.astype(jnp.float32)[..., None] * frequency
    cosine = jnp.cos(angles)[..., None, :]
    sine_part = jnp.sin(angles)[..., None, :]
    leading = tensor[..., :half_rot]
    trailing = tensor[..., half_rot:ROT]
    return jnp.concatenate(
        [
            leading * cosine - trailing * sine_part,
            trailing * cosine + leading * sine_part,
            tensor[..., ROT:],
        ],
        axis=-1,
    )


def gelu_tanh(values_in):
    return (
        0.5
        * values_in
        * (
            1.0
            + jnp.tanh(
                0.7978845608028654 * (values_in + 0.044715 * values_in * values_in * values_in)
            )
        )
    )


def layer_norm(inputs, gain_full, shift_full):
    centred = inputs - jnp.mean(inputs, axis=-1, keepdims=True)
    spread = jnp.mean(centred * centred, axis=-1, keepdims=True)
    return centred * lax.rsqrt(spread + epsilon) * gain_full + shift_full


def block_probs(queries, keys_block, log_total, query_pos, key_pos):
    raw_scores = jnp.einsum(
        "sqhe,skhe->shqk", queries, keys_block, preferred_element_type=jnp.float32
    )
    allowed = key_pos[:, None, None, :] <= query_pos[:, None, :, None]
    return jnp.where(allowed, jnp.exp(raw_scores * HEAD_DIM ** (-0.5) - log_total[..., None]), 0.0)


def score_grads(
    queries, keys_block, values_block, log_total, row_delta, out_grad, query_pos, key_pos
):
    probs_full = block_probs(queries, keys_block, log_total, query_pos, key_pos)
    prob_grad = jnp.einsum(
        "sqhe,skhe->shqk", out_grad, values_block, preferred_element_type=jnp.float32
    )
    score_grad = (probs_full * (prob_grad - row_delta[..., None]) * HEAD_DIM ** (-0.5)).astype(
        jnp.bfloat16
    )
    return (probs_full.astype(jnp.bfloat16), score_grad)


def key_slice(keys_all, offset, key_rows, head_count):
    seq_count = keys_all.shape[0]
    return lax.dynamic_slice_in_dim(keys_all, offset, key_rows, 1).reshape(
        seq_count, key_rows, head_count, HEAD_DIM
    )


def log_totals(queries, keys_all, query_pos, pos_table, key_rows):
    seq_count, query_rows, head_count, head_size = queries.shape
    turn_count = keys_all.shape[1] // key_rows

    def log_one_turn(turn_index, state_in):
        running_max, running_sum = state_in
        offset = turn_index * key_rows
        keys_block = key_slice(keys_all, offset, key_rows, head_count)
        key_pos = lax.dynamic_slice_in_dim(pos_table, offset, key_rows, 1)
        raw_scores = jnp.einsum(
            "sqhe,skhe->shqk", queries, keys_block, preferred_element_type=jnp.float32
        ) * HEAD_DIM ** (-0.5)
        allowed = key_pos[:, None, None, :] <= query_pos[:, None, :, None]
        masked = jnp.where(allowed, raw_scores, -1e30)
        new_max = jnp.maximum(running_max, jnp.max(masked, axis=-1))
        kept_terms = jnp.where(allowed, jnp.exp(masked - new_max[..., None]), 0.0)
        return (
            new_max,
            running_sum * jnp.exp(running_max - new_max) + jnp.sum(kept_terms, axis=-1),
        )

    initial = (
        jnp.full((seq_count, head_count, query_rows), -1e30, jnp.float32),
        jnp.zeros((seq_count, head_count, query_rows), jnp.float32),
    )
    final_max, final_sum = lax.fori_loop(0, turn_count, log_one_turn, initial)
    return final_max + jnp.log(final_sum)


def attend_values(queries, keys_all, values_all, log_total, query_pos, pos_table, key_rows):
    head_count = queries.shape[2]
    turn_count = keys_all.shape[1] // key_rows

    def attend_one_turn(turn_index, running):
        offset = turn_index * key_rows
        keys_block = key_slice(keys_all, offset, key_rows, head_count)
        values_block = key_slice(values_all, offset, key_rows, head_count)
        key_pos = lax.dynamic_slice_in_dim(pos_table, offset, key_rows, 1)
        weights_low = block_probs(queries, keys_block, log_total, query_pos, key_pos).astype(
            jnp.bfloat16
        )
        return running + jnp.einsum(
            "shqk,skhe->sqhe", weights_low, values_block, preferred_element_type=jnp.float32
        )

    return lax.fori_loop(0, turn_count, attend_one_turn, jnp.zeros(queries.shape, jnp.float32))


def full_grads(
    queries, keys_all, values_all, log_total, row_delta, out_grad, query_pos, pos_table, key_rows
):
    seq_count, query_rows, head_count, head_size = queries.shape
    turn_count = keys_all.shape[1] // key_rows

    def full_one_turn(turn_index, state_in):
        query_grad, key_terms, value_terms = state_in
        offset = turn_index * key_rows
        keys_block = key_slice(keys_all, offset, key_rows, head_count)
        values_block = key_slice(values_all, offset, key_rows, head_count)
        key_pos = lax.dynamic_slice_in_dim(pos_table, offset, key_rows, 1)
        weights_low, score_grad = score_grads(
            queries, keys_block, values_block, log_total, row_delta, out_grad, query_pos, key_pos
        )
        query_grad = query_grad + jnp.einsum(
            "shqk,skhe->sqhe", score_grad, keys_block, preferred_element_type=jnp.float32
        )
        key_part = jnp.einsum(
            "shqk,sqhe->skhe", score_grad, queries, preferred_element_type=jnp.float32
        ).reshape(seq_count, key_rows, head_count * head_size)
        value_part = jnp.einsum(
            "shqk,sqhe->skhe", weights_low, out_grad, preferred_element_type=jnp.float32
        ).reshape(seq_count, key_rows, head_count * head_size)
        key_terms = lax.dynamic_update_slice_in_dim(key_terms, key_part, offset, 1)
        value_terms = lax.dynamic_update_slice_in_dim(value_terms, value_part, offset, 1)
        return (query_grad, key_terms, value_terms)

    initial = (
        jnp.zeros(queries.shape, jnp.float32),
        jnp.zeros(keys_all.shape, jnp.float32),
        jnp.zeros(values_all.shape, jnp.float32),
    )
    return lax.fori_loop(0, turn_count, full_one_turn, initial)


def general_local(
    tokens,
    pair_index,
    norm_gain,
    norm_shift,
    w_attention_in,
    w_attention_out,
    w_expand,
    w_contract,
    cotangent,
):
    seq_count, shard_rows, model_width = tokens.shape
    gain_full, shift_full, attention_in, attention_out, expand_full, contract_full = (
        lax.all_gather(norm_gain, "ctx", axis=0, tiled=True),
        lax.all_gather(norm_shift, "ctx", axis=0, tiled=True),
        lax.all_gather(w_attention_in, "ctx", axis=1, tiled=True),
        lax.all_gather(w_attention_out, "ctx", axis=1, tiled=True),
        lax.all_gather(w_expand, "ctx", axis=0, tiled=True),
        lax.all_gather(w_contract, "ctx", axis=1, tiled=True),
    )
    local_width = attention_in.shape[2]
    head_count = local_width // HEAD_DIM
    flat_rows = seq_count * shard_rows
    pos_table = position_table(pair_index, shard_rows)
    total_rows = pos_table.shape[1]
    own_pos = lax.dynamic_slice_in_dim(pos_table, lax.axis_index("ctx") * shard_rows, shard_rows, 1)
    key_rows = min(total_rows, 1024)
    inputs = tokens.astype(jnp.float32)
    normed_full, norm_pull = jax.vjp(
        layer_norm, inputs, gain_full.astype(jnp.float32), shift_full.astype(jnp.float32)
    )
    normed = normed_full.astype(jnp.bfloat16).reshape(flat_rows, model_width)
    projected = jnp.einsum("td,kde->kte", normed, attention_in, preferred_element_type=jnp.float32)
    split_heads = projected.reshape(3, seq_count, shard_rows, head_count, HEAD_DIM)
    rotated, rotate_pull = jax.vjp(lambda pair_part: rotate(pair_part, own_pos), split_heads[:2])
    queries = rotated[0].astype(jnp.bfloat16)
    own_keys = rotated[1].astype(jnp.bfloat16)
    own_values = split_heads[2].astype(jnp.bfloat16)
    keys_all, values_all = (
        lax.all_gather(
            own_keys.reshape(seq_count, shard_rows, local_width), "ctx", axis=1, tiled=True
        ),
        lax.all_gather(
            own_values.reshape(seq_count, shard_rows, local_width), "ctx", axis=1, tiled=True
        ),
    )
    log_total = log_totals(queries, keys_all, own_pos, pos_table, key_rows)
    attended = attend_values(queries, keys_all, values_all, log_total, own_pos, pos_table, key_rows)
    mixed = attended.reshape(flat_rows, local_width).astype(jnp.bfloat16)
    hidden_pre = jnp.dot(normed, expand_full, preferred_element_type=jnp.float32)
    activated_full, gelu_pull = jax.vjp(gelu_tanh, hidden_pre)
    activated = activated_full.astype(jnp.bfloat16)
    branch = jnp.dot(mixed, attention_out, preferred_element_type=jnp.float32) + jnp.dot(
        activated, contract_full, preferred_element_type=jnp.float32
    )
    branch = lax.psum(branch.astype(jnp.bfloat16), "tp").astype(jnp.float32)
    output = (inputs + branch.reshape(seq_count, shard_rows, model_width)).astype(jnp.bfloat16)
    upstream = cotangent.reshape(flat_rows, model_width)
    contract_grad = jnp.einsum("tf,td->fd", activated, upstream, preferred_element_type=jnp.float32)
    (gelu_grad,) = gelu_pull(
        jnp.einsum("td,fd->tf", upstream, contract_full, preferred_element_type=jnp.float32)
    )
    hidden_grad = gelu_grad.astype(jnp.bfloat16)
    expand_grad = jnp.einsum("td,tf->df", normed, hidden_grad, preferred_element_type=jnp.float32)
    mixed_grad = jnp.einsum(
        "td,ed->te", upstream, attention_out, preferred_element_type=jnp.float32
    ).astype(jnp.bfloat16)
    attention_out_grad = jnp.einsum(
        "te,td->ed", mixed, upstream, preferred_element_type=jnp.float32
    )
    out_grad = mixed_grad.reshape(seq_count, shard_rows, head_count, HEAD_DIM)
    row_delta = jnp.sum(out_grad.astype(jnp.float32) * attended, axis=-1).transpose(0, 2, 1)
    query_grad, key_terms, value_terms = full_grads(
        queries, keys_all, values_all, log_total, row_delta, out_grad, own_pos, pos_table, key_rows
    )
    key_grad, value_grad = (
        lax.psum_scatter(
            key_terms.astype(jnp.bfloat16), "ctx", scatter_dimension=1, tiled=True
        ).astype(jnp.float32),
        lax.psum_scatter(
            value_terms.astype(jnp.bfloat16), "ctx", scatter_dimension=1, tiled=True
        ).astype(jnp.float32),
    )
    key_grad = key_grad.reshape(seq_count, shard_rows, head_count, HEAD_DIM)
    value_grad = value_grad.reshape(seq_count, shard_rows, head_count, HEAD_DIM)
    (rotated_grad,) = rotate_pull(jnp.stack([query_grad, key_grad]))
    projected_grad = (
        jnp.concatenate([rotated_grad, value_grad[None]], axis=0)
        .reshape(3, flat_rows, local_width)
        .astype(jnp.bfloat16)
    )
    attention_in_grad = jnp.einsum(
        "td,kte->kde", normed, projected_grad, preferred_element_type=jnp.float32
    )
    normed_grad = jnp.einsum(
        "kte,kde->td", projected_grad, attention_in, preferred_element_type=jnp.float32
    )
    normed_grad = normed_grad + jnp.einsum(
        "tf,df->td", hidden_grad, expand_full, preferred_element_type=jnp.float32
    )
    normed_grad = lax.psum(normed_grad.astype(jnp.bfloat16), "tp").astype(jnp.float32)
    input_part, gain_grad, shift_grad = norm_pull(
        normed_grad.reshape(seq_count, shard_rows, model_width)
    )
    input_grad = input_part + cotangent.astype(jnp.float32)
    reduced = (
        lax.psum_scatter(
            gain_grad.astype(jnp.bfloat16), "ctx", scatter_dimension=0, tiled=True
        ).astype(jnp.float32),
        lax.psum_scatter(
            shift_grad.astype(jnp.bfloat16), "ctx", scatter_dimension=0, tiled=True
        ).astype(jnp.float32),
        lax.psum_scatter(
            attention_in_grad.astype(jnp.bfloat16), "ctx", scatter_dimension=1, tiled=True
        ).astype(jnp.float32),
        lax.psum_scatter(
            attention_out_grad.astype(jnp.bfloat16), "ctx", scatter_dimension=1, tiled=True
        ).astype(jnp.float32),
        lax.psum_scatter(
            expand_grad.astype(jnp.bfloat16), "ctx", scatter_dimension=0, tiled=True
        ).astype(jnp.float32),
        lax.psum_scatter(
            contract_grad.astype(jnp.bfloat16), "ctx", scatter_dimension=1, tiled=True
        ).astype(jnp.float32),
    )
    return (
        output,
        input_grad,
        reduced[0],
        reduced[1],
        reduced[2],
        reduced[3],
        reduced[4],
        reduced[5],
    )


MESH = pl.DeviceIdType.MESH
MB = 1 << 20
EPS = 1e-05
BF = jnp.bfloat16
F4 = jnp.float32
NT = (((1,), (1,)), ((), ()))
FAR = (1, 2, 3, 0)


def place():
    c = lax.axis_index("ctx")
    t = lax.axis_index("tp")
    return c // 2, c % 2, t // 2, t % 2


def device(z, x, y, k):
    return (z * 2 + x, y * 2 + k)


def remote(src, dst, send_sem, recv_sem, target):
    return pltpu.make_async_remote_copy(
        src_ref=src, dst_ref=dst, send_sem=send_sem, recv_sem=recv_sem,
        device_id=target, device_id_type=MESH,
    )


def meet(peers):
    barrier = pltpu.get_barrier_semaphore()
    for peer in peers:
        pl.semaphore_signal(barrier, inc=1, device_id=peer, device_id_type=MESH)
    pl.semaphore_wait(barrier, len(peers))


def peers_of(z, x, y, k):
    c = z * 2 + x
    others = [((c + i) % 8, lax.axis_index("tp")) for i in range(1, 8)]
    return others, others + [device(z, x, 1 - y, k), device(z, x, y, 1 - k)]


def columns(n, i):
    return pl.ds(pl.multiple_of(n * i, n), n)


def dot(a, b):
    return jnp.dot(a, b, preferred_element_type=F4)


def dot_t(a, b):
    return lax.dot_general(a, b, NT, preferred_element_type=F4)


def mirrored(z, e):
    return jnp.where(z < 2, 4 - e, e) if e in (1, 3) else e


def far_first(z, i):
    return (3 * (1 - z // 2), z // 2 + 2 * (1 - z % 2), 1 + z % 2, z)[i]


def add_into(dst, src):
    lead, rows = dst.shape[:-2], dst.shape[-2]
    for idx in itertools.product(*(range(n) for n in lead)):
        @pl.loop(0, rows // 16)
        def _(i):
            at = idx + (pl.ds(pl.multiple_of(16 * i, 16), 16), slice(None))
            dst[at] = (dst[at].astype(F4) + src[at].astype(F4)).astype(BF)


class TokenGather:
    def __init__(self, whole, sems):
        self.whole = whole
        self.xs, self.xr, self.zs, self.zr, self.ys, self.yr, self.cs, self.cr = sems
        self.z, self.x, self.y, self.k = place()
        self.q = 2 * self.y + self.k

    def chunk(self, zz, s, q):
        xx = self.x if s == 0 else 1 - self.x
        return self.whole.at[zz, xx, pl.ds(64 * q, 64), :]

    def send_x(self, src):
        z, x, y, k = self.z, self.x, self.y, self.k
        return remote(src, self.whole.at[z, x, pl.ds(64 * self.q, 64), :], self.xs, self.xr, device(z, 1 - x, y, k))

    def send_up(self, zz, s, src):
        return remote(src, self.chunk(zz, s, self.q), self.zs.at[zz, s, 0], self.zr.at[zz, s],
                      device(jnp.minimum(self.z + 1, 3), self.x, self.y, self.k))

    def send_down(self, zz, s, src):
        return remote(src, self.chunk(zz, s, self.q), self.zs.at[zz, s, 1], self.zr.at[zz, s],
                      device(jnp.maximum(self.z - 1, 0), self.x, self.y, self.k))

    def send_y(self, zz, s):
        c = self.chunk(zz, s, self.q)
        return remote(c, c, self.ys.at[zz, s], self.yr.at[zz, s], device(self.z, self.x, 1 - self.y, self.k))

    def send_core(self, zz, s, j):
        yy = self.y if j == 0 else 1 - self.y
        c = self.chunk(zz, s, 2 * yy + self.k)
        return remote(c, c, self.cs.at[zz, s, j], self.cr.at[zz, s, j], device(self.z, self.x, self.y, 1 - self.k))

    def both_ways(self, s, src):
        z = self.z

        @pl.when(z < 3)
        def _():
            self.send_up(z, s, src).start()

        @pl.when(z > 0)
        def _():
            self.send_down(z, s, src).start()

    def start(self, own_quarter, other_quarter):
        self.send_x(other_quarter).start()
        self.both_ways(0, own_quarter)

    def after_x(self):
        c = self.chunk(self.z, 1, self.q)
        remote(c, c, self.xs, self.xr, device(self.z, 1 - self.x, self.y, self.k)).wait_recv()
        self.both_ways(1, c)
        self.send_y(self.z, 1).start()
        self.send_core(self.z, 1, 0).start()

    def hop(self, d, s):
        z = self.z

        @pl.when(z >= d)
        def _():
            zz = z - d
            c = self.chunk(zz, s, self.q)
            self.send_down(zz, s, c).wait_recv()

            @pl.when(z < 3)
            def _():
                self.send_up(zz, s, c).start()

            self.send_y(zz, s).start()
            self.send_core(zz, s, 0).start()

        @pl.when(z + d <= 3)
        def _():
            zz = z + d
            c = self.chunk(zz, s, self.q)
            self.send_up(zz, s, c).wait_recv()

            @pl.when(z > 0)
            def _():
                self.send_down(zz, s, c).start()

            self.send_y(zz, s).start()
            self.send_core(zz, s, 0).start()

    def y_in(self, zz, s):
        c = self.chunk(zz, s, 2 * (1 - self.y) + self.k)
        remote(c, c, self.ys.at[zz, s], self.yr.at[zz, s], device(self.z, self.x, 1 - self.y, self.k)).wait_recv()
        self.send_core(zz, s, 1).start()

    def y_hop(self, d):
        z = self.z
        if d == 0:
            self.y_in(z, 1)
            return
        for s in range(2):
            pl.when(z >= d)(lambda: self.y_in(z - d, s))
            pl.when(z + d <= 3)(lambda: self.y_in(z + d, s))

    def landed(self, zz):
        def rest(s):
            for j in range(2):
                yy = self.y if j == 0 else 1 - self.y
                c = self.chunk(zz, s, 2 * yy + 1 - self.k)
                remote(c, c, self.cs.at[zz, s, j], self.cr.at[zz, s, j], device(self.z, self.x, self.y, 1 - self.k)).wait_recv()

        pl.when(self.z != zz)(lambda: rest(0))
        rest(1)

    def sent_own(self, own_quarter, other_quarter):
        z = self.z
        self.send_x(other_quarter).wait_send()
        pl.when(z < 3)(lambda: self.send_up(z, 0, own_quarter).wait_send())
        pl.when(z > 0)(lambda: self.send_down(z, 0, own_quarter).wait_send())

    def finish(self):
        z = self.z
        for zz in range(4):
            for s in range(2):
                def rest():
                    self.send_y(zz, s).wait_send()
                    for j in range(2):
                        self.send_core(zz, s, j).wait_send()
                if s == 0:
                    pl.when(z != zz)(rest)
                else:
                    rest()
                c = self.chunk(zz, s, self.q)

                pl.when((z < 3) & (zz < z + s))(lambda: self.send_up(zz, s, c).wait_send())
                pl.when((z > 0) & (zz > z - s))(lambda: self.send_down(zz, s, c).wait_send())


def token_sems():
    D = pltpu.SemaphoreType.DMA
    return [D, D, D((4, 2, 2)), D((4, 2)), D((4, 2)), D((4, 2)), D((4, 2, 2)), D((4, 2, 2))]


class WeightGather:
    def __init__(self, pairs, sems):
        self.pairs = pairs
        self.zs, self.zr, self.xs, self.xr, self.loc = sems
        self.z, self.x, self.y, self.k = place()

    def z_send(self, d, w):
        src, dst = self.pairs[w]
        to = (self.z + d) % 4
        return remote(src(to), dst(self.z, self.x), self.zs.at[d, w], self.zr.at[d, w], device(to, self.x, self.y, self.k))

    def z_recv(self, d, w):
        dst = self.pairs[w][1]
        frm = (self.z - d + 4) % 4
        return remote(dst(frm, self.x), dst(frm, self.x), self.zs.at[d, w], self.zr.at[d, w], device(frm, self.x, self.y, self.k))

    def x_send(self, d, w):
        src, dst = self.pairs[w]
        frm = (self.z - d + 4) % 4
        s = src(self.z) if isinstance(d, int) and d == 0 else dst(frm, self.x)
        return remote(s, dst(frm, self.x), self.xs.at[d, w], self.xr.at[d, w], device(self.z, 1 - self.x, self.y, self.k))

    def x_recv(self, d, w):
        frm = (self.z - d + 4) % 4
        r = self.pairs[w][1](frm, 1 - self.x)
        return remote(r, r, self.xs.at[d, w], self.xr.at[d, w], device(self.z, 1 - self.x, self.y, self.k))

    def local(self, w):
        src, dst = self.pairs[w]
        return pltpu.make_async_copy(src(self.z), dst(self.z, self.x), self.loc.at[w])

    def send(self, ws, e):
        d = mirrored(self.z, e)
        for w in ws:
            if e:
                self.z_send(d, w).start()
            else:
                self.x_send(0, w).start()
                self.local(w).start()

    def forward(self, ws, e):
        d = mirrored(self.z, e)
        for w in ws:
            self.z_recv(d, w).wait_recv()
            self.x_send(d, w).start()

    def landed(self, w):
        self.local(w).wait()
        for d in range(4):
            self.x_recv(d, w).wait_recv()

    def finish(self, w):
        for d in range(4):
            if d:
                self.z_send(d, w).wait_send()
            self.x_send(d, w).wait_send()


def weight_sems(n):
    D = pltpu.SemaphoreType.DMA
    return [D((4, n)), D((4, n)), D((4, n)), D((4, n)), D((n,))]


class TokenReduce:
    def __init__(self, out, bufs, sems):
        self.out = out
        self.S, self.r1, self.r2, self.rz, self.rf = bufs
        (self.cs, self.cr, self.ys, self.yr, self.zs, self.zr, self.xs, self.xr,
         self.fl, self.fys, self.fyr, self.fcs, self.fcr) = sems
        self.z, self.x, self.y, self.k = place()
        self.q = 2 * self.y + self.k

    def slot(self, s):
        return self.x if s == 0 else 1 - self.x

    def core(self, i, slot=0):
        zz = far_first(self.z, i)
        return remote(self.S.at[slot], self.r1.at[zz], self.cs.at[zz], self.cr.at[zz], device(self.z, self.x, self.y, 1 - self.k))

    def yex(self, zz, s):
        xx = self.slot(s)
        return remote(self.r1.at[zz, 1 - self.y, xx], self.r2.at[zz, xx], self.ys.at[zz, s], self.yr.at[zz, s],
                      device(self.z, self.x, 1 - self.y, self.k))

    def mine(self, zz, s):
        return self.r1.at[zz, self.y, self.slot(s)]

    def up(self, zz, s):
        return remote(self.mine(zz, s), self.rz.at[zz, s], self.zs.at[zz, s], self.zr.at[zz, s],
                      device(jnp.minimum(self.z + 1, 3), self.x, self.y, self.k))

    def down(self, zz, s):
        slot = jnp.where(zz == self.z - 1, 4, zz)
        return remote(self.mine(zz, s), self.rz.at[slot, s], self.zs.at[zz, s], self.zr.at[slot, s],
                      device(jnp.maximum(self.z - 1, 0), self.x, self.y, self.k))

    def arrive(self, zz, s, slot):
        r = self.rz.at[slot, s]
        remote(r, r, self.zs.at[0, s], self.zr.at[slot, s], device(self.z, self.x, self.y, 1 - self.k)).wait_recv()
        add_into(self.mine(zz, s), r)

    def xex(self):
        return remote(self.mine(self.z, 1), self.rf, self.xs, self.xr, device(self.z, 1 - self.x, self.y, self.k))

    def rows(self, i, kk, lhs):
        zz = far_first(self.z, i)
        return jnp.concatenate([lhs(zz, xx, 64 * (2 * yy + kk)) for yy in range(2) for xx in range(2)], axis=0)

    def fill(self, i, slot, lhs, rhs):
        a = self.rows(i, 1 - self.k, lhs)

        @pl.loop(0, 4)
        def _(j):
            at = columns(512, j)
            self.S[slot, :, :, :, at] = rhs(a, j).astype(BF).reshape(2, 2, 64, 512)
        self.core(i, slot).start()

    def after_core(self, i, lhs, rhs):
        zz = far_first(self.z, i)
        a = self.rows(i, self.k, lhs)
        self.core(i).wait_recv()

        @pl.loop(0, 4)
        def _(j):
            at = columns(512, j)
            got = self.r1[zz, :, :, :, at].reshape(256, 512).astype(F4)
            self.r1[zz, :, :, :, at] = (rhs(a, j) + got).astype(BF).reshape(2, 2, 64, 512)
        for s in (1, 0):
            self.yex(zz, s).start()

    def line(self, i, s):
        z = self.z
        zz = far_first(z, i)
        self.yex(zz, s).wait_recv()
        add_into(self.mine(zz, s), self.r2.at[zz, self.slot(s)])
        if i < 3:
            @pl.when(zz > z)
            def _():
                pl.when(z > 0)(lambda: self.arrive(zz, s, zz))
                self.up(zz, s).start()

            @pl.when(zz < z)
            def _():
                pl.when(z < 3)(lambda: self.arrive(zz, s, zz))
                self.down(zz, s).start()
        else:
            pl.when(z > 0)(lambda: self.arrive(z, s, z))
            pl.when(z < 3)(lambda: self.arrive(z, s, 4))
            if s == 1:
                self.xex().start()

    def spot(self, s, q):
        return self.out.at[self.slot(s), pl.ds(64 * q, 64), :]

    def fin_copies(self, s):
        src = self.mine(self.z, 0) if s == 0 else self.rf
        here = self.spot(s, self.q)
        return (pltpu.make_async_copy(src, here, self.fl.at[s]),
                remote(src, here, self.fys.at[s], self.fyr.at[s], device(self.z, self.x, 1 - self.y, self.k)),
                remote(src, here, self.fcs.at[s, 0], self.fcr.at[s, 0], device(self.z, self.x, self.y, 1 - self.k)))

    def relay(self, s):
        r = self.spot(s, 2 * (1 - self.y) + self.k)
        return remote(r, r, self.fcs.at[s, 1], self.fcr.at[s, 1], device(self.z, self.x, self.y, 1 - self.k))

    def spread(self, s, base=None):
        if s == 1:
            self.xex().wait_recv()
        if base is not None:
            add_into(self.mine(self.z, 0) if s == 0 else self.rf, base(self.slot(s), pl.ds(64 * self.q, 64)))
        for cp in self.fin_copies(s):
            cp.start()

    def spread_y(self, s):
        r = self.spot(s, 2 * (1 - self.y) + self.k)
        remote(r, r, self.fys.at[s], self.fyr.at[s], device(self.z, self.x, 1 - self.y, self.k)).wait_recv()
        self.relay(s).start()

    def finish(self):
        z = self.z
        for zz in range(4):
            for s in range(2):
                self.yex(zz, s).wait_send()
                pl.when(z != zz)(lambda: self.up(zz, s).wait_send())
        self.xex().wait_send()
        for s in range(2):
            for copy in self.fin_copies(s)[1:]:
                copy.wait_send()
            self.relay(s).wait_send()

    def landed(self, s):
        self.fin_copies(s)[0].wait()
        for j, yy in ((0, self.y), (1, 1 - self.y)):
            r = self.spot(s, 2 * yy + 1 - self.k)
            remote(r, r, self.fcs.at[s, j], self.fcr.at[s, j], device(self.z, self.x, self.y, 1 - self.k)).wait_recv()


def reduce_sems():
    D = pltpu.SemaphoreType.DMA
    return [D((4,)), D((4,)), D((4, 2)), D((4, 2)), D((4, 2)), D((5, 2)), D, D,
            D((2,)), D((2,)), D((2,)), D((2, 2)), D((2, 2))]


def reduce_bufs():
    V = lambda *s: pltpu.VMEM(s, BF)
    return [V(4, 2, 2, 64, 2048), V(4, 2, 64, 2048), V(5, 2, 64, 2048), V(64, 2048)]


class GradReduce:
    def __init__(self, parts, away, got, sems):
        self.parts, self.away, self.got = parts, away, got
        self.xs, self.xr, self.zs, self.zr = sems
        self.z, self.x, self.y, self.k = place()

    def x_send(self, e):
        i = FAR.index(e)
        return remote(self.away.at[i % 2], self.got.at[i], self.xs.at[i], self.xr.at[i], device(self.z, 1 - self.x, self.y, self.k))

    def z_sends(self, e):
        d = mirrored(self.z, e)
        for i, (part, there) in enumerate(self.parts):
            src, dst = self.got.at[(FAR.index(e),) + part], there(self.z)
            if e == 0:
                yield pltpu.make_async_copy(src, dst, self.zs.at[0, i])
            else:
                yield remote(src, dst, self.zs.at[d, i], self.zr.at[d, i], device((self.z + d) % 4, self.x, self.y, self.k))

    def give(self, e, terms):
        i = FAR.index(e)
        if i >= 2:
            self.x_send(FAR[i - 2]).wait_send()
        self.away[i % 2] = terms.astype(BF)
        self.x_send(e).start()

    def keep(self, e, terms):
        i = FAR.index(e)
        self.x_send(e).wait_recv()
        self.got[i] = (terms + self.got[i].astype(F4)).astype(BF)
        for cp in self.z_sends(e):
            cp.start()

    def finish(self):
        for cp in self.z_sends(0):
            cp.wait()
        for e in FAR[2:]:
            self.x_send(e).wait_send()
        for d in range(1, 4):
            frm = (self.z - d + 4) % 4
            for cp in self.z_sends(d):
                cp.wait_send()
            for i, (part, there) in enumerate(self.parts):
                r = there(frm)
                remote(r, r, self.zs.at[d, i], self.zr.at[d, i], device(frm, self.x, self.y, self.k)).wait_recv()


def grad_scratch(block, parts):
    D = pltpu.SemaphoreType.DMA
    V = pltpu.VMEM
    return [V((2,) + block, BF), V((4,) + block, BF)] + [D((4,))] * 2 + [D((4, parts))] * 2


def norm_rows(rows, gain, shift):
    v = rows.astype(F4)
    centred = v - jnp.mean(v, axis=-1, keepdims=True)
    spread = jnp.mean(centred * centred, axis=-1, keepdims=True)
    return (centred * lax.rsqrt(spread + EPS) * gain + shift).astype(BF)


def turn(v, tab):
    cos, lo, hi = tab
    return v * cos + pltpu.roll(v, 112, 1) * lo + pltpu.roll(v, 16, 1) * hi


def turn_back(v, tab):
    cos, lo, hi = tab
    return v * cos - pltpu.roll(v, 112, 1) * lo - pltpu.roll(v, 16, 1) * hi


def angle_table(within, cb, sb):
    cr, sr = within[0], within[1]
    cos, sin = cb * cr - sb * sr, sb * cr + cb * sr
    entry = lax.broadcasted_iota(jnp.int32, cos.shape, 1) % 64
    return cos, jnp.where(entry < 16, -sin, 0.0), jnp.where(entry < 16, 0.0, sin)


def angles(rows, step):
    frequency = (10000.0 ** (-2.0 * np.arange(16) / 32)).astype(np.float32).astype(np.float64)
    lanes = np.concatenate([frequency, frequency, np.zeros(32)] * 2)
    angle = step * np.arange(rows)[:, None] * lanes
    return np.stack([np.cos(angle), np.sin(angle)]).astype(np.float32)


def pick(index, parts):
    chosen = parts(0)
    for j in range(1, 8):
        chosen = jnp.where(index == j, parts(j), chosen)
    return chosen


def one_head(v, h, axis):
    entry = lax.broadcasted_iota(jnp.int32, v.shape, axis)
    return jnp.where((entry < 64) == (h == 0), v, jnp.zeros_like(v))


def masked(st, kr):
    row = lax.broadcasted_iota(jnp.int32, (256, 256), 0)
    column = lax.broadcasted_iota(jnp.int32, (256, 256), 1)
    last = jnp.where(row <= column, st[kr - 256:], -1e30)
    return last if kr == 256 else jnp.concatenate([st[:kr - 256], last], axis=0)


def flip(v):
    return v.astype(F4).T.astype(BF)


def norm_backward(s, tok, cot, ng, gains, out, stage, ssem, sums):
    gain = jnp.concatenate([gains[i, 0:1, :] for i in range(8)], axis=1)

    def store(i):
        return pltpu.make_async_copy(stage.at[i % 2], out.at[s, pl.ds(pl.multiple_of(32 * i, 32), 32)], ssem.at[i % 2])

    @pl.loop(0, 8)
    def _(i):
        at = pl.ds(pl.multiple_of(32 * i, 32), 32)
        v = tok[s, at].astype(F4)
        centred = v - jnp.mean(v, axis=-1, keepdims=True)
        scale = lax.rsqrt(jnp.mean(centred * centred, axis=-1, keepdims=True) + EPS)
        xhat = centred * scale
        n = ng[s, at].astype(F4)
        g = n * gain
        along = jnp.mean(g * xhat, axis=-1, keepdims=True)

        @pl.when(i >= 2)
        def _():
            store(i - 2).wait()
        stage[i % 2] = cot[s, at].astype(F4) + (g - jnp.mean(g, axis=-1, keepdims=True) - xhat * along) * scale
        store(i).start()
        both = n * xhat
        sums[0] += both[:8] + both[8:16] + both[16:24] + both[24:]
        sums[1] += n[:8] + n[8:16] + n[16:24] + n[24:]

    store(6).wait()
    store(7).wait()


(
    START, NORM, SEND, PASS, HAVE, OPEN, CROSS, HOP, TWIN, PROJECT, ARRANGE, ATTEND, MIX, SLOPE, TURN, RETURN, PROJECTED, HIDDEN,
    PULL, FILL, CORE, LINE, SPREAD, RELAY, DONE, GIVE, KEEP, LAST, GRADIENTS,
) = range(29)
ORDER = (
    (START,), (SEND, 0, 2), (SEND, 0, 1), (SEND, 1, 1), (SEND, 0, 3), (SEND, 0, 0), (NORM,), (SEND, 1, 0), (OPEN, 0), (CROSS, 0),
    (TWIN, 0, 0), (SEND, 1, 2), (SEND, 2, 0), (HOP, 0, 1, 0), (PASS, 0, 2), (HOP, 0, 1, 1), (SEND, 1, 3), (PASS, 1, 3),
    (HOP, 0, 2, 0), (PASS, 0, 3), (OPEN, 1), (PASS, 0, 1), (HOP, 0, 2, 1), (HOP, 0, 3, 0), (CROSS, 1), (TWIN, 0, 2), (HOP, 0, 3, 1),
    (TWIN, 0, 3), (SEND, 2, 2), (PASS, 1, 2), (HOP, 1, 1, 0), (TWIN, 0, 1), (SEND, 2, 1), (HAVE, 0), (PROJECT, 0), (PROJECT, 1),
    (SEND, 2, 3), (PASS, 1, 1), (PROJECT, 2), (PROJECT, 3), (ARRANGE,), (HAVE, 1), (HIDDEN, 0), (HOP, 1, 1, 1), (HIDDEN, 1),
    (TWIN, 1, 0), (PASS, 2, 1), (ATTEND, 0), (PASS, 2, 2), (ATTEND, 1), (ATTEND, 2), (ATTEND, 3), (ATTEND, 4), (HOP, 1, 2, 1),
    (HOP, 1, 2, 0), (HAVE, 3), (ATTEND, 5), (PASS, 2, 3), (TWIN, 1, 1), (ATTEND, 6), (HIDDEN, 2), (ATTEND, 7), (SLOPE, 0), (MIX,),
    (HOP, 1, 3, 1), (SLOPE, 1), (HAVE, 2), (FILL, 1, 0), (FILL, 1, 1), (TWIN, 1, 2), (HOP, 1, 3, 0), (HIDDEN, 3), (CORE, 1, 0),
    (CORE, 1, 1), (TWIN, 1, 3), (FILL, 1, 2), (SLOPE, 2), (SLOPE, 3), (TURN,), (RETURN, 0), (PULL, 0), (RETURN, 1), (RETURN, 2),
    (LINE, 1, 0, 0), (RETURN, 3), (CORE, 1, 2), (LINE, 1, 0, 1), (RETURN, 4), (RETURN, 5), (RETURN, 6), (LINE, 1, 1, 0), (RETURN, 7),
    (LINE, 1, 1, 1), (PROJECTED,), (FILL, 0, 0), (GIVE, 0, 1), (LINE, 1, 2, 0), (GIVE, 0, 2), (FILL, 1, 3), (CORE, 0, 0),
    (LINE, 1, 2, 1), (PULL, 1), (FILL, 0, 1), (KEEP, 0, 1), (GIVE, 0, 3), (GIVE, 0, 0), (CORE, 0, 1), (KEEP, 0, 2), (PULL, 2),
    (PULL, 3), (GIVE, 1, 1), (GIVE, 1, 2), (LINE, 0, 0, 1), (CORE, 1, 3), (FILL, 0, 2), (FILL, 0, 3), (GIVE, 1, 3), (LINE, 0, 0, 0),
    (CORE, 0, 2), (LINE, 1, 3, 1), (KEEP, 1, 1), (LINE, 0, 1, 1), (LINE, 0, 1, 0), (LINE, 1, 3, 0), (KEEP, 0, 3), (CORE, 0, 3),
    (LINE, 0, 2, 1), (SPREAD, 1, 1), (LINE, 0, 2, 0), (SPREAD, 1, 0), (KEEP, 1, 3), (LINE, 0, 3, 1), (LINE, 0, 3, 0), (SPREAD, 0, 0),
    (KEEP, 1, 2), (GIVE, 1, 0), (KEEP, 0, 0), (RELAY, 1, 1), (DONE, 1, 1), (RELAY, 0, 0), (DONE, 0, 0), (SPREAD, 0, 1), (LAST, 0),
    (KEEP, 1, 0), (RELAY, 1, 0), (RELAY, 0, 1), (DONE, 1, 0), (DONE, 0, 1), (LAST, 1), (GRADIENTS,),
)


def block_kernel(pairs_of, gains, within, block, tok, cot, win, wout, wexp, wcon,
                 out, ig, vectors, gin, gout, gexp, gcon, xn, ct,
                 wx, wco, hp, am, S, ctr, ng, gs, gs_all, vec, vecs,
                 gsem_s, gsem_r, lsem, rsem, csem, ssem, vs, vr, *rest):
    z, x, y, k = place()
    c, q = z * 2 + x, 2 * y + k
    rest = list(rest)
    take = lambda n: [rest.pop(0) for _ in range(n)]
    nt, nb, ns = len(token_sems()), len(reduce_bufs()), len(reduce_sems())
    tx = TokenGather(xn, take(nt))
    tc = TokenGather(ct, take(nt))
    pairs = [
        (lambda zz, j=j: win.at[j, :, columns(128, zz)], lambda zz, xx, j=j: wx.at[zz, xx, :, pl.ds(512 + 128 * j, 128)])
        for j in range(3)
    ] + [
        (lambda zz: wexp.at[:, columns(512, zz)], lambda zz, xx: wx.at[zz, xx, :, pl.ds(0, 512)]),
        (lambda zz: wcon.at[columns(512, zz), :], lambda zz, xx: wco.at[pl.ds(0, 512), columns(256, zz * 2 + xx)]),
        (lambda zz: wout.at[columns(128, zz), :], lambda zz, xx: wco.at[pl.ds(512, 128), columns(256, zz * 2 + xx)]),
    ]
    wg = WeightGather(pairs, take(len(weight_sems(6))))
    tn = TokenReduce(ng, [S] + take(nb), take(ns))
    to = TokenReduce(out, [S] + take(nb), take(ns))
    whole = slice(None)
    g1 = GradReduce([((pl.ds(0, 512), whole), lambda zz: gcon.at[columns(512, zz), :]),
                     ((pl.ds(512, 128), whole), lambda zz: gout.at[columns(128, zz), :])], *take(2), take(4))
    g2 = GradReduce([((whole, pl.ds(0, 512)), lambda zz: gexp.at[:, columns(512, zz)])]
                    + [((whole, pl.ds(512 + 128 * j, 128)), lambda zz, j=j: gin.at[j, :, columns(128, zz)]) for j in range(3)],
                    *take(2), take(4))
    others, everyone = peers_of(z, x, y, k)

    def pair_at(slot):
        return pairs_of[x, slot]

    def slot_of(pair):
        found = jnp.int32(0)
        for j in range(8):
            found = jnp.where(pairs_of[x, j] == pair, j, found)
        return found


    V = pltpu.VMEM
    steps = {}
    flags = set()
    load_tok = lambda: pltpu.make_async_copy(tok, ctr.at[0], lsem.at[0])
    load_cot = lambda: pltpu.make_async_copy(cot, ctr.at[1], lsem.at[1])
    xl, xo, cl = ctr.at[1, 0], S.at[0, 0, 0], ctr.at[1, 1]
    near_cot = lambda: pltpu.make_async_copy(cot.at[x], cl, lsem.at[1])
    own_cot = lambda: pltpu.make_async_copy(cl, ct.at[z, x], lsem.at[2])
    own_xn = lambda: pltpu.make_async_copy(xl, xn.at[z, x], lsem.at[3])
    gcopies = lambda: [remote(gs, gs_all.at[c], gsem_s.at[i], gsem_r.at[i], others[i]) for i in range(7)]
    mine, cot_mine = xl.at[pl.ds(64 * q, 64)], cot.at[x, pl.ds(64 * q, 64)]
    cot_other = cot.at[1 - x, pl.ds(64 * q, 64)]

    def once(name, act):
        if name not in flags:
            flags.add(name)
            act()

    users = [n for n in ORDER if n[0] in (PROJECT, SLOPE, HIDDEN, PULL)]

    def rows_in(n, xx):
        kind, i = users[n]
        zz = far_first(z, i if kind in (HIDDEN, PULL) else 3 - i)
        src = xn if kind in (PROJECT, HIDDEN) else ct
        return zz, pltpu.make_async_copy(src.at[zz, xx], ctr.at[n % 2, xx], rsem.at[n % 2, xx])

    def begin_rows(n):
        flags.add(n)
        for xx in range(2):
            rows_in(n, xx)[1].start()

    def each_half(name, act):
        n = users.index(name)
        if n not in flags:
            begin_rows(n)
        for xx in range(2):
            zz, cp = rows_in(n, xx)
            cp.wait()
            if name[0] in (PROJECT, SLOPE):
                act(zz, xx, ctr.at[n % 2, xx], pl.multiple_of(512 * zz + 256 * xx, 256))
        if name[0] in (HIDDEN, PULL):
            act(ctr.at[n % 2], pl.multiple_of(512 * zz, 512))
        flags.add(name)
        for m in (n + 1, n + 2):
            if m < len(users) and m not in flags and {HIDDEN: (PROJECT, 3), PULL: (SLOPE, 3)}.get(users[m][0]) in flags:
                begin_rows(m)
        if n + 1 == len(users):
            load_tok().start()
            load_cot().start()

    def start():
        load_tok().start()
        gs[...] = jnp.zeros_like(gs)
        gs[0:2, :] = gains[...]
        meet(everyone)
        for g in gcopies():
            g.start()
        gs_all[c] = gs[...]
        near_cot().start()

    def norm():
        for i in range(7):
            frm = gs_all.at[(c - i - 1 + 8) % 8]
            remote(frm, frm, gsem_s.at[i], gsem_r.at[i], others[i]).wait_recv()
        gain = jnp.concatenate([gs_all[i, 0:1, :] for i in range(8)], axis=1)
        shift = jnp.concatenate([gs_all[i, 1:2, :] for i in range(8)], axis=1)
        load_tok().wait()

        @pl.loop(0, 2)
        def _(i):
            xo[pl.ds(32 * i, 32)] = norm_rows(ctr[0, 1 - x, pl.ds(64 * q + 32 * i, 32)], gain, shift)

        @pl.loop(0, 8)
        def _(i):
            xl[pl.ds(32 * i, 32)] = norm_rows(ctr[0, x, pl.ds(32 * i, 32)], gain, shift)

        own_xn().start()
        near_cot().wait()
        own_cot().start()

    steps[START,], steps[NORM,] = start, norm
    for u, ws in enumerate(((0, 1, 2, 5), (3,), (4,))):
        for d in range(4):
            steps[SEND, u, d] = functools.partial(wg.send, ws, d)
            steps[PASS, u, d] = functools.partial(wg.forward, ws, d)
    for u, ws in enumerate(((0, 1, 2), (3,), (4,), (5,))):
        steps[HAVE, u] = functools.partial(lambda ws: [wg.landed(w) for w in ws], ws)
    steps[OPEN, 0] = lambda: tx.start(mine, xo)
    steps[OPEN, 1] = lambda: tc.start(cot_mine, cot_other)
    for name, t in enumerate((tx, tc)):
        steps[CROSS, name] = t.after_x
        for d in range(4):
            steps[TWIN, name, d] = functools.partial(t.y_hop, d)
            for s in range(2):
                steps[HOP, name, d, s] = functools.partial(t.hop, d, s)

    def hidden(rows, row):
        at = pl.ds(row, 512)
        u = dot(rows[...].reshape(512, 2048), wx[:, :, :, pl.ds(0, 512)].reshape(2048, 512))
        square = u * u
        t = jnp.tanh(0.7978845608028654 * (u + 0.044715 * u * square))
        half = 0.5 * (1.0 + t)
        am[at, pl.ds(0, 512)] = (u * half).astype(BF)
        hp[at, pl.ds(0, 512)] = (half + 0.5 * u * (1.0 - t * t) * (0.7978845608028654 * (1.0 + 3 * 0.044715 * square))).astype(BF)

    def pull(rows, row):
        at = (pl.ds(row, 512), pl.ds(0, 512))
        hp[at] = (dot_t(rows[...].reshape(512, 2048), wco[pl.ds(0, 512)]) * hp[at].astype(F4)).astype(BF)

    for i in range(4):
        steps[HIDDEN, i] = functools.partial(each_half, (HIDDEN, i), hidden)
        steps[PULL, i] = functools.partial(each_half, (PULL, i), pull)

    def piece(ref):
        return lambda zz, xx, r: ref[pl.ds(pl.multiple_of(512 * zz + 256 * xx + r, 64), 64)]

    of = ((piece(hp), lambda a, j: dot_t(a, wx[j].reshape(512, 896))), (piece(am), lambda a, j: dot(a, wco[:, columns(512, j)])))
    filled = []

    def fill(name, t, i):
        if len(filled) >= 2:
            sent(filled[-2])
        filled.append((t, i))
        t.fill(i, (len(filled) - 1) % 2, *of[name])

    def sent(one):
        one[0].core(one[1]).wait_send()

    def to_base(seq, rows):
        once(load_tok, lambda: load_tok().wait())
        return ctr.at[0, seq, rows]

    for name, t in enumerate((tn, to)):
        for i in range(4):
            steps[FILL, name, i] = functools.partial(fill, name, t, i)
            steps[CORE, name, i] = functools.partial(t.after_core, i, *of[name])
            for s in range(2):
                steps[LINE, name, i, s] = functools.partial(t.line, i, s)
        for s in range(2):
            steps[SPREAD, name, s] = functools.partial(t.spread, s, to_base if t is to else None)
            steps[RELAY, name, s] = functools.partial(t.spread_y, s)
            steps[DONE, name, s] = functools.partial(t.landed, s)

    def by_block(zz, xx, half):
        p = pair_at(2 * zz + xx)
        return [pick(p, lambda j: block[i, pl.ds(j if half == 0 else 15 - j, 1)]) for i in range(2)]

    cut = ORDER.index((PROJECTED,)) + 1

    def attention(ps, qkv, qt, kt, vt, gt, ot, logs, gpos, dqt, dk, dv):
        def project(zz, xx, rows, row):
            three = dot(rows[...], wx[:, :, :, pl.ds(512, 384)].reshape(2048, 384))
            for half in range(2):
                v = three[128 * half:128 * half + 128]
                t = angle_table(within, *by_block(zz, xx, half))
                at = pl.ds(row + 128 * half, 128)
                ps[at, pl.ds(0, 128)] = turn(v[:, 0:128], t).astype(BF) * BF(0.125)
                ps[at, pl.ds(128, 128)] = turn(v[:, 128:256], t).astype(BF)
                ps[at, pl.ds(256, 128)] = v[:, 256:384].astype(BF)

        def slope(zz, xx, rows, row):
            ps[pl.ds(row, 256), pl.ds(0, 128)] = dot_t(rows[...], wco[pl.ds(512, 128)]).astype(BF)

        def landed(i, kind, t, act):
            once(own_rows, own_rows)
            t.landed(far_first(z, 3 - i))
            each_half((kind, i), act)

        def own_rows():
            own_xn().wait()
            own_cot().wait()
            tx.sent_own(mine, xo)

        for i in range(4):
            steps[PROJECT, i] = functools.partial(landed, i, PROJECT, tx, project)
            steps[SLOPE, i] = functools.partial(landed, i, SLOPE, tc, slope)

        def by_position(b, cols):
            half = b // 8
            pair = b + half * (15 - 2 * b)
            return pick(slot_of(pair), lambda j: ps[pl.ds(pl.multiple_of(256 * j + 128 * half, 128), 128), cols].astype(F4))

        def by_rows(c2, half):
            p = pair_at(c2)
            return lambda ref: pick(p, lambda j: ref[pl.ds(128 * (j if half == 0 else 15 - j), 128)])

        def blocks(act):
            @pl.loop(0, 16)
            def _(b):
                act(b, pl.ds(pl.multiple_of(b * 128, 128), 128))

        def slots(act):
            for half in range(2):
                @pl.loop(0, 8)
                def _(c2):
                    act(by_rows(c2, half), pl.ds(pl.multiple_of(256 * c2 + 128 * half, 128), 128))

        def rope():
            def act(b, here):
                three = by_position(b, slice(None))
                for j, ref in enumerate((qt, kt, vt)):
                    v = three[:, 128 * j:128 * j + 128]
                    qkv[j, here] = v.astype(BF)
                    ref[:, here] = v.T.astype(BF)
            blocks(act)

        def score(i, h):
            kr = 256 * (i + 1)
            return masked(dot(qkv[1, :kr], one_head(qt[:, pl.ds(256 * i, 256)], h, 0)), kr)

        ahead = []

        def forward(i):
            kr, here = 256 * (i + 1), pl.ds(256 * i, 256)
            for h in range(2):
                st = ahead.pop() if ahead else score(0, 0)
                if (i, h) != (7, 1):
                    ahead.append(score(i + h, 1 - h))
                peak = jnp.max(st, axis=0, keepdims=True)
                p = jnp.exp(st - peak)
                total = jnp.sum(p, axis=0, keepdims=True)
                o = dot(vt[:, :kr], p.astype(BF)) * (1.0 / total)
                ot[pl.ds(64 * h, 64), here] = o[64 * h:64 * h + 64]
                logs[pl.ds(h, 1), here] = peak + jnp.log(total)

        def mix():
            def turned(b, here):
                gpos[here] = ot[:, here].T

            def placed(pos, row):
                am[row, pl.ds(512, 128)] = pos(gpos).astype(BF)
            blocks(turned)
            slots(placed)

        def gflip():
            def act(b, here):
                g = by_position(b, pl.ds(0, 128))
                gpos[here] = g
                gt[:, here] = g.T.astype(BF)
            blocks(act)
            dk[...] = jnp.zeros_like(dk)
            dv[...] = jnp.zeros_like(dv)

        def backward(i):
            kr, here = 256 * (i + 1), pl.ds(256 * i, 256)
            for h in range(2):
                p = jnp.exp(score(i, h) - logs[pl.ds(h, 1), here])
                low = p.astype(BF)
                at = pl.ds(64 * h, 64)
                delta = jnp.sum(ot[at, here] * gt[at, here].astype(F4), axis=0, keepdims=True)
                ds = (p * (dot(qkv[2, :kr], one_head(gt[:, here], h, 0)) - delta)).astype(BF)
                dv[:kr] += dot(low, one_head(gpos[here].astype(BF), h, 1))
                dk[:kr] += dot(ds, one_head(qkv[0, here], h, 1))
                dqt[at, here] = dot(kt[:, :kr], ds)[64 * h:64 * h + 64] * 0.125

        def gradients():
            def turned(b, here):
                t = angle_table(within, block[0, pl.ds(b, 1)], block[1, pl.ds(b, 1)])
                gpos[here] = turn_back(dqt[:, here].T, t)
                dk[here] = turn_back(dk[here], t)

            def placed(pos, row):
                for j, ref in enumerate((gpos, dk, dv)):
                    hp[row, pl.ds(512 + 128 * j, 128)] = pos(ref).astype(BF)
            blocks(turned)
            slots(placed)

        steps[ARRANGE,], steps[MIX,], steps[TURN,], steps[PROJECTED,] = rope, mix, gflip, gradients
        for i in range(8):
            steps[ATTEND, i] = functools.partial(forward, i)
            steps[RETURN, i] = functools.partial(backward, i)
        for name in ORDER[:cut]:
            steps[name]()

    pl.run_scoped(
        attention, V((2048, 384), BF), V((3, 2048, 128), BF), V((128, 2048), BF), V((128, 2048), BF), V((128, 2048), BF),
        V((128, 2048), BF), V((128, 2048), F4), V((8, 2048), F4), V((2048, 128), F4), V((128, 2048), F4),
        V((2048, 128), F4), V((2048, 128), F4))

    def rest_of(col, stage, sums):
        plan = [n for n in ORDER if n[0] in (GIVE, KEEP)]

        def block_load(n):
            kind, j, e = plan[n]
            src, d, xx = (ct, xn)[j], mirrored(z, e), 1 - x if kind == GIVE else x
            return pltpu.make_async_copy(src.at[:, :, :, columns(256, 2 * ((z + d) % 4) + xx)], col.at[n % 3], csem.at[n % 3])

        def grad(n):
            kind, j, e = plan[n]
            block_load(n).wait()
            terms = dot(flip(col[n % 3].reshape(2048, 256)), (am, hp)[j][...])
            g = (g1, g2)[j]
            (g.give if kind == GIVE else g.keep)(e, terms if j else terms.T)
            if n + 3 < len(plan):
                block_load(n + 3).start()

        for n in range(3):
            block_load(n).start()
        copies = [remote(vec.at[(c + i + 1) % 8], vecs.at[c], vs.at[i], vr.at[i], others[i]) for i in range(7)]

        def normed_gradient(s):
            once(load_tok, lambda: load_tok().wait())
            once(load_cot, lambda: load_cot().wait())
            if s == 0:
                sums[...] = jnp.zeros_like(sums)
            norm_backward(x if s == 0 else 1 - x, ctr.at[0], ctr.at[1], ng, gs_all, ig, stage, ssem, sums)
            if s == 0:
                return
            for i in range(8):
                at = slice(256 * i, 256 * i + 256)
                for j in range(2):
                    vec[i, j:j + 1, :] = jnp.sum(sums[j, :, at], axis=0, keepdims=True)
                vec[i, 2:8, :] = jnp.zeros((6, 256), F4)
            vecs[c] = vec[c]
            for cp in copies:
                cp.start()

        def gradients():
            g1.finish()
            g2.finish()

        steps[GRADIENTS,] = gradients
        for s in range(2):
            steps[LAST, s] = functools.partial(normed_gradient, s)
        for n, name in enumerate(plan):
            steps[name] = functools.partial(grad, n)
        for name in ORDER[cut:]:
            steps[name]()
        for i in range(7):
            frm = vecs.at[(c - i - 1 + 8) % 8]
            remote(frm, frm, vs.at[i], vr.at[i], others[i]).wait_recv()
        total = vecs[0]
        for i in range(1, 8):
            total = total + vecs[i]
        vectors[...] = total
        for cp in copies:
            cp.wait_send()

    pl.run_scoped(rest_of, V((3, 4, 2, 256, 256), BF), V((2, 32, 2048), F4), V((2, 8, 2048), F4))
    for one in filled[-2:]:
        sent(one)
    tn.finish()
    to.finish()
    tx.finish()
    tc.sent_own(cot_mine, cot_other)
    tc.finish()
    for w in range(6):
        wg.finish(w)
    for g in gcopies():
        g.wait_send()


def block_call(pairs_of, gains, tok, cot, win, wout, wexp, wcon):
    S = jax.ShapeDtypeStruct
    ANY = pl.BlockSpec(memory_space=pl.ANY)
    VM = pl.BlockSpec(memory_space=pltpu.VMEM)
    D = pltpu.SemaphoreType.DMA
    V = pltpu.VMEM
    rows = (4, 2, 256, 2048)
    return pl.pallas_call(
        block_kernel,
        out_shape=[S((2, 256, 2048), BF), S((2, 256, 2048), F4), S((8, 256), F4),
                   S((3, 256, 512), BF), S((512, 256), BF), S((256, 2048), BF), S((2048, 256), BF), S(rows, BF), S(rows, BF)],
        in_specs=[pl.BlockSpec(memory_space=pltpu.SMEM)] + [VM] * 3 + [ANY] * 6,
        out_specs=[ANY, ANY, VM] + [ANY] * 6,
        scratch_shapes=[V((4, 2, 256, 896), BF), V((640, 2048), BF), V((2048, 896), BF), V((2048, 640), BF), V((2, 2, 2, 64, 2048), BF),
                        V((2, 2, 256, 2048), BF), V((2, 256, 2048), BF), V((8, 256), F4), V((8, 8, 256), F4), V((8, 8, 256), F4), V((8, 8, 256), F4),
                        D((7,)), D((7,)), D((4,)), D((2, 2)), D((3,)), D((2,)), D((7,)), D((7,))]
        + token_sems() * 2 + weight_sems(6) + (reduce_bufs() + reduce_sems()) * 2 + grad_scratch((640, 256), 2) + grad_scratch((256, 896), 4),
        compiler_params=pltpu.CompilerParams(collective_id=0, has_side_effects=True, vmem_limit_bytes=63 * MB),
        name="block",
    )(pairs_of, gains, jnp.asarray(angles(128, 1)), jnp.asarray(angles(16, 128)), tok, cot, win, wout, wexp, wcon)


def finish_kernel(out, ig, gin, gout, gexp, gcon, out_to, ig_to, gin_to, gout_to, gexp_to, gcon_to,
                  vin, vout, vexp, vcon, fin, fout, fexp, fcon, through, wide, isem, osem):
    work = ((gexp, vexp, fexp, gexp_to), (gcon, vcon, fcon, gcon_to), (gin, vin, fin, gin_to), (gout, vout, fout, gout_to),
            (ig, wide, wide, ig_to), (out, through, through, out_to))
    loads = [pltpu.make_async_copy(w[0], w[1], isem.at[i]) for i, w in enumerate(work)]
    stores = [pltpu.make_async_copy(w[2], w[3], osem.at[i]) for i, w in enumerate(work)]
    for copy in loads:
        copy.start()
    for (_, low, full, _), load, store in zip(work, loads, stores):
        load.wait()
        if low is not full:
            rows = low.shape[-2]
            for j in range(low.shape[0] if len(low.shape) == 3 else 1):
                @pl.loop(0, rows // 128)
                def _(i):
                    at = (pl.ds(pl.multiple_of(128 * i, 128), 128),)
                    at = (j,) + at if len(low.shape) == 3 else at
                    full[at] = low[at].astype(F4)
        store.start()
    for copy in stores:
        copy.wait()


def finish_call(out, ig, *grads):
    S = jax.ShapeDtypeStruct
    ANY = pl.BlockSpec(memory_space=pl.ANY)
    D = pltpu.SemaphoreType.DMA
    V = pltpu.VMEM
    shapes = [g.shape for g in grads]
    return pl.pallas_call(
        finish_kernel,
        out_shape=[S(out.shape, BF), S(ig.shape, F4)] + [S(s, F4) for s in shapes],
        in_specs=[ANY] * 6,
        out_specs=[ANY] * 6,
        scratch_shapes=[V(s, BF) for s in shapes] + [V(s, F4) for s in shapes] + [V(out.shape, BF), V(ig.shape, F4), D((6,)), D((6,))],
        compiler_params=pltpu.CompilerParams(vmem_limit_bytes=60 * MB),
        name="finish",
    )(out, ig, *grads)


def own_local(tokens, pair_index, norm_gain, norm_shift, w_attention_in, w_attention_out, w_expand, w_contract, cotangent):
    gains = jnp.stack([norm_gain, norm_shift]).astype(F4)
    output, input_grad, vectors, *grads = block_call(
        pair_index, gains, tokens, cotangent, w_attention_in, w_attention_out, w_expand, w_contract)
    output, input_grad, *grads = finish_call(output, input_grad, *grads[:4])
    return (output, input_grad, vectors[0], vectors[1], *grads)


def local(tokens, pair_index, norm_gain, norm_shift, w_attention_in, w_attention_out, w_expand, w_contract, cotangent):
    args = (tokens, pair_index, norm_gain, norm_shift, w_attention_in, w_attention_out, w_expand, w_contract, cotangent)
    sizes = (lax.axis_size("ctx"), lax.axis_size("tp")) + tokens.shape + w_attention_in.shape[2:] + w_expand.shape[1:]
    if sizes == (8, 4, 2, 256, 2048, 512, 2048):
        return own_local(*args)
    return general_local(*args)


def solution(mesh):
    in_specs = (
        P(None, "ctx", None),
        P(),
        P("ctx"),
        P("ctx"),
        P(None, "ctx", "tp"),
        P("tp", "ctx"),
        P("ctx", "tp"),
        P("tp", "ctx"),
        P(None, "ctx", None),
    )
    out_specs = (
        P(None, "ctx", None),
        P(None, "ctx", None),
        P("ctx"),
        P("ctx"),
        P(None, "ctx", "tp"),
        P("tp", "ctx"),
        P("ctx", "tp"),
        P("tp", "ctx"),
    )
    return jax.shard_map(local, mesh=mesh, in_specs=in_specs, out_specs=out_specs, check_vma=False)
```
